32 devices in a mesh: dp: 8 (over z, core), replica: 4 (over y, x).
Axes of the slice: x: 2, y: 2, z: 4, core: 2. Of those that a mesh axis runs over, the one named last changes fastest.
Arguments:
- images: bfloat16 [64, 3, 32, 32], P(('dp', 'replica')), may hold values from -6 to 6
- labels: int32 [64], P(('dp', 'replica')), may hold values from 0 to 9
- counts: int32 [32], P(('dp', 'replica')), may hold values from 1 to 2, as said below
- noise_table: float32 [64, 10], replicated, may hold values from -4 to 4
- noise_index: int32 [64, 10], P(('dp', 'replica')), may hold values from 0 to 63
- power_start: float32 [2, 640], replicated, may hold values from -5 to 5
- conv_weight: float32 [7372800], P(('dp', 'replica')), may hold values from -0.078125 to 0.078125
- conv_first: float32 [7372800], P(('dp', 'replica')), may hold values from -0.00061035156 to 0.00061035156
- conv_second: float32 [7372800], P(('dp', 'replica')), may hold values from 1.40625e-10 to 5.625e-10
- stem_weight: float32 [27, 640], replicated, may hold values from -1.25 to 1.25
- stem_first: float32 [27, 640], replicated, may hold values from -0.00010681152 to 0.00010681152
- stem_second: float32 [27, 640], replicated, may hold values from 3.90625e-12 to 1.5625e-11
- norm_params: float32 [4, 640], replicated, may hold values from -0.6 to 1.4, as said below
- norm_first: float32 [4, 640], replicated, may hold values from -0.00390625 to 0.00390625
- norm_second: float32 [4, 640], replicated, may hold values from 6.25e-09 to 2.5e-08
- inducing: float32 [20, 640], replicated, may hold values from -3 to 3
- inducing_first: float32 [20, 640], replicated, may hold values from -0.0012207031 to 0.0012207031
- inducing_second: float32 [20, 640], replicated, may hold values from 5.625e-10 to 2.25e-09
- lengthscale: float32 [640], replicated, may hold values from 4 to 10
- length_first: float32 [640], replicated, may hold values from -0.0004272461 to 0.0004272461
- length_second: float32 [640], replicated, may hold values from 6.25e-11 to 2.5e-10
- var_mean: float32 [10, 20], replicated, may hold values from -4 to 4
- mean_first: float32 [10, 20], replicated, may hold values from -0.0390625 to 0.0390625
- mean_second: float32 [10, 20], replicated, may hold values from 5.493164e-07 to 2.1972655e-06
- var_lower: float32 [10, 20, 20], replicated, may hold values from -3 to 3
- lower_first: float32 [10, 20, 20], replicated, may hold values from -0.013671875 to 0.013671875
- lower_second: float32 [10, 20, 20], replicated, may hold values from 6.103516e-08 to 2.4414064e-07
Outputs:
- loss_parts: float32 [2], replicated
- new_conv: float32 [7372800], P(('dp', 'replica'))
- new_conv_first: float32 [7372800], P(('dp', 'replica'))
- new_conv_second: float32 [7372800], P(('dp', 'replica'))
- conv_copy: bfloat16 [7372800], P(('dp', 'replica'))
- new_stem: float32 [27, 640], replicated
- new_stem_first: float32 [27, 640], replicated
- new_stem_second: float32 [27, 640], replicated
- new_norms: float32 [4, 640], replicated
- new_norm_first: float32 [4, 640], replicated
- new_norm_second: float32 [4, 640], replicated
- new_inducing: float32 [20, 640], replicated
- new_inducing_first: float32 [20, 640], replicated
- new_inducing_second: float32 [20, 640], replicated
- new_length: float32 [640], replicated
- new_length_first: float32 [640], replicated
- new_length_second: float32 [640], replicated
- new_mean: float32 [10, 20], replicated
- new_mean_first: float32 [10, 20], replicated
- new_mean_second: float32 [10, 20], replicated
- new_lower: float32 [10, 20, 20], replicated
- new_lower_first: float32 [10, 20, 20], replicated
- new_lower_second: float32 [10, 20, 20], replicated
- spectral_norms: float32 [2], replicated
- rms_values: float32 [2], replicated
The draws below stay inside these ranges and needn't reach their ends.
Inputs may be any that keep to these rules, and one draw needn't show every extreme that they name: Device d holds images in its first counts[d] slots; some device fills all 2 slots and some device holds a single image. `norm_params`: rows 0 and 2 are gains, rows 1 and 3 biases.
All inputs are finite; a program needn't handle non-finite values.
Results may differ from the reference program's by a relative error of at most 0.0047.
The reference program's roundings to bfloat16 on the way count: a program that leaves them out, or rounds other values in their place, can miss the bound.
Values may be sent and summed in bfloat16 or wider, within the bound.
A program may use at most 320 MiB of HBM per device.

```python
import math
import jax
import jax.numpy as jnp
from jax import lax

C = 640
CLASSES = 10
INDUCING = 20
CIN = 3
SIDE = 32
SAMPLES = 10
POOL = 64
STEP = 10
IMG_DEV = 2
IMAGES = 64
TOTAL = 7372800
DEVICES = 32


def draw_counts(key, part):
    key = jax.random.fold_in(key, 11)
    key_one, key_two = jax.random.split(key)
    drawn_counts = jax.random.randint(key_one, (DEVICES,), 1, IMG_DEV + 1)
    ordering = jax.random.permutation(key_two, DEVICES)
    drawn_counts = drawn_counts.at[ordering[0]].set(IMG_DEV)
    drawn_counts = drawn_counts.at[ordering[1]].set(1)
    return drawn_counts.astype(jnp.int32)


def draw_norm_params(key, part):
    key = jax.random.fold_in(key, 23)
    gain_values = jax.random.uniform(key, (4, C), jnp.float32, 0.6, 1.4)
    bias_values = jax.random.uniform(jax.random.fold_in(key, 5), (4, C), jnp.float32, -0.6, 0.6)
    gain_rows = (jnp.arange(4) % 2 == 0)[:, None]
    return jnp.where(gain_rows, gain_values, bias_values)


def place_ends(entries, key, smallest, high):
    dims = entries.shape
    spot = [jax.random.randint(jax.random.fold_in(key, axis), (), 0, dims[axis]) for axis in range(len(dims))]
    entries = entries.at[tuple(spot)].set(smallest)
    longest = dims.index(max(dims))
    spot[longest] = (spot[longest] + 1) % dims[longest]
    return entries.at[tuple(spot)].set(high)


def levels(own_key, shape, shards, smallest, high):
    level = 1.0
    for dim, shards_of in shards:
        steps = jax.random.uniform(jax.random.fold_in(jax.random.fold_in(own_key, 6), dim), (shards_of,), jnp.float32, smallest / len(shards), high / len(shards))
        level = level * jnp.repeat(jnp.exp(steps), shape[dim] // shards_of).reshape((-1,) + (1,) * (len(shape) - 1 - dim))
    return level


def gaussian(stream_key, dims, width, most, shards=(), kind=jnp.bfloat16):
    entries = jax.random.normal(stream_key, dims, jnp.float32) * width
    if len(shards) > 0:
        entries = levels(stream_key, dims, shards, -0.22, 0.18) * entries
    return jnp.clip(entries, min=-most, max=most).astype(kind)


def setup_inputs(seed: int = 0) -> dict:
    streams_of = jax.random.split(jax.random.key(seed), 28)
    return {
        "images": gaussian(streams_of[0], (IMAGES, CIN, SIDE, SIDE), 1.0, 6.0, ((0, 32),)),
        "labels": place_ends(jax.random.randint(streams_of[1], (IMAGES,), 0, CLASSES), jax.random.fold_in(streams_of[1], 1), 0, CLASSES - 1).astype(jnp.int32),
        "counts": draw_counts(jax.random.fold_in(streams_of[27], 71), 0),
        "noise_table": gaussian(streams_of[3], (POOL, CLASSES), 1.0, 4.0, (), jnp.float32),
        "noise_index": place_ends(jax.random.randint(streams_of[4], (IMAGES, SAMPLES), 0, POOL), jax.random.fold_in(streams_of[4], 1), 0, POOL - 1).astype(jnp.int32),
        "power_start": gaussian(streams_of[5], (2, C), 1.0, 5.0, (), jnp.float32),
        "conv_weight": gaussian(streams_of[6], (TOTAL,), (9 * C) ** -0.5, 0.078125, ((0, 32),), jnp.float32),
        "conv_first": gaussian(streams_of[7], (TOTAL,), (0.11 * 0.003 / (DEVICES * IMG_DEV) ** 0.5), 0.00061035156, ((0, 32),), jnp.float32),
        "conv_second": jnp.clip(jnp.exp(math.log(5.624999910303075e-10) - 1.3862944 * jax.random.uniform(streams_of[8], (TOTAL,), jnp.float32) ** levels(streams_of[8], (TOTAL,), ((0, 32),), -0.2, 0.2)), 1.4062499775757686e-10, 5.624999910303075e-10),
        "stem_weight": gaussian(streams_of[9], (9 * CIN, C), (9 * CIN) ** -0.5, 1.25, (), jnp.float32),
        "stem_first": gaussian(streams_of[10], (9 * CIN, C), (0.11 * 0.0005 / (DEVICES * IMG_DEV) ** 0.5), 0.00010681152, (), jnp.float32),
        "stem_second": jnp.clip(jnp.exp(jax.random.uniform(streams_of[11], (9 * CIN, C), jnp.float32, math.log(3.906249889523705e-12), math.log(1.562499955809482e-11))), 3.906249889523705e-12, 1.562499955809482e-11),
        "norm_params": draw_norm_params(jax.random.fold_in(streams_of[27], 71), 0),
        "norm_first": gaussian(streams_of[13], (4, C), (0.11 * 0.02 / (DEVICES * IMG_DEV) ** 0.5), 0.00390625, (), jnp.float32),
        "norm_second": jnp.clip(jnp.exp(jax.random.uniform(streams_of[14], (4, C), jnp.float32, math.log(6.250000073038109e-09), math.log(2.5000000292152436e-08))), 6.250000073038109e-09, 2.5000000292152436e-08),
        "inducing": gaussian(streams_of[15], (INDUCING, C), 0.3, 3.0, (), jnp.float32),
        "inducing_first": gaussian(streams_of[16], (INDUCING, C), (0.11 * 0.006 / (DEVICES * IMG_DEV) ** 0.5), 0.0012207031, (), jnp.float32),
        "inducing_second": jnp.clip(jnp.exp(jax.random.uniform(streams_of[17], (INDUCING, C), jnp.float32, math.log(5.624999910303075e-10), math.log(2.24999996412123e-09))), 5.624999910303075e-10, 2.24999996412123e-09),
        "lengthscale": jnp.clip(jnp.exp(jax.random.uniform(streams_of[18], (C,), jnp.float32, math.log(4.0), math.log(10.0))), 4.0, 10.0),
        "length_first": gaussian(streams_of[19], (C,), (0.11 * 0.002 / (DEVICES * IMG_DEV) ** 0.5), 0.0004272461, (), jnp.float32),
        "length_second": jnp.clip(jnp.exp(jax.random.uniform(streams_of[20], (C,), jnp.float32, math.log(6.249999823237928e-11), math.log(2.4999999292951713e-10))), 6.249999823237928e-11, 2.4999999292951713e-10),
        "var_mean": gaussian(streams_of[21], (CLASSES, INDUCING), 1.0, 4.0, (), jnp.float32),
        "mean_first": gaussian(streams_of[22], (CLASSES, INDUCING), (0.11 * 1.5 / (DEVICES * IMG_DEV)), 0.0390625, (), jnp.float32),
        "mean_second": jnp.clip(jnp.exp(jax.random.uniform(streams_of[23], (CLASSES, INDUCING), jnp.float32, math.log(5.493163826031378e-07), math.log(2.197265530412551e-06))), 5.493163826031378e-07, 2.197265530412551e-06),
        "var_lower": gaussian(streams_of[24], (CLASSES, INDUCING, INDUCING), 0.3, 3.0, (), jnp.float32),
        "lower_first": gaussian(streams_of[25], (CLASSES, INDUCING, INDUCING), (0.11 * 0.5 / (DEVICES * IMG_DEV)), 0.013671875, (), jnp.float32),
        "lower_second": jnp.clip(jnp.exp(jax.random.uniform(streams_of[26], (CLASSES, INDUCING, INDUCING), jnp.float32, math.log(6.103515914901436e-08), math.log(2.4414063659605745e-07))), 6.103515914901436e-08, 2.4414063659605745e-07),
    }


HIGH = lax.Precision.HIGHEST
EPS_NORM = 1e-05
JITTER = 0.001
BETA_ONE = 0.9
BETA_TWO = 0.999
RATE = 0.3
DECAY = 0.01
EPS_ADAM = 1e-08

@jax.custom_vjp
def low(v):
    return lax.optimization_barrier(v.astype(jnp.bfloat16)).astype(jnp.float32)

@jax.custom_vjp
def low_back(v):
    return v

def low_keep(v):
    return (low(v), None)

def low_pass(kept, grad):
    return (grad,)

def back_keep(v):
    return (v, None)

def back_low(kept, grad):
    return (low(grad),)
low.defvjp(low_keep, low_pass)
low_back.defvjp(back_keep, back_low)

def conv_taps(values, kernel):
    side = values.shape[1]
    padded = jnp.pad(values, ((0, 0), (1, 1), (1, 1), (0, 0)))
    result = jnp.zeros(values.shape[:3] + (kernel.shape[2],), jnp.float32)
    for position in range(9):
        down_by, right_by = (position // 3, position % 3)
        window = padded[:, down_by:down_by + side, right_by:right_by + side]
        result = result + jnp.einsum('nhwc,cd->nhwd', window, kernel[position], precision=HIGH)
    return result

def spectral(kernel, start_vector):
    matrix = kernel.reshape(-1, kernel.shape[-1])
    right_vec = jnp.dot(matrix, start_vector, precision=HIGH)
    right_vec = right_vec / jnp.sqrt(jnp.sum(right_vec * right_vec))
    image_vec = jnp.dot(right_vec, matrix, precision=HIGH)
    left_vec = image_vec / jnp.sqrt(jnp.sum(image_vec * image_vec))
    return jnp.dot(left_vec, image_vec, precision=HIGH)

def batch_norm(values, gain, bias, valid, pixels):
    average = lax.optimization_barrier(jnp.sum(values * valid, axis=(0, 1, 2))) / pixels
    centred = values - average
    variance = lax.optimization_barrier(jnp.sum(centred * centred * valid, axis=(0, 1, 2))) / pixels
    return centred * lax.rsqrt(variance + EPS_NORM) * gain + bias

def kernel_rbf(left_pts, right_pts):
    offsets = left_pts[:, None, :] - right_pts[None, :, :]
    return jnp.exp(-0.5 * lax.optimization_barrier(jnp.sum(offsets * offsets, axis=-1)))

def lower_solve(factor, rhs):
    solved = []
    for position in range(factor.shape[0]):
        remainder = rhs[position]
        for earlier in range(position):
            remainder = remainder - factor[position, earlier] * solved[earlier]
        solved.append(remainder / factor[position, position])
    return jnp.stack(solved)

def scale_factor(var_lower):
    identity = jnp.eye(var_lower.shape[1], dtype=jnp.float32)
    diagonal = jnp.diagonal(var_lower, 0, 1, 2)
    return jnp.tril(var_lower, -1) + identity[None] * jnp.exp(diagonal)[:, :, None]

def data_term(pooled, inducing, lengthscale, var_mean, var_lower, noise_draws, labels, slot_mask):
    scaled_x = pooled / lengthscale
    scaled_z = inducing / lengthscale
    size_m = inducing.shape[0]
    factor = jnp.linalg.cholesky(kernel_rbf(scaled_z, scaled_z) + JITTER * jnp.eye(size_m, dtype=jnp.float32))
    project = lower_solve(factor, kernel_rbf(scaled_z, scaled_x))
    average = jnp.dot(project.T, var_mean.T, precision=HIGH)
    spread = jnp.einsum('kji,jn->kin', scale_factor(var_lower), project, precision=HIGH)
    variance = 1.0 - lax.optimization_barrier(jnp.sum(project * project, axis=0))[:, None] + lax.optimization_barrier(jnp.sum(spread * spread, axis=1)).T
    samples = average[:, None, :] + jnp.sqrt(variance)[:, None, :] * noise_draws
    largest = lax.optimization_barrier(jnp.max(samples, axis=-1, keepdims=True))
    log_prob = samples - largest - jnp.log(lax.optimization_barrier(jnp.sum(jnp.exp(samples - largest), axis=-1, keepdims=True)))
    picked = lax.optimization_barrier(jnp.sum(log_prob * jax.nn.one_hot(labels, var_mean.shape[0], dtype=jnp.float32)[:, None, :], axis=-1))
    return -jnp.sum(slot_mask * lax.optimization_barrier(jnp.mean(picked, axis=1)))

def kl_term(var_mean, var_lower):
    factor = scale_factor(var_lower)
    diagonal = jnp.diagonal(var_lower, 0, 1, 2)
    return 0.5 * jnp.sum(factor * factor) + 0.5 * jnp.sum(var_mean * var_mean) - 0.5 * var_mean.shape[0] * var_mean.shape[1] - jnp.sum(diagonal)

def lamb_moments(weight, gradient, moment_one, moment_two):
    new_one = BETA_ONE * moment_one + (1.0 - BETA_ONE) * gradient
    new_two = BETA_TWO * moment_two + (1.0 - BETA_TWO) * gradient * gradient
    direction = new_one / (1.0 - BETA_ONE ** STEP) / (jnp.sqrt(new_two / (1.0 - BETA_TWO ** STEP)) + EPS_ADAM) + DECAY * weight
    return (new_one, new_two, direction)

def lamb_update(weight, gradient, moment_one, moment_two, groups):
    new_one, new_two, direction = lamb_moments(weight, gradient, moment_one, moment_two)
    flat_weight = weight.reshape(groups, -1)
    flat_step = direction.reshape(groups, -1)
    trust_ratio = jnp.sqrt(lax.optimization_barrier(jnp.sum(flat_weight * flat_weight, axis=1))) / jnp.sqrt(lax.optimization_barrier(jnp.sum(flat_step * flat_step, axis=1)))
    new_weight = (flat_weight - RATE * trust_ratio[:, None] * flat_step).reshape(weight.shape)
    return (new_weight, new_one, new_two)

def forward(params, pictures, labels, slot_mask, noise_draws, totals, power_start):
    conv_weight, stem_weight, norm_params, inducing, lengthscale, var_mean, var_lower = params
    kernels = low(conv_weight).reshape(2, 9, C, C)
    sigma_one = spectral(kernels[0], power_start[0])
    sigma_two = spectral(kernels[1], power_start[1])
    kernel_one = low(kernels[0] / sigma_one)
    kernel_two = low(kernels[1] / sigma_two)
    pixels = totals * (SIDE * SIDE)
    valid = slot_mask[:, None, None, None]
    stem_out = low_back(conv_taps(pictures, low(stem_weight).reshape(9, CIN, C)))
    act_one = low(jax.nn.gelu(batch_norm(stem_out, norm_params[0], norm_params[1], valid, pixels)))
    branch_one = low_back(conv_taps(act_one, kernel_one))
    act_two = low(jax.nn.gelu(batch_norm(branch_one, norm_params[2], norm_params[3], valid, pixels)))
    branch_two = low_back(conv_taps(act_two, kernel_two))
    output = stem_out + branch_two
    pooled = lax.optimization_barrier(jnp.mean(output, axis=(1, 2)))
    loss_sum = data_term(pooled, inducing, lengthscale, var_mean, var_lower, noise_draws, labels, slot_mask) + kl_term(var_mean, var_lower)
    rms_values = jnp.stack([jnp.sqrt(jnp.sum(valid * stem_out * stem_out) / (pixels * C)), jnp.sqrt(jnp.sum(valid * branch_two * branch_two) / (pixels * C))])
    return (loss_sum / totals, (loss_sum, jnp.stack([sigma_one, sigma_two]), rms_values))

def reference(images, labels, counts, noise_table, noise_index, power_start, conv_weight, conv_first, conv_second, stem_weight, stem_first, stem_second, norm_params, norm_first, norm_second, inducing, inducing_first, inducing_second, lengthscale, length_first, length_second, var_mean, mean_first, mean_second, var_lower, lower_first, lower_second):
    slot_mask = (jnp.arange(IMG_DEV)[None, :] < counts[:, None]).astype(jnp.float32).reshape(-1)
    totals = jnp.sum(counts).astype(jnp.float32)
    pictures = jnp.transpose(images.astype(jnp.float32), (0, 2, 3, 1))
    noise_draws = noise_table[noise_index]
    params = (conv_weight, stem_weight, norm_params, inducing, lengthscale, var_mean, var_lower)

    def loss_of(*values):
        return forward(values, pictures, labels, slot_mask, noise_draws, totals, power_start)
    loss_value, back_fn, extras = jax.vjp(loss_of, *params, has_aux=True)
    grads = back_fn(jnp.ones((), jnp.float32))
    loss_sum, sigmas, rms_values = extras
    conv_new = lamb_update(conv_weight, grads[0], conv_first, conv_second, 2)
    stem_new = lamb_update(stem_weight, grads[1], stem_first, stem_second, 1)
    norm_new = lamb_update(norm_params, grads[2], norm_first, norm_second, 4)
    inducing_new = lamb_update(inducing, grads[3], inducing_first, inducing_second, 1)
    length_new = lamb_update(lengthscale, grads[4], length_first, length_second, 1)
    mean_new = lamb_update(var_mean, grads[5], mean_first, mean_second, 1)
    lower_new = lamb_update(var_lower, grads[6], lower_first, lower_second, 1)
    return (jnp.stack([loss_sum, totals]), conv_new[0], conv_new[1], conv_new[2], conv_new[0].astype(jnp.bfloat16), stem_new[0], stem_new[1], stem_new[2], norm_new[0], norm_new[1], norm_new[2], inducing_new[0], inducing_new[1], inducing_new[2], length_new[0], length_new[1], length_new[2], mean_new[0], mean_new[1], mean_new[2], lower_new[0], lower_new[1], lower_new[2], sigmas, rms_values)
```

```python
import functools

import jax
import jax.numpy as jnp
from jax import lax
from jax.experimental import pallas as pl
from jax.experimental.pallas import tpu as pltpu
from jax.sharding import PartitionSpec as P

STEP = 10
HIGH = lax.Precision.HIGHEST
EPS_NORM = 1e-05
JITTER = 0.001
BETA_ONE = 0.9
BETA_TWO = 0.999
RATE = 0.3
DECAY = 0.01
EPS_ADAM = 1e-08
AXES = ("dp", "replica")


def conv_full(values, kernel):
    return lax.conv_general_dilated(
        values,
        kernel.reshape(3, 3, *kernel.shape[1:]),
        (1, 1),
        ((1, 1), (1, 1)),
        dimension_numbers=("NHWC", "HWIO", "NHWC"),
        preferred_element_type=jnp.float32,
    )


def taps_grad(values, gradient):
    out = lax.conv_general_dilated(
        values,
        gradient,
        (1, 1),
        ((1, 1), (1, 1)),
        dimension_numbers=("CHWN", "IHWO", "HWNC"),
        preferred_element_type=jnp.float32,
    )
    return out.reshape(9, out.shape[2], out.shape[3])


def scale_factor(var_lower):
    identity = jnp.eye(var_lower.shape[1], dtype=jnp.float32)
    diagonal = jnp.diagonal(var_lower, 0, 1, 2)
    return jnp.tril(var_lower, -1) + identity[None] * jnp.exp(diagonal)[:, :, None]


def kl_term(var_mean, var_lower):
    factor = scale_factor(var_lower)
    diagonal = jnp.diagonal(var_lower, 0, 1, 2)
    return (
        0.5 * jnp.sum(factor * factor)
        + 0.5 * jnp.sum(var_mean * var_mean)
        - 0.5 * var_mean.shape[0] * var_mean.shape[1]
        - jnp.sum(diagonal)
    )


def lamb_moments(weight, gradient, moment_one, moment_two):
    new_one = BETA_ONE * moment_one + (1.0 - BETA_ONE) * gradient
    new_two = BETA_TWO * moment_two + (1.0 - BETA_TWO) * gradient * gradient
    direction = (
        new_one / (1.0 - BETA_ONE**STEP) / (jnp.sqrt(new_two / (1.0 - BETA_TWO**STEP)) + EPS_ADAM)
        + DECAY * weight
    )
    return (new_one, new_two, direction)


def lamb_update(weight, gradient, moment_one, moment_two, groups):
    new_one, new_two, direction = lamb_moments(weight, gradient, moment_one, moment_two)
    flat_weight = weight.reshape(groups, -1)
    flat_step = direction.reshape(groups, -1)
    trust_ratio = jnp.sqrt(jnp.sum(flat_weight * flat_weight, axis=1)) / jnp.sqrt(
        jnp.sum(flat_step * flat_step, axis=1)
    )
    new_weight = (flat_weight - RATE * trust_ratio[:, None] * flat_step).reshape(weight.shape)
    return (new_weight, new_one, new_two)


def local_moments(values, valid, local_cells):
    average = jnp.sum(values * valid, axis=(0, 1, 2)) / local_cells
    centred = (values - average) * valid
    return average, jnp.sum(centred * centred, axis=(0, 1, 2))


def joined_moments(average, spread, local_cells):
    averages, spreads, cells = lax.all_gather((average, spread, local_cells), AXES)
    pixels = jnp.sum(cells)
    whole = jnp.sum(averages * cells[:, None], axis=0) / pixels
    offsets = averages - whole
    squares = jnp.sum(spreads + cells[:, None] * offsets * offsets, axis=0)
    return whole, lax.rsqrt(squares / pixels + EPS_NORM), pixels


def gelu_back(pre, grad):
    return jax.vjp(jax.nn.gelu, pre)[1](grad)[0]


def window_sums(act):
    act = act.astype(jnp.float32)
    side = act.shape[1]
    total = jnp.sum(act, axis=(1, 2))
    row = {0: jnp.sum(act[:, side - 1], axis=1), 1: 0.0, 2: jnp.sum(act[:, 0], axis=1)}
    col = {0: jnp.sum(act[:, :, side - 1], axis=1), 1: 0.0, 2: jnp.sum(act[:, :, 0], axis=1)}
    edge = {0: side - 1, 2: 0}
    taps = []
    for r in range(3):
        for c in range(3):
            corner = act[:, edge[r], edge[c]] if r != 1 and c != 1 else 0.0
            taps.append(total - row[r] - col[c] + corner)
    return jnp.stack(taps, axis=1)


def spread_back(taps_back, side):
    grid = taps_back.reshape(taps_back.shape[0], 3, 3, -1)

    def edges(x, axis):
        x = jnp.moveaxis(x, axis, 0)
        low, mid, high = x[0] + x[1], x[0] + x[1] + x[2], x[1] + x[2]
        middle = jnp.broadcast_to(mid[None], (side - 2,) + mid.shape)
        return jnp.moveaxis(jnp.concatenate([low[None], middle, high[None]]), 0, axis)

    return edges(edges(grid, 1), 2)


def head_prepare(inducing, lengthscale):
    scaled_z = inducing / lengthscale
    offsets = scaled_z[:, None, :] - scaled_z[None, :, :]
    kzz = jnp.exp(-0.5 * jnp.sum(offsets * offsets, axis=-1))
    size = inducing.shape[0]
    factor = jnp.linalg.cholesky(kzz + JITTER * jnp.eye(size, dtype=jnp.float32))
    inverse = lax.linalg.triangular_solve(
        factor, jnp.eye(size, dtype=jnp.float32), left_side=True, lower=True
    )
    return scaled_z, kzz, factor, inverse


def head_local(pooled, scaled_z, inverse, lengthscale, var_mean, factors, noise, labels, mask, scale):
    scaled_x = pooled / lengthscale
    offsets = scaled_z[:, None, :] - scaled_x[None, :, :]
    kzx = jnp.exp(-0.5 * jnp.sum(offsets * offsets, axis=-1))
    proj = jnp.dot(inverse, kzx, precision=HIGH)
    average = jnp.dot(proj.T, var_mean.T, precision=HIGH)
    spread = jnp.einsum("cji,jn->cin", factors, proj, precision=HIGH)
    variance = 1.0 - jnp.sum(proj * proj, axis=0)[:, None] + jnp.sum(spread * spread, axis=1).T
    std = jnp.sqrt(variance)
    samples = average[:, None, :] + std[:, None, :] * noise
    shifted = samples - jnp.max(samples, axis=-1, keepdims=True)
    exps = jnp.exp(shifted)
    sums = jnp.sum(exps, axis=-1, keepdims=True)
    hot = jax.nn.one_hot(labels, var_mean.shape[0], dtype=jnp.float32)[:, None, :]
    picked = jnp.sum((shifted - jnp.log(sums)) * hot, axis=-1)
    loss = -jnp.sum(mask * jnp.mean(picked, axis=1))
    g_samples = (exps / sums - hot) * (mask * (scale / noise.shape[1]))[:, None, None]
    g_avg = jnp.sum(g_samples, axis=1)
    g_var = 0.5 * jnp.sum(g_samples * noise, axis=1) / std
    g_spread = 2.0 * spread * g_var.T[:, None, :]
    g_proj = (
        jnp.dot(var_mean.T, g_avg.T, precision=HIGH)
        - 2.0 * proj * jnp.sum(g_var, axis=1)
        + jnp.einsum("cji,cin->jn", factors, g_spread, precision=HIGH)
    )
    g_mean = jnp.dot(g_avg.T, proj.T, precision=HIGH)
    g_factors = jnp.einsum("jn,cin->cji", proj, g_spread, precision=HIGH)
    g_kzx = jnp.dot(inverse.T, g_proj, precision=HIGH)
    g_chol = -jnp.tril(jnp.dot(g_kzx, proj.T, precision=HIGH))
    weights = -kzx * g_kzx
    g_x = -jnp.sum(weights[:, :, None] * offsets, axis=0)
    g_z = jnp.sum(weights[:, :, None] * offsets, axis=1)
    return loss, g_x / lengthscale, jnp.sum(g_x * scaled_x, axis=0), g_z, g_chol, g_mean, g_factors


def head_finish(scaled_z, kzz, factor, inverse, lengthscale, g_zx, g_xx, g_chol):
    lower = jnp.dot(factor.T, g_chol, precision=HIGH)
    phi = jnp.tril(lower) - 0.5 * jnp.diag(jnp.diagonal(lower))
    back = jnp.dot(inverse.T, jnp.dot(phi, inverse, precision=HIGH), precision=HIGH)
    weights = -0.5 * kzz * (back + back.T)
    g_z = g_zx + 2.0 * (
        scaled_z * jnp.sum(weights, axis=1)[:, None] - jnp.dot(weights, scaled_z, precision=HIGH)
    )
    return g_z / lengthscale, -(g_xx + jnp.sum(g_z * scaled_z, axis=0)) / lengthscale


MESH = pl.DeviceIdType.MESH
ANY = pl.BlockSpec(memory_space=pl.ANY)
VMEM = pl.BlockSpec(memory_space=pltpu.VMEM)
SMEM = pl.BlockSpec(memory_space=pltpu.SMEM)
F32 = jnp.float32
BF16 = jnp.bfloat16


def remote(src, dst, send, recv, where):
    return pltpu.make_async_remote_copy(
        src_ref=src, dst_ref=dst, send_sem=send, recv_sem=recv,
        device_id=where, device_id_type=MESH,
    )


def greet(n_dp, n_rep):
    dp, rep = lax.axis_index("dp"), lax.axis_index("replica")
    barrier = pltpu.get_barrier_semaphore()
    for j in range(1, n_dp):
        pl.semaphore_signal(
            barrier, inc=1, device_id={"dp": lax.rem(dp + j, n_dp)}, device_id_type=MESH
        )
    for j in range(1, n_rep):
        pl.semaphore_signal(
            barrier, inc=1, device_id={"replica": lax.rem(rep + j, n_rep)}, device_id_type=MESH
        )
    pl.semaphore_wait(barrier, n_dp + n_rep - 2)


class Spread:
    def __init__(self, axis, size, src, dst, send, recv):
        self.axis, self.size, self.src, self.dst, self.send, self.recv = axis, size, src, dst, send, recv
        self.me = lax.axis_index(axis)

    def copies(self):
        for j in range(1, self.size):
            yield remote(
                self.src, self.dst.at[self.me], self.send.at[j], self.recv.at[j],
                {self.axis: lax.rem(self.me + j, self.size)},
            )

    def start(self):
        for copy in self.copies():
            copy.start()

    def wait(self):
        for j in range(1, self.size):
            source = lax.rem(self.me + self.size - j, self.size)
            remote(
                self.src, self.dst.at[source], self.send.at[j], self.recv.at[j],
                {self.axis: source},
            ).wait_recv()

    def drain(self):
        for copy in self.copies():
            copy.wait_send()


def rows_of(refs, row):
    return [refs[i, row : row + 1, :] for i in range(refs.shape[0])]


def total(values):
    result = values[0]
    for value in values[1:]:
        result = result + value
    return result


def join_moments(refs):
    averages, squares, counts = rows_of(refs, 0), rows_of(refs, 1), rows_of(refs, 2)
    count = total(counts)
    average = total([a * n for a, n in zip(averages, counts)]) / count
    spread = total(
        [s + n * (a - average) * (a - average) for a, s, n in zip(averages, squares, counts)]
    )
    return average, spread, count


def hdot(a, b, dims=((1,), (0,))):
    return lax.dot_general(
        a, b, (dims, ((), ())), precision=HIGH, preferred_element_type=F32
    )


def bdot(a, b, dims=((1,), (0,))):
    return lax.dot_general(a, b, (dims, ((), ())), preferred_element_type=F32)


class Gather:
    def __init__(self, which, n_dp, n_rep, share, pieces, buffer, sems):
        self.which, self.n_dp, self.n_rep, self.share = which, n_dp, n_rep, share
        self.pieces, self.buffer = pieces, buffer
        self.z_send, self.z_recv, self.r_send, self.r_recv, self.c_send, self.c_recv = [
            s.at[which] for s in sems
        ]
        self.dp, self.rep = lax.axis_index("dp"), lax.axis_index("replica")
        self.core, self.z = lax.rem(self.dp, 2), self.dp // 2
        self.n_z = n_dp // 2
        self.sources = n_dp // 4

    def place(self, zi, core, rep, piece):
        owner = (zi * 2 + core) * self.n_rep + rep
        first = (owner // 2) * (2 * self.share) + lax.rem(owner, 2) * (self.share + 8)
        start, rows = self.pieces[piece]
        return self.buffer.at[pl.ds(pl.multiple_of(first + start, 16), rows), :]

    def back(self, j):
        return lax.rem(self.rep + self.n_rep - j, self.n_rep)

    def column(self, zi, piece):
        source = zi + self.which * self.sources
        ref = self.place(zi, self.core, self.rep, piece)
        up = remote(
            ref, ref, self.z_send.at[zi, piece, 0], self.z_recv.at[zi, piece],
            {"dp": lax.rem(self.dp + 2, self.n_dp)},
        )
        down = remote(
            ref, ref, self.z_send.at[zi, piece, 1], self.z_recv.at[zi, piece],
            {"dp": lax.rem(self.dp + self.n_dp - 2, self.n_dp)},
        )
        ups = (self.z >= source) & (self.z < self.n_z - 1)
        downs = (self.z <= source) & (self.z > 0)
        across = [
            remote(
                ref, ref, self.r_send.at[zi, piece, j], self.r_recv.at[zi, piece, j],
                {"replica": lax.rem(self.rep + j, self.n_rep)},
            )
            for j in range(1, self.n_rep)
        ]
        return up, ups, down, downs, across + [self.over(zi, piece, 0)]

    def over(self, zi, piece, j):
        ref = self.place(zi, self.core, self.back(j), piece)
        return remote(
            ref, ref, self.c_send.at[zi, piece, j], self.c_recv.at[zi, piece, j],
            {"dp": self.dp + 1 - 2 * self.core},
        )

    def send_column(self, zi, piece):
        up, ups, down, downs, rest = self.column(zi, piece)
        pl.when(ups)(up.start)
        pl.when(downs)(down.start)
        for copy in rest:
            copy.start()

    def own(self):
        for zi in range(self.sources):
            @pl.when(self.z == zi + self.which * self.sources)
            def _():
                for piece in range(len(self.pieces)):
                    self.send_column(zi, piece)

    def from_z(self, piece):
        for zi in range(self.sources):
            @pl.when(self.z != zi + self.which * self.sources)
            def _():
                self.column(zi, piece)[0].wait_recv()
                self.send_column(zi, piece)

    def from_replicas(self, piece):
        for zi in range(self.sources):
            for j in range(1, self.n_rep):
                ref = self.place(zi, self.core, self.back(j), piece)
                remote(
                    ref, ref, self.r_send.at[zi, piece, j], self.r_recv.at[zi, piece, j],
                    {"replica": self.back(j)},
                ).wait_recv()
                self.over(zi, piece, j).start()

    def from_core(self):
        for piece in range(len(self.pieces)):
            for zi in range(self.sources):
                for j in range(self.n_rep):
                    ref = self.place(zi, 1 - self.core, self.back(j), piece)
                    remote(
                        ref, ref, self.c_send.at[zi, piece, j], self.c_recv.at[zi, piece, j],
                        {"dp": self.dp + 1 - 2 * self.core},
                    ).wait_recv()

    def drain(self):
        for piece in range(len(self.pieces)):
            for zi in range(self.sources):
                up, ups, down, downs, rest = self.column(zi, piece)
                pl.when(ups)(up.wait_send)
                pl.when(downs)(down.wait_send)
                for copy in rest:
                    copy.wait_send()
                for j in range(1, self.n_rep):
                    self.over(zi, piece, j).wait_send()


def pixel_column(rows, side):
    return lax.rem(lax.broadcasted_iota(jnp.int32, (rows, 1), 0), side)


def store_shifted(ref, image, first, block, values, side):
    width = values.shape[1]
    rows = block * side
    column = pixel_column(rows, side)
    left = jnp.where(column == 0, 0.0, pltpu.roll(values, 1, 0))
    right = jnp.where(column == side - 1, 0.0, pltpu.roll(values, rows - 1, 0))
    for c, moved in enumerate((left, values, right)):
        ref[image, pl.ds(first + 1, block), :, c * width : (c + 1) * width] = (
            moved.astype(BF16).reshape(block, side, width)
        )


def window_matrix(side):
    shape = (side * side, 16)
    pixel = lax.broadcasted_iota(jnp.int32, shape, 0)
    tap = lax.broadcasted_iota(jnp.int32, shape, 1)
    r, c = tap // 3, lax.rem(tap, 3)
    h, w = pixel // side, lax.rem(pixel, side)
    keep = (
        (tap < 9)
        & ~((r == 0) & (h == side - 1)) & ~((r == 2) & (h == 0))
        & ~((c == 0) & (w == side - 1)) & ~((c == 2) & (w == 0))
    )
    return jnp.where(keep, 1.0, 0.0).astype(BF16)


BLOCK = 8


def forward_kernel(
    n_dp, n_rep, side, share, fused,
    counts, main, bound, patches, stem, start, norms,
    k1_out, k2_out, x_out, y_out, act_out, windows, stem_pool, stats,
    k1, xcat, y, act, seam, ex_a, ex_b, one_a, one_b, bounds,
    z_send, z_recv, r_send, r_recv, c_send, c_recv,
    a_send, a_recv, b_send, b_recv, s_send, s_recv, local,
):
    images = patches.shape[0]
    width = stem.shape[1]
    cells = side * side
    dp, rep = lax.axis_index("dp"), lax.axis_index("replica")
    half = n_dp // 2
    greet(n_dp, n_rep)

    if fused:
        pieces = []
        rows = share - 8
        tiles = rows // 16
        for first, last in ((0, tiles // 2), (tiles // 2, tiles)):
            pieces.append((first * 16, (last - first) * 16))
        sems = (z_send, z_recv, r_send, r_recv, c_send, c_recv)
        gathers = [
            Gather(l, n_dp, n_rep, share, pieces, buffer, sems)
            for l, buffer in enumerate((k1, k2_out))
        ]
        one, two = gathers

        def own_place(buffer):
            owner = lax.rem(dp, half) * n_rep + rep
            first = (owner // 2) * (2 * share) + lax.rem(owner, 2) * (share + 8)
            return buffer.at[pl.ds(pl.multiple_of(first, 16), rows), :]

        @pl.when(dp < half)
        def _():
            copy = pltpu.make_async_copy(main, own_place(k1), local.at[0])
            copy.start()
            copy.wait()

        @pl.when(dp >= half)
        def _():
            copy = pltpu.make_async_copy(main, own_place(k2_out), local.at[0])
            copy.start()
            copy.wait()

        one.own()
        bounds[rep, dp] = bound[...]
        seam_a = Spread("dp", n_dp, bounds.at[rep, dp], bounds.at[rep], s_send.at[0], s_recv.at[0])
        seam_b = Spread("replica", n_rep, bounds.at[rep], bounds, s_send.at[1], s_recv.at[1])
        seam_a.start()
    else:
        copy_in = pltpu.make_async_copy(main, k1, local.at[0])
        copy_in.start()

    weight = stem[...].astype(F32)
    count = counts[0]
    valid = [jnp.where(count > n, 1.0, 0.0) for n in range(images)]
    held = count.astype(F32) * cells
    ones = jnp.ones((8, cells), BF16)
    grams, sums = [], []
    for n in range(images):
        grams.append(bdot(patches[n], patches[n], ((0,), (0,))))
        sums.append(bdot(ones, patches[n]))
        stem_pool[n : n + 1, :] = hdot(sums[n], weight)[0:1] * (1.0 / cells)
    gram = total([g * v for g, v in zip(grams, valid)])
    summed = total([s * v for s, v in zip(sums, valid)])
    square = jnp.sum(weight * hdot(gram, weight), axis=0, keepdims=True)
    cover = gram - hdot(summed, summed, ((0,), (0,))) / (8.0 * held)
    zero = jnp.zeros((1, width), F32)
    payload = one_a.at[0]
    payload[...] = jnp.zeros(payload.shape, F32)
    payload[0:1, :] = hdot(summed, weight)[0:1] / held
    payload[1:2, :] = jnp.sum(weight * hdot(cover, weight), axis=0, keepdims=True)
    payload[2:3, :] = zero + held
    payload[5:6, :] = square

    if fused:
        vector = start[...]
        own_rows = main[...].astype(F32)
        edge_rows = bound[...].astype(F32)
        along = jnp.sum(own_rows * vector, axis=1, keepdims=True)
        edge_along = jnp.sum(edge_rows * vector, axis=1, keepdims=True)
        payload[3:4, :] = jnp.sum(own_rows * along, axis=0, keepdims=True) + jnp.sum(
            edge_rows * edge_along, axis=0, keepdims=True
        )
        payload[4:5, :] = zero + (
            jnp.sum(along * along, axis=0, keepdims=True)
            + jnp.sum(edge_along * edge_along, axis=0, keepdims=True)
        )
    else:
        payload[3:4, :] = start[0:1, :]
        payload[4:5, :] = start[1:2, :]

    first = ex_a.at[0]
    first[dp] = payload[...]
    one_level = Spread("dp", n_dp, payload, first, a_send.at[0], a_recv.at[0])
    one_level.start()
    for n in range(images):
        blank = jnp.zeros((1, side, 3 * width), BF16)
        xcat[n, 0:1] = blank
        xcat[n, side + 1 : side + 2] = blank
    if fused:
        one.from_z(0)
    one_level.wait()
    second = ex_b.at[0]
    mean, spread, cell_count = join_moments(first)
    passed = one_b.at[0]
    passed[...] = jnp.zeros(passed.shape, F32)
    passed[0:1, :] = mean
    passed[1:2, :] = spread
    passed[2:3, :] = cell_count
    vectors, squares = rows_of(first, 3), rows_of(first, 4)
    passed[3:4, :] = total(vectors[:half])
    passed[4:5, :] = total(vectors[half:])
    passed[5:6, :] = total(squares[:half])
    passed[6:7, :] = total(squares[half:])
    passed[7:8, :] = total(rows_of(first, 5))
    second[rep] = passed[...]
    two_level = Spread("replica", n_rep, passed, second, b_send.at[0], b_recv.at[0])
    two_level.start()
    if fused:
        seam_a.wait()
        seam_b.start()
        one.from_z(1)
    two_level.wait()
    mean, spread, pixels = join_moments(second)
    inverse_one = lax.rsqrt(spread / pixels + EPS_NORM)
    joined = [total(rows_of(second, row)) for row in range(3, 8)]
    sigma_rows, start_rows = [], []
    for l in range(2):
        vec = jnp.sqrt(jnp.sum(joined[l] * joined[l], axis=1, keepdims=True))
        base = jnp.sqrt(joined[2 + l])
        sigma_rows.append(zero + vec / base)
        start_rows.append(base)
        stats[8 + l : 9 + l, :] = joined[l] / vec
    stats[0:1, :] = mean
    stats[1:2, :] = inverse_one
    stats[2:3, :] = pixels
    stats[4:5, :] = sigma_rows[0]
    stats[5:6, :] = sigma_rows[1]
    stats[6:7, :] = start_rows[0]
    stats[7:8, :] = start_rows[1]
    stats[10:11, :] = joined[4]
    scale_one = inverse_one * norms[0:1, :]
    shift_one = norms[1:2, :] - mean * scale_one

    def act_one(n):
        def step(i, carry):
            first_row = i * BLOCK
            pixel = pl.ds(pl.multiple_of(first_row * side, BLOCK * side), BLOCK * side)
            out = bdot(patches[n, pixel, :], stem[...])
            values = jax.nn.gelu(out * scale_one + shift_one)
            store_shifted(xcat, n, first_row, BLOCK, values, side)
            return carry
        lax.fori_loop(0, side // BLOCK, step, 0)

    for n in range(images):
        act_one(n)
        if fused and n < 2:
            one.from_replicas(n)
    if fused:
        one.from_core()
        seam_b.wait()
        pairs = half * n_rep // 2
        for l in range(2):
            for k in range(pairs):
                tile = total([
                    bounds[o % n_rep, l * half + o // n_rep].astype(F32) for o in (2 * k, 2 * k + 1)
                ]).astype(BF16)
                if l == 0:
                    k1[2 * share * k + rows : 2 * share * k + rows + 16, :] = tile
                else:
                    seam[k] = tile
        seam_copies = [
            pltpu.make_async_copy(
                seam.at[k],
                k2_out.at[pl.ds(2 * share * k + rows, 16), :],
                local.at[8 + k],
            )
            for k in range(pairs)
        ]
        for copy in seam_copies:
            copy.start()
        two.own()
    else:
        copy_in.wait()
    k1_copy = pltpu.make_async_copy(k1, k1_out, local.at[1])
    k1_copy.start()
    x_copies = [
        pltpu.make_async_copy(
            xcat.at[n, pl.ds(1, side), :, pl.ds(width, width)], x_out.at[n], local.at[2 + n]
        )
        for n in range(images)
    ]
    for copy in x_copies:
        copy.start()

    moments = []
    y_copies = []
    for n in range(images):
        def step(i, carry):
            first_row = i * BLOCK * 2
            pixel = pl.ds(pl.multiple_of(n * cells + first_row * side, 16), 2 * BLOCK * side)
            acc = None
            for r in range(3):
                lhs = xcat[n, pl.ds(first_row + r, 2 * BLOCK)].reshape(2 * BLOCK * side, 3 * width)
                part = bdot(lhs, k1[r * 3 * width : (r + 1) * 3 * width, :])
                acc = part if acc is None else acc + part
            y[pixel, :] = acc
            return carry + jnp.sum(acc, axis=0, keepdims=True)
        whole = lax.fori_loop(0, side // (2 * BLOCK), step, zero)
        if fused:
            two.from_z(n)
        average = whole / cells
        def spread_step(i, carry):
            pixel = pl.ds(pl.multiple_of(n * cells + i * BLOCK * side, 16), BLOCK * side)
            off = y[pixel, :] - average
            return carry + jnp.sum(off * off, axis=0, keepdims=True)
        moments.append((average, lax.fori_loop(0, side // BLOCK, spread_step, zero)))
        copy = pltpu.make_async_copy(
            y.at[pl.ds(n * cells, cells), :], y_out.at[pl.ds(n * cells, cells), :], local.at[4 + n]
        )
        copy.start()
        y_copies.append(copy)
    payload_two = one_a.at[1]
    counts_in = [v * cells for v in valid]
    average = total([m[0] * c for m, c in zip(moments, counts_in)]) / held
    payload_two[...] = jnp.zeros(payload_two.shape, F32)
    payload_two[0:1, :] = average
    payload_two[1:2, :] = total([
        v * m[1] + c * (m[0] - average) * (m[0] - average)
        for m, c, v in zip(moments, counts_in, valid)
    ])
    payload_two[2:3, :] = zero + held
    first = ex_a.at[1]
    first[dp] = payload_two[...]
    three_level = Spread("dp", n_dp, payload_two, first, a_send.at[1], a_recv.at[1])
    three_level.start()
    three_level.wait()
    mean, spread, cell_count = join_moments(first)
    second = ex_b.at[1]
    passed = one_b.at[1]
    passed[...] = jnp.zeros(passed.shape, F32)
    passed[0:1, :] = mean
    passed[1:2, :] = spread
    passed[2:3, :] = cell_count
    second[rep] = passed[...]
    four_level = Spread("replica", n_rep, passed, second, b_send.at[1], b_recv.at[1])
    four_level.start()
    if fused:
        two.from_replicas(0)
    four_level.wait()
    mean, spread, _ = join_moments(second)
    sigma = sigma_rows[0]
    variance = spread / pixels / (sigma * sigma)
    inverse_two = lax.rsqrt(variance + EPS_NORM) / sigma
    stats[3:4, :] = mean
    stats[11:12, :] = inverse_two
    scale_two = inverse_two * norms[2:3, :]
    shift_two = norms[3:4, :] - mean * scale_two
    select = window_matrix(side)
    act_copies = []
    for n in range(images):
        def step(i, carry):
            pixel = pl.ds(pl.multiple_of(n * cells + i * BLOCK * side, 16), BLOCK * side)
            act[pixel, :] = jax.nn.gelu(y[pixel, :] * scale_two + shift_two).astype(BF16)
            return carry
        lax.fori_loop(0, side // BLOCK, step, 0)
        copy = pltpu.make_async_copy(
            act.at[pl.ds(n * cells, cells), :], act_out.at[pl.ds(n * cells, cells), :], local.at[6 + n]
        )
        copy.start()
        act_copies.append(copy)
        windows[n] = bdot(select, act[n * cells : (n + 1) * cells, :], ((0,), (0,)))
    if fused:
        two.from_replicas(1)
        two.from_core()
        one.drain()
        two.drain()
        seam_a.drain()
        seam_b.drain()
        for copy in seam_copies:
            copy.wait()
    for level in (one_level, two_level, three_level, four_level):
        level.drain()
    for copy in [k1_copy] + x_copies + y_copies + act_copies:
        copy.wait()


def forward(n_dp, n_rep, side, share, fused, counts, main, bound, patches, stem, start, norms):
    images, cells = patches.shape[0], side * side
    width = stem.shape[1]
    half = n_dp // 2
    sources = max(n_dp // 4, 1)
    pairs = max(half * n_rep // 2, 1)
    shape = jax.ShapeDtypeStruct
    sem = pltpu.SemaphoreType.DMA
    kernel_rows = 9 * width
    return pl.pallas_call(
        functools.partial(forward_kernel, n_dp, n_rep, side, share, fused),
        out_shape=(
            shape((kernel_rows, width), BF16),
            shape((kernel_rows, width), BF16),
            shape((images, side, side, width), BF16),
            shape((images * cells, width), F32),
            shape((images * cells, width), BF16),
            shape((images, 16, width), F32),
            shape((images, width), F32),
            shape((16, width), F32),
        ),
        in_specs=[SMEM, VMEM if fused else ANY, VMEM, VMEM, VMEM, VMEM, VMEM],
        out_specs=(ANY,) * 5 + (VMEM,) * 3,
        scratch_shapes=[
            pltpu.VMEM((kernel_rows, width), BF16),
            pltpu.VMEM((images, side + 2, side, 3 * width), BF16),
            pltpu.VMEM((images * cells, width), F32),
            pltpu.VMEM((images * cells, width), BF16),
            pltpu.VMEM((pairs, 16, width), BF16),
            pltpu.VMEM((2, n_dp, 8, width), F32),
            pltpu.VMEM((2, n_rep, 8, width), F32),
            pltpu.VMEM((2, 8, width), F32),
            pltpu.VMEM((2, 8, width), F32),
            pltpu.VMEM((n_rep, n_dp, 16, width), BF16),
            sem((2, sources, 2, 2)),
            sem((2, sources, 2)),
            sem((2, sources, 2, n_rep)),
            sem((2, sources, 2, n_rep)),
            sem((2, sources, 2, n_rep)),
            sem((2, sources, 2, n_rep)),
            sem((2, n_dp)),
            sem((2, n_dp)),
            sem((2, n_rep)),
            sem((2, n_rep)),
            sem((2, max(n_dp, n_rep))),
            sem((2, max(n_dp, n_rep))),
            sem((8 + pairs,)),
        ],
        compiler_params=pltpu.CompilerParams(
            collective_id=0, has_side_effects=True, vmem_limit_bytes=56 << 20
        ),
    )(counts, main, bound, patches, stem, start, norms)


def on_device(
    images, labels, counts, noise_table, noise_index, power_start,
    conv_weight, conv_first, conv_second,
    stem_weight, stem_first, stem_second,
    norm_params, norm_first, norm_second,
    inducing, inducing_first, inducing_second,
    lengthscale, length_first, length_second,
    var_mean, mean_first, mean_second,
    var_lower, lower_first, lower_second,
):
    width = stem_weight.shape[1]
    side = images.shape[2]
    cells = side * side
    devices = lax.axis_size(AXES)
    owner = lax.axis_index(AXES) // (devices // 2)
    select = (jnp.arange(2) == owner).astype(jnp.float32)

    n_dp, n_rep = lax.axis_size("dp"), lax.axis_size("replica")
    rows = conv_weight.astype(jnp.bfloat16).reshape(-1, width)
    share = rows.shape[0]
    fused = share % 16 == 8 and n_rep % 2 == 0
    start = jnp.sum(select[:, None] * power_start, axis=0)
    image_rows = jnp.sum(rows.astype(jnp.float32) * start, axis=1)
    bound = jnp.zeros((16, width), jnp.bfloat16)
    if fused:
        odd = lax.axis_index(AXES) % 2 == 1
        blank = jnp.zeros((8, width), jnp.bfloat16)
        main = jnp.where(odd, rows[8:], rows[:-8])
        bound = jnp.where(
            odd, jnp.concatenate([blank, rows[:8]]), jnp.concatenate([rows[-8:], blank])
        )
        extra = start[None]
    else:
        gathered = lax.all_gather(rows, AXES, axis=0, tiled=True)
        main = gathered[: 9 * width]
        back_rows = jnp.sum(rows.astype(jnp.float32) * image_rows[:, None], axis=0)
        extra = jnp.stack([back_rows, jnp.full((width,), jnp.sum(image_rows * image_rows))])
    padded = jnp.pad(images, ((0, 0), (0, 0), (1, 1), (1, 1)))
    patches = jnp.stack(
        [padded[:, :, r : r + side, c : c + side] for r in range(3) for c in range(3)], axis=1
    )
    patches = patches.reshape(images.shape[0], -1, cells)
    colours = patches.shape[1]
    patches = jnp.pad(patches, ((0, 0), (0, 32 - colours), (0, 0))).transpose(0, 2, 1)
    stem_kernel = jnp.pad(stem_weight.astype(jnp.bfloat16), ((0, 32 - colours), (0, 0)))
    k_one, k_two, act_one, raw_one, act_two, windows, stem_pool, stats = forward(
        n_dp, n_rep, side, share, fused, counts, main, bound, patches, stem_kernel, extra, norm_params
    )
    if not fused:
        k_two = gathered[9 * width :]
    rows = rows.astype(jnp.float32)
    pixels = stats[2, 0]
    totals = pixels / cells
    sigmas = stats[4:6, 0]
    start_norms = stats[6:8, 0]
    unit_vectors = stats[8:10]
    mean_one, inverse_one = stats[0], stats[1]
    kernel_one = (k_one.astype(jnp.float32) / sigmas[0]).astype(jnp.bfloat16).reshape(9, width, width)
    kernel_two = (k_two.astype(jnp.float32) / sigmas[1]).astype(jnp.bfloat16).reshape(9, width, width)
    slot_mask = (jnp.arange(images.shape[0]) < counts[0]).astype(jnp.float32)
    valid = slot_mask[:, None, None, None]
    pictures = jnp.transpose(images, (0, 2, 3, 1))
    stem_out = jnp.dot(patches, stem_kernel, preferred_element_type=jnp.float32).reshape(
        images.shape[0], side, side, width
    )
    normed_one = (stem_out - mean_one) * inverse_one
    pre_one = normed_one * norm_params[0] + norm_params[1]
    raw_one = raw_one.reshape(act_one.shape)
    branch_one = raw_one / sigmas[0]
    normed_two = (raw_one - stats[3]) * stats[11]
    inverse_two = stats[11] * sigmas[0]
    pre_two = normed_two * norm_params[2] + norm_params[3]
    act_two = act_two.reshape(act_one.shape)
    windows = windows[:, :9]
    pooled_branch = (
        jnp.dot(
            windows.reshape(windows.shape[0], -1),
            kernel_two.reshape(-1, width).astype(jnp.float32),
            precision=HIGH,
        )
        / cells
    )
    pooled = stem_pool + pooled_branch

    chosen = (noise_index[:, :, None] == jnp.arange(noise_table.shape[0])[None, None, :]).astype(
        jnp.float32
    )
    noise = jnp.einsum("nsp,pk->nsk", chosen, noise_table, precision=HIGH)
    loss_scale = 1.0 / totals
    scaled_z, kzz, factor, chol_inverse = head_prepare(inducing, lengthscale)
    factors = scale_factor(var_lower)
    local_loss, d_pooled, g_xx, g_zx, g_chol, g_mean, g_factors = head_local(
        pooled, scaled_z, chol_inverse, lengthscale, var_mean, factors, noise, labels,
        slot_mask, loss_scale,
    )
    d_branch_two = (d_pooled / cells).astype(jnp.bfloat16)

    taps_two = jnp.einsum(
        "nd,tcd->ntc", d_branch_two, kernel_two, preferred_element_type=jnp.float32
    )
    d_act_two = spread_back(taps_two, side)
    d_pre_two = gelu_back(pre_two, d_act_two)
    bias_two, gain_two = lax.psum(
        (
            jnp.sum(d_pre_two * valid, axis=(0, 1, 2)),
            jnp.sum(d_pre_two * normed_two * valid, axis=(0, 1, 2)),
        ),
        AXES,
    )
    d_branch_one = (
        inverse_two
        * norm_params[2]
        * (d_pre_two - bias_two / pixels - normed_two * gain_two / pixels)
        * valid
    ).astype(jnp.bfloat16)
    grad_one = taps_grad(act_one, d_branch_one)
    d_act_one = conv_full(d_branch_one, jnp.transpose(kernel_one[::-1], (0, 2, 1)))
    d_pre_one = gelu_back(pre_one, d_act_one)
    bias_one, gain_one = lax.psum(
        (
            jnp.sum(d_pre_one * valid, axis=(0, 1, 2)),
            jnp.sum(d_pre_one * normed_one * valid, axis=(0, 1, 2)),
        ),
        AXES,
    )
    d_stem_norm = (
        inverse_one
        * norm_params[0]
        * (d_pre_one - bias_one / pixels - normed_one * gain_one / pixels)
        * valid
    )
    d_stem = (d_stem_norm + (d_pooled / cells)[:, None, None, :]).astype(jnp.bfloat16)
    stem_grad = taps_grad(pictures, d_stem).reshape(-1, width)

    branch_two = conv_full(act_two, kernel_two)
    rms_local = jnp.stack(
        [jnp.sum(stem_out * stem_out * valid), jnp.sum(branch_two * branch_two * valid)]
    )
    along = jnp.stack(
        [
            jnp.sum(branch_one * d_branch_one.astype(jnp.float32)),
            jnp.sum(pooled_branch * cells * d_branch_two.astype(jnp.float32)),
        ]
    )
    (
        stem_sum, g_zx, g_xx, g_chol, g_mean, g_factors, loss_total, rms_sums, along,
    ) = lax.psum(
        (stem_grad, g_zx, g_xx, g_chol, g_mean, g_factors, local_loss, rms_local, along), AXES
    )

    part_one = lax.psum_scatter(
        jnp.concatenate([grad_one.reshape(-1), jnp.zeros((grad_one.size,), jnp.float32)]),
        AXES, scatter_dimension=0, tiled=True,
    ).reshape(-1, width)
    all_windows, all_grads = lax.all_gather((windows, d_branch_two), AXES, tiled=True)
    all_windows = all_windows.reshape(all_windows.shape[0], -1)
    per_kernel = devices // 2
    place = lax.rem(lax.axis_index(AXES), per_kernel) * rows.shape[0]
    mine = lax.dynamic_slice_in_dim(all_windows, place, rows.shape[0], axis=1)
    part_two = jnp.dot(mine.T, all_grads.astype(jnp.float32), precision=HIGH)
    part = jnp.where(owner == 0, part_one, part_two)

    my_sigma = jnp.sum(select * sigmas)
    my_norm = jnp.sum(select * start_norms)
    my_vector = jnp.sum(select[:, None] * unit_vectors, axis=0)
    d_sigma = -jnp.sum(select * along) / my_sigma
    left = image_rows / my_norm
    d_left = (jnp.sum(rows * (my_vector / my_norm), axis=1) - left * (my_sigma / my_norm))
    conv_part = part / my_sigma + d_sigma * (
        left[:, None] * my_vector[None, :] + d_left[:, None] * start[None, :]
    )
    conv_part = conv_part.reshape(-1)

    new_one, new_two, direction = lamb_moments(conv_weight, conv_part, conv_first, conv_second)
    weight_sq, step_sq = lax.psum(
        (select * jnp.sum(conv_weight * conv_weight), select * jnp.sum(direction * direction)),
        AXES,
    )
    trust_ratio = jnp.sum(select * jnp.sqrt(weight_sq) / jnp.sqrt(step_sq))
    new_conv = conv_weight - RATE * trust_ratio * direction

    inducing_sum, length_sum = head_finish(
        scaled_z, kzz, factor, chol_inverse, lengthscale, g_zx, g_xx, g_chol
    )
    kl_value, kl_back = jax.vjp(kl_term, var_mean, var_lower)
    kl_mean, kl_lower = kl_back(loss_scale)
    eye = jnp.eye(var_lower.shape[1], dtype=jnp.float32)
    g_lower = jnp.tril(g_factors, -1) + eye * g_factors * factors
    loss_sum = loss_total + kl_value
    rms_values = jnp.sqrt(rms_sums / (pixels * width))
    norm_grad = jnp.stack([gain_one, bias_one, gain_two, bias_two])
    stem_new = lamb_update(stem_weight, stem_sum, stem_first, stem_second, 1)
    norm_new = lamb_update(norm_params, norm_grad, norm_first, norm_second, 4)
    inducing_new = lamb_update(inducing, inducing_sum, inducing_first, inducing_second, 1)
    length_new = lamb_update(lengthscale, length_sum, length_first, length_second, 1)
    mean_new = lamb_update(var_mean, g_mean + kl_mean, mean_first, mean_second, 1)
    lower_new = lamb_update(var_lower, g_lower + kl_lower, lower_first, lower_second, 1)
    return (
        jnp.stack([loss_sum, totals]),
        new_conv, new_one, new_two, new_conv.astype(jnp.bfloat16),
        *stem_new, *norm_new, *inducing_new, *length_new, *mean_new, *lower_new,
        sigmas, rms_values,
    )


def solution(mesh):
    split = P(AXES)
    return jax.shard_map(
        on_device,
        mesh=mesh,
        in_specs=(split, split, split, P(), split, P(), split, split, split) + (P(),) * 18,
        out_specs=(P(),) + (split,) * 4 + (P(),) * 20,
        check_vma=False,
    )
```

```python
import functools

import jax
import jax.numpy as jnp
from jax import lax
from jax.experimental import pallas as pl
from jax.experimental.pallas import tpu as pltpu
from jax.sharding import PartitionSpec as P

STEP = 10
HIGH = lax.Precision.HIGHEST
EPS_NORM = 1e-05
JITTER = 0.001
BETA_ONE = 0.9
BETA_TWO = 0.999
RATE = 0.3
DECAY = 0.01
EPS_ADAM = 1e-08
AXES = ("dp", "replica")


def lamb_moments(weight, gradient, moment_one, moment_two):
    new_one = BETA_ONE * moment_one + (1.0 - BETA_ONE) * gradient
    new_two = BETA_TWO * moment_two + (1.0 - BETA_TWO) * gradient * gradient
    direction = (
        new_one / (1.0 - BETA_ONE**STEP) / (jnp.sqrt(new_two / (1.0 - BETA_TWO**STEP)) + EPS_ADAM)
        + DECAY * weight
    )
    return (new_one, new_two, direction)


MESH = pl.DeviceIdType.MESH
ANY = pl.BlockSpec(memory_space=pl.ANY)
VMEM = pl.BlockSpec(memory_space=pltpu.VMEM)
SMEM = pl.BlockSpec(memory_space=pltpu.SMEM)
F32 = jnp.float32
BF16 = jnp.bfloat16


def remote(src, dst, send, recv, where):
    return pltpu.make_async_remote_copy(
        src_ref=src, dst_ref=dst, send_sem=send, recv_sem=recv,
        device_id=where, device_id_type=MESH,
    )


def greet(n_dp, n_rep):
    dp, rep = lax.axis_index("dp"), lax.axis_index("replica")
    barrier = pltpu.get_barrier_semaphore()
    for j in range(1, n_dp):
        pl.semaphore_signal(
            barrier, inc=1, device_id={"dp": lax.rem(dp + j, n_dp)}, device_id_type=MESH
        )
    for j in range(1, n_rep):
        pl.semaphore_signal(
            barrier, inc=1, device_id={"replica": lax.rem(rep + j, n_rep)}, device_id_type=MESH
        )
    pl.semaphore_wait(barrier, n_dp + n_rep - 2)


class Spread:
    def __init__(self, axis, size, src, dst, send, recv):
        self.axis, self.size, self.src, self.dst, self.send, self.recv = axis, size, src, dst, send, recv
        self.me = lax.axis_index(axis)

    def copies(self):
        for j in range(1, self.size):
            yield remote(
                self.src, self.dst.at[self.me], self.send.at[j], self.recv.at[j],
                {self.axis: lax.rem(self.me + j, self.size)},
            )

    def start(self):
        for copy in self.copies():
            copy.start()

    def wait(self):
        for j in range(1, self.size):
            source = lax.rem(self.me + self.size - j, self.size)
            remote(
                self.src, self.dst.at[source], self.send.at[j], self.recv.at[j],
                {self.axis: source},
            ).wait_recv()

    def drain(self):
        for copy in self.copies():
            copy.wait_send()


def rows_of(refs, row):
    return [refs[i, row : row + 1, :] for i in range(refs.shape[0])]


def total(values):
    result = values[0]
    for value in values[1:]:
        result = result + value
    return result


def join_moments(refs):
    averages, squares, counts = rows_of(refs, 0), rows_of(refs, 1), rows_of(refs, 2)
    count = total(counts)
    average = total([a * n for a, n in zip(averages, counts)]) / count
    spread = total(
        [s + n * (a - average) * (a - average) for a, s, n in zip(averages, squares, counts)]
    )
    return average, spread, count


def hdot(a, b, dims=((1,), (0,))):
    return lax.dot_general(
        a, b, (dims, ((), ())), precision=HIGH, preferred_element_type=F32
    )


def bdot(a, b, dims=((1,), (0,))):
    return lax.dot_general(a, b, (dims, ((), ())), preferred_element_type=F32)


class Gather:
    def __init__(self, which, n_dp, n_rep, share, pieces, buffer, sems):
        self.which, self.n_dp, self.n_rep, self.share = which, n_dp, n_rep, share
        self.pieces, self.buffer = pieces, buffer
        self.z_send, self.z_recv, self.r_send, self.r_recv, self.c_send, self.c_recv = [
            s.at[which] for s in sems
        ]
        self.dp, self.rep = lax.axis_index("dp"), lax.axis_index("replica")
        self.core, self.z = lax.rem(self.dp, 2), self.dp // 2
        self.n_z = n_dp // 2
        self.sources = n_dp // 4

    def place(self, zi, core, rep, piece):
        owner = (zi * 2 + core) * self.n_rep + rep
        first = (owner // 2) * (2 * self.share) + lax.rem(owner, 2) * (self.share + 8)
        start, rows = self.pieces[piece]
        return self.buffer.at[pl.ds(pl.multiple_of(first + start, 16), rows), :]

    def back(self, j):
        return lax.rem(self.rep + self.n_rep - j, self.n_rep)

    def column(self, zi, piece):
        source = zi + self.which * self.sources
        ref = self.place(zi, self.core, self.rep, piece)
        up = remote(
            ref, ref, self.z_send.at[zi, piece, 0], self.z_recv.at[zi, piece],
            {"dp": lax.rem(self.dp + 2, self.n_dp)},
        )
        down = remote(
            ref, ref, self.z_send.at[zi, piece, 1], self.z_recv.at[zi, piece],
            {"dp": lax.rem(self.dp + self.n_dp - 2, self.n_dp)},
        )
        ups = (self.z >= source) & (self.z < self.n_z - 1)
        downs = (self.z <= source) & (self.z > 0)
        across = [
            remote(
                ref, ref, self.r_send.at[zi, piece, j], self.r_recv.at[zi, piece, j],
                {"replica": lax.rem(self.rep + j, self.n_rep)},
            )
            for j in range(1, self.n_rep)
        ]
        return up, ups, down, downs, across + [self.over(zi, piece, 0)]

    def over(self, zi, piece, j):
        ref = self.place(zi, self.core, self.back(j), piece)
        return remote(
            ref, ref, self.c_send.at[zi, piece, j], self.c_recv.at[zi, piece, j],
            {"dp": self.dp + 1 - 2 * self.core},
        )

    def send_column(self, zi, piece):
        up, ups, down, downs, rest = self.column(zi, piece)
        pl.when(ups)(up.start)
        pl.when(downs)(down.start)
        for copy in rest:
            copy.start()

    def own(self):
        for zi in range(self.sources):
            @pl.when(self.z == zi + self.which * self.sources)
            def _():
                for piece in range(len(self.pieces)):
                    self.send_column(zi, piece)

    def from_z(self, piece):
        for zi in range(self.sources):
            @pl.when(self.z != zi + self.which * self.sources)
            def _():
                self.column(zi, piece)[0].wait_recv()
                self.send_column(zi, piece)

    def from_replicas(self, piece):
        for zi in range(self.sources):
            for j in range(1, self.n_rep):
                ref = self.place(zi, self.core, self.back(j), piece)
                remote(
                    ref, ref, self.r_send.at[zi, piece, j], self.r_recv.at[zi, piece, j],
                    {"replica": self.back(j)},
                ).wait_recv()
                self.over(zi, piece, j).start()

    def from_core(self):
        for piece in range(len(self.pieces)):
            for zi in range(self.sources):
                for j in range(self.n_rep):
                    ref = self.place(zi, 1 - self.core, self.back(j), piece)
                    remote(
                        ref, ref, self.c_send.at[zi, piece, j], self.c_recv.at[zi, piece, j],
                        {"dp": self.dp + 1 - 2 * self.core},
                    ).wait_recv()

    def drain(self):
        for piece in range(len(self.pieces)):
            for zi in range(self.sources):
                up, ups, down, downs, rest = self.column(zi, piece)
                pl.when(ups)(up.wait_send)
                pl.when(downs)(down.wait_send)
                for copy in rest:
                    copy.wait_send()
                for j in range(1, self.n_rep):
                    self.over(zi, piece, j).wait_send()


def pixel_column(rows, side):
    return lax.rem(lax.broadcasted_iota(jnp.int32, (rows, 1), 0), side)


def store_shifted(ref, image, first, block, values, side):
    width = values.shape[1]
    rows = block * side
    column = pixel_column(rows, side)
    left = jnp.where(column == 0, 0.0, pltpu.roll(values, 1, 0))
    right = jnp.where(column == side - 1, 0.0, pltpu.roll(values, rows - 1, 0))
    for c, moved in enumerate((left, values, right)):
        ref[image, pl.ds(first + 1, block), :, c * width : (c + 1) * width] = (
            moved.astype(BF16).reshape(block, side, width)
        )


def window_matrix(side):
    shape = (side * side, 16)
    pixel = lax.broadcasted_iota(jnp.int32, shape, 0)
    tap = lax.broadcasted_iota(jnp.int32, shape, 1)
    r, c = tap // 3, lax.rem(tap, 3)
    h, w = pixel // side, lax.rem(pixel, side)
    keep = (
        (tap < 9)
        & ~((r == 0) & (h == side - 1)) & ~((r == 2) & (h == 0))
        & ~((c == 0) & (w == side - 1)) & ~((c == 2) & (w == 0))
    )
    return jnp.where(keep, 1.0, 0.0).astype(BF16)


BLOCK = 8


def forward_kernel(
    n_dp, n_rep, side, share, fused,
    counts, main, bound, patches, stem, start, norms,
    k1_out, k2_out, x_out, y_out, act_out, windows, stem_pool, stats,
    k1, xcat, y, act, seam, ex_a, ex_b, one_a, one_b, bounds,
    z_send, z_recv, r_send, r_recv, c_send, c_recv,
    a_send, a_recv, b_send, b_recv, s_send, s_recv, local,
):
    images = patches.shape[0]
    width = stem.shape[1]
    cells = side * side
    dp, rep = lax.axis_index("dp"), lax.axis_index("replica")
    half = n_dp // 2
    greet(n_dp, n_rep)

    if fused:
        pieces = []
        rows = share - 8
        tiles = rows // 16
        for first, last in ((0, tiles // 2), (tiles // 2, tiles)):
            pieces.append((first * 16, (last - first) * 16))
        sems = (z_send, z_recv, r_send, r_recv, c_send, c_recv)
        gathers = [
            Gather(l, n_dp, n_rep, share, pieces, buffer, sems)
            for l, buffer in enumerate((k1, k2_out))
        ]
        one, two = gathers

        def own_place(buffer):
            owner = lax.rem(dp, half) * n_rep + rep
            first = (owner // 2) * (2 * share) + lax.rem(owner, 2) * (share + 8)
            return buffer.at[pl.ds(pl.multiple_of(first, 16), rows), :]

        @pl.when(dp < half)
        def _():
            copy = pltpu.make_async_copy(main, own_place(k1), local.at[0])
            copy.start()
            copy.wait()

        @pl.when(dp >= half)
        def _():
            copy = pltpu.make_async_copy(main, own_place(k2_out), local.at[0])
            copy.start()
            copy.wait()

        one.own()
        bounds[rep, dp] = bound[...]
        seam_a = Spread("dp", n_dp, bounds.at[rep, dp], bounds.at[rep], s_send.at[0], s_recv.at[0])
        seam_b = Spread("replica", n_rep, bounds.at[rep], bounds, s_send.at[1], s_recv.at[1])
        seam_a.start()
    else:
        copy_in = pltpu.make_async_copy(main, k1, local.at[0])
        copy_in.start()

    weight = stem[...].astype(F32)
    count = counts[0]
    valid = [jnp.where(count > n, 1.0, 0.0) for n in range(images)]
    held = count.astype(F32) * cells
    ones = jnp.ones((8, cells), BF16)
    grams, sums = [], []
    for n in range(images):
        grams.append(bdot(patches[n], patches[n], ((0,), (0,))))
        sums.append(bdot(ones, patches[n]))
        stem_pool[n : n + 1, :] = hdot(sums[n], weight)[0:1] * (1.0 / cells)
    gram = total([g * v for g, v in zip(grams, valid)])
    summed = total([s * v for s, v in zip(sums, valid)])
    square = jnp.sum(weight * hdot(gram, weight), axis=0, keepdims=True)
    cover = gram - hdot(summed, summed, ((0,), (0,))) / (8.0 * held)
    zero = jnp.zeros((1, width), F32)
    payload = one_a.at[0]
    payload[...] = jnp.zeros(payload.shape, F32)
    payload[0:1, :] = hdot(summed, weight)[0:1] / held
    payload[1:2, :] = jnp.sum(weight * hdot(cover, weight), axis=0, keepdims=True)
    payload[2:3, :] = zero + held
    payload[5:6, :] = square

    if fused:
        vector = start[...]
        own_rows = main[...].astype(F32)
        edge_rows = bound[...].astype(F32)
        along = jnp.sum(own_rows * vector, axis=1, keepdims=True)
        edge_along = jnp.sum(edge_rows * vector, axis=1, keepdims=True)
        payload[3:4, :] = jnp.sum(own_rows * along, axis=0, keepdims=True) + jnp.sum(
            edge_rows * edge_along, axis=0, keepdims=True
        )
        payload[4:5, :] = zero + (
            jnp.sum(along * along, axis=0, keepdims=True)
            + jnp.sum(edge_along * edge_along, axis=0, keepdims=True)
        )
    else:
        payload[3:4, :] = start[0:1, :]
        payload[4:5, :] = start[1:2, :]

    first = ex_a.at[0]
    first[dp] = payload[...]
    one_level = Spread("dp", n_dp, payload, first, a_send.at[0], a_recv.at[0])
    one_level.start()
    for n in range(images):
        blank = jnp.zeros((1, side, 3 * width), BF16)
        xcat[n, 0:1] = blank
        xcat[n, side + 1 : side + 2] = blank
    if fused:
        one.from_z(0)
    one_level.wait()
    second = ex_b.at[0]
    mean, spread, cell_count = join_moments(first)
    passed = one_b.at[0]
    passed[...] = jnp.zeros(passed.shape, F32)
    passed[0:1, :] = mean
    passed[1:2, :] = spread
    passed[2:3, :] = cell_count
    vectors, squares = rows_of(first, 3), rows_of(first, 4)
    passed[3:4, :] = total(vectors[:half])
    passed[4:5, :] = total(vectors[half:])
    passed[5:6, :] = total(squares[:half])
    passed[6:7, :] = total(squares[half:])
    passed[7:8, :] = total(rows_of(first, 5))
    second[rep] = passed[...]
    two_level = Spread("replica", n_rep, passed, second, b_send.at[0], b_recv.at[0])
    two_level.start()
    if fused:
        seam_a.wait()
        seam_b.start()
        one.from_z(1)
    two_level.wait()
    mean, spread, pixels = join_moments(second)
    inverse_one = lax.rsqrt(spread / pixels + EPS_NORM)
    joined = [total(rows_of(second, row)) for row in range(3, 8)]
    sigma_rows, start_rows = [], []
    for l in range(2):
        vec = jnp.sqrt(jnp.sum(joined[l] * joined[l], axis=1, keepdims=True))
        base = jnp.sqrt(joined[2 + l])
        sigma_rows.append(zero + vec / base)
        start_rows.append(base)
        stats[8 + l : 9 + l, :] = joined[l] / vec
    stats[0:1, :] = mean
    stats[1:2, :] = inverse_one
    stats[2:3, :] = pixels
    stats[4:5, :] = sigma_rows[0]
    stats[5:6, :] = sigma_rows[1]
    stats[6:7, :] = start_rows[0]
    stats[7:8, :] = start_rows[1]
    stats[10:11, :] = joined[4]
    scale_one = inverse_one * norms[0:1, :]
    shift_one = norms[1:2, :] - mean * scale_one

    def act_one(n):
        def step(i, carry):
            first_row = i * BLOCK
            pixel = pl.ds(pl.multiple_of(first_row * side, BLOCK * side), BLOCK * side)
            out = bdot(patches[n, pixel, :], stem[...])
            values = jax.nn.gelu(out * scale_one + shift_one)
            store_shifted(xcat, n, first_row, BLOCK, values, side)
            return carry
        lax.fori_loop(0, side // BLOCK, step, 0)

    for n in range(images):
        act_one(n)
        if fused and n < 2:
            one.from_replicas(n)
    if fused:
        one.from_core()
        seam_b.wait()
        pairs = half * n_rep // 2
        for l in range(2):
            for k in range(pairs):
                tile = total([
                    bounds[o % n_rep, l * half + o // n_rep].astype(F32) for o in (2 * k, 2 * k + 1)
                ]).astype(BF16)
                if l == 0:
                    k1[2 * share * k + rows : 2 * share * k + rows + 16, :] = tile
                else:
                    seam[k] = tile
        seam_copies = [
            pltpu.make_async_copy(
                seam.at[k],
                k2_out.at[pl.ds(2 * share * k + rows, 16), :],
                local.at[8 + k],
            )
            for k in range(pairs)
        ]
        for copy in seam_copies:
            copy.start()
        two.own()
    else:
        copy_in.wait()
    k1_copy = pltpu.make_async_copy(k1, k1_out, local.at[1])
    k1_copy.start()
    x_copies = [
        pltpu.make_async_copy(
            xcat.at[n, pl.ds(1, side), :, pl.ds(width, width)], x_out.at[n], local.at[2 + n]
        )
        for n in range(images)
    ]
    for copy in x_copies:
        copy.start()

    moments = []
    y_copies = []
    for n in range(images):
        def step(i, carry):
            first_row = i * BLOCK * 2
            pixel = pl.ds(pl.multiple_of(n * cells + first_row * side, 16), 2 * BLOCK * side)
            acc = None
            for r in range(3):
                lhs = xcat[n, pl.ds(first_row + r, 2 * BLOCK)].reshape(2 * BLOCK * side, 3 * width)
                part = bdot(lhs, k1[r * 3 * width : (r + 1) * 3 * width, :])
                acc = part if acc is None else acc + part
            y[pixel, :] = acc
            return carry + jnp.sum(acc, axis=0, keepdims=True)
        whole = lax.fori_loop(0, side // (2 * BLOCK), step, zero)
        if fused:
            two.from_z(n)
        average = whole / cells
        def spread_step(i, carry):
            pixel = pl.ds(pl.multiple_of(n * cells + i * BLOCK * side, 16), BLOCK * side)
            off = y[pixel, :] - average
            return carry + jnp.sum(off * off, axis=0, keepdims=True)
        moments.append((average, lax.fori_loop(0, side // BLOCK, spread_step, zero)))
        copy = pltpu.make_async_copy(
            y.at[pl.ds(n * cells, cells), :], y_out.at[pl.ds(n * cells, cells), :], local.at[4 + n]
        )
        copy.start()
        y_copies.append(copy)
    payload_two = one_a.at[1]
    counts_in = [v * cells for v in valid]
    average = total([m[0] * c for m, c in zip(moments, counts_in)]) / held
    payload_two[...] = jnp.zeros(payload_two.shape, F32)
    payload_two[0:1, :] = average
    payload_two[1:2, :] = total([
        v * m[1] + c * (m[0] - average) * (m[0] - average)
        for m, c, v in zip(moments, counts_in, valid)
    ])
    payload_two[2:3, :] = zero + held
    first = ex_a.at[1]
    first[dp] = payload_two[...]
    three_level = Spread("dp", n_dp, payload_two, first, a_send.at[1], a_recv.at[1])
    three_level.start()
    three_level.wait()
    mean, spread, cell_count = join_moments(first)
    second = ex_b.at[1]
    passed = one_b.at[1]
    passed[...] = jnp.zeros(passed.shape, F32)
    passed[0:1, :] = mean
    passed[1:2, :] = spread
    passed[2:3, :] = cell_count
    second[rep] = passed[...]
    four_level = Spread("replica", n_rep, passed, second, b_send.at[1], b_recv.at[1])
    four_level.start()
    if fused:
        two.from_replicas(0)
    four_level.wait()
    mean, spread, _ = join_moments(second)
    sigma = sigma_rows[0]
    variance = spread / pixels / (sigma * sigma)
    inverse_two = lax.rsqrt(variance + EPS_NORM) / sigma
    stats[3:4, :] = mean
    stats[11:12, :] = inverse_two
    scale_two = inverse_two * norms[2:3, :]
    shift_two = norms[3:4, :] - mean * scale_two
    select = window_matrix(side)
    act_copies = []
    for n in range(images):
        def step(i, carry):
            pixel = pl.ds(pl.multiple_of(n * cells + i * BLOCK * side, 16), BLOCK * side)
            act[pixel, :] = jax.nn.gelu(y[pixel, :] * scale_two + shift_two).astype(BF16)
            return carry
        lax.fori_loop(0, side // BLOCK, step, 0)
        copy = pltpu.make_async_copy(
            act.at[pl.ds(n * cells, cells), :], act_out.at[pl.ds(n * cells, cells), :], local.at[6 + n]
        )
        copy.start()
        act_copies.append(copy)
        windows[n] = bdot(select, act[n * cells : (n + 1) * cells, :], ((0,), (0,)))
    if fused:
        two.from_replicas(1)
        two.from_core()
        one.drain()
        two.drain()
        seam_a.drain()
        seam_b.drain()
        for copy in seam_copies:
            copy.wait()
    for level in (one_level, two_level, three_level, four_level):
        level.drain()
    for copy in [k1_copy] + x_copies + y_copies + act_copies:
        copy.wait()


def forward(n_dp, n_rep, side, share, fused, counts, main, bound, patches, stem, start, norms):
    images, cells = patches.shape[0], side * side
    width = stem.shape[1]
    half = n_dp // 2
    sources = max(n_dp // 4, 1)
    pairs = max(half * n_rep // 2, 1)
    shape = jax.ShapeDtypeStruct
    sem = pltpu.SemaphoreType.DMA
    kernel_rows = 9 * width
    return pl.pallas_call(
        functools.partial(forward_kernel, n_dp, n_rep, side, share, fused),
        out_shape=(
            shape((kernel_rows, width), BF16),
            shape((kernel_rows, width), BF16),
            shape((images, side, side, width), BF16),
            shape((images * cells, width), F32),
            shape((images * cells, width), BF16),
            shape((images, 16, width), F32),
            shape((images, width), F32),
            shape((16, width), F32),
        ),
        in_specs=[SMEM, VMEM if fused else ANY, VMEM, VMEM, VMEM, VMEM, VMEM],
        out_specs=(ANY,) * 5 + (VMEM,) * 3,
        scratch_shapes=[
            pltpu.VMEM((kernel_rows, width), BF16),
            pltpu.VMEM((images, side + 2, side, 3 * width), BF16),
            pltpu.VMEM((images * cells, width), F32),
            pltpu.VMEM((images * cells, width), BF16),
            pltpu.VMEM((pairs, 16, width), BF16),
            pltpu.VMEM((2, n_dp, 8, width), F32),
            pltpu.VMEM((2, n_rep, 8, width), F32),
            pltpu.VMEM((2, 8, width), F32),
            pltpu.VMEM((2, 8, width), F32),
            pltpu.VMEM((n_rep, n_dp, 16, width), BF16),
            sem((2, sources, 2, 2)),
            sem((2, sources, 2)),
            sem((2, sources, 2, n_rep)),
            sem((2, sources, 2, n_rep)),
            sem((2, sources, 2, n_rep)),
            sem((2, sources, 2, n_rep)),
            sem((2, n_dp)),
            sem((2, n_dp)),
            sem((2, n_rep)),
            sem((2, n_rep)),
            sem((2, max(n_dp, n_rep))),
            sem((2, max(n_dp, n_rep))),
            sem((8 + pairs,)),
        ],
        compiler_params=pltpu.CompilerParams(
            collective_id=0, has_side_effects=True, vmem_limit_bytes=56 << 20
        ),
    )(counts, main, bound, patches, stem, start, norms)


class Reduce:
    def __init__(self, n_dp, n_rep, src, parts, whole, planes, out, sems):
        self.n_dp, self.n_rep = n_dp, n_rep
        self.src, self.parts, self.whole, self.planes, self.out = src, parts, whole, planes, out
        (self.a_send, self.a_recv, self.b_send, self.b_recv, self.c_send, self.c_recv) = sems
        self.dp, self.rep = lax.axis_index("dp"), lax.axis_index("replica")

    def scatter(self):
        for j in range(1, self.n_dp):
            peer = lax.rem(self.dp + j, self.n_dp)
            yield remote(
                self.src.at[peer], self.parts.at[self.dp], self.a_send.at[j], self.a_recv.at[j],
                {"dp": peer},
            )

    def start(self):
        for copy in self.scatter():
            copy.start()
        self.parts[self.dp] = self.src[self.dp]

    def middle(self):
        for j in range(1, self.n_dp):
            source = lax.rem(self.dp + self.n_dp - j, self.n_dp)
            remote(
                self.src.at[source], self.parts.at[source], self.a_send.at[j], self.a_recv.at[j],
                {"dp": source},
            ).wait_recv()
        self.whole[...] = total([self.parts[i] for i in range(self.n_dp)])
        self.planes[self.rep] = self.whole[...]
        self.second = Spread(
            "replica", self.n_rep, self.whole, self.planes, self.b_send, self.b_recv
        )
        self.second.start()

    def last(self):
        self.second.wait()
        self.out[self.dp] = total([self.planes[i] for i in range(self.n_rep)])
        self.third = Spread("dp", self.n_dp, self.out.at[self.dp], self.out, self.c_send, self.c_recv)
        self.third.start()

    def finish(self):
        self.third.wait()
        for copy in self.scatter():
            copy.wait_send()
        self.second.drain()
        self.third.drain()


def reduce_scratch(n_dp, n_rep, rows, width):
    per = -(-rows // n_dp)
    sem = pltpu.SemaphoreType.DMA
    return [
        pltpu.VMEM((n_dp, per, width), F32),
        pltpu.VMEM((n_dp, per, width), F32),
        pltpu.VMEM((per, width), F32),
        pltpu.VMEM((n_rep, per, width), F32),
        pltpu.VMEM((n_dp, per, width), F32),
        sem((n_dp,)), sem((n_dp,)), sem((n_rep,)), sem((n_rep,)), sem((n_dp,)), sem((n_dp,)),
    ]


def put_rows(ref, first, values):
    per = ref.shape[1]
    for k in range(values.shape[0]):
        row = first + k
        ref[row // per, row % per : row % per + 1, :] = values[k : k + 1, :]


def gelu_slope(x):
    c = 0.7978845608028654
    square = x * x
    th = jnp.tanh(c * x * (1.0 + 0.044715 * square))
    return 0.5 * (1.0 + th) + 0.5 * x * (1.0 - th * th) * (c * (1.0 + 3 * 0.044715 * square))


def fold(values):
    return jnp.sum(values.reshape(values.shape[0] // 8, 8, values.shape[1]), axis=0)


IND = 32


def cholesky_steps(matrix, size):
    lane = lax.broadcasted_iota(jnp.int32, (size, IND), 1)
    line = lax.broadcasted_iota(jnp.int32, (size, IND), 0)
    left = matrix
    right = jnp.where(lane == line, 1.0, 0.0)
    factor = jnp.zeros((size, IND), F32)
    row_of = lax.broadcasted_iota(jnp.int32, (size, 1), 0)
    for k in range(size):
        inverse = lax.rsqrt(left[k : k + 1, k : k + 1])
        column = jnp.where(row_of >= k, left[:, k : k + 1] * inverse, 0.0)
        below = jnp.where(row_of > k, column, 0.0)
        row = left[k : k + 1, :] * inverse
        other = right[k : k + 1, :] * inverse
        factor = jnp.where(lane == k, column, factor)
        left = left - below * row
        right = jnp.where(line == k, other, right - below * other)
    return factor, right


def scale_rows(lower):
    size = lower.shape[0]
    line = lax.broadcasted_iota(jnp.int32, (size, size), 0)
    lane = lax.broadcasted_iota(jnp.int32, (size, size), 1)
    return jnp.where(line > lane, lower, jnp.where(line == lane, jnp.exp(lower), 0.0))


def head_kernel(
    n_dp, n_rep, side,
    counts, labels, indices, table, k2_in, y_in, windows, stem_pool, stats, norms,
    inducing, lengthscale, var_mean, var_lower,
    cat_out, head_out, grads_out, chol_out,
    k2, y, d_pre, cat, pattern, z_pad, l_pad, v_pad, f_pad, x_pad, kx_pad, noise, d_rows,
    ex_a, ex_b, one_a, one_b, a_send, a_recv, b_send, b_recv, local,
):
    images = stem_pool.shape[0]
    width = stem_pool.shape[1]
    cells = side * side
    size = inducing.shape[0]
    classes = var_mean.shape[0]
    samples = indices.shape[1]
    dp, rep = lax.axis_index("dp"), lax.axis_index("replica")
    loads = [
        pltpu.make_async_copy(k2_in, k2, local.at[0]),
        pltpu.make_async_copy(y_in, y, local.at[1]),
    ]
    for copy in loads:
        copy.start()
    greet(n_dp, n_rep)

    sigma_one, sigma_two = stats[4:5, :], stats[5:6, :]
    pixels = stats[2:3, :]
    scale = cells / stats[2:3, 0:1]
    ell = lengthscale[...]

    z_pad[...] = jnp.zeros(z_pad.shape, F32)
    z_pad[0:size, :] = inducing[...] / ell
    zs = z_pad[...]
    ones = jnp.ones((8, width), F32)
    lane = lax.broadcasted_iota(jnp.int32, (size, IND), 1)
    line = lax.broadcasted_iota(jnp.int32, (size, IND), 0)
    kzz = jnp.zeros((size, IND), F32)
    for m in range(size):
        off = zs[0:size, :] - zs[m : m + 1, :]
        kzz = jnp.where(lane == m, jnp.exp(-0.5 * jnp.sum(off * off, axis=1, keepdims=True)), kzz)
    factor, inverse = cholesky_steps(jnp.where(lane == line, kzz + JITTER, kzz), size)
    chol_out[...] = jnp.zeros(chol_out.shape, F32)
    chol_out[0, 0:size, :] = kzz
    chol_out[1, 0:size, :] = factor
    chol_out[2, 0:size, :] = inverse
    l_pad[...] = jnp.zeros(l_pad.shape, F32)
    l_pad[0:size, :] = inverse
    v_pad[...] = jnp.zeros(v_pad.shape, F32)
    v_pad[0:classes, 0:size] = var_mean[...]
    f_pad[...] = jnp.zeros(f_pad.shape, F32)
    for c in range(classes):
        f_pad[0:size, c * IND : c * IND + size] = scale_rows(var_lower[c])
    group = lax.broadcasted_iota(jnp.int32, (classes * IND, 16), 0) // IND
    which = lax.broadcasted_iota(jnp.int32, (classes * IND, 16), 1)
    groups = jnp.where(group == which, 1.0, 0.0)
    noise[...] = jnp.zeros(noise.shape, F32)
    for n in range(images):
        for s in range(samples):
            noise[n, s : s + 1, 0:classes] = table[pl.ds(indices[n, s], 1), :]

    loads[0].wait()
    pooled_raw = jnp.zeros((16, width), F32)
    for t in range(9):
        parts = []
        rest = [windows[n, t : t + 1, :] for n in range(images)]
        for _ in range(3):
            parts += [r.astype(BF16).astype(F32) for r in rest]
            rest = [r - p for r, p in zip(rest, parts[-images:])]
        parts.append(jnp.zeros((16 - 3 * images, width), F32))
        lhs = jnp.concatenate(parts, axis=0).astype(BF16)
        pooled_raw = pooled_raw + bdot(lhs, k2[t * width : (t + 1) * width, :])
    x_pad[...] = jnp.zeros(x_pad.shape, F32)
    branch_pool = []
    for n in range(images):
        row = total([pooled_raw[k * images + n : k * images + n + 1] for k in range(3)])
        branch_pool.append(row / (cells * sigma_two))
        x_pad[n : n + 1, :] = (stem_pool[n : n + 1, :] + branch_pool[n]) / ell
    xs = x_pad[...]

    kx_pad[...] = jnp.zeros(kx_pad.shape, F32)
    for n in range(images):
        off = zs - xs[n : n + 1, :]
        kx_pad[n : n + 1, :] = jnp.exp(-0.5 * hdot(ones, off * off, ((1,), (1,))))[0:1]
    lanes = lax.broadcasted_iota(jnp.int32, (8, IND), 1)
    kx = jnp.where(lanes < size, kx_pad[...], 0.0)
    inv = l_pad[...]
    means = v_pad[...]
    factors = f_pad[...]
    proj = hdot(kx, inv, ((1,), (1,)))
    average = hdot(proj, means, ((1,), (1,)))
    spread = hdot(proj, factors)
    variance = (
        1.0 - jnp.sum(proj * proj, axis=1, keepdims=True) + hdot(spread * spread, groups)
    )
    std = jnp.sqrt(variance)
    class_lane = lax.broadcasted_iota(jnp.int32, (1, 16), 1)
    sample_row = lax.broadcasted_iota(jnp.int32, (16, 16), 0)
    inside = (lax.broadcasted_iota(jnp.int32, (16, 16), 1) < classes) & (sample_row < samples)
    count = counts[0]
    loss = jnp.zeros((1, 1), F32)
    g_avg_rows, g_var_rows = [], []
    for n in range(images):
        drawn = average[n : n + 1, :] + std[n : n + 1, :] * noise[n]
        drawn = jnp.where(inside, drawn, -1e30)
        shifted = drawn - jnp.max(drawn, axis=1, keepdims=True)
        exps = jnp.where(inside, jnp.exp(shifted), 0.0)
        sums = jnp.sum(exps, axis=1, keepdims=True)
        sums = jnp.where(sample_row[:, 0:1] < samples, sums, 1.0)
        hot = jnp.where(class_lane == labels[n], 1.0, 0.0)
        picked = jnp.where(inside, (shifted - jnp.log(sums)) * hot, 0.0)
        held = jnp.where(count > n, 1.0 / samples, 0.0)
        loss = loss - held * jnp.sum(jnp.sum(picked, axis=1, keepdims=True), axis=0, keepdims=True)
        g_samples = jnp.where(inside, exps / sums - hot, 0.0) * (held * scale)
        g_avg_rows.append(jnp.sum(g_samples, axis=0, keepdims=True))
        g_var_rows.append(
            0.5 * jnp.sum(g_samples * noise[n], axis=0, keepdims=True) / std[n : n + 1, :]
        )
    blank = [jnp.zeros((8 - images, 16), F32)]
    g_avg = jnp.concatenate(g_avg_rows + blank, axis=0)
    g_var = jnp.concatenate(g_var_rows + blank, axis=0)
    g_spread = 2.0 * spread * hdot(g_var, groups, ((1,), (1,)))
    g_proj = (
        hdot(g_avg, means)
        - 2.0 * proj * jnp.sum(g_var, axis=1, keepdims=True)
        + hdot(g_spread, factors, ((1,), (1,)))
    )
    g_kx = hdot(g_proj, inv)
    weights = -kx * g_kx
    g_x = xs * jnp.sum(weights, axis=1, keepdims=True) - hdot(weights, zs)
    d_pooled = g_x / ell
    d_rows[...] = jnp.zeros(d_rows.shape, BF16)
    d_rows[0:8, :] = (d_pooled / cells).astype(BF16)
    d_two = d_rows[...]

    taps = [
        bdot(d_two, k2[t * width : (t + 1) * width, :], ((1,), (1,))) / sigma_two for t in range(9)
    ]
    wide = lax.broadcasted_iota(jnp.int32, (side, 1), 0)
    for n in range(images):
        for kind, kept in enumerate(((0, 1), (0, 1, 2), (1, 2))):
            across = [total([taps[3 * r + c][n : n + 1] for r in kept]) for c in range(3)]
            middle = across[0] + across[1] + across[2]
            pattern[n, kind] = jnp.where(
                wide == 0, across[0] + across[1],
                jnp.where(wide == side - 1, across[1] + across[2], middle),
            )

    loads[1].wait()
    mean_two, inverse_two = stats[3:4, :], stats[11:12, :]
    gain, bias = norms[2:3, :], norms[3:4, :]
    none = jnp.zeros((8, width), F32)
    sums = (none, none)
    for n in range(images):
        def step(h, carry):
            kind = jnp.where(h == 0, 0, jnp.where(h == side - 1, 2, 1))
            at = pl.ds(pl.multiple_of(n * cells + h * side, side), side)
            normed = (y[at, :] - mean_two) * inverse_two
            grad = gelu_slope(normed * gain + bias) * pattern[n, kind]
            d_pre[at, :] = grad
            return carry[0] + fold(grad), carry[1] + fold(grad * normed)
        sums = lax.fori_loop(0, side, step, sums)
    one_a[...] = jnp.zeros(one_a.shape, F32)
    one_a[0:1, :] = jnp.sum(sums[0], axis=0, keepdims=True)
    one_a[1:2, :] = jnp.sum(sums[1], axis=0, keepdims=True)
    ex_a[dp] = one_a[...]
    first = Spread("dp", n_dp, one_a, ex_a, a_send, a_recv)
    first.start()

    grads_out[...] = jnp.zeros(grads_out.shape, F32)
    over = hdot(weights, jnp.ones((8, 128), F32), ((0,), (0,)))[:, 0:1]
    g_z = zs * over - hdot(weights, xs, ((0,), (0,)))
    grads_out[0:size, :] = g_z[0:size]
    grads_out[20:21, :] = jnp.sum(g_x * xs, axis=0, keepdims=True)
    grads_out[22:23, :] = total([
        cells * branch_pool[n] * d_two[n : n + 1, :].astype(F32) for n in range(images)
    ])
    grads_out[23:24, :] = jnp.zeros((1, width), F32) + loss
    grads_out[32:64, 0 : classes * IND] = hdot(proj, g_spread, ((0,), (0,)))
    grads_out[32:64, 384 : 384 + IND] = hdot(g_kx, proj, ((0,), (0,)))
    grads_out[32:48, 512 : 512 + IND] = hdot(g_avg, proj, ((0,), (0,)))
    head_out[...] = jnp.zeros(head_out.shape, F32)
    head_out[0:8, :] = d_pooled
    head_out[8:16, :] = d_two[0:8, :].astype(F32)
    for n in range(images):
        edge = jnp.zeros((1, side, 3 * width), BF16)
        cat[n, 0:1] = edge
        cat[n, side + 1 : side + 2] = edge

    first.wait()
    one_b[...] = total([ex_a[i] for i in range(n_dp)])
    ex_b[rep] = one_b[...]
    second = Spread("replica", n_rep, one_b, ex_b, b_send, b_recv)
    second.start()
    second.wait()
    joined = total([ex_b[i] for i in range(n_rep)])
    d_bias, d_gain = joined[0:1, :], joined[1:2, :]
    head_out[16:17, :] = d_gain
    head_out[17:18, :] = d_bias
    true_scale = inverse_two * sigma_one * gain
    cat_copies = []
    along = none
    for n in range(images):
        held = jnp.where(count > n, 1.0, 0.0)
        def step(i, carry):
            rows = BLOCK * side
            at = pl.ds(pl.multiple_of(n * cells + i * rows, rows), rows)
            raw = y[at, :]
            normed = (raw - mean_two) * inverse_two
            grad = (true_scale * held) * (
                d_pre[at, :] - d_bias / pixels - normed * (d_gain / pixels)
            )
            grad = grad.astype(BF16).astype(F32)
            store_shifted(cat, n, i * BLOCK, BLOCK, grad, side)
            return carry + fold(raw * grad)
        along = lax.fori_loop(0, side // BLOCK, step, along)
        copy = pltpu.make_async_copy(cat.at[n], cat_out.at[n], local.at[2 + n])
        copy.start()
        cat_copies.append(copy)
    grads_out[21:22, :] = jnp.sum(along, axis=0, keepdims=True) / sigma_one
    for level in (first, second):
        level.drain()
    for copy in cat_copies:
        copy.wait()


def head(n_dp, n_rep, side, counts, labels, indices, table, k2, y, windows, stem_pool, stats,
         norms, inducing, lengthscale, var_mean, var_lower):
    images, width = stem_pool.shape
    cells = side * side
    classes = var_mean.shape[0]
    shape = jax.ShapeDtypeStruct
    sem = pltpu.SemaphoreType.DMA
    return pl.pallas_call(
        functools.partial(head_kernel, n_dp, n_rep, side),
        out_shape=(
            shape((images, side + 2, side, 3 * width), BF16),
            shape((24, width), F32),
            shape((64, width), F32),
            shape((3, IND, IND), F32),
        ),
        in_specs=[SMEM, SMEM, SMEM, VMEM, ANY, ANY] + [VMEM] * 8,
        out_specs=(ANY, VMEM, VMEM, VMEM),
        scratch_shapes=[
            pltpu.VMEM(k2.shape, BF16),
            pltpu.VMEM(y.shape, F32),
            pltpu.VMEM(y.shape, F32),
            pltpu.VMEM((images, side + 2, side, 3 * width), BF16),
            pltpu.VMEM((images, 3, side, width), F32),
            pltpu.VMEM((IND, width), F32),
            pltpu.VMEM((IND, IND), F32),
            pltpu.VMEM((16, IND), F32),
            pltpu.VMEM((IND, classes * IND), F32),
            pltpu.VMEM((8, width), F32),
            pltpu.VMEM((8, IND), F32),
            pltpu.VMEM((images, 16, 16), F32),
            pltpu.VMEM((16, width), BF16),
            pltpu.VMEM((n_dp, 8, width), F32),
            pltpu.VMEM((n_rep, 8, width), F32),
            pltpu.VMEM((8, width), F32),
            pltpu.VMEM((8, width), F32),
            sem((n_dp,)), sem((n_dp,)), sem((n_rep,)), sem((n_rep,)),
            sem((2 + images,)),
        ],
        compiler_params=pltpu.CompilerParams(
            collective_id=1, has_side_effects=True, vmem_limit_bytes=56 << 20
        ),
    )(counts, labels, indices, table, k2, y, windows, stem_pool, stats, norms,
      inducing, lengthscale, var_mean, var_lower)


def greet_all(n_dp, n_rep):
    here = lax.axis_index("dp") * n_rep + lax.axis_index("replica")
    count = n_dp * n_rep
    barrier = pltpu.get_barrier_semaphore()

    def signal(j, carry):
        other = lax.rem(here + j, count)
        pl.semaphore_signal(
            barrier, inc=1, device_id={"dp": other // n_rep, "replica": lax.rem(other, n_rep)},
            device_id_type=MESH,
        )
        return carry

    lax.fori_loop(1, count, signal, 0)
    pl.semaphore_wait(barrier, count - 1)


def chunk_plan(share, width, count):
    plan, done, carried = [], 0, 0
    for r in range(3):
        first, last = r * 3 * width, (r + 1) * 3 * width
        items = []
        while done < count and (done + 1) * share <= last:
            begin = max(done * share, first)
            items.append((done, carried, begin - first, (done + 1) * share - begin))
            carried = 0
            done += 1
        rest = last - max(done * share, first)
        plan.append((items, (carried, last - first - rest, rest)))
        carried += rest
    return plan


def backward_kernel(
    n_dp, n_rep, side, share, fused,
    counts, cat_in, x_in, k1_in, k2_in, act_in, patches, stem, stats, norms, windows, head_rows, grads,
    part_out, big_out, sums_out, stem_out,
    cat, x, k1, total_rows, carry, mine, sib, rin, zin, zout, part, comb, wall, flat, flat_d,
    *rest,
):
    early = rest[0:11]
    late = rest[11:22]
    (c_send, c_recv, r_send, r_recv, z_send, z_recv, w_send, w_recv, local) = rest[22:]
    images = patches.shape[0]
    width = stem.shape[1]
    cells = side * side
    dp, rep = lax.axis_index("dp"), lax.axis_index("replica")
    core, z = lax.rem(dp, 2), dp // 2
    n_z, half = n_dp // 2, n_dp // 2
    sources = max(n_dp // 4, 1)
    owners = half * n_rep
    here = dp * n_rep + rep
    loads = [
        pltpu.make_async_copy(cat_in, cat, local.at[0]),
        pltpu.make_async_copy(x_in, x, local.at[1]),
        pltpu.make_async_copy(k1_in, k1, local.at[2]),
    ]
    for copy in loads:
        copy.start()
    greet_all(n_dp, n_rep)
    count = counts[0]
    valid = [jnp.where(count > n, 1.0, 0.0) for n in range(images)]

    early_sum = Reduce(n_dp, n_rep, *early[:5], early[5:])
    source = early[0]
    source[...] = jnp.zeros(source.shape, F32)
    put_rows(source, 0, grads[...])
    gram = total([
        bdot(patches[n], patches[n], ((0,), (0,))) * valid[n] for n in range(images)
    ])
    wide = jnp.concatenate([gram, jnp.zeros((32, 128 - 32), F32)], axis=1)
    per = source.shape[1]
    for k in range(32):
        row = 64 + k
        source[row // per, row % per : row % per + 1, 0:128] = wide[k : k + 1, :]
    early_sum.start()

    if fused:
        for t in range(9):
            comb[t, 0:images, :] = jnp.concatenate(
                [windows[n, t : t + 1, :] for n in range(images)], axis=0
            )
            comb[t, images : 2 * images, :] = head_rows[8 : 8 + images, :]

        def first_tap(owner):
            return jnp.minimum((owner * share) // width, 7)

        def window_copy(owner):
            return remote(
                comb.at[pl.ds(first_tap(owner), 2)], wall.at[here], w_send.at[owner], w_recv.at[here],
                {"dp": half + owner // n_rep, "replica": lax.rem(owner, n_rep)},
            )

        def send_windows(j, c):
            owner = lax.rem(here + j, owners)

            @pl.when(half * n_rep + owner != here)
            def _():
                window_copy(owner).start()
            return c

        lax.fori_loop(0, owners, send_windows, 0)

    def row_of_taps(r):
        acc = total([
            lax.dot_general(
                x[n].reshape(cells, width),
                cat[n, pl.ds(2 - r, side)].reshape(cells, 3 * width),
                (((0,), (0,)), ((), ())),
                preferred_element_type=F32,
            )
            for n in range(images)
        ])
        for c in range(3):
            total_rows[c * width : (c + 1) * width, :] = acc[:, (2 - c) * width : (3 - c) * width]

    def sib_copy(o):
        return remote(
            mine.at[o], sib.at[(o // (2 * n_rep)) * n_rep + o % n_rep],
            c_send.at[o], c_recv.at[(o // (2 * n_rep)) * n_rep + o % n_rep],
            {"dp": dp + 1 - 2 * core},
        )

    def ship(items, leftover):
        for o, carried, first, rows in items:
            if carried:
                carry[carried : carried + rows, :] = total_rows[first : first + rows, :]
                mine[o, 0:share, :] = carry[0:share, :].astype(BF16)
            else:
                mine[o, 0:share, :] = total_rows[first : first + rows, :].astype(BF16)
            pl.when(core != (o // n_rep) % 2)(sib_copy(o).start)
        carried, first, rows = leftover
        if rows:
            carry[carried : carried + rows, :] = total_rows[first : first + rows, :]

    def rep_copy(zi, j):
        peer = lax.rem(rep + j, n_rep)
        return remote(
            mine.at[(zi * 2 + core) * n_rep + peer], rin.at[zi, j - 1],
            r_send.at[zi, j], r_recv.at[zi, j], {"replica": peer},
        )

    def join_cores(zi):
        for j in list(range(1, n_rep)) + [0]:
            peer = lax.rem(rep + j, n_rep)
            at = zi * n_rep + peer
            remote(
                mine.at[0], sib.at[at], c_send.at[0], c_recv.at[at], {"dp": dp + 1 - 2 * core}
            ).wait_recv()
            o = (zi * 2 + core) * n_rep + peer
            joined = mine[o].astype(F32) + sib[at].astype(F32)
            mine[o] = joined.astype(BF16)
            if j:
                rep_copy(zi, j).start()

    z_pieces = ((0, 192), (192, share + 8 - 192)) if share > 200 else ((0, share + 8),)

    def z_copy(zi, piece, down):
        start, rows = z_pieces[piece]
        at = pl.ds(start, rows)
        step = n_dp - 2 if down else 2
        return remote(
            zout.at[zi, at, :], zin.at[zi, int(down), at, :],
            z_send.at[zi, piece], z_recv.at[zi, piece, int(down)],
            {"dp": lax.rem(dp + step, n_dp)},
        )

    def join_replicas(zi):
        for j in range(1, n_rep):
            rep_copy_in = remote(
                mine.at[0], rin.at[zi, j - 1], r_send.at[zi, j], r_recv.at[zi, j],
                {"replica": lax.rem(rep + n_rep - j, n_rep)},
            )
            rep_copy_in.wait_recv()
        o = (zi * 2 + core) * n_rep + rep
        for piece, (start, rows) in enumerate(z_pieces):
            value = mine[o, start : start + rows, :].astype(F32)
            for j in range(1, n_rep):
                value = value + rin[zi, j - 1, start : start + rows, :].astype(F32)
            part[zi, start : start + rows, :] = value

    def chain(zi):
        for piece, (start, rows) in enumerate(z_pieces):
            def arrived(down):
                z_copy(zi, piece, down).wait_recv()
                return zin[zi, int(down), start : start + rows, :].astype(F32)

            @pl.when(z > zi)
            def _():
                @pl.when(z < n_z - 1)
                def _():
                    part[zi, start : start + rows, :] += arrived(True)
                zout[zi, start : start + rows, :] = part[zi, start : start + rows, :].astype(BF16)
                z_copy(zi, piece, True).start()

            @pl.when(z < zi)
            def _():
                @pl.when(z > 0)
                def _():
                    part[zi, start : start + rows, :] += arrived(False)
                zout[zi, start : start + rows, :] = part[zi, start : start + rows, :].astype(BF16)
                z_copy(zi, piece, False).start()

            @pl.when(z == zi)
            def _():
                if n_z > zi + 1:
                    part[zi, start : start + rows, :] += arrived(True)
                if zi > 0:
                    part[zi, start : start + rows, :] += arrived(False)

    loads[0].wait()
    loads[1].wait()
    if fused:
        plan = chunk_plan(share, width, owners)
        for r in range(3):
            row_of_taps(r)
            ship(*plan[r])
            if r == 0:
                early_sum.middle()
            if r == 1:
                join_cores(0)
        for zi in range(1, sources):
            join_cores(zi)
    else:
        for r in range(3):
            row_of_taps(r)
            out_copy = pltpu.make_async_copy(
                total_rows, part_out.at[pl.ds(r * 3 * width, 3 * width), :], local.at[4]
            )
            out_copy.start()
            out_copy.wait()
        early_sum.middle()

    loads[2].wait()
    sigma = stats[4:5, :]
    mean_one, inverse_one, pixels = stats[0:1, :], stats[1:2, :], stats[2:3, :]
    gain, bias = norms[0:1, :], norms[1:2, :]
    none = jnp.zeros((8, width), F32)
    sums = (none, none, jnp.zeros((32, width), F32))
    for n in range(images):
        held = valid[n]
        def step(i, carried):
            rows = 2 * BLOCK * side
            acc = None
            for r in range(3):
                for c in range(3):
                    t = 8 - (3 * r + c)
                    lhs = cat[
                        n, pl.ds(i * 2 * BLOCK + r, 2 * BLOCK), :, c * width : (c + 1) * width
                    ].reshape(rows, width)
                    one = bdot(lhs, k1[t * width : (t + 1) * width, :], ((1,), (1,)))
                    acc = one if acc is None else acc + one
            at = pl.ds(pl.multiple_of(i * rows, rows), rows)
            pixel = patches[n, at, :]
            normed = (bdot(pixel, stem[...]) - mean_one) * inverse_one
            grad = gelu_slope(normed * gain + bias) * acc * (held / sigma)
            down = (grad * (inverse_one * gain) + head_rows[n : n + 1, :] / cells).astype(BF16)
            return (
                carried[0] + fold(grad),
                carried[1] + fold(grad * normed),
                carried[2] + bdot(pixel, down, ((0,), (0,))),
            )
        sums = lax.fori_loop(0, side // (2 * BLOCK), step, sums)
        if fused and n == 0:
            join_replicas(0)
            chain(0)
    if fused:
        join_replicas(1)
    late_sum = Reduce(n_dp, n_rep, *late[:5], late[5:])
    source_late = late[0]
    source_late[...] = jnp.zeros(source_late.shape, F32)
    put_rows(source_late, 0, sums[2][0:27])
    put_rows(source_late, 27, jnp.sum(sums[0], axis=0, keepdims=True))
    put_rows(source_late, 28, jnp.sum(sums[1], axis=0, keepdims=True))
    late_sum.start()
    early_sum.last()

    act_copy = pltpu.make_async_copy(act_in, x, local.at[5])
    act_copy.start()
    k2_copy = pltpu.make_async_copy(k2_in, k1, local.at[3])
    k2_copy.start()
    act_copy.wait()
    squares = none
    for n in range(images):
        def shift(i, carried):
            rows = BLOCK * side
            values = x[n, pl.ds(i * BLOCK, BLOCK)].reshape(rows, width).astype(F32)
            store_shifted(cat, n, i * BLOCK, BLOCK, values, side)
            return carried
        lax.fori_loop(0, side // BLOCK, shift, 0)
    late_sum.middle()
    k2_copy.wait()
    for n in range(images):
        held = valid[n]
        def step(i, carried):
            rows = 2 * BLOCK * side
            acc = None
            for r in range(3):
                lhs = cat[n, pl.ds(i * 2 * BLOCK + r, 2 * BLOCK)].reshape(rows, 3 * width)
                one = bdot(lhs, k1[r * 3 * width : (r + 1) * 3 * width, :])
                acc = one if acc is None else acc + one
            return carried + held * fold(acc * acc)
        squares = lax.fori_loop(0, side // (2 * BLOCK), step, squares)
        if n == 0:
            late_sum.last()
            if fused:
                chain(1)
    sigma_two = stats[5:6, :]
    sums_out[...] = jnp.zeros(sums_out.shape, F32)
    sums_out[0:1, :] = jnp.sum(squares, axis=0, keepdims=True) / (sigma_two * sigma_two)

    if fused:
        @pl.when(dp < half)
        def _():
            for zi in range(sources):
                @pl.when(z == zi)
                def _():
                    part_out[...] = part[zi, 0:share, :]

        @pl.when(dp >= half)
        def _():
            owner = here - owners
            wall[here] = comb[pl.ds(first_tap(owner), 2)]

            def take(j, c):
                origin = lax.rem(here + j, n_dp * n_rep)
                remote(
                    comb.at[pl.ds(0, 2)], wall.at[origin], w_send.at[0], w_recv.at[origin],
                    {"dp": origin // n_rep, "replica": lax.rem(origin, n_rep)},
                ).wait_recv()
                return c

            lax.fori_loop(1, n_dp * n_rep, take, 0)
            for s in range(n_dp * n_rep):
                for tap in range(2):
                    flat[tap, s * images : (s + 1) * images, :] = wall[s, tap, 0:images, :]
                flat_d[s * images : (s + 1) * images, :] = wall[s, 0, images : 2 * images, :]
            for tap in range(2):
                total_rows[tap * width : (tap + 1) * width, :] = hdot(
                    flat[tap], flat_d[...], ((0,), (0,))
                )
            offset = owner * share - first_tap(owner) * width
            part_out[...] = total_rows[pl.ds(pl.multiple_of(offset, 8), share), :]

        def drain_windows(j, c):
            owner = lax.rem(here + j, owners)

            @pl.when(half * n_rep + owner != here)
            def _():
                window_copy(owner).wait_send()
            return c

        lax.fori_loop(0, owners, drain_windows, 0)
        for o in range(owners):
            pl.when(core != (o // n_rep) % 2)(sib_copy(o).wait_send)
        for zi in range(sources):
            for j in range(1, n_rep):
                rep_copy(zi, j).wait_send()
            for piece in range(len(z_pieces)):
                pl.when(z > zi)(z_copy(zi, piece, True).wait_send)
                pl.when(z < zi)(z_copy(zi, piece, False).wait_send)
    early_sum.finish()
    late_sum.finish()
    for s in range(n_dp):
        for k in range(early[4].shape[1]):
            big_out[s * early[4].shape[1] + k : s * early[4].shape[1] + k + 1, :] = early[4][s, k : k + 1, :]
        for k in range(late[4].shape[1]):
            stem_out[s * late[4].shape[1] + k : s * late[4].shape[1] + k + 1, :] = late[4][s, k : k + 1, :]


def backward(n_dp, n_rep, side, share, fused, counts, cat, x, k1, k2, act, patches, stem, stats, norms,
             windows, head_rows, grads):
    images, width = patches.shape[0], stem.shape[1]
    half = n_dp // 2
    sources = max(n_dp // 4, 1)
    owners = half * n_rep
    devices = n_dp * n_rep
    shape = jax.ShapeDtypeStruct
    sem = pltpu.SemaphoreType.DMA
    rows = share + 8
    small = (1, 8, 128)
    early = reduce_scratch(n_dp, n_rep, 96, width)
    late = reduce_scratch(n_dp, n_rep, 32, width)
    early_rows = early[0].shape[0] * early[0].shape[1]
    late_rows = late[0].shape[0] * late[0].shape[1]
    part_rows = share if fused else 9 * width
    pieces = 2 if share > 200 else 1
    return pl.pallas_call(
        functools.partial(backward_kernel, n_dp, n_rep, side, share, fused),
        out_shape=(
            shape((part_rows, width), F32),
            shape((early_rows, width), F32),
            shape((8, width), F32),
            shape((late_rows, width), F32),
        ),
        in_specs=[SMEM] + [ANY] * 5 + [VMEM] * 7,
        out_specs=(VMEM if fused else ANY, VMEM, VMEM, VMEM),
        scratch_shapes=[
            pltpu.VMEM(cat.shape, BF16),
            pltpu.VMEM(x.shape, BF16),
            pltpu.VMEM(k1.shape, BF16),
            pltpu.VMEM((3 * width, width), F32),
            pltpu.VMEM((rows if fused else 8, width), F32),
            pltpu.VMEM((owners, rows, width) if fused else small, BF16),
            pltpu.VMEM((sources * n_rep, rows, width) if fused else small, BF16),
            pltpu.VMEM((sources, n_rep - 1, rows, width) if fused else small, BF16),
            pltpu.VMEM((sources, 2, rows, width) if fused else small, BF16),
            pltpu.VMEM((sources, rows, width) if fused else small, BF16),
            pltpu.VMEM((sources, rows, width) if fused else small, F32),
            pltpu.VMEM((10, 2 * images, width) if fused else small, F32),
            pltpu.VMEM((devices, 2, 2 * images, width) if fused else small, F32),
            pltpu.VMEM((2, devices * images, width) if fused else small, F32),
            pltpu.VMEM((devices * images, width) if fused else small[1:], F32),
            *early,
            *late,
            sem((owners,)), sem((sources * n_rep,)),
            sem((sources, n_rep)), sem((sources, n_rep)),
            sem((sources, pieces)), sem((sources, pieces, 2)),
            sem((owners,)), sem((devices,)),
            sem((6,)),
        ],
        compiler_params=pltpu.CompilerParams(
            collective_id=2, has_side_effects=True, vmem_limit_bytes=62 << 20
        ),
    )(counts, cat, x, k1, k2, act, patches, stem, stats, norms, windows, head_rows, grads)


def whole_sum(values):
    return jnp.sum(jnp.sum(values, axis=1, keepdims=True), axis=0, keepdims=True)


def lamb_step(weight, gradient, first, second, out, rows=False):
    new_one, new_two, direction = lamb_moments(weight, gradient, first, second)
    if rows:
        sizes = [jnp.sum(v * v, axis=1, keepdims=True) for v in (weight, direction)]
    else:
        sizes = [whole_sum(v * v) for v in (weight, direction)]
    out[0][...] = weight - RATE * (jnp.sqrt(sizes[0]) / jnp.sqrt(sizes[1])) * direction
    out[1][...] = new_one
    out[2][...] = new_two


def finish_kernel(
    n_dp, n_rep,
    conv_sq, sums, big, late, head_rows, stats, chol, norms_all, stem, stem_w, stem_m, stem_s,
    norm_w, norm_m, norm_s, ind_w, ind_m, ind_s, len_w, len_m, len_s,
    mean_w, mean_m, mean_s, low_w, low_m, low_s, *rest,
):
    outs = rest[:19]
    (z_pad, w_pad, factor_pad, inverse_pad, ex_a, ex_b, one_a, one_b, a_send, a_recv, b_send, b_recv) = rest[19:]
    misc = outs[18]
    width = stem.shape[1]
    half = n_dp // 2
    dp, rep = lax.axis_index("dp"), lax.axis_index("replica")
    size, classes = ind_w.shape[0], mean_w.shape[0]
    greet(n_dp, n_rep)
    one_a[...] = jnp.zeros(one_a.shape, F32)
    one_a[0:2, 0:128] = conv_sq[0:2, :]
    one_a[2:3, :] = sums[0:1, :]
    ex_a[dp] = one_a[...]
    first = Spread("dp", n_dp, one_a, ex_a, a_send, a_recv)
    first.start()

    pixels = stats[2:3, :]
    scale_row = 1024.0 / pixels
    mean_one, inverse_one = stats[0:1, :], stats[1:2, :]
    scale = head_rows[18:19, 0:1]

    gram = big[64:96, 0:32]
    patch_sums = gram[:, 31:32]
    weights = stem[...].astype(F32)
    centred = inverse_one * (hdot(gram, weights) - patch_sums * mean_one)
    d_bias, d_gain = late[27:28, :], late[28:29, :]
    stem_grad = late[0:32, :] - (inverse_one * norms_all[0:1, :] / pixels) * (
        patch_sums * d_bias + centred * d_gain
    )
    lamb_step(stem_w[...], stem_grad[0 : stem_w.shape[0]], stem_m[...], stem_s[...], outs[0:3])
    norm_grad = jnp.concatenate([d_gain, d_bias, head_rows[16:18, :]], axis=0)
    lamb_step(norm_w[...], norm_grad, norm_m[...], norm_s[...], outs[3:6], rows=True)

    ell = len_w[...]
    z_pad[...] = jnp.zeros(z_pad.shape, F32)
    z_pad[0:size, :] = ind_w[...] / ell
    zs = z_pad[...]
    kzz, factor, inverse = chol[0], chol[1], chol[2]
    line = lax.broadcasted_iota(jnp.int32, (IND, IND), 0)
    lane = lax.broadcasted_iota(jnp.int32, (IND, IND), 1)
    g_chol = jnp.where(line >= lane, -big[32:64, 384 : 384 + IND], 0.0)
    lower = hdot(factor, g_chol, ((0,), (0,)))
    phi = jnp.where(line > lane, lower, jnp.where(line == lane, 0.5 * lower, 0.0))
    back = hdot(inverse, hdot(phi, inverse), ((0,), (0,)))
    back_t = hdot(inverse, hdot(phi, inverse, ((0,), (0,))), ((0,), (0,)))
    weights_z = -0.5 * kzz * (back + back_t)
    g_z = big[0:32, :]
    g_z = jnp.where(lax.broadcasted_iota(jnp.int32, (IND, 1), 0) < size, g_z, 0.0) + 2.0 * (
        zs * jnp.sum(weights_z, axis=1, keepdims=True) - hdot(weights_z, zs)
    )
    lamb_step(ind_w[...], (g_z / ell)[0:size], ind_m[...], ind_s[...], outs[6:9])
    g_len = -(big[20:21, :] + jnp.sum(g_z * zs, axis=0, keepdims=True)) / ell
    lamb_step(ell, g_len, len_m[...], len_s[...], outs[9:12])

    means = mean_w[...]
    g_mean = big[32 : 32 + classes, 512 : 512 + size] + means * scale
    lamb_step(means, g_mean, mean_m[...], mean_s[...], outs[12:15])
    small_line = lax.broadcasted_iota(jnp.int32, (size, size), 0)
    small_lane = lax.broadcasted_iota(jnp.int32, (size, size), 1)
    kl = 0.5 * whole_sum(means * means) - 0.5 * classes * size
    weight_sq, step_sq = jnp.zeros((1, 1), F32), jnp.zeros((1, 1), F32)
    steps = []
    for c in range(classes):
        weight = low_w[c]
        factors = scale_rows(weight)
        inner = big[32 : 32 + size, c * IND : c * IND + size] + factors * scale
        grad = jnp.where(
            small_line > small_lane, inner,
            jnp.where(small_line == small_lane, factors * inner - scale, 0.0),
        )
        new_one, new_two, direction = lamb_moments(weight, grad, low_m[c], low_s[c])
        outs[16][c] = new_one
        outs[17][c] = new_two
        weight_sq = weight_sq + whole_sum(weight * weight)
        step_sq = step_sq + whole_sum(direction * direction)
        diagonal = jnp.where(small_line == small_lane, weight, 0.0)
        kl = kl + 0.5 * whole_sum(factors * factors) - whole_sum(diagonal)
        steps.append(direction)
    ratio = RATE * jnp.sqrt(weight_sq) / jnp.sqrt(step_sq)
    for c in range(classes):
        outs[15][c] = low_w[c] - ratio * steps[c]

    first.wait()
    one_b[...] = jnp.zeros(one_b.shape, F32)
    for l in range(2):
        near = range(l * half, (l + 1) * half)
        one_b[l : l + 1, :] = total([ex_a[i, 0:1, :] for i in near])
        one_b[2 + l : 3 + l, :] = total([ex_a[i, 1:2, :] for i in near])
    one_b[4:5, :] = total(rows_of(ex_a, 2))
    ex_b[rep] = one_b[...]
    second = Spread("replica", n_rep, one_b, ex_b, b_send, b_recv)
    second.start()
    second.wait()
    joined = total([ex_b[i] for i in range(n_rep)])
    misc[...] = jnp.zeros(misc.shape, F32)
    for l in range(2):
        misc[l : l + 1, :] = jnp.sqrt(joined[l : l + 1, 0:128]) / jnp.sqrt(joined[2 + l : 3 + l, 0:128])
    lanes = jnp.zeros((1, 128), F32)
    cells_all = pixels[:, 0:1] * width
    misc[2:3, :] = lanes + jnp.sqrt(jnp.sum(stats[10:11, :], axis=1, keepdims=True) / cells_all)
    misc[3:4, :] = lanes + jnp.sqrt(jnp.sum(joined[4:5, :], axis=1, keepdims=True) / cells_all)
    misc[4:5, :] = lanes + (big[23:24, 0:1] + kl)
    first.drain()
    second.drain()


def finish(n_dp, n_rep, *args):
    width = args[8].shape[1]
    shape = jax.ShapeDtypeStruct
    sem = pltpu.SemaphoreType.DMA
    params = args[9:27:3]
    outs = tuple(shape(p.shape, F32) for p in params for _ in range(3)) + (shape((8, 128), F32),)
    return pl.pallas_call(
        functools.partial(finish_kernel, n_dp, n_rep),
        out_shape=outs,
        in_specs=[VMEM] * len(args),
        out_specs=(VMEM,) * len(outs),
        scratch_shapes=[
            pltpu.VMEM((IND, width), F32),
            pltpu.VMEM((IND, width), F32),
            pltpu.VMEM((IND, IND), F32),
            pltpu.VMEM((IND, IND), F32),
            pltpu.VMEM((n_dp, 8, width), F32),
            pltpu.VMEM((n_rep, 8, width), F32),
            pltpu.VMEM((8, width), F32),
            pltpu.VMEM((8, width), F32),
            sem((n_dp,)), sem((n_dp,)), sem((n_rep,)), sem((n_rep,)),
        ],
        compiler_params=pltpu.CompilerParams(
            collective_id=3, has_side_effects=True, vmem_limit_bytes=32 << 20
        ),
    )(*args)


def on_device(
    images, labels, counts, noise_table, noise_index, power_start,
    conv_weight, conv_first, conv_second,
    stem_weight, stem_first, stem_second,
    norm_params, norm_first, norm_second,
    inducing, inducing_first, inducing_second,
    lengthscale, length_first, length_second,
    var_mean, mean_first, mean_second,
    var_lower, lower_first, lower_second,
):
    width = stem_weight.shape[1]
    side = images.shape[2]
    cells = side * side
    n_dp, n_rep = lax.axis_size("dp"), lax.axis_size("replica")
    here = lax.axis_index(AXES)
    per_kernel = n_dp * n_rep // 2
    owner = here // per_kernel
    select = (jnp.arange(2) == owner).astype(F32)
    geometry = (n_dp, n_rep, side)

    rows = conv_weight.astype(BF16).reshape(-1, width)
    share = rows.shape[0]
    fused = share % 16 == 8 and n_rep % 2 == 0 and n_dp % 4 == 0
    start = jnp.sum(select[:, None] * power_start, axis=0)
    bound = jnp.zeros((16, width), BF16)
    if fused:
        odd = here % 2 == 1
        blank = jnp.zeros((8, width), BF16)
        main = jnp.where(odd, rows[8:], rows[:-8])
        bound = jnp.where(
            odd, jnp.concatenate([blank, rows[:8]]), jnp.concatenate([rows[-8:], blank])
        )
        extra = start[None]
    else:
        gathered = lax.all_gather(rows, AXES, axis=0, tiled=True)
        main = gathered[: 9 * width]
        own = rows.astype(F32)
        own_along = jnp.sum(own * start, axis=1)
        back_rows = jnp.sum(own * own_along[:, None], axis=0)
        extra = jnp.stack([back_rows, jnp.full((width,), jnp.sum(own_along * own_along))])
    padded = jnp.pad(images, ((0, 0), (0, 0), (1, 1), (1, 1)))
    patches = jnp.stack(
        [padded[:, :, r : r + side, c : c + side] for r in range(3) for c in range(3)], axis=1
    )
    patches = patches.reshape(images.shape[0], -1, cells)
    colours = patches.shape[1]
    patches = jnp.concatenate(
        [
            patches,
            jnp.zeros((images.shape[0], 31 - colours, cells), BF16),
            jnp.ones((images.shape[0], 1, cells), BF16),
        ],
        axis=1,
    ).transpose(0, 2, 1)
    stem_kernel = jnp.pad(stem_weight.astype(BF16), ((0, 32 - colours), (0, 0)))
    k_one, k_two, act_one, raw_one, act_two, windows, stem_pool, stats = forward(
        *geometry, share, fused, counts, main, bound, patches, stem_kernel, extra, norm_params
    )
    if not fused:
        k_two = gathered[9 * width :]
    lengths = lengthscale[None]
    cat, head_rows, grads, chol = head(
        *geometry, counts, labels, noise_index, noise_table, k_two, raw_one, windows, stem_pool,
        stats, norm_params, inducing, lengths, var_mean, var_lower,
    )
    part, big, sums, late = backward(
        *geometry, share, fused, counts, cat, act_one, k_one, k_two,
        act_two.reshape(act_one.shape), patches, stem_kernel, stats, norm_params, windows,
        head_rows, grads,
    )
    if not fused:
        part_one = lax.psum_scatter(
            jnp.concatenate([part.reshape(-1), jnp.zeros((part.size,), F32)]),
            AXES, scatter_dimension=0, tiled=True,
        ).reshape(-1, width)
        all_windows, all_grads = lax.all_gather(
            (windows[:, :9], head_rows[8 : 8 + images.shape[0]]), AXES, tiled=True
        )
        all_windows = all_windows.reshape(all_windows.shape[0], -1)
        mine = lax.dynamic_slice_in_dim(
            all_windows, lax.rem(here, per_kernel) * share, share, axis=1
        )
        part = jnp.where(owner == 0, part_one, jnp.dot(mine.T, all_grads, precision=HIGH))

    pixels = stats[2, 0]
    totals = pixels / cells
    sigmas = stats[4:6, 0]
    rows = rows.astype(F32)
    my_sigma = jnp.sum(select * sigmas)
    my_norm = jnp.sum(select * stats[6:8, 0])
    my_vector = jnp.sum(select[:, None] * stats[8:10], axis=0)
    d_sigma = -jnp.sum(select * jnp.sum(big[21:23], axis=1)) / my_sigma
    left = jnp.sum(rows * start, axis=1) / my_norm
    d_left = jnp.sum(rows * (my_vector / my_norm), axis=1) - left * (my_sigma / my_norm)
    conv_part = part / my_sigma + d_sigma * (
        left[:, None] * my_vector[None, :] + d_left[:, None] * start[None, :]
    )
    new_one, new_two, direction = lamb_moments(
        conv_weight, conv_part.reshape(-1), conv_first, conv_second
    )
    squares = jnp.stack([jnp.sum(conv_weight * conv_weight), jnp.sum(direction * direction)])
    conv_sq = jnp.broadcast_to(jnp.pad(squares, (0, 6))[:, None], (8, 128))
    head_rows = head_rows.at[18].set(1.0 / totals)
    done = finish(
        n_dp, n_rep, conv_sq, sums, big, late, head_rows, stats, chol, norm_params, stem_kernel,
        stem_weight, stem_first, stem_second, norm_params, norm_first, norm_second,
        inducing, inducing_first, inducing_second, lengths, length_first[None], length_second[None],
        var_mean, mean_first, mean_second, var_lower, lower_first, lower_second,
    )
    misc = done[18][:, 0]
    new_conv = conv_weight - (RATE * jnp.sum(select * misc[:2])) * direction
    small = [v.reshape(-1) if 9 <= i < 12 else v for i, v in enumerate(done[:18])]
    return (
        jnp.stack([misc[4], totals]),
        new_conv, new_one, new_two, new_conv.astype(BF16),
        *small,
        sigmas, misc[2:4],
    )


def solution(mesh):
    split = P(AXES)
    return jax.shard_map(
        on_device,
        mesh=mesh,
        in_specs=(split, split, split, P(), split, P(), split, split, split) + (P(),) * 18,
        out_specs=(P(),) + (split,) * 4 + (P(),) * 20,
        check_vma=False,
    )
```

```python
import functools

import jax
import jax.numpy as jnp
from jax import lax
from jax.experimental import pallas as pl
from jax.experimental.pallas import tpu as pltpu
from jax.sharding import PartitionSpec as P

STEP = 10
HIGH = lax.Precision.HIGHEST
EPS_NORM = 1e-05
JITTER = 0.001
BETA_ONE = 0.9
BETA_TWO = 0.999
RATE = 0.3
DECAY = 0.01
EPS_ADAM = 1e-08
AXES = ("dp", "replica")


def lamb_moments(weight, gradient, moment_one, moment_two):
    new_one = BETA_ONE * moment_one + (1.0 - BETA_ONE) * gradient
    new_two = BETA_TWO * moment_two + (1.0 - BETA_TWO) * gradient * gradient
    direction = (
        new_one / (1.0 - BETA_ONE**STEP) / (jnp.sqrt(new_two / (1.0 - BETA_TWO**STEP)) + EPS_ADAM)
        + DECAY * weight
    )
    return (new_one, new_two, direction)


MESH = pl.DeviceIdType.MESH
ANY = pl.BlockSpec(memory_space=pl.ANY)
VMEM = pl.BlockSpec(memory_space=pltpu.VMEM)
SMEM = pl.BlockSpec(memory_space=pltpu.SMEM)
F32 = jnp.float32
BF16 = jnp.bfloat16


def remote(src, dst, send, recv, where):
    return pltpu.make_async_remote_copy(
        src_ref=src, dst_ref=dst, send_sem=send, recv_sem=recv,
        device_id=where, device_id_type=MESH,
    )


def greet(n_dp, n_rep):
    dp, rep = lax.axis_index("dp"), lax.axis_index("replica")
    barrier = pltpu.get_barrier_semaphore()
    for j in range(1, n_dp):
        pl.semaphore_signal(
            barrier, inc=1, device_id={"dp": lax.rem(dp + j, n_dp)}, device_id_type=MESH
        )
    for j in range(1, n_rep):
        pl.semaphore_signal(
            barrier, inc=1, device_id={"replica": lax.rem(rep + j, n_rep)}, device_id_type=MESH
        )
    return lambda: pl.semaphore_wait(barrier, n_dp + n_rep - 2)


class Spread:
    def __init__(self, axis, size, src, dst, send, recv):
        self.axis, self.size, self.src, self.dst, self.send, self.recv = axis, size, src, dst, send, recv
        self.me = lax.axis_index(axis)

    def copies(self):
        for j in range(1, self.size):
            yield remote(
                self.src, self.dst.at[self.me], self.send.at[j], self.recv.at[j],
                {self.axis: lax.rem(self.me + j, self.size)},
            )

    def start(self):
        for copy in self.copies():
            copy.start()

    def wait(self):
        for j in range(1, self.size):
            source = lax.rem(self.me + self.size - j, self.size)
            remote(
                self.src, self.dst.at[source], self.send.at[j], self.recv.at[j],
                {self.axis: source},
            ).wait_recv()

    def drain(self):
        for copy in self.copies():
            copy.wait_send()


def rows_of(refs, row):
    return [refs[i, row : row + 1, :] for i in range(refs.shape[0])]


def total(values):
    result = values[0]
    for value in values[1:]:
        result = result + value
    return result


def join_moments(refs):
    averages, squares, counts = rows_of(refs, 0), rows_of(refs, 1), rows_of(refs, 2)
    count = total(counts)
    average = total([a * n for a, n in zip(averages, counts)]) / count
    spread = total(
        [s + n * (a - average) * (a - average) for a, s, n in zip(averages, squares, counts)]
    )
    return average, spread, count


def hdot(a, b, dims=((1,), (0,))):
    return lax.dot_general(
        a, b, (dims, ((), ())), precision=HIGH, preferred_element_type=F32
    )


def bdot(a, b, dims=((1,), (0,))):
    return lax.dot_general(a, b, (dims, ((), ())), preferred_element_type=F32)


class Gather:
    def __init__(self, which, n_dp, share, buffer, sems):
        self.which, self.n_dp, self.share, self.buffer = which, n_dp, share, buffer
        tiles = (share - 8) // 16
        edges = [tiles * i // PIECES * 16 for i in range(PIECES + 1)]
        self.pieces = list(zip(edges, [hi - lo for lo, hi in zip(edges, edges[1:])]))
        self.z_send, self.z_recv, self.r_send, self.r_recv, self.c_send, self.c_recv = [
            s.at[which] for s in sems
        ]
        self.dp, rep = lax.axis_index("dp"), lax.axis_index("replica")
        self.reps = (rep, rep + 1 - 2 * lax.rem(rep, 2), rep + 2 - 4 * (rep // 2), 3 - rep)
        self.core, self.z = lax.rem(self.dp, 2), self.dp // 2
        self.n_z = n_dp // 2
        self.sources = n_dp // 4
        self.order = range(self.sources) if which else range(self.sources - 1, -1, -1)

    def first(self, zi, core, k):
        owner = (zi * 2 + core) * 4 + self.reps[k]
        return (owner // 2) * (2 * self.share) + lax.rem(owner, 2) * (self.share + 8)

    def each(self, zi, core, k, piece, act):
        start, rows = self.pieces[piece]
        begin = pl.multiple_of(self.first(zi, core, k) + start, 16)
        if piece < len(self.pieces) - 1:
            act(self.buffer.at[pl.ds(begin, rows), :])
            return
        even = lax.rem(self.reps[k], 2) == 0
        pl.when(even)(lambda: act(self.buffer.at[pl.ds(begin, rows + 16), :]))
        pl.when(~even)(lambda: act(self.buffer.at[pl.ds(begin, rows), :]))

    def source(self, zi):
        return zi + self.which * self.sources

    def along(self, zi, piece, what, ways=(0, 1)):
        def act(ref):
            for way in ways:
                condition = (
                    ((self.z <= self.source(zi)) & (self.z > 0)) if way
                    else ((self.z >= self.source(zi)) & (self.z < self.n_z - 1))
                )
                step = self.n_dp - 2 if way else 2
                copy = remote(
                    ref, ref, self.z_send.at[zi, piece, way], self.z_recv.at[zi, piece],
                    {"dp": lax.rem(self.dp + step, self.n_dp)},
                )
                if what == "wait_recv":
                    copy.wait_recv()
                    return
                pl.when(condition)(getattr(copy, what))
        self.each(zi, self.core, 0, piece, act)

    def goes_on(self, zi):
        gap = self.z - self.source(zi)
        return ((gap < 0) & (self.z > 0)) | ((gap > 0) & (self.z < self.n_z - 1))

    def near(self, zi, piece, k, what):
        def act(ref):
            getattr(remote(
                ref, ref, self.r_send.at[zi, piece, k], self.r_recv.at[zi, piece, k],
                {"replica": self.reps[k]},
            ), what)()
        self.each(zi, self.core, k if what == "wait_recv" else 0, piece, act)

    def passed(self, zi, piece, what):
        k = 1 + piece % 2
        def act(ref):
            getattr(remote(
                ref, ref, self.r_send.at[zi, piece, 3], self.r_recv.at[zi, piece, 3],
                {"replica": self.reps[3 - k]},
            ), what)()
        self.each(zi, self.core, 3 if what == "wait_recv" else k, piece, act)

    def over(self, zi, piece, k, what):
        def act(ref):
            getattr(remote(
                ref, ref, self.c_send.at[zi, piece, k], self.c_recv.at[zi, piece, k],
                {"dp": self.dp + 1 - 2 * self.core},
            ), what)()
        self.each(zi, 1 - self.core if what == "wait_recv" else self.core, k, piece, act)

    def send_plane(self, zi, piece):
        for k in (1, 2):
            self.near(zi, piece, k, "start")
        self.over(zi, piece, 0, "start")

    def own(self, pieces, ways, plane):
        for zi in range(self.sources):
            @pl.when(self.z == self.source(zi))
            def _():
                for piece in pieces:
                    self.along(zi, piece, "start", ways)
                    if plane:
                        self.send_plane(zi, piece)

    def column(self, zi, pieces):
        @pl.when(self.z != self.source(zi))
        def _():
            for piece in pieces:
                self.along(zi, piece, "wait_recv")
                self.along(zi, piece, "start")
                self.send_plane(zi, piece)

    def hop(self, distance):
        for zi in self.order:
            gap = self.z - self.source(zi)
            @pl.when(self.goes_on(zi) & ((gap == distance) | (gap == -distance)))
            def _():
                for piece in range(len(self.pieces)):
                    self.along(zi, piece, "wait_recv")
                    self.along(zi, piece, "start")

    def plane(self, zi):
        for piece in range(len(self.pieces)):
            pl.when((self.z != self.source(zi)) & ~self.goes_on(zi))(
                functools.partial(self.along, zi, piece, "wait_recv")
            )
            self.send_plane(zi, piece)

    def neighbours(self, zi, pieces):
        for piece in pieces:
            for k in (1, 2):
                self.near(zi, piece, k, "wait_recv")
                if k == 1 + piece % 2:
                    self.passed(zi, piece, "start")
                self.over(zi, piece, k, "start")

    def opposite(self, zi):
        for piece in range(len(self.pieces)):
            self.passed(zi, piece, "wait_recv")
            self.over(zi, piece, 3, "start")

    def from_core(self, zi):
        for piece in range(len(self.pieces)):
            for k in range(4):
                self.over(zi, piece, k, "wait_recv")

    def drain(self):
        for piece in range(len(self.pieces)):
            for zi in range(self.sources):
                self.along(zi, piece, "wait_send")
                for k in (1, 2):
                    self.near(zi, piece, k, "wait_send")
                self.passed(zi, piece, "wait_send")
                for k in range(4):
                    self.over(zi, piece, k, "wait_send")


PIECES = 4


def pixel_column(rows, side):
    return lax.rem(lax.broadcasted_iota(jnp.int32, (rows, 1), 0), side)


def store_shifted(ref, image, first, block, values, side):
    width = values.shape[1]
    rows = block * side
    column = pixel_column(rows, side)
    left = jnp.where(column == 0, 0.0, pltpu.roll(values, 1, 0))
    right = jnp.where(column == side - 1, 0.0, pltpu.roll(values, rows - 1, 0))
    for c, moved in enumerate((left, values, right)):
        ref[image, pl.ds(first + 1, block), :, c * width : (c + 1) * width] = (
            moved.astype(BF16).reshape(block, side, width)
        )


def window_matrix(side):
    shape = (side * side, 16)
    pixel = lax.broadcasted_iota(jnp.int32, shape, 0)
    tap = lax.broadcasted_iota(jnp.int32, shape, 1)
    r, c = tap // 3, lax.rem(tap, 3)
    h, w = pixel // side, lax.rem(pixel, side)
    keep = (
        (tap < 9)
        & ~((r == 0) & (h == side - 1)) & ~((r == 2) & (h == 0))
        & ~((c == 0) & (w == side - 1)) & ~((c == 2) & (w == 0))
    )
    return jnp.where(keep, 1.0, 0.0).astype(BF16)


BLOCK = 8


def make_patches(images, side, patches, line):
    cells = side * side
    pixel = lax.broadcasted_iota(jnp.int32, (1, cells), 1)
    h, w = pixel // side, lax.rem(pixel, side)
    colours = images.shape[1]
    for n in range(images.shape[0]):
        line[...] = jnp.where(
            lax.broadcasted_iota(jnp.int32, line.shape, 0) == 31, 1.0, 0.0
        )
        values = images[n]
        for t in range(9):
            down, right = t // 3 - 1, t % 3 - 1
            shift = down * side + right
            moved = pltpu.roll(values, (-shift) % cells, 1) if shift else values
            inside = (h + down >= 0) & (h + down < side) & (w + right >= 0) & (w + right < side)
            line[colours * t : colours * (t + 1), :] = jnp.where(inside, moved, 0.0)
        patches[n] = line[...].astype(BF16)


def forward_kernel(
    n_dp, n_rep, side, share, fused,
    counts, main, bound, pictures, stem_in, start, norms,
    k1_out, k2_out, x_out, y_out, act_out, windows, stem_pool, stats, patches, stem,
    line, k1, xcat, y, act, seam, ex_a, ex_b, one_a, one_b,
    z_send, z_recv, r_send, r_recv, c_send, c_recv,
    a_send, a_recv, b_send, b_recv, s_send, s_recv, local,
):
    images = pictures.shape[0]
    width = stem_in.shape[1]
    cells = side * side
    dp, rep = lax.axis_index("dp"), lax.axis_index("replica")
    half = n_dp // 2
    greeted = greet(n_dp, n_rep)

    if fused:
        rows = share - 8
        sems = (z_send, z_recv, r_send, r_recv, c_send, c_recv)
        one, two = [
            Gather(l, n_dp, share, buffer, sems) for l, buffer in enumerate((k1, k2_out))
        ]
        every = range(PIECES)
        early, final = every[:-1], every[-1:]
        even = lax.rem(rep, 2) == 0
        owner = lax.rem(dp, half) * n_rep + rep
        own_first = (owner // 2) * (2 * share) + lax.rem(owner, 2) * (share + 8)
        seam_copy = remote(
            bound, seam.at[1], s_send.at[0], s_recv.at[0],
            {"replica": rep + 1 - 2 * lax.rem(rep, 2)},
        )

        def own_copies(what):
            for l, buffer in enumerate((k1, k2_out)):
                @pl.when((dp < half) if l == 0 else (dp >= half))
                def _():
                    at = pl.ds(pl.multiple_of(own_first, 16), rows)
                    getattr(pltpu.make_async_copy(main, buffer.at[at, :], local.at[0]), what)()

        def put_seam():
            @pl.when(even)
            def _():
                seam_copy.wait_recv()
                seam[0] = (bound[...].astype(F32) + seam[1].astype(F32)).astype(BF16)
                for l, buffer in enumerate((k1, k2_out)):
                    @pl.when((dp < half) if l == 0 else (dp >= half))
                    def _():
                        at = pl.ds(pl.multiple_of(own_first + rows, 16), 16)
                        copy = pltpu.make_async_copy(seam.at[0], buffer.at[at, :], local.at[8])
                        copy.start()
                        copy.wait()

        own_copies("start")
    else:
        copy_in = pltpu.make_async_copy(main, k1, local.at[0])
        copy_in.start()

    if fused:
        own_copies("wait")
    greeted()
    if fused:
        pl.when(~even)(seam_copy.start)
        one.own(every[:2], (0, 1), True)
        two.own(every[:2], (1,), False)
    line[:, 0:width] = jnp.zeros((32, width), F32)
    line[0 : stem_in.shape[0], 0:width] = stem_in[...]
    stem[...] = line[:, 0:width].astype(BF16)
    weight = stem[...].astype(F32)
    count = counts[0]
    valid = [jnp.where(count > n, 1.0, 0.0) for n in range(images)]
    held = count.astype(F32) * cells
    make_patches(pictures, side, patches, line)
    grams, sums = [], []
    for n in range(images):
        grams.append(bdot(patches[n], patches[n], ((1,), (1,))))
        sums.append(grams[n][24:32])
        stem_pool[n : n + 1, :] = hdot(sums[n], weight)[7:8] * (1.0 / cells)
    gram = total([g * v for g, v in zip(grams, valid)])
    summed = total([s * v for s, v in zip(sums, valid)])
    square = jnp.sum(weight * hdot(gram, weight), axis=0, keepdims=True)
    last = jnp.where(lax.broadcasted_iota(jnp.int32, summed.shape, 0) == 7, summed, 0.0)
    cover = gram - hdot(last, last, ((0,), (0,))) / held
    zero = jnp.zeros((1, width), F32)
    payload = one_a.at[0]
    payload[...] = jnp.zeros(payload.shape, F32)
    payload[0:1, :] = hdot(summed, weight)[7:8] / held
    payload[1:2, :] = jnp.sum(weight * hdot(cover, weight), axis=0, keepdims=True)
    payload[2:3, :] = zero + held
    payload[5:6, :] = square

    if fused:
        vector = jnp.where(dp < half, start[0:1, :], start[1:2, :])
        own_rows = main[...].astype(F32)
        edge_rows = bound[...].astype(F32)
        along = jnp.sum(own_rows * vector, axis=1, keepdims=True)
        edge_along = jnp.sum(edge_rows * vector, axis=1, keepdims=True)
        payload[3:4, :] = jnp.sum(own_rows * along, axis=0, keepdims=True) + jnp.sum(
            edge_rows * edge_along, axis=0, keepdims=True
        )
        payload[4:5, :] = zero + (
            jnp.sum(along * along, axis=0, keepdims=True)
            + jnp.sum(edge_along * edge_along, axis=0, keepdims=True)
        )
    else:
        payload[3:4, :] = start[0:1, :]
        payload[4:5, :] = start[1:2, :]

    first = ex_a.at[0]
    first[dp] = payload[...]
    one_level = Spread("dp", n_dp, payload, first, a_send.at[0], a_recv.at[0])
    one_level.start()
    if fused:
        one.own(early[2:], (0, 1), True)
        two.own(early[2:], (1,), False)
    for n in range(images):
        blank = jnp.zeros((1, side, 3 * width), BF16)
        xcat[n, 0:1] = blank
        xcat[n, side + 1 : side + 2] = blank
    one_level.wait()
    second = ex_b.at[0]
    mean, spread, cell_count = join_moments(first)
    passed = one_b.at[0]
    passed[...] = jnp.zeros(passed.shape, F32)
    passed[0:1, :] = mean
    passed[1:2, :] = spread
    passed[2:3, :] = cell_count
    vectors, squares = rows_of(first, 3), rows_of(first, 4)
    passed[3:4, :] = total(vectors[:half])
    passed[4:5, :] = total(vectors[half:])
    passed[5:6, :] = total(squares[:half])
    passed[6:7, :] = total(squares[half:])
    passed[7:8, :] = total(rows_of(first, 5))
    second[rep] = passed[...]
    two_level = Spread("replica", n_rep, passed, second, b_send.at[0], b_recv.at[0])
    two_level.start()
    if fused:
        put_seam()
        one.own(final, (0, 1), True)
        two.own(final, (1,), False)
        one.column(1, every)
    two_level.wait()
    mean, spread, pixels = join_moments(second)
    inverse_one = lax.rsqrt(spread / pixels + EPS_NORM)
    joined = [total(rows_of(second, row)) for row in range(3, 8)]
    sigma_rows, start_rows = [], []
    for l in range(2):
        vec = jnp.sqrt(jnp.sum(joined[l] * joined[l], axis=1, keepdims=True))
        base = jnp.sqrt(joined[2 + l])
        sigma_rows.append(zero + vec / base)
        start_rows.append(base)
        stats[8 + l : 9 + l, :] = joined[l] / vec
    stats[0:1, :] = mean
    stats[1:2, :] = inverse_one
    stats[2:3, :] = pixels
    stats[4:5, :] = sigma_rows[0]
    stats[5:6, :] = sigma_rows[1]
    stats[6:7, :] = start_rows[0]
    stats[7:8, :] = start_rows[1]
    stats[10:11, :] = joined[4]
    scale_one = inverse_one * norms[0:1, :]
    shift_one = norms[1:2, :] - mean * scale_one

    def act_one(n, part):
        def step(i, carry):
            first_row = i * BLOCK
            pixel = pl.ds(pl.multiple_of(first_row * side, BLOCK * side), BLOCK * side)
            out = bdot(patches[n, :, pixel], stem[...], ((0,), (0,)))
            values = jax.nn.gelu(out * scale_one + shift_one)
            store_shifted(xcat, n, first_row, BLOCK, values, side)
            return carry
        half_steps = side // BLOCK // 2
        lax.fori_loop(part * half_steps, (part + 1) * half_steps, step, 0)

    for n in range(images):
        for part in range(2):
            act_one(n, part)
            if fused and n == 0 and part == 0:
                one.neighbours(1, every[:2])
                one.column(0, every[:2])
                one.neighbours(1, every[2:])
            elif fused and n == 0:
                one.column(0, every[2:])
                two.own(every, (0,), False)
                two.hop(1)
                one.neighbours(0, every[:2])
            elif fused and n == 1 and part == 0:
                two.hop(2)
                one.neighbours(0, every[2:])
    if fused:
        for zi in two.order:
            two.plane(zi)
        one.opposite(1)
        one.from_core(1)
    else:
        copy_in.wait()
    x_copies = [
        pltpu.make_async_copy(
            xcat.at[n, pl.ds(1, side), :, pl.ds(width, width)], x_out.at[n], local.at[2 + n]
        )
        for n in range(images)
    ]
    for copy in x_copies:
        copy.start()

    tap_row = 3 * width
    middle = -(-(9 * width // 2 - tap_row) // 128) * 128
    rows_step = 2 * BLOCK * side

    def window(n, i, r, lanes):
        return xcat[n, pl.ds(i * 2 * BLOCK + r, 2 * BLOCK), :, lanes].reshape(rows_step, -1)

    def at_rows(n, i):
        return pl.ds(pl.multiple_of(n * cells + i * rows_step, rows_step), rows_step)

    for n in range(images):
        def later_half(i, carry):
            y[at_rows(n, i), :] = bdot(
                window(n, i, 2, slice(0, tap_row)), k1[2 * tap_row : 3 * tap_row, :]
            ) + bdot(
                window(n, i, 1, slice(middle, tap_row)), k1[tap_row + middle : 2 * tap_row, :]
            )
            return carry
        lax.fori_loop(0, side // (2 * BLOCK), later_half, 0)
        if fused and n == 0:
            one.opposite(0)
    if fused:
        one.from_core(0)
    k1_copy = pltpu.make_async_copy(k1, k1_out, local.at[1])
    k1_copy.start()
    moments = []
    y_copies = []
    for n in range(images):
        def first_half(i, carry):
            acc = (
                y[at_rows(n, i), :]
                + bdot(window(n, i, 0, slice(0, tap_row)), k1[0:tap_row, :])
                + bdot(window(n, i, 1, slice(0, middle)), k1[tap_row : tap_row + middle, :])
            )
            y[at_rows(n, i), :] = acc
            return carry + jnp.sum(acc, axis=0, keepdims=True)
        whole = lax.fori_loop(0, side // (2 * BLOCK), first_half, zero)
        if fused:
            two.neighbours(n, every)
        average = whole / cells
        def spread_step(i, carry):
            pixel = pl.ds(pl.multiple_of(n * cells + i * BLOCK * side, 16), BLOCK * side)
            off = y[pixel, :] - average
            return carry + jnp.sum(off * off, axis=0, keepdims=True)
        moments.append((average, lax.fori_loop(0, side // BLOCK, spread_step, zero)))
        copy = pltpu.make_async_copy(
            y.at[pl.ds(n * cells, cells), :], y_out.at[pl.ds(n * cells, cells), :], local.at[4 + n]
        )
        copy.start()
        y_copies.append(copy)
    payload_two = one_a.at[1]
    counts_in = [v * cells for v in valid]
    average = total([m[0] * c for m, c in zip(moments, counts_in)]) / held
    payload_two[...] = jnp.zeros(payload_two.shape, F32)
    payload_two[0:1, :] = average
    payload_two[1:2, :] = total([
        v * m[1] + c * (m[0] - average) * (m[0] - average)
        for m, c, v in zip(moments, counts_in, valid)
    ])
    payload_two[2:3, :] = zero + held
    first = ex_a.at[1]
    first[dp] = payload_two[...]
    three_level = Spread("dp", n_dp, payload_two, first, a_send.at[1], a_recv.at[1])
    three_level.start()
    three_level.wait()
    mean, spread, cell_count = join_moments(first)
    second = ex_b.at[1]
    passed = one_b.at[1]
    passed[...] = jnp.zeros(passed.shape, F32)
    passed[0:1, :] = mean
    passed[1:2, :] = spread
    passed[2:3, :] = cell_count
    second[rep] = passed[...]
    four_level = Spread("replica", n_rep, passed, second, b_send.at[1], b_recv.at[1])
    four_level.start()
    four_level.wait()
    mean, spread, _ = join_moments(second)
    sigma = sigma_rows[0]
    variance = spread / pixels / (sigma * sigma)
    inverse_two = lax.rsqrt(variance + EPS_NORM) / sigma
    stats[3:4, :] = mean
    stats[11:12, :] = inverse_two
    scale_two = inverse_two * norms[2:3, :]
    shift_two = norms[3:4, :] - mean * scale_two
    select = window_matrix(side)
    act_copies = []
    for n in range(images):
        def step(i, carry):
            pixel = pl.ds(pl.multiple_of(n * cells + i * BLOCK * side, 16), BLOCK * side)
            act[pixel, :] = jax.nn.gelu(y[pixel, :] * scale_two + shift_two).astype(BF16)
            return carry
        lax.fori_loop(0, side // BLOCK, step, 0)
        copy = pltpu.make_async_copy(
            act.at[pl.ds(n * cells, cells), :], act_out.at[pl.ds(n * cells, cells), :], local.at[6 + n]
        )
        copy.start()
        act_copies.append(copy)
        windows[n] = bdot(select, act[n * cells : (n + 1) * cells, :], ((0,), (0,)))
    if fused:
        for zi in two.order:
            two.opposite(zi)
        for zi in two.order:
            two.from_core(zi)
        one.drain()
        two.drain()
        pl.when(~even)(seam_copy.wait_send)
    for level in (one_level, two_level, three_level, four_level):
        level.drain()
    for copy in [k1_copy] + x_copies + y_copies + act_copies:
        copy.wait()


def forward(n_dp, n_rep, side, share, fused, counts, main, bound, pictures, stem, start, norms):
    images, cells = pictures.shape[0], side * side
    width = stem.shape[1]
    half = n_dp // 2
    sources = max(n_dp // 4, 1)
    shape = jax.ShapeDtypeStruct
    sem = pltpu.SemaphoreType.DMA
    kernel_rows = 9 * width
    return pl.pallas_call(
        functools.partial(forward_kernel, n_dp, n_rep, side, share, fused),
        out_shape=(
            shape((kernel_rows, width), BF16),
            shape((kernel_rows, width), BF16),
            shape((images, side, side, width), BF16),
            shape((images * cells, width), F32),
            shape((images * cells, width), BF16),
            shape((images, 16, width), F32),
            shape((images, width), F32),
            shape((16, width), F32),
            shape((images, 32, cells), BF16),
            shape((32, width), BF16),
        ),
        in_specs=[SMEM, VMEM if fused else ANY, VMEM, VMEM, VMEM, VMEM, VMEM],
        out_specs=(ANY,) * 5 + (VMEM,) * 5,
        scratch_shapes=[
            pltpu.VMEM((32, cells), F32),
            pltpu.VMEM((kernel_rows, width), BF16),
            pltpu.VMEM((images, side + 2, side, 3 * width), BF16),
            pltpu.VMEM((images * cells, width), F32),
            pltpu.VMEM((images * cells, width), BF16),
            pltpu.VMEM((2, 16, width), BF16),
            pltpu.VMEM((2, n_dp, 8, width), F32),
            pltpu.VMEM((2, n_rep, 8, width), F32),
            pltpu.VMEM((2, 8, width), F32),
            pltpu.VMEM((2, 8, width), F32),
            sem((2, sources, PIECES, 2)),
            sem((2, sources, PIECES)),
            sem((2, sources, PIECES, 4)),
            sem((2, sources, PIECES, 4)),
            sem((2, sources, PIECES, 4)),
            sem((2, sources, PIECES, 4)),
            sem((2, n_dp)),
            sem((2, n_dp)),
            sem((2, n_rep)),
            sem((2, n_rep)),
            sem((1,)),
            sem((1,)),
            sem((9,)),
        ],
        compiler_params=pltpu.CompilerParams(
            collective_id=0, has_side_effects=True, vmem_limit_bytes=56 << 20
        ),
    )(counts, main, bound, pictures, stem, start, norms)


class Reduce:
    def __init__(self, near, far, src, parts, whole, planes, out, sems):
        (self.axis, self.size), (self.other, self.others) = near, far
        self.src, self.parts, self.whole, self.planes, self.out = src, parts, whole, planes, out
        (self.a_send, self.a_recv, self.b_send, self.b_recv, self.c_send, self.c_recv) = sems
        self.me = lax.axis_index(self.axis)

    def scatter(self):
        for j in range(1, self.size):
            peer = lax.rem(self.me + j, self.size)
            yield remote(
                self.src.at[peer], self.parts.at[self.me], self.a_send.at[j], self.a_recv.at[j],
                {self.axis: peer},
            )

    def start(self):
        for copy in self.scatter():
            copy.start()
        self.parts[self.me] = self.src[self.me]

    def middle(self):
        for j in range(1, self.size):
            source = lax.rem(self.me + self.size - j, self.size)
            remote(
                self.src.at[source], self.parts.at[source], self.a_send.at[j], self.a_recv.at[j],
                {self.axis: source},
            ).wait_recv()
        self.whole[...] = total([self.parts[i] for i in range(self.size)])
        self.planes[lax.axis_index(self.other)] = self.whole[...]
        self.second = Spread(
            self.other, self.others, self.whole, self.planes, self.b_send, self.b_recv
        )
        self.second.start()

    def last(self):
        self.second.wait()
        self.out[self.me] = total([self.planes[i] for i in range(self.others)])
        self.third = Spread(
            self.axis, self.size, self.out.at[self.me], self.out, self.c_send, self.c_recv
        )
        self.third.start()

    def finish(self):
        self.third.wait()
        for copy in self.scatter():
            copy.wait_send()
        self.second.drain()
        self.third.drain()


def reduce_scratch(size, others, rows, width):
    per = -(-rows // size)
    sem = pltpu.SemaphoreType.DMA
    return [
        pltpu.VMEM((size, per, width), F32),
        pltpu.VMEM((size, per, width), F32),
        pltpu.VMEM((per, width), F32),
        pltpu.VMEM((others, per, width), F32),
        pltpu.VMEM((size, per, width), F32),
        sem((size,)), sem((size,)), sem((others,)), sem((others,)), sem((size,)), sem((size,)),
    ]


def put_rows(ref, first, values):
    per = ref.shape[1]
    for k in range(values.shape[0]):
        row = first + k
        ref[row // per, row % per : row % per + 1, :] = values[k : k + 1, :]


def gelu_slope(x):
    c = 0.7978845608028654
    square = x * x
    th = jnp.tanh(c * x * (1.0 + 0.044715 * square))
    return 0.5 * (1.0 + th) + 0.5 * x * (1.0 - th * th) * (c * (1.0 + 3 * 0.044715 * square))


def fold(values):
    return jnp.sum(values.reshape(values.shape[0] // 8, 8, values.shape[1]), axis=0)


IND = 32


def cholesky_steps(matrix, size):
    lane = lax.broadcasted_iota(jnp.int32, (size, IND), 1)
    line = lax.broadcasted_iota(jnp.int32, (size, IND), 0)
    left = matrix
    right = jnp.where(lane == line, 1.0, 0.0)
    factor = jnp.zeros((size, IND), F32)
    row_of = lax.broadcasted_iota(jnp.int32, (size, 1), 0)
    for k in range(size):
        inverse = lax.rsqrt(left[k : k + 1, k : k + 1])
        column = jnp.where(row_of >= k, left[:, k : k + 1] * inverse, 0.0)
        below = jnp.where(row_of > k, column, 0.0)
        row = left[k : k + 1, :] * inverse
        other = right[k : k + 1, :] * inverse
        factor = jnp.where(lane == k, column, factor)
        left = left - below * row
        right = jnp.where(line == k, other, right - below * other)
    return factor, right


def scale_rows(lower):
    size = lower.shape[0]
    line = lax.broadcasted_iota(jnp.int32, (size, size), 0)
    lane = lax.broadcasted_iota(jnp.int32, (size, size), 1)
    return jnp.where(line > lane, lower, jnp.where(line == lane, jnp.exp(lower), 0.0))


def head_kernel(
    n_dp, n_rep, side,
    counts, labels, indices, table, k2_in, y_in, windows, stem_pool, stats, norms,
    inducing, lengthscale, var_mean, var_lower,
    cat_out, head_out, grads_out, chol_out,
    k2, y, d_pre, cat, pattern, z_pad, l_pad, v_pad, f_pad, x_pad, kx_pad, noise, d_rows,
    ex_a, ex_b, one_a, one_b, a_send, a_recv, b_send, b_recv, local,
):
    images = stem_pool.shape[0]
    width = stem_pool.shape[1]
    cells = side * side
    size = inducing.shape[0]
    classes = var_mean.shape[0]
    samples = indices.shape[1]
    dp, rep = lax.axis_index("dp"), lax.axis_index("replica")
    loads = [
        pltpu.make_async_copy(k2_in, k2, local.at[0]),
        pltpu.make_async_copy(y_in, y, local.at[1]),
    ]
    for copy in loads:
        copy.start()
    greet(n_dp, n_rep)()

    sigma_one, sigma_two = stats[4:5, :], stats[5:6, :]
    pixels = stats[2:3, :]
    scale = cells / stats[2:3, 0:1]
    ell = lengthscale[...].reshape(1, width)

    z_pad[...] = jnp.zeros(z_pad.shape, F32)
    z_pad[0:size, :] = inducing[...] / ell
    zs = z_pad[...]
    ones = jnp.ones((8, width), F32)
    lane = lax.broadcasted_iota(jnp.int32, (size, IND), 1)
    line = lax.broadcasted_iota(jnp.int32, (size, IND), 0)
    kzz = jnp.zeros((size, IND), F32)
    for m in range(size):
        off = zs[0:size, :] - zs[m : m + 1, :]
        kzz = jnp.where(lane == m, jnp.exp(-0.5 * jnp.sum(off * off, axis=1, keepdims=True)), kzz)
    factor, inverse = cholesky_steps(jnp.where(lane == line, kzz + JITTER, kzz), size)
    chol_out[...] = jnp.zeros(chol_out.shape, F32)
    chol_out[0, 0:size, :] = kzz
    chol_out[1, 0:size, :] = factor
    chol_out[2, 0:size, :] = inverse
    l_pad[...] = jnp.zeros(l_pad.shape, F32)
    l_pad[0:size, :] = inverse
    v_pad[...] = jnp.zeros(v_pad.shape, F32)
    v_pad[0:classes, 0:size] = var_mean[...]
    f_pad[...] = jnp.zeros(f_pad.shape, F32)
    for c in range(classes):
        f_pad[0:size, c * IND : c * IND + size] = scale_rows(var_lower[c])
    group = lax.broadcasted_iota(jnp.int32, (classes * IND, 16), 0) // IND
    which = lax.broadcasted_iota(jnp.int32, (classes * IND, 16), 1)
    groups = jnp.where(group == which, 1.0, 0.0)
    noise[...] = jnp.zeros(noise.shape, F32)
    for n in range(images):
        for s in range(samples):
            noise[n, s : s + 1, 0:classes] = table[pl.ds(indices[n, s], 1), :]

    loads[0].wait()
    pooled_raw = jnp.zeros((16, width), F32)
    for t in range(9):
        parts = []
        rest = [windows[n, t : t + 1, :] for n in range(images)]
        for _ in range(3):
            parts += [r.astype(BF16).astype(F32) for r in rest]
            rest = [r - p for r, p in zip(rest, parts[-images:])]
        parts.append(jnp.zeros((16 - 3 * images, width), F32))
        lhs = jnp.concatenate(parts, axis=0).astype(BF16)
        pooled_raw = pooled_raw + bdot(lhs, k2[t * width : (t + 1) * width, :])
    x_pad[...] = jnp.zeros(x_pad.shape, F32)
    branch_pool = []
    for n in range(images):
        row = total([pooled_raw[k * images + n : k * images + n + 1] for k in range(3)])
        branch_pool.append(row / (cells * sigma_two))
        x_pad[n : n + 1, :] = (stem_pool[n : n + 1, :] + branch_pool[n]) / ell
    xs = x_pad[...]

    kx_pad[...] = jnp.zeros(kx_pad.shape, F32)
    for n in range(images):
        off = zs - xs[n : n + 1, :]
        kx_pad[n : n + 1, :] = jnp.exp(-0.5 * hdot(ones, off * off, ((1,), (1,))))[0:1]
    lanes = lax.broadcasted_iota(jnp.int32, (8, IND), 1)
    kx = jnp.where(lanes < size, kx_pad[...], 0.0)
    inv = l_pad[...]
    means = v_pad[...]
    factors = f_pad[...]
    proj = hdot(kx, inv, ((1,), (1,)))
    average = hdot(proj, means, ((1,), (1,)))
    spread = hdot(proj, factors)
    variance = (
        1.0 - jnp.sum(proj * proj, axis=1, keepdims=True) + hdot(spread * spread, groups)
    )
    std = jnp.sqrt(variance)
    class_lane = lax.broadcasted_iota(jnp.int32, (1, 16), 1)
    sample_row = lax.broadcasted_iota(jnp.int32, (16, 16), 0)
    inside = (lax.broadcasted_iota(jnp.int32, (16, 16), 1) < classes) & (sample_row < samples)
    count = counts[0]
    loss = jnp.zeros((1, 1), F32)
    g_avg_rows, g_var_rows = [], []
    for n in range(images):
        drawn = average[n : n + 1, :] + std[n : n + 1, :] * noise[n]
        drawn = jnp.where(inside, drawn, -1e30)
        shifted = drawn - jnp.max(drawn, axis=1, keepdims=True)
        exps = jnp.where(inside, jnp.exp(shifted), 0.0)
        sums = jnp.sum(exps, axis=1, keepdims=True)
        sums = jnp.where(sample_row[:, 0:1] < samples, sums, 1.0)
        hot = jnp.where(class_lane == labels[n], 1.0, 0.0)
        picked = jnp.where(inside, (shifted - jnp.log(sums)) * hot, 0.0)
        held = jnp.where(count > n, 1.0 / samples, 0.0)
        loss = loss - held * jnp.sum(jnp.sum(picked, axis=1, keepdims=True), axis=0, keepdims=True)
        g_samples = jnp.where(inside, exps / sums - hot, 0.0) * (held * scale)
        g_avg_rows.append(jnp.sum(g_samples, axis=0, keepdims=True))
        g_var_rows.append(
            0.5 * jnp.sum(g_samples * noise[n], axis=0, keepdims=True) / std[n : n + 1, :]
        )
    blank = [jnp.zeros((8 - images, 16), F32)]
    g_avg = jnp.concatenate(g_avg_rows + blank, axis=0)
    g_var = jnp.concatenate(g_var_rows + blank, axis=0)
    g_spread = 2.0 * spread * hdot(g_var, groups, ((1,), (1,)))
    g_proj = (
        hdot(g_avg, means)
        - 2.0 * proj * jnp.sum(g_var, axis=1, keepdims=True)
        + hdot(g_spread, factors, ((1,), (1,)))
    )
    g_kx = hdot(g_proj, inv)
    weights = -kx * g_kx
    g_x = xs * jnp.sum(weights, axis=1, keepdims=True) - hdot(weights, zs)
    d_pooled = g_x / ell
    d_rows[...] = jnp.zeros(d_rows.shape, BF16)
    d_rows[0:8, :] = (d_pooled / cells).astype(BF16)
    d_two = d_rows[...]

    taps = [
        bdot(d_two, k2[t * width : (t + 1) * width, :], ((1,), (1,))) / sigma_two for t in range(9)
    ]
    wide = lax.broadcasted_iota(jnp.int32, (side, 1), 0)
    for n in range(images):
        for kind, kept in enumerate(((0, 1), (0, 1, 2), (1, 2))):
            across = [total([taps[3 * r + c][n : n + 1] for r in kept]) for c in range(3)]
            middle = across[0] + across[1] + across[2]
            pattern[n, kind] = jnp.where(
                wide == 0, across[0] + across[1],
                jnp.where(wide == side - 1, across[1] + across[2], middle),
            )

    loads[1].wait()
    mean_two, inverse_two = stats[3:4, :], stats[11:12, :]
    gain, bias = norms[2:3, :], norms[3:4, :]
    none = jnp.zeros((8, width), F32)
    sums = (none, none)
    for n in range(images):
        def step(h, carry):
            kind = jnp.where(h == 0, 0, jnp.where(h == side - 1, 2, 1))
            at = pl.ds(pl.multiple_of(n * cells + h * side, side), side)
            normed = (y[at, :] - mean_two) * inverse_two
            grad = gelu_slope(normed * gain + bias) * pattern[n, kind]
            d_pre[at, :] = grad
            return carry[0] + fold(grad), carry[1] + fold(grad * normed)
        sums = lax.fori_loop(0, side, step, sums)
    one_a[...] = jnp.zeros(one_a.shape, F32)
    one_a[0:1, :] = jnp.sum(sums[0], axis=0, keepdims=True)
    one_a[1:2, :] = jnp.sum(sums[1], axis=0, keepdims=True)
    one_a[2:3, :] = total([
        cells * branch_pool[n] * d_two[n : n + 1, :].astype(F32) for n in range(images)
    ])
    ex_a[dp] = one_a[...]
    first = Spread("dp", n_dp, one_a, ex_a, a_send, a_recv)
    first.start()

    grads_out[...] = jnp.zeros(grads_out.shape, F32)
    over = hdot(weights, jnp.ones((8, 128), F32), ((0,), (0,)))[:, 0:1]
    g_z = zs * over - hdot(weights, xs, ((0,), (0,)))
    grads_out[0:size, :] = g_z[0:size]
    grads_out[20:21, :] = jnp.sum(g_x * xs, axis=0, keepdims=True)
    grads_out[23:24, :] = jnp.zeros((1, width), F32) + loss
    grads_out[32:64, 0 : classes * IND] = hdot(proj, g_spread, ((0,), (0,)))
    grads_out[32:64, 384 : 384 + IND] = hdot(g_kx, proj, ((0,), (0,)))
    grads_out[32:48, 512 : 512 + IND] = hdot(g_avg, proj, ((0,), (0,)))
    head_out[...] = jnp.zeros(head_out.shape, F32)
    head_out[0:8, :] = d_pooled
    head_out[18:19, :] = cells / pixels
    head_out[8:16, :] = d_two[0:8, :].astype(F32)
    for n in range(images):
        edge = jnp.zeros((1, side, 3 * width), BF16)
        cat[n, 0:1] = edge
        cat[n, side + 1 : side + 2] = edge

    first.wait()
    one_b[...] = total([ex_a[i] for i in range(n_dp)])
    ex_b[rep] = one_b[...]
    second = Spread("replica", n_rep, one_b, ex_b, b_send, b_recv)
    second.start()
    second.wait()
    joined = total([ex_b[i] for i in range(n_rep)])
    d_bias, d_gain = joined[0:1, :], joined[1:2, :]
    head_out[16:17, :] = d_gain
    head_out[17:18, :] = d_bias
    head_out[19:20, :] = joined[2:3, :]
    true_scale = inverse_two * sigma_one * gain
    cat_copies = []
    for n in range(images):
        held = jnp.where(count > n, 1.0, 0.0)
        def step(i, carry):
            rows = BLOCK * side
            at = pl.ds(pl.multiple_of(n * cells + i * rows, rows), rows)
            normed = (y[at, :] - mean_two) * inverse_two
            grad = (true_scale * held) * (
                d_pre[at, :] - d_bias / pixels - normed * (d_gain / pixels)
            )
            grad = grad.astype(BF16).astype(F32)
            store_shifted(cat, n, i * BLOCK, BLOCK, grad, side)
            return carry
        lax.fori_loop(0, side // BLOCK, step, 0)
        copy = pltpu.make_async_copy(cat.at[n], cat_out.at[n], local.at[2 + n])
        copy.start()
        cat_copies.append(copy)
    for level in (first, second):
        level.drain()
    for copy in cat_copies:
        copy.wait()


def head(n_dp, n_rep, side, counts, labels, indices, table, k2, y, windows, stem_pool, stats,
         norms, inducing, lengthscale, var_mean, var_lower):
    images, width = stem_pool.shape
    cells = side * side
    classes = var_mean.shape[0]
    shape = jax.ShapeDtypeStruct
    sem = pltpu.SemaphoreType.DMA
    return pl.pallas_call(
        functools.partial(head_kernel, n_dp, n_rep, side),
        out_shape=(
            shape((images, side + 2, side, 3 * width), BF16),
            shape((24, width), F32),
            shape((64, width), F32),
            shape((3, IND, IND), F32),
        ),
        in_specs=[SMEM, SMEM, SMEM, VMEM, ANY, ANY] + [VMEM] * 8,
        out_specs=(ANY, VMEM, VMEM, VMEM),
        scratch_shapes=[
            pltpu.VMEM(k2.shape, BF16),
            pltpu.VMEM(y.shape, F32),
            pltpu.VMEM(y.shape, F32),
            pltpu.VMEM((images, side + 2, side, 3 * width), BF16),
            pltpu.VMEM((images, 3, side, width), F32),
            pltpu.VMEM((IND, width), F32),
            pltpu.VMEM((IND, IND), F32),
            pltpu.VMEM((16, IND), F32),
            pltpu.VMEM((IND, classes * IND), F32),
            pltpu.VMEM((8, width), F32),
            pltpu.VMEM((8, IND), F32),
            pltpu.VMEM((images, 16, 16), F32),
            pltpu.VMEM((16, width), BF16),
            pltpu.VMEM((n_dp, 8, width), F32),
            pltpu.VMEM((n_rep, 8, width), F32),
            pltpu.VMEM((8, width), F32),
            pltpu.VMEM((8, width), F32),
            sem((n_dp,)), sem((n_dp,)), sem((n_rep,)), sem((n_rep,)),
            sem((2 + images,)),
        ],
        compiler_params=pltpu.CompilerParams(
            collective_id=1, has_side_effects=True, vmem_limit_bytes=56 << 20
        ),
    )(counts, labels, indices, table, k2, y, windows, stem_pool, stats, norms,
      inducing, lengthscale, var_mean, var_lower)


def greet_all(n_dp, n_rep):
    here = lax.axis_index("dp") * n_rep + lax.axis_index("replica")
    count = n_dp * n_rep
    barrier = pltpu.get_barrier_semaphore()

    def signal(j, carry):
        other = lax.rem(here + j, count)
        pl.semaphore_signal(
            barrier, inc=1, device_id={"dp": other // n_rep, "replica": lax.rem(other, n_rep)},
            device_id_type=MESH,
        )
        return carry

    lax.fori_loop(1, count, signal, 0)
    pl.semaphore_wait(barrier, count - 1)


def chunk_plan(share, width, count):
    def segments(first, last, base):
        result = []
        while first < last:
            c = (first - base) // width
            end = min(last, base + (c + 1) * width)
            result.append((c, first - base - c * width, end - base - c * width))
            first = end
        return result

    plan, done, carried = [], 0, 0
    for r in range(3):
        first, last = r * 3 * width, (r + 1) * 3 * width
        items = []
        while done < count and (done + 1) * share <= last:
            begin = max(done * share, first)
            items.append((done, carried, segments(begin, (done + 1) * share, first)))
            carried = 0
            done += 1
        begin = max(done * share, first)
        plan.append((items, segments(begin, last, first)))
        carried = last - begin
    return plan


def backward_kernel(
    n_dp, n_rep, side, share, fused,
    counts, cat_in, x_in, k1_in, k2_in, act_in, patches, stem, stats, norms, windows, head_rows, grads,
    part_out, big_out, sums_out, late_out,
    cat, x, k1, held_rows, carry, mine, sib, rin, zin, zout, part, comb, wall, flat, flat_d,
    *rest,
):
    early = rest[0:11]
    (c_send, c_recv, r_send, r_recv, z_send, z_recv, w_send, w_recv, local) = rest[11:]
    images = patches.shape[0]
    width = stem.shape[1]
    cells = side * side
    dp, rep = lax.axis_index("dp"), lax.axis_index("replica")
    core, z = lax.rem(dp, 2), dp // 2
    n_z, half = n_dp // 2, n_dp // 2
    sources = max(n_dp // 4, 1)
    owners = half * n_rep
    here = dp * n_rep + rep
    loads = [
        pltpu.make_async_copy(cat_in, cat, local.at[0]),
        pltpu.make_async_copy(x_in, x, local.at[1]),
        pltpu.make_async_copy(k1_in, k1, local.at[2]),
    ]
    for copy in loads:
        copy.start()
    greet_all(n_dp, n_rep)
    count = counts[0]
    valid = [jnp.where(count > n, 1.0, 0.0) for n in range(images)]

    early_sum = Reduce(("dp", n_dp), ("replica", n_rep), *early[:5], early[5:])
    source = early[0]
    source[...] = jnp.zeros(source.shape, F32)
    put_rows(source, 0, grads[...])
    gram = total([
        bdot(patches[n], patches[n], ((1,), (1,))) * valid[n] for n in range(images)
    ])
    wide = jnp.concatenate([gram, jnp.zeros((32, 128 - 32), F32)], axis=1)
    per = source.shape[1]
    for k in range(32):
        row = 64 + k
        source[row // per, row % per : row % per + 1, 0:128] = wide[k : k + 1, :]
    early_sum.start()

    if fused:
        for t in range(9):
            comb[t, 0:images, :] = jnp.concatenate(
                [windows[n, t : t + 1, :] for n in range(images)], axis=0
            )
            comb[t, images : 2 * images, :] = head_rows[8 : 8 + images, :]

        def first_tap(owner):
            return jnp.minimum((owner * share) // width, 7)

        def window_copy(owner):
            return remote(
                comb.at[pl.ds(first_tap(owner), 2)], wall.at[here], w_send.at[owner], w_recv.at[here],
                {"dp": half + owner // n_rep, "replica": lax.rem(owner, n_rep)},
            )

        def send_windows(j, c):
            owner = lax.rem(here + j, owners)

            @pl.when(half * n_rep + owner != here)
            def _():
                window_copy(owner).start()
            return c

        lax.fori_loop(0, owners, send_windows, 0)

    def row_of_taps(r):
        return total([
            lax.dot_general(
                x[n].reshape(cells, width),
                cat[n, pl.ds(2 - r, side)].reshape(cells, 3 * width),
                (((0,), (0,)), ((), ())),
                preferred_element_type=F32,
            )
            for n in range(images)
        ])

    def joined(acc, parts):
        pieces = [acc[a:b, (2 - c) * width : (3 - c) * width] for c, a, b in parts]
        return pieces[0] if len(pieces) == 1 else jnp.concatenate(pieces, axis=0)

    def sib_copy(o):
        return remote(
            mine.at[o], sib.at[(o // (2 * n_rep)) * n_rep + o % n_rep],
            c_send.at[o], c_recv.at[(o // (2 * n_rep)) * n_rep + o % n_rep],
            {"dp": dp + 1 - 2 * core},
        )

    def ship(acc, items, leftover):
        for o, carried, parts in items:
            value = joined(acc, parts)
            if carried:
                value = jnp.concatenate([carry[0:carried, :], value], axis=0)
            mine[o, 0:share, :] = value.astype(BF16)
            pl.when(core != (o // n_rep) % 2)(sib_copy(o).start)
        if leftover:
            value = joined(acc, leftover)
            carry[0 : value.shape[0], :] = value

    reps = (rep, rep + 1 - 2 * lax.rem(rep, 2), rep + 2 - 4 * (rep // 2), 3 - rep)
    cut = (share + 8) // 32 * 16
    halves = (pl.ds(0, cut), pl.ds(cut, share + 8 - cut))

    def slot(zi, k):
        return (zi * 2 + core) * n_rep + reps[k]

    def plane_copies(zi, step):
        for h in range(2):
            near, far = 1 + h, 2 - h
            at = halves[h]
            if step == 0:
                for s, k in enumerate((near, 3)):
                    yield remote(
                        mine.at[slot(zi, k), at, :], rin.at[zi, s, at, :],
                        r_send.at[zi, 2 * s + h], r_recv.at[zi, 2 * s + h], {"replica": reps[near]},
                    )
            else:
                yield remote(
                    mine.at[slot(zi, far), at, :], rin.at[zi, 2, at, :],
                    r_send.at[zi, 4 + h], r_recv.at[zi, 4 + h], {"replica": reps[far]},
                )

    def join_cores(zi):
        for k in (3, 1, 2, 0):
            at = zi * n_rep + reps[k]
            remote(
                mine.at[0], sib.at[at], c_send.at[0], c_recv.at[at], {"dp": dp + 1 - 2 * core}
            ).wait_recv()
            mine[slot(zi, k)] = (
                mine[slot(zi, k)].astype(F32) + sib[at].astype(F32)
            ).astype(BF16)
        for copy in plane_copies(zi, 0):
            copy.start()

    def join_near(zi):
        for copy in plane_copies(zi, 0):
            copy.wait_recv()
        for h in range(2):
            at, o = halves[h], slot(zi, 2 - h)
            mine[o, at, :] = (
                mine[o, at, :].astype(F32) + rin[zi, 1, at, :].astype(F32)
            ).astype(BF16)
        for copy in plane_copies(zi, 1):
            copy.start()

    def join_far(zi):
        for copy in plane_copies(zi, 1):
            copy.wait_recv()
        part[zi] = (
            mine[slot(zi, 0)].astype(F32) + rin[zi, 0].astype(F32) + rin[zi, 2].astype(F32)
        )

    z_pieces = ((0, 192), (192, share + 8 - 192)) if share > 200 else ((0, share + 8),)

    def z_copy(zi, piece, down):
        start, rows = z_pieces[piece]
        at = pl.ds(start, rows)
        step = n_dp - 2 if down else 2
        return remote(
            zout.at[zi, at, :], zin.at[zi, int(down), at, :],
            z_send.at[zi, piece], z_recv.at[zi, piece, int(down)],
            {"dp": lax.rem(dp + step, n_dp)},
        )

    def chain(zi, distance, pieces=(0, 1)):
        for down in (True, False):
            reach = n_z - 1 - zi if down else zi
            if distance > reach:
                continue
            offset = distance if down else -distance
            @pl.when(z == zi + offset)
            def _():
                for piece in pieces:
                    start, rows = z_pieces[piece]
                    at = pl.ds(start, rows)
                    if distance < reach:
                        z_copy(zi, piece, down).wait_recv()
                        part[zi, at, :] += zin[zi, int(down), at, :].astype(F32)
                    if distance:
                        zout[zi, at, :] = part[zi, at, :].astype(BF16)
                        z_copy(zi, piece, down).start()

    loads[0].wait()
    loads[1].wait()
    if fused:
        plan = chunk_plan(share, width, owners)
        for r in range(3):
            acc = row_of_taps(r)
            if r > 0:
                pl.when(core == r - 1)(lambda: join_cores(0))
            ship(acc, *plan[r])
            if r == 1:
                early_sum.middle()
    else:
        for r in range(3):
            acc = row_of_taps(r)
            for c in range(3):
                held_rows[0:width, :] = acc[:, (2 - c) * width : (3 - c) * width]
                out_copy = pltpu.make_async_copy(
                    held_rows.at[pl.ds(0, width), :],
                    part_out.at[pl.ds((3 * r + c) * width, width), :],
                    local.at[4],
                )
                out_copy.start()
                out_copy.wait()
        early_sum.middle()

    loads[2].wait()
    sigma = stats[4:5, :]
    mean_one, inverse_one, pixels = stats[0:1, :], stats[1:2, :], stats[2:3, :]
    gain, bias = norms[0:1, :], norms[1:2, :]
    none = jnp.zeros((8, width), F32)
    block_rows = 2 * BLOCK * side
    per_image = side // (2 * BLOCK)
    blocks = images * per_image

    def input_gradient(b):
        n, i = b // per_image, b % per_image
        acc = None
        for r in range(3):
            for c in range(3):
                t = 8 - (3 * r + c)
                lhs = cat[
                    n, pl.ds(i * 2 * BLOCK + r, 2 * BLOCK), :, c * width : (c + 1) * width
                ].reshape(block_rows, width)
                one = bdot(lhs, k1[t * width : (t + 1) * width, :], ((1,), (1,)))
                acc = one if acc is None else acc + one
        first = (b % 2) * width
        held_rows[first : first + block_rows, :] = acc

    def through_gelu(b, carried):
        n, i = b // per_image, b % per_image
        first = (b % 2) * width
        pixel = patches[n, :, i * block_rows : (i + 1) * block_rows]
        normed = (bdot(pixel, stem[...], ((0,), (0,))) - mean_one) * inverse_one
        grad = gelu_slope(normed * gain + bias) * held_rows[first : first + block_rows, :] * (
            valid[n] / sigma
        )
        down = (grad * (inverse_one * gain) + head_rows[n : n + 1, :] / cells).astype(BF16)
        return (
            carried[0] + fold(grad),
            carried[1] + fold(grad * normed),
            carried[2] + bdot(pixel, down),
        )

    sums = (none, none, jnp.zeros((32, width), F32))
    between = {
        0: [lambda: join_near(0), lambda: join_cores(1)],
        1: [lambda: join_far(0), lambda: chain(0, 3)],
        2: [lambda: chain(0, 2, (0,)), lambda: join_near(1)],
        3: [lambda: chain(0, 2, (1,)), lambda: chain(0, 1, (0,))],
    }
    for b in range(blocks + 1):
        if b < blocks:
            input_gradient(b)
        if b > 0:
            sums = through_gelu(b - 1, sums)
        if fused:
            for event in between.get(b, ()):
                event()
    late_out[...] = sums[2]
    late_out[27:28, :] = jnp.sum(sums[0], axis=0, keepdims=True)
    late_out[28:29, :] = jnp.sum(sums[1], axis=0, keepdims=True)
    early_sum.last()

    act_copy = pltpu.make_async_copy(act_in, x, local.at[5])
    act_copy.start()
    k2_copy = pltpu.make_async_copy(k2_in, k1, local.at[3])
    k2_copy.start()
    act_copy.wait()
    def shift(n):
        def step(i, carried):
            rows = BLOCK * side
            values = x[n, pl.ds(i * BLOCK, BLOCK)].reshape(rows, width).astype(F32)
            store_shifted(cat, n, i * BLOCK, BLOCK, values, side)
            return carried
        lax.fori_loop(0, side // BLOCK, step, 0)

    squares = none
    between = {
        0: [
            lambda: join_far(1), lambda: chain(1, 2), lambda: chain(0, 1, (1,)),
            lambda: chain(0, 0, (0,)),
        ],
        1: [lambda: chain(1, 1), lambda: chain(0, 0, (1,))],
        2: [lambda: chain(1, 0)],
    }
    for b in range(blocks):
        n, i = b // per_image, b % per_image
        if i == 0:
            shift(n)
        if b == 0:
            k2_copy.wait()
        acc = None
        for r in range(3):
            lhs = cat[n, pl.ds(i * 2 * BLOCK + r, 2 * BLOCK)].reshape(block_rows, 3 * width)
            one = bdot(lhs, k1[r * 3 * width : (r + 1) * 3 * width, :])
            acc = one if acc is None else acc + one
        squares = squares + valid[n] * fold(acc * acc)
        if fused:
            for event in between.get(b, ()):
                event()
    sigma_two = stats[5:6, :]
    sums_out[...] = jnp.zeros(sums_out.shape, F32)
    sums_out[0:1, :] = jnp.sum(squares, axis=0, keepdims=True) / (sigma_two * sigma_two)

    if fused:
        @pl.when(dp < half)
        def _():
            for zi in range(sources):
                @pl.when(z == zi)
                def _():
                    part_out[...] = part[zi, 0:share, :]

        @pl.when(dp >= half)
        def _():
            owner = here - owners
            wall[here] = comb[pl.ds(first_tap(owner), 2)]

            def take(j, c):
                origin = lax.rem(here + j, n_dp * n_rep)
                remote(
                    comb.at[pl.ds(0, 2)], wall.at[origin], w_send.at[0], w_recv.at[origin],
                    {"dp": origin // n_rep, "replica": lax.rem(origin, n_rep)},
                ).wait_recv()
                return c

            lax.fori_loop(1, n_dp * n_rep, take, 0)
            for s in range(n_dp * n_rep):
                for tap in range(2):
                    flat[tap, s * images : (s + 1) * images, :] = wall[s, tap, 0:images, :]
                flat_d[s * images : (s + 1) * images, :] = wall[s, 0, images : 2 * images, :]
            for tap in range(2):
                held_rows[tap * width : (tap + 1) * width, :] = hdot(
                    flat[tap], flat_d[...], ((0,), (0,))
                )
            offset = owner * share - first_tap(owner) * width
            part_out[...] = held_rows[pl.ds(pl.multiple_of(offset, 8), share), :]

        def drain_windows(j, c):
            owner = lax.rem(here + j, owners)

            @pl.when(half * n_rep + owner != here)
            def _():
                window_copy(owner).wait_send()
            return c

        lax.fori_loop(0, owners, drain_windows, 0)
        for o in range(owners):
            pl.when(core != (o // n_rep) % 2)(sib_copy(o).wait_send)
        for zi in range(sources):
            for step in range(2):
                for copy in plane_copies(zi, step):
                    copy.wait_send()
            for piece in range(len(z_pieces)):
                pl.when(z > zi)(z_copy(zi, piece, True).wait_send)
                pl.when(z < zi)(z_copy(zi, piece, False).wait_send)
    early_sum.finish()
    per = early[4].shape[1]
    for s in range(n_dp):
        for j in range(per):
            big_out[s * per + j : s * per + j + 1, :] = early[4][s, j : j + 1, :]


def backward(n_dp, n_rep, side, share, fused, counts, cat, x, k1, k2, act, patches, stem, stats, norms,
             windows, head_rows, grads):
    images, width = patches.shape[0], stem.shape[1]
    half = n_dp // 2
    sources = max(n_dp // 4, 1)
    owners = half * n_rep
    devices = n_dp * n_rep
    shape = jax.ShapeDtypeStruct
    sem = pltpu.SemaphoreType.DMA
    rows = share + 8
    small = (1, 8, 128)
    early = reduce_scratch(n_dp, n_rep, 96, width)
    early_rows = early[0].shape[0] * early[0].shape[1]
    part_rows = share if fused else 9 * width
    pieces = 2 if share > 200 else 1
    return pl.pallas_call(
        functools.partial(backward_kernel, n_dp, n_rep, side, share, fused),
        out_shape=(
            shape((part_rows, width), F32),
            shape((early_rows, width), F32),
            shape((8, width), F32),
            shape((32, width), F32),
        ),
        in_specs=[SMEM] + [ANY] * 5 + [VMEM] * 7,
        out_specs=(VMEM if fused else ANY, VMEM, VMEM, VMEM),
        scratch_shapes=[
            pltpu.VMEM(cat.shape, BF16),
            pltpu.VMEM(x.shape, BF16),
            pltpu.VMEM(k1.shape, BF16),
            pltpu.VMEM((2 * width, width), F32),
            pltpu.VMEM((rows if fused else 8, width), F32),
            pltpu.VMEM((owners, rows, width) if fused else small, BF16),
            pltpu.VMEM((sources * n_rep, rows, width) if fused else small, BF16),
            pltpu.VMEM((sources, 3, rows, width) if fused else small, BF16),
            pltpu.VMEM((sources, 2, rows, width) if fused else small, BF16),
            pltpu.VMEM((sources, rows, width) if fused else small, BF16),
            pltpu.VMEM((sources, rows, width) if fused else small, F32),
            pltpu.VMEM((10, 2 * images, width) if fused else small, F32),
            pltpu.VMEM((devices, 2, 2 * images, width) if fused else small, F32),
            pltpu.VMEM((2, devices * images, width) if fused else small, F32),
            pltpu.VMEM((devices * images, width) if fused else small[1:], F32),
            *early,
            sem((owners,)), sem((sources * n_rep,)),
            sem((sources, 6)), sem((sources, 6)),
            sem((sources, pieces)), sem((sources, pieces, 2)),
            sem((owners,)), sem((devices,)),
            sem((6,)),
        ],
        compiler_params=pltpu.CompilerParams(
            collective_id=2, has_side_effects=True, vmem_limit_bytes=62 << 20
        ),
    )(counts, cat, x, k1, k2, act, patches, stem, stats, norms, windows, head_rows, grads)


def whole_sum(values):
    return jnp.sum(jnp.sum(values, axis=1, keepdims=True), axis=0, keepdims=True)


def lamb_step(weight, gradient, first, second, out, rows=False):
    new_one, new_two, direction = lamb_moments(weight, gradient, first, second)
    if rows:
        sizes = [jnp.sum(v * v, axis=1, keepdims=True) for v in (weight, direction)]
    else:
        sizes = [whole_sum(v * v) for v in (weight, direction)]
    new_weight = weight - RATE * (jnp.sqrt(sizes[0]) / jnp.sqrt(sizes[1])) * direction
    for ref, value in zip(out, (new_weight, new_one, new_two)):
        ref[...] = value.reshape(ref.shape)


def conv_kernel(kernel_of, part, conv_w, conv_m, conv_s, start, sums, head_rows, stats, norm_w,
                conv_one, conv_two, conv_step, tally, flat, own):
    width = stats.shape[1]
    share = part.shape[0]
    lanes = width // 128
    first = kernel_of[0] == 0
    def pick(row):
        return jnp.where(first, stats[row : row + 1, :], stats[row + 1 : row + 2, :])
    sigma, norm, unit = pick(4)[:, 0:1], pick(6)[:, 0:1], pick(8)
    inverse = stats[11:12, :] * stats[4:5, :]
    along = jnp.where(
        first,
        norm_w[2:3, :] * head_rows[16:17, :] * (EPS_NORM * inverse * inverse),
        head_rows[19:20, :],
    )
    d_sigma = -jnp.sum(along, axis=1, keepdims=True) / sigma
    vector = jnp.where(first, start[0:1, :], start[1:2, :])
    for k in range(lanes):
        own[:, k * 128 : (k + 1) * 128] = (
            conv_w[pl.ds(k, share, stride=lanes), :].astype(BF16).astype(F32)
        )
    rows = own[...]
    left = jnp.sum(rows * vector, axis=1, keepdims=True) / norm
    back = jnp.sum(rows * (unit / norm), axis=1, keepdims=True) - left * (sigma / norm)
    grad = part[...] / sigma + (left * d_sigma) * unit + (back * d_sigma) * vector
    for k in range(lanes):
        flat[pl.ds(k, share, stride=lanes), :] = grad[:, k * 128 : (k + 1) * 128]
    weight = conv_w[...]
    new_one, new_two, direction = lamb_moments(weight, flat[...], conv_m[...], conv_s[...])
    conv_one[...] = new_one
    conv_two[...] = new_two
    conv_step[...] = direction
    tally[...] = jnp.zeros(tally.shape, F32)
    tally[0:1, :] = jnp.sum(weight * weight, axis=0, keepdims=True)
    tally[1:2, :] = jnp.sum(direction * direction, axis=0, keepdims=True)
    tally[2:3, :] = total([sums[0:1, k * 128 : (k + 1) * 128] for k in range(lanes)])


def small_kernel(
    big, late, joined, head_rows, stats, chol, stem_w, stem_m, stem_s,
    norm_w, norm_m, norm_s, ind_w, ind_m, ind_s, len_w, len_m, len_s,
    mean_w, mean_m, mean_s, low_w, low_m, low_s, *rest,
):
    outs = rest[:18]
    parts_out, sigmas_out, rms_out, z_pad, stem_pad = rest[18:]
    width = stem_w.shape[1]
    size, classes = ind_w.shape[0], mean_w.shape[0]
    pixels = stats[2:3, :]
    mean_one, inverse_one = stats[0:1, :], stats[1:2, :]
    scale = head_rows[18:19, 0:1]
    parts_out[1] = jnp.sum(1.0 / scale)
    sigmas_out[0] = jnp.sum(stats[4:5, 0:1])
    sigmas_out[1] = jnp.sum(stats[5:6, 0:1])
    cells_all = pixels[:, 0:1] * width
    rms_out[0] = jnp.sum(
        jnp.sqrt(jnp.sum(stats[10:11, :], axis=1, keepdims=True) / cells_all)
    )
    rms_out[1] = jnp.sum(jnp.sqrt(joined[4:5, 0:1] / cells_all))

    gram = big[64:96, 0:32]
    patch_sums = gram[:, 31:32]
    stem_pad[...] = jnp.zeros(stem_pad.shape, F32)
    stem_pad[0 : stem_w.shape[0], :] = stem_w[...].astype(BF16).astype(F32)
    weights = stem_pad[...]
    centred = inverse_one * (hdot(gram, weights) - patch_sums * mean_one)
    d_bias, d_gain = late[27:28, :], late[28:29, :]
    stem_grad = late[0:32, :] - (inverse_one * norm_w[0:1, :] / pixels) * (
        patch_sums * d_bias + centred * d_gain
    )
    lamb_step(stem_w[...], stem_grad[0 : stem_w.shape[0]], stem_m[...], stem_s[...], outs[0:3])
    norm_grad = jnp.concatenate([d_gain, d_bias, head_rows[16:18, :]], axis=0)
    lamb_step(norm_w[...], norm_grad, norm_m[...], norm_s[...], outs[3:6], rows=True)

    ell = len_w[...].reshape(1, width)
    z_pad[...] = jnp.zeros(z_pad.shape, F32)
    z_pad[0:size, :] = ind_w[...] / ell
    zs = z_pad[...]
    kzz, factor, inverse = chol[0], chol[1], chol[2]
    line = lax.broadcasted_iota(jnp.int32, (IND, IND), 0)
    lane = lax.broadcasted_iota(jnp.int32, (IND, IND), 1)
    g_chol = jnp.where(line >= lane, -big[32:64, 384 : 384 + IND], 0.0)
    lower = hdot(factor, g_chol, ((0,), (0,)))
    phi = jnp.where(line > lane, lower, jnp.where(line == lane, 0.5 * lower, 0.0))
    back = hdot(inverse, hdot(phi, inverse), ((0,), (0,)))
    back_t = hdot(inverse, hdot(phi, inverse, ((0,), (0,))), ((0,), (0,)))
    weights_z = -0.5 * kzz * (back + back_t)
    g_z = big[0:32, :]
    g_z = jnp.where(lax.broadcasted_iota(jnp.int32, (IND, 1), 0) < size, g_z, 0.0) + 2.0 * (
        zs * jnp.sum(weights_z, axis=1, keepdims=True) - hdot(weights_z, zs)
    )
    lamb_step(ind_w[...], (g_z / ell)[0:size], ind_m[...], ind_s[...], outs[6:9])
    g_len = -(big[20:21, :] + jnp.sum(g_z * zs, axis=0, keepdims=True)) / ell
    lamb_step(ell, g_len, len_m[...].reshape(1, width), len_s[...].reshape(1, width), outs[9:12])

    means = mean_w[...]
    g_mean = big[32 : 32 + classes, 512 : 512 + size] + means * scale
    lamb_step(means, g_mean, mean_m[...], mean_s[...], outs[12:15])
    small_line = lax.broadcasted_iota(jnp.int32, (size, size), 0)
    small_lane = lax.broadcasted_iota(jnp.int32, (size, size), 1)
    kl = 0.5 * jnp.sum(means * means, axis=0, keepdims=True)
    weight_sq = jnp.zeros((1, size), F32)
    step_sq = weight_sq
    steps = []
    for c in range(classes):
        weight = low_w[c]
        factors = scale_rows(weight)
        inner = big[32 : 32 + size, c * IND : c * IND + size] + factors * scale
        grad = jnp.where(
            small_line > small_lane, inner,
            jnp.where(small_line == small_lane, factors * inner - scale, 0.0),
        )
        new_one, new_two, direction = lamb_moments(weight, grad, low_m[c], low_s[c])
        outs[16][c] = new_one
        outs[17][c] = new_two
        weight_sq = weight_sq + jnp.sum(weight * weight, axis=0, keepdims=True)
        step_sq = step_sq + jnp.sum(direction * direction, axis=0, keepdims=True)
        diagonal = jnp.where(small_line == small_lane, weight, 0.0)
        kl = kl + jnp.sum(0.5 * factors * factors - diagonal, axis=0, keepdims=True)
        steps.append(direction)
    ratio = RATE * jnp.sqrt(jnp.sum(weight_sq, axis=1, keepdims=True)) / jnp.sqrt(
        jnp.sum(step_sq, axis=1, keepdims=True)
    )
    for c in range(classes):
        outs[15][c] = low_w[c] - ratio * steps[c]
    kl = jnp.sum(kl, axis=1, keepdims=True) - 0.5 * classes * size
    parts_out[0] = jnp.sum(big[23:24, 0:1] + kl)


def staged(body, n_in, n_out, n_first, n_last, *refs):
    first, refs = refs[:n_first], refs[n_first:]
    ins, refs = refs[:n_in], refs[n_in:]
    outs, refs = refs[:n_out], refs[n_out:]
    last, refs = refs[:n_last], refs[n_last:]
    held, refs = refs[:n_in], refs[n_in:]
    made, refs = refs[:n_out], refs[n_out:]
    scratch, (sem_in, sem_out) = refs[:-2], refs[-2:]
    loads = [
        pltpu.make_async_copy(ref, held[i], sem_in.at[i]) for i, ref in enumerate(ins)
    ]
    for copy in loads:
        copy.start()
    for copy in loads:
        copy.wait()
    body(*first, *held, *made, *last, *scratch)
    stores = [
        pltpu.make_async_copy(made[i], ref, sem_out.at[i]) for i, ref in enumerate(outs)
    ]
    for copy in stores:
        copy.start()
    for copy in stores:
        copy.wait()


def local_call(body, first, ins, outs, last, scratch):
    sem = pltpu.SemaphoreType.DMA
    return pl.pallas_call(
        functools.partial(staged, body, len(ins), len(outs), len(first), len(last)),
        out_shape=tuple(outs) + tuple(last),
        in_specs=[SMEM] * len(first) + [ANY] * len(ins),
        out_specs=(ANY,) * len(outs) + (SMEM,) * len(last),
        scratch_shapes=[
            *[pltpu.VMEM(a.shape, a.dtype) for a in ins],
            *[pltpu.VMEM(o.shape, o.dtype) for o in outs],
            *scratch,
            sem((len(ins),)),
            sem((len(outs),)),
        ],
        compiler_params=pltpu.CompilerParams(vmem_limit_bytes=60 << 20),
    )(*first, *ins)


def update_conv(kernel_of, *ins):
    shape = jax.ShapeDtypeStruct
    part, conv = ins[0], ins[1]
    outs = [shape(conv.shape, F32)] * 3 + [shape((8, 128), F32)]
    return local_call(
        conv_kernel, [kernel_of], ins, outs, [],
        [pltpu.VMEM(conv.shape, F32), pltpu.VMEM(part.shape, F32)],
    )


def update_small(*ins):
    shape = jax.ShapeDtypeStruct
    width = ins[6].shape[1]
    outs = [shape(p.shape, F32) for p in ins[6:24:3] for _ in range(3)]
    return local_call(
        small_kernel, [], ins, outs, [shape((2,), F32)] * 3,
        [pltpu.VMEM((IND, width), F32), pltpu.VMEM((32, width), F32)],
    )


def tally_kernel(n_dp, n_rep, tally, late, out, ratios, late_out, ex_a, ex_b, one_b,
                 a_send, a_recv, b_send, b_recv, *scratch):
    half = n_dp // 2
    dp, rep = lax.axis_index("dp"), lax.axis_index("replica")
    greeted = greet(n_dp, n_rep)
    late_sum = Reduce(("dp", n_dp), ("replica", n_rep), *scratch[:5], scratch[5:])
    scratch[0][...] = jnp.zeros(scratch[0].shape, F32)
    put_rows(scratch[0], 0, late[...])
    ex_a[dp] = tally[...]
    first = Spread("dp", n_dp, tally, ex_a, a_send, a_recv)
    greeted()
    first.start()
    late_sum.start()
    first.wait()
    one_b[...] = jnp.zeros(one_b.shape, F32)
    for l in range(2):
        near = range(l * half, (l + 1) * half)
        one_b[l : l + 1, :] = total([ex_a[i, 0:1, :] for i in near])
        one_b[2 + l : 3 + l, :] = total([ex_a[i, 1:2, :] for i in near])
    one_b[4:5, :] = total(rows_of(ex_a, 2))
    ex_b[rep] = one_b[...]
    second = Spread("replica", n_rep, one_b, ex_b, b_send, b_recv)
    second.start()
    late_sum.middle()
    second.wait()
    joined = jnp.sum(total([ex_b[i] for i in range(n_rep)]), axis=1, keepdims=True)
    out[...] = jnp.zeros(out.shape, F32) + joined
    trust = jnp.sqrt(joined[0:2]) / jnp.sqrt(joined[2:4])
    ratios[0] = jnp.sum(trust[0:1])
    ratios[1] = jnp.sum(trust[1:2])
    late_sum.last()
    first.drain()
    second.drain()
    late_sum.finish()
    made = scratch[4]
    per = made.shape[1]
    for k in range(late_out.shape[0]):
        late_out[k : k + 1, :] = made[k // per, k % per : k % per + 1, :]


def join_tally(n_dp, n_rep, tally, late):
    sem = pltpu.SemaphoreType.DMA
    shape = jax.ShapeDtypeStruct
    return pl.pallas_call(
        functools.partial(tally_kernel, n_dp, n_rep),
        out_shape=(shape((8, 128), F32), shape((2,), F32), shape(late.shape, F32)),
        in_specs=[VMEM, VMEM],
        out_specs=(VMEM, SMEM, VMEM),
        scratch_shapes=[
            pltpu.VMEM((n_dp, 8, 128), F32),
            pltpu.VMEM((n_rep, 8, 128), F32),
            pltpu.VMEM((8, 128), F32),
            sem((n_dp,)), sem((n_dp,)), sem((n_rep,)), sem((n_rep,)),
            *reduce_scratch(n_dp, n_rep, late.shape[0], late.shape[1]),
        ],
        compiler_params=pltpu.CompilerParams(collective_id=3, has_side_effects=True),
    )(tally, late)


def on_device(
    images, labels, counts, noise_table, noise_index, power_start,
    conv_weight, conv_first, conv_second,
    stem_weight, stem_first, stem_second,
    norm_params, norm_first, norm_second,
    inducing, inducing_first, inducing_second,
    lengthscale, length_first, length_second,
    var_mean, mean_first, mean_second,
    var_lower, lower_first, lower_second,
):
    width = stem_weight.shape[1]
    side = images.shape[2]
    cells = side * side
    n_dp, n_rep = lax.axis_size("dp"), lax.axis_size("replica")
    here = lax.axis_index(AXES)
    per_kernel = n_dp * n_rep // 2
    owner = here // per_kernel
    select = (jnp.arange(2) == owner).astype(F32)
    geometry = (n_dp, n_rep, side)

    rows = conv_weight.astype(BF16).reshape(-1, width)
    share = rows.shape[0]
    fused = share % 16 == 8 and n_rep == 4 and n_dp == 8
    bound = jnp.zeros((16, width), BF16)
    if fused:
        odd = here % 2 == 1
        blank = jnp.zeros((8, width), BF16)
        main = jnp.where(odd, rows[8:], rows[:-8])
        bound = jnp.where(
            odd, jnp.concatenate([blank, rows[:8]]), jnp.concatenate([rows[-8:], blank])
        )
        extra = power_start
    else:
        gathered = lax.all_gather(rows, AXES, axis=0, tiled=True)
        main = gathered[: 9 * width]
        own = rows.astype(F32)
        start = jnp.sum(select[:, None] * power_start, axis=0)
        own_along = jnp.sum(own * start, axis=1)
        back_rows = jnp.sum(own * own_along[:, None], axis=0)
        extra = jnp.stack([back_rows, jnp.full((width,), jnp.sum(own_along * own_along))])
    pictures = images.astype(F32).reshape(images.shape[0], images.shape[1], cells)
    k_one, k_two, act_one, raw_one, act_two, windows, stem_pool, stats, patches, stem_kernel = forward(
        *geometry, share, fused, counts, main, bound, pictures, stem_weight, extra, norm_params
    )
    if not fused:
        k_two = gathered[9 * width :]
    cat, head_rows, grads, chol = head(
        *geometry, counts, labels, noise_index, noise_table, k_two, raw_one, windows, stem_pool,
        stats, norm_params, inducing, lengthscale, var_mean, var_lower,
    )
    part, big, sums, late = backward(
        *geometry, share, fused, counts, cat, act_one, k_one, k_two,
        act_two.reshape(act_one.shape), patches, stem_kernel, stats, norm_params, windows,
        head_rows, grads,
    )
    if not fused:
        part_one = lax.psum_scatter(
            jnp.concatenate([part.reshape(-1), jnp.zeros((part.size,), F32)]),
            AXES, scatter_dimension=0, tiled=True,
        ).reshape(-1, width)
        all_windows, all_grads = lax.all_gather(
            (windows[:, :9], head_rows[8 : 8 + images.shape[0]]), AXES, tiled=True
        )
        all_windows = all_windows.reshape(all_windows.shape[0], -1)
        mine = lax.dynamic_slice_in_dim(
            all_windows, lax.rem(here, per_kernel) * share, share, axis=1
        )
        part = jnp.where(owner == 0, part_one, jnp.dot(mine.T, all_grads, precision=HIGH))

    wide = (-1, 128)
    new_one, new_two, direction, tally = update_conv(
        owner.astype(jnp.int32)[None], part, conv_weight.reshape(wide),
        conv_first.reshape(wide), conv_second.reshape(wide), power_start,
        sums, head_rows, stats, norm_params,
    )
    joined, ratios, late = join_tally(n_dp, n_rep, tally, late)
    small = update_small(
        big, late, joined, head_rows, stats, chol,
        stem_weight, stem_first, stem_second, norm_params, norm_first, norm_second,
        inducing, inducing_first, inducing_second, lengthscale, length_first, length_second,
        var_mean, mean_first, mean_second, var_lower, lower_first, lower_second,
    )
    loss_parts, sigmas, rms = small[18:]
    ratio = jnp.where(owner == 0, ratios[0], ratios[1])
    new_conv = conv_weight - (RATE * ratio) * direction.reshape(-1)
    return (
        loss_parts,
        new_conv, new_one.reshape(-1), new_two.reshape(-1), new_conv.astype(BF16),
        *small[:18],
        sigmas, rms,
    )


def solution(mesh):
    split = P(AXES)
    return jax.shard_map(
        on_device,
        mesh=mesh,
        in_specs=(split, split, split, P(), split, P(), split, split, split) + (P(),) * 18,
        out_specs=(P(),) + (split,) * 4 + (P(),) * 20,
        check_vma=False,
    )
```

```python
import functools

import jax
import jax.numpy as jnp
from jax import lax
from jax.experimental import pallas as pl
from jax.experimental.pallas import tpu as pltpu
from jax.sharding import PartitionSpec as P

STEP = 10
HIGH = lax.Precision.HIGHEST
EPS_NORM = 1e-05
JITTER = 0.001
BETA_ONE = 0.9
BETA_TWO = 0.999
RATE = 0.3
DECAY = 0.01
EPS_ADAM = 1e-08
AXES = ("dp", "replica")


def lamb_moments(weight, gradient, moment_one, moment_two):
    new_one = BETA_ONE * moment_one + (1.0 - BETA_ONE) * gradient
    new_two = BETA_TWO * moment_two + (1.0 - BETA_TWO) * gradient * gradient
    direction = (
        new_one / (1.0 - BETA_ONE**STEP) / (jnp.sqrt(new_two / (1.0 - BETA_TWO**STEP)) + EPS_ADAM)
        + DECAY * weight
    )
    return (new_one, new_two, direction)


MESH = pl.DeviceIdType.MESH
ANY = pl.BlockSpec(memory_space=pl.ANY)
VMEM = pl.BlockSpec(memory_space=pltpu.VMEM)
SMEM = pl.BlockSpec(memory_space=pltpu.SMEM)
F32 = jnp.float32
BF16 = jnp.bfloat16
F8 = jnp.float8_e4m3fn
ACT_SCALE = 0.25
KERNEL_SCALE = 2048.0


def remote(src, dst, send, recv, where):
    return pltpu.make_async_remote_copy(
        src_ref=src, dst_ref=dst, send_sem=send, recv_sem=recv,
        device_id=where, device_id_type=MESH,
    )


def greet(n_dp, n_rep):
    dp, rep = lax.axis_index("dp"), lax.axis_index("replica")
    barrier = pltpu.get_barrier_semaphore()
    for j in range(1, n_dp):
        pl.semaphore_signal(
            barrier, inc=1, device_id={"dp": lax.rem(dp + j, n_dp)}, device_id_type=MESH
        )
    for j in range(1, n_rep):
        pl.semaphore_signal(
            barrier, inc=1, device_id={"replica": lax.rem(rep + j, n_rep)}, device_id_type=MESH
        )
    return lambda: pl.semaphore_wait(barrier, n_dp + n_rep - 2)


class Spread:
    def __init__(self, axis, size, src, dst, send, recv):
        self.axis, self.size, self.src, self.dst, self.send, self.recv = axis, size, src, dst, send, recv
        self.me = lax.axis_index(axis)

    def copies(self):
        for j in range(1, self.size):
            yield remote(
                self.src, self.dst.at[self.me], self.send.at[j], self.recv.at[j],
                {self.axis: lax.rem(self.me + j, self.size)},
            )

    def start(self):
        for copy in self.copies():
            copy.start()

    def wait(self):
        for j in range(1, self.size):
            source = lax.rem(self.me + self.size - j, self.size)
            remote(
                self.src, self.dst.at[source], self.send.at[j], self.recv.at[j],
                {self.axis: source},
            ).wait_recv()

    def drain(self):
        for copy in self.copies():
            copy.wait_send()


def rows_of(refs, row):
    return [refs[i, row : row + 1, :] for i in range(refs.shape[0])]


def total(values):
    result = values[0]
    for value in values[1:]:
        result = result + value
    return result


def join_moments(refs):
    averages, squares, counts = rows_of(refs, 0), rows_of(refs, 1), rows_of(refs, 2)
    count = total(counts)
    average = total([a * n for a, n in zip(averages, counts)]) / count
    spread = total(
        [s + n * (a - average) * (a - average) for a, s, n in zip(averages, squares, counts)]
    )
    return average, spread, count


def hdot(a, b, dims=((1,), (0,))):
    return lax.dot_general(
        a, b, (dims, ((), ())), precision=HIGH, preferred_element_type=F32
    )


def bdot(a, b, dims=((1,), (0,))):
    return lax.dot_general(a, b, (dims, ((), ())), preferred_element_type=F32)


class Gather:
    def __init__(self, which, n_dp, share, buffer, sems):
        self.which, self.n_dp, self.share, self.buffer = which, n_dp, share, buffer
        tiles = (share - 8) // 16
        edges = [tiles * i // PIECES * 16 for i in range(PIECES + 1)]
        self.pieces = list(zip(edges, [hi - lo for lo, hi in zip(edges, edges[1:])]))
        self.z_send, self.z_recv, self.r_send, self.r_recv, self.c_send, self.c_recv = [
            s.at[which] for s in sems
        ]
        self.dp, rep = lax.axis_index("dp"), lax.axis_index("replica")
        self.reps = (rep, rep + 1 - 2 * lax.rem(rep, 2), rep + 2 - 4 * (rep // 2), 3 - rep)
        self.core, self.z = lax.rem(self.dp, 2), self.dp // 2
        self.n_z = n_dp // 2
        self.sources = n_dp // 4
        self.order = range(self.sources) if which else range(self.sources - 1, -1, -1)

    def first(self, zi, core, k):
        owner = (zi * 2 + core) * 4 + self.reps[k]
        return (owner // 2) * (2 * self.share) + lax.rem(owner, 2) * (self.share + 8)

    def each(self, zi, core, k, piece, act):
        start, rows = self.pieces[piece]
        begin = pl.multiple_of(self.first(zi, core, k) + start, 16)
        if piece < len(self.pieces) - 1:
            act(self.buffer.at[pl.ds(begin, rows), :])
            return
        even = lax.rem(self.reps[k], 2) == 0
        pl.when(even)(lambda: act(self.buffer.at[pl.ds(begin, rows + 16), :]))
        pl.when(~even)(lambda: act(self.buffer.at[pl.ds(begin, rows), :]))

    def source(self, zi):
        return zi + self.which * self.sources

    def along(self, zi, piece, what, ways=(0, 1)):
        def act(ref):
            for way in ways:
                condition = (
                    ((self.z <= self.source(zi)) & (self.z > 0)) if way
                    else ((self.z >= self.source(zi)) & (self.z < self.n_z - 1))
                )
                step = self.n_dp - 2 if way else 2
                copy = remote(
                    ref, ref, self.z_send.at[zi, piece, way], self.z_recv.at[zi, piece],
                    {"dp": lax.rem(self.dp + step, self.n_dp)},
                )
                if what == "wait_recv":
                    copy.wait_recv()
                    return
                pl.when(condition)(getattr(copy, what))
        self.each(zi, self.core, 0, piece, act)

    def goes_on(self, zi):
        gap = self.z - self.source(zi)
        return ((gap < 0) & (self.z > 0)) | ((gap > 0) & (self.z < self.n_z - 1))

    def near(self, zi, piece, k, what):
        def act(ref):
            getattr(remote(
                ref, ref, self.r_send.at[zi, piece, k], self.r_recv.at[zi, piece, k],
                {"replica": self.reps[k]},
            ), what)()
        self.each(zi, self.core, k if what == "wait_recv" else 0, piece, act)

    def passed(self, zi, piece, what):
        k = 1 + piece % 2
        def act(ref):
            getattr(remote(
                ref, ref, self.r_send.at[zi, piece, 3], self.r_recv.at[zi, piece, 3],
                {"replica": self.reps[3 - k]},
            ), what)()
        self.each(zi, self.core, 3 if what == "wait_recv" else k, piece, act)

    def over(self, zi, piece, k, what):
        def act(ref):
            getattr(remote(
                ref, ref, self.c_send.at[zi, piece, k], self.c_recv.at[zi, piece, k],
                {"dp": self.dp + 1 - 2 * self.core},
            ), what)()
        self.each(zi, 1 - self.core if what == "wait_recv" else self.core, k, piece, act)

    def send_plane(self, zi, piece):
        for k in (1, 2):
            self.near(zi, piece, k, "start")
        self.over(zi, piece, 0, "start")

    def own(self, pieces, ways, plane):
        for zi in range(self.sources):
            @pl.when(self.z == self.source(zi))
            def _():
                for piece in pieces:
                    self.along(zi, piece, "start", ways)
                    if plane:
                        self.send_plane(zi, piece)

    def column(self, zi, pieces):
        @pl.when(self.z != self.source(zi))
        def _():
            for piece in pieces:
                self.along(zi, piece, "wait_recv")
                self.along(zi, piece, "start")
                self.send_plane(zi, piece)

    def hop(self, distance):
        for zi in self.order:
            gap = self.z - self.source(zi)
            @pl.when(self.goes_on(zi) & ((gap == distance) | (gap == -distance)))
            def _():
                for piece in range(len(self.pieces)):
                    self.along(zi, piece, "wait_recv")
                    self.along(zi, piece, "start")

    def plane(self, zi, condition):
        @pl.when(condition)
        def _():
            for piece in range(len(self.pieces)):
                pl.when((self.z != self.source(zi)) & ~self.goes_on(zi))(
                    functools.partial(self.along, zi, piece, "wait_recv")
                )
                self.send_plane(zi, piece)

    def neighbours(self, zi, pieces):
        for piece in pieces:
            for k in (1, 2):
                self.near(zi, piece, k, "wait_recv")
                if k == 1 + piece % 2:
                    self.passed(zi, piece, "start")
                self.over(zi, piece, k, "start")

    def opposite(self, zi):
        for piece in range(len(self.pieces)):
            self.passed(zi, piece, "wait_recv")
            self.over(zi, piece, 3, "start")

    def from_core(self, zi):
        for piece in range(len(self.pieces)):
            for k in range(4):
                self.over(zi, piece, k, "wait_recv")

    def drain(self):
        for piece in range(len(self.pieces)):
            for zi in range(self.sources):
                self.along(zi, piece, "wait_send")
                for k in (1, 2):
                    self.near(zi, piece, k, "wait_send")
                self.passed(zi, piece, "wait_send")
                for k in range(4):
                    self.over(zi, piece, k, "wait_send")


PIECES = 4


def pixel_column(rows, side):
    return lax.rem(lax.broadcasted_iota(jnp.int32, (rows, 1), 0), side)


def store_shifted(ref, image, first, block, values, side):
    width = values.shape[1]
    rows = block * side
    column = pixel_column(rows, side)
    left = jnp.where(column == 0, 0.0, pltpu.roll(values, 1, 0))
    right = jnp.where(column == side - 1, 0.0, pltpu.roll(values, rows - 1, 0))
    for c, moved in enumerate((left, values, right)):
        ref[image, pl.ds(first + 1, block), :, c * width : (c + 1) * width] = (
            moved.astype(ref.dtype).reshape(block, side, width)
        )


def gelu_both(x):
    c = 0.7978845608028654
    square = x * x
    th = jnp.tanh(c * x * (1.0 + 0.044715 * square))
    half = 0.5 * (1.0 + th)
    return x * half, half + 0.5 * x * (1.0 - th * th) * (c * (1.0 + 3 * 0.044715 * square))


def window_matrix(side):
    shape = (side * side, 16)
    pixel = lax.broadcasted_iota(jnp.int32, shape, 0)
    tap = lax.broadcasted_iota(jnp.int32, shape, 1)
    r, c = tap // 3, lax.rem(tap, 3)
    h, w = pixel // side, lax.rem(pixel, side)
    keep = (
        (tap < 9)
        & ~((r == 0) & (h == side - 1)) & ~((r == 2) & (h == 0))
        & ~((c == 0) & (w == side - 1)) & ~((c == 2) & (w == 0))
    )
    return jnp.where(keep, 1.0, 0.0).astype(BF16)


BLOCK = 8


def make_patches(images, side, patches, line):
    cells = side * side
    pixel = lax.broadcasted_iota(jnp.int32, (1, cells), 1)
    h, w = pixel // side, lax.rem(pixel, side)
    colours = images.shape[1]
    for n in range(images.shape[0]):
        line[...] = jnp.where(
            lax.broadcasted_iota(jnp.int32, line.shape, 0) == 31, 1.0, 0.0
        )
        values = images[n]
        for t in range(9):
            down, right = t // 3 - 1, t % 3 - 1
            shift = down * side + right
            moved = pltpu.roll(values, (-shift) % cells, 1) if shift else values
            inside = (h + down >= 0) & (h + down < side) & (w + right >= 0) & (w + right < side)
            line[colours * t : colours * (t + 1), :] = jnp.where(inside, moved, 0.0)
        patches[n] = line[...].astype(BF16)


def forward_kernel(
    n_dp, n_rep, side, share, fused,
    counts, weights, pictures, stem_in, start, norms,
    k1_out, k2_out, x_out, y_out, slope_out, cat8_out, windows, stem_pool, stats, patches, stem,
    line, own_f32, main, bound, k1, xcat, y, act, slope, cat8, seam, ex_a, ex_b, one_a, one_b, tw_a, tw_b, tw_one,
    z_send, z_recv, r_send, r_recv, c_send, c_recv,
    a_send, a_recv, b_send, b_recv, s_send, s_recv, local,
):
    images = pictures.shape[0]
    width = stem_in.shape[1]
    cells = side * side
    dp, rep = lax.axis_index("dp"), lax.axis_index("replica")
    half = n_dp // 2
    greeted = greet(n_dp, n_rep)

    if fused:
        rows = share - 8
        sems = (z_send, z_recv, r_send, r_recv, c_send, c_recv)
        one, two = [
            Gather(l, n_dp, share, buffer, sems) for l, buffer in enumerate((k1, k2_out))
        ]
        every = range(PIECES)
        early, final = every[:-1], every[-1:]
        even = lax.rem(rep, 2) == 0
        owner = lax.rem(dp, half) * n_rep + rep
        own_first = (owner // 2) * (2 * share) + lax.rem(owner, 2) * (share + 8)
        seam_copy = remote(
            bound, seam.at[1], s_send.at[0], s_recv.at[0],
            {"replica": rep + 1 - 2 * lax.rem(rep, 2)},
        )

        def own_copies(what):
            for l, buffer in enumerate((k1, k2_out)):
                @pl.when((dp < half) if l == 0 else (dp >= half))
                def _():
                    at = pl.ds(pl.multiple_of(own_first, 16), rows)
                    getattr(pltpu.make_async_copy(main, buffer.at[at, :], local.at[0]), what)()

        def put_seam():
            @pl.when(even)
            def _():
                seam_copy.wait_recv()
                seam[0] = (bound[...].astype(F32) + seam[1].astype(F32)).astype(BF16)
                for l, buffer in enumerate((k1, k2_out)):
                    @pl.when((dp < half) if l == 0 else (dp >= half))
                    def _():
                        at = pl.ds(pl.multiple_of(own_first + rows, 16), 16)
                        copy = pltpu.make_async_copy(seam.at[0], buffer.at[at, :], local.at[10])
                        copy.start()
                        copy.wait()

        lanes = width // 128
        for k in range(lanes):
            own_f32[:, k * 128 : (k + 1) * 128] = weights[pl.ds(k, share, stride=lanes), :]
        blank = jnp.zeros((8, width), F32)
        head_rows, tail_rows = own_f32[0:8, :], own_f32[share - 8 : share, :]
        main[...] = jnp.where(even, own_f32[0:rows, :], own_f32[8:share, :]).astype(BF16)
        bound[...] = jnp.where(
            even,
            jnp.concatenate([tail_rows, blank], axis=0),
            jnp.concatenate([blank, head_rows], axis=0),
        ).astype(BF16)
        own_copies("start")
    else:
        copy_in = pltpu.make_async_copy(weights, k1, local.at[0])
        copy_in.start()

    if fused:
        own_copies("wait")
    greeted()
    if fused:
        pl.when(~even)(seam_copy.start)
        one.own(every[:2], (0, 1), True)
        two.own(every[:2], (1,), False)
    line[:, 0:width] = jnp.zeros((32, width), F32)
    line[0 : stem_in.shape[0], 0:width] = stem_in[...]
    stem[...] = line[:, 0:width].astype(BF16)
    weight = stem[...].astype(F32)
    count = counts[0]
    valid = [jnp.where(count > n, 1.0, 0.0) for n in range(images)]
    held = count.astype(F32) * cells
    make_patches(pictures, side, patches, line)
    grams, sums = [], []
    for n in range(images):
        grams.append(bdot(patches[n], patches[n], ((1,), (1,))))
        sums.append(grams[n][24:32])
        stem_pool[n : n + 1, :] = hdot(sums[n], weight)[7:8] * (1.0 / cells)
    gram = total([g * v for g, v in zip(grams, valid)])
    summed = total([s * v for s, v in zip(sums, valid)])
    square = jnp.sum(weight * hdot(gram, weight), axis=0, keepdims=True)
    last = jnp.where(lax.broadcasted_iota(jnp.int32, summed.shape, 0) == 7, summed, 0.0)
    cover = gram - hdot(last, last, ((0,), (0,))) / held
    zero = jnp.zeros((1, width), F32)
    payload = one_a.at[0]
    payload[...] = jnp.zeros(payload.shape, F32)
    payload[0:1, :] = hdot(summed, weight)[7:8] / held
    payload[1:2, :] = jnp.sum(weight * hdot(cover, weight), axis=0, keepdims=True)
    payload[2:3, :] = zero + held
    payload[5:6, :] = square

    if fused:
        vector = jnp.where(dp < half, start[0:1, :], start[1:2, :])
        own_rows = main[...].astype(F32)
        edge_rows = bound[...].astype(F32)
        along = jnp.sum(own_rows * vector, axis=1, keepdims=True)
        edge_along = jnp.sum(edge_rows * vector, axis=1, keepdims=True)
        payload[3:4, :] = jnp.sum(own_rows * along, axis=0, keepdims=True) + jnp.sum(
            edge_rows * edge_along, axis=0, keepdims=True
        )
        payload[4:5, :] = zero + (
            jnp.sum(along * along, axis=0, keepdims=True)
            + jnp.sum(edge_along * edge_along, axis=0, keepdims=True)
        )
    else:
        payload[3:4, :] = start[0:1, :]
        payload[4:5, :] = start[1:2, :]

    first = ex_a.at[0]
    first[dp] = payload[...]
    one_level = Spread("dp", n_dp, payload, first, a_send.at[0], a_recv.at[0])
    one_level.start()
    if fused:
        one.own(early[2:], (0, 1), True)
        two.own(early[2:], (1,), False)
        put_seam()
        one.own(final, (0, 1), True)
        two.own(final, (1,), False)
    for n in range(images):
        for ref in (xcat, cat8):
            blank = jnp.zeros((1, side, 3 * width), ref.dtype)
            ref[n, 0:1] = blank
            ref[n, side + 1 : side + 2] = blank
    if fused:
        one.column(1, every)
    one_level.wait()
    second = ex_b.at[0]
    mean, spread, cell_count = join_moments(first)
    passed = one_b.at[0]
    passed[...] = jnp.zeros(passed.shape, F32)
    passed[0:1, :] = mean
    passed[1:2, :] = spread
    passed[2:3, :] = cell_count
    vectors, squares = rows_of(first, 3), rows_of(first, 4)
    passed[3:4, :] = total(vectors[:half])
    passed[4:5, :] = total(vectors[half:])
    passed[5:6, :] = total(squares[:half])
    passed[6:7, :] = total(squares[half:])
    passed[7:8, :] = total(rows_of(first, 5))
    second[rep] = passed[...]
    two_level = Spread("replica", n_rep, passed, second, b_send.at[0], b_recv.at[0])
    two_level.start()
    if fused:
        one.neighbours(1, every[:2])
        one.column(0, every[:2])
        one.neighbours(1, every[2:])
        one.column(0, every[2:])
        two.own(every, (0,), False)
        two.hop(1)
    two_level.wait()
    mean, spread, pixels = join_moments(second)
    inverse_one = lax.rsqrt(spread / pixels + EPS_NORM)
    joined = [total(rows_of(second, row)) for row in range(3, 8)]
    sigma_rows, start_rows = [], []
    for l in range(2):
        vec = jnp.sqrt(jnp.sum(joined[l] * joined[l], axis=1, keepdims=True))
        base = jnp.sqrt(joined[2 + l])
        sigma_rows.append(zero + vec / base)
        start_rows.append(base)
        stats[8 + l : 9 + l, :] = joined[l] / vec
    stats[0:1, :] = mean
    stats[1:2, :] = inverse_one
    stats[2:3, :] = pixels
    stats[4:5, :] = sigma_rows[0]
    stats[5:6, :] = sigma_rows[1]
    stats[6:7, :] = start_rows[0]
    stats[7:8, :] = start_rows[1]
    stats[10:11, :] = joined[4]
    scale_one = inverse_one * norms[0:1, :]
    shift_one = norms[1:2, :] - mean * scale_one

    def act_one(n, part):
        def step(i, carry):
            first_row = i * BLOCK
            pixel = pl.ds(pl.multiple_of(first_row * side, BLOCK * side), BLOCK * side)
            out = bdot(patches[n, :, pixel], stem[...], ((0,), (0,)))
            values = jax.nn.gelu(out * scale_one + shift_one)
            store_shifted(xcat, n, first_row, BLOCK, values, side)
            return carry
        half_steps = side // BLOCK // 2
        lax.fori_loop(part * half_steps, (part + 1) * half_steps, step, 0)

    for n in range(images):
        for part in range(2):
            act_one(n, part)
        if fused and n == 0:
            one.neighbours(0, every[:2])
    if fused:
        one.opposite(1)
        one.from_core(1)
    else:
        copy_in.wait()
    x_copies = [
        pltpu.make_async_copy(
            xcat.at[n, pl.ds(1, side), :, pl.ds(width, width)], x_out.at[n], local.at[2 + n]
        )
        for n in range(images)
    ]
    for copy in x_copies:
        copy.start()

    tap_row = 3 * width
    middle = -(-(9 * width // 2 - tap_row) // 128) * 128
    rows_step = 2 * BLOCK * side

    def window(n, i, r, lanes):
        return xcat[n, pl.ds(i * 2 * BLOCK + r, 2 * BLOCK), :, lanes].reshape(rows_step, -1)

    def at_rows(n, i):
        return pl.ds(pl.multiple_of(n * cells + i * rows_step, rows_step), rows_step)

    for n in range(images):
        def later_half(i, carry):
            y[at_rows(n, i), :] = bdot(
                window(n, i, 2, slice(0, tap_row)), k1[2 * tap_row : 3 * tap_row, :]
            ) + bdot(
                window(n, i, 1, slice(middle, tap_row)), k1[tap_row + middle : 2 * tap_row, :]
            )
            return carry
        lax.fori_loop(0, side // (2 * BLOCK), later_half, 0)
        if fused and n == 0:
            one.neighbours(0, every[2:])
            two.hop(2)
            two.plane(0, two.z >= 0)
            two.plane(1, two.z > 0)
    if fused:
        one.opposite(0)
        one.from_core(0)
    k1_copy = pltpu.make_async_copy(k1, k1_out, local.at[1])
    k1_copy.start()
    moments = []
    y_copies = []
    for n in range(images):
        def first_half(i, carry):
            acc = (
                y[at_rows(n, i), :]
                + bdot(window(n, i, 0, slice(0, tap_row)), k1[0:tap_row, :])
                + bdot(window(n, i, 1, slice(0, middle)), k1[tap_row : tap_row + middle, :])
            )
            y[at_rows(n, i), :] = acc
            return carry + jnp.sum(acc, axis=0, keepdims=True)
        whole = lax.fori_loop(0, side // (2 * BLOCK), first_half, zero)
        if fused and n == 0:
            two.plane(1, two.z == 0)
        average = whole / cells
        def spread_step(i, carry):
            pixel = pl.ds(pl.multiple_of(n * cells + i * BLOCK * side, 16), BLOCK * side)
            off = y[pixel, :] - average
            return carry + jnp.sum(off * off, axis=0, keepdims=True)
        moments.append((average, lax.fori_loop(0, side // BLOCK, spread_step, zero)))
        copy = pltpu.make_async_copy(
            y.at[pl.ds(n * cells, cells), :], y_out.at[pl.ds(n * cells, cells), :], local.at[4 + n]
        )
        copy.start()
        y_copies.append(copy)
    payload_two = tw_one.at[0]
    counts_in = [v * cells for v in valid]
    average = total([m[0] * c for m, c in zip(moments, counts_in)]) / held
    payload_two[...] = jnp.zeros(payload_two.shape, F32)
    payload_two[0:1, :] = average
    payload_two[1:2, :] = total([
        v * m[1] + c * (m[0] - average) * (m[0] - average)
        for m, c, v in zip(moments, counts_in, valid)
    ])
    payload_two[2:3, :] = zero + held
    first = tw_a
    first[dp] = payload_two[...]
    three_level = Spread("dp", n_dp, payload_two, first, a_send.at[1], a_recv.at[1])
    three_level.start()
    if fused:
        two.neighbours(0, every)
    three_level.wait()
    mean, spread, cell_count = join_moments(first)
    second = tw_b
    passed = tw_one.at[1]
    passed[...] = jnp.zeros(passed.shape, F32)
    passed[0:1, :] = mean
    passed[1:2, :] = spread
    passed[2:3, :] = cell_count
    second[rep] = passed[...]
    four_level = Spread("replica", n_rep, passed, second, b_send.at[1], b_recv.at[1])
    four_level.start()
    if fused:
        two.neighbours(1, every[:2])
    four_level.wait()
    mean, spread, _ = join_moments(second)
    sigma = sigma_rows[0]
    variance = spread / pixels / (sigma * sigma)
    inverse_two = lax.rsqrt(variance + EPS_NORM) / sigma
    stats[3:4, :] = mean
    stats[11:12, :] = inverse_two
    scale_two = inverse_two * norms[2:3, :]
    shift_two = norms[3:4, :] - mean * scale_two
    select = window_matrix(side)
    act_copies = []
    for n in range(images):
        def step(i, carry):
            pixel = pl.ds(pl.multiple_of(n * cells + i * BLOCK * side, 16), BLOCK * side)
            values, steep = gelu_both(y[pixel, :] * scale_two + shift_two)
            slope[pixel, :] = steep
            act[pixel, :] = values.astype(BF16)
            store_shifted(cat8, n, i * BLOCK, BLOCK, values * ACT_SCALE, side)
            return carry
        lax.fori_loop(0, side // BLOCK, step, 0)
        pixels_of = pl.ds(n * cells, cells)
        for k, (made, out) in enumerate((
            (slope.at[pixels_of, :], slope_out.at[pixels_of, :]), (cat8.at[n], cat8_out.at[n]),
        )):
            copy = pltpu.make_async_copy(made, out, local.at[6 + 2 * k + n])
            copy.start()
            act_copies.append(copy)
        windows[n] = bdot(select, act[n * cells : (n + 1) * cells, :], ((0,), (0,)))
        if fused and n == 0:
            two.neighbours(1, every[2:])
            two.opposite(two.order[0])
    if fused:
        two.opposite(two.order[1])
        for zi in two.order:
            two.from_core(zi)
        one.drain()
        two.drain()
        pl.when(~even)(seam_copy.wait_send)
    for level in (one_level, two_level, three_level, four_level):
        level.drain()
    for copy in [k1_copy] + x_copies + y_copies + act_copies:
        copy.wait()


def forward(n_dp, n_rep, side, share, fused, counts, weights, pictures, stem, start, norms):
    images, cells = pictures.shape[0], side * side
    width = stem.shape[1]
    half = n_dp // 2
    sources = max(n_dp // 4, 1)
    shape = jax.ShapeDtypeStruct
    sem = pltpu.SemaphoreType.DMA
    kernel_rows = 9 * width
    return pl.pallas_call(
        functools.partial(forward_kernel, n_dp, n_rep, side, share, fused),
        out_shape=(
            shape((kernel_rows, width), BF16),
            shape((kernel_rows, width), BF16),
            shape((images, side, side, width), BF16),
            shape((images * cells, width), F32),
            shape((images * cells, width), F32),
            shape((images, side + 2, side, 3 * width), F8),
            shape((images, 16, width), F32),
            shape((images, width), F32),
            shape((16, width), F32),
            shape((images, 32, cells), BF16),
            shape((32, width), BF16),
        ),
        in_specs=[SMEM, VMEM if fused else ANY, VMEM, VMEM, VMEM, VMEM],
        out_specs=(ANY,) * 6 + (VMEM,) * 5,
        scratch_shapes=[
            pltpu.VMEM((32, cells), F32),
            pltpu.VMEM((share if fused else 8, width), F32),
            pltpu.VMEM((share - 8 if fused else 16, width), BF16),
            pltpu.VMEM((16, width), BF16),
            pltpu.VMEM((kernel_rows, width), BF16),
            pltpu.VMEM((images, side + 2, side, 3 * width), BF16),
            pltpu.VMEM((images * cells, width), F32),
            pltpu.VMEM((images * cells, width), BF16),
            pltpu.VMEM((images * cells, width), F32),
            pltpu.VMEM((images, side + 2, side, 3 * width), F8),
            pltpu.VMEM((2, 16, width), BF16),
            pltpu.VMEM((1, n_dp, 8, width), F32),
            pltpu.VMEM((1, n_rep, 8, width), F32),
            pltpu.VMEM((1, 8, width), F32),
            pltpu.VMEM((1, 8, width), F32),
            pltpu.VMEM((n_dp, 4, width), F32),
            pltpu.VMEM((n_rep, 4, width), F32),
            pltpu.VMEM((2, 4, width), F32),
            sem((2, sources, PIECES, 2)),
            sem((2, sources, PIECES)),
            sem((2, sources, PIECES, 4)),
            sem((2, sources, PIECES, 4)),
            sem((2, sources, PIECES, 4)),
            sem((2, sources, PIECES, 4)),
            sem((2, n_dp)),
            sem((2, n_dp)),
            sem((2, n_rep)),
            sem((2, n_rep)),
            sem((1,)),
            sem((1,)),
            sem((11,)),
        ],
        compiler_params=pltpu.CompilerParams(
            collective_id=0, has_side_effects=True, vmem_limit_bytes=56 << 20
        ),
    )(counts, weights, pictures, stem, start, norms)


class Reduce:
    def __init__(self, near, far, src, parts, whole, planes, out, sems):
        (self.axis, self.size), (self.other, self.others) = near, far
        self.src, self.parts, self.whole, self.planes, self.out = src, parts, whole, planes, out
        self.a_send, self.a_recv = sems[:2]
        self.b_send, self.b_recv, self.c_send, self.c_recv = sems[2:] or [None] * 4
        self.me = lax.axis_index(self.axis)

    def scatter(self):
        for j in range(1, self.size):
            peer = lax.rem(self.me + j, self.size)
            yield remote(
                self.src.at[peer], self.parts.at[self.me], self.a_send.at[j], self.a_recv.at[j],
                {self.axis: peer},
            )

    def start(self):
        for copy in self.scatter():
            copy.start()
        self.parts[self.me] = self.src[self.me]

    def arrive(self):
        for j in range(1, self.size):
            source = lax.rem(self.me + self.size - j, self.size)
            remote(
                self.src.at[source], self.parts.at[source], self.a_send.at[j], self.a_recv.at[j],
                {self.axis: source},
            ).wait_recv()
        self.whole[...] = total([self.parts[i] for i in range(self.size)])

    def middle(self):
        self.arrive()
        self.across()

    def across(self):
        self.planes[lax.axis_index(self.other)] = self.whole[...]
        self.second = Spread(
            self.other, self.others, self.whole, self.planes, self.b_send, self.b_recv
        )
        self.second.start()

    def last(self):
        self.second.wait()
        self.out[self.me] = total([self.planes[i] for i in range(self.others)])
        self.third = Spread(
            self.axis, self.size, self.out.at[self.me], self.out, self.c_send, self.c_recv
        )
        self.third.start()

    def finish(self):
        self.finish_last()
        self.drain()

    def drain(self):
        for copy in self.scatter():
            copy.wait_send()

    def finish_last(self):
        self.third.wait()
        self.second.drain()
        self.third.drain()


def reduce_scratch(size, others, rows, width):
    per = -(-rows // size)
    sem = pltpu.SemaphoreType.DMA
    return [
        pltpu.VMEM((size, per, width), F32),
        pltpu.VMEM((size, per, width), F32),
        pltpu.VMEM((per, width), F32),
        pltpu.VMEM((others, per, width), F32),
        pltpu.VMEM((size, per, width), F32),
        sem((size,)), sem((size,)), sem((others,)), sem((others,)), sem((size,)), sem((size,)),
    ]


def put_rows(ref, first, values):
    per = ref.shape[1]
    for k in range(values.shape[0]):
        row = first + k
        ref[row // per, row % per : row % per + 1, :] = values[k : k + 1, :]


def gelu_slope(x):
    return gelu_both(x)[1]


def fold(values):
    return jnp.sum(values.reshape(values.shape[0] // 8, 8, values.shape[1]), axis=0)


IND = 32


def cholesky_steps(matrix, size):
    lane = lax.broadcasted_iota(jnp.int32, (size, IND), 1)
    line = lax.broadcasted_iota(jnp.int32, (size, IND), 0)
    left = matrix
    right = jnp.where(lane == line, 1.0, 0.0)
    factor = jnp.zeros((size, IND), F32)
    row_of = lax.broadcasted_iota(jnp.int32, (size, 1), 0)
    for k in range(size):
        inverse = lax.rsqrt(left[k : k + 1, k : k + 1])
        column = jnp.where(row_of >= k, left[:, k : k + 1] * inverse, 0.0)
        below = jnp.where(row_of > k, column, 0.0)
        row = left[k : k + 1, :] * inverse
        other = right[k : k + 1, :] * inverse
        factor = jnp.where(lane == k, column, factor)
        left = left - below * row
        right = jnp.where(line == k, other, right - below * other)
    return factor, right


def scale_rows(lower):
    size = lower.shape[0]
    line = lax.broadcasted_iota(jnp.int32, (size, size), 0)
    lane = lax.broadcasted_iota(jnp.int32, (size, size), 1)
    return jnp.where(line > lane, lower, jnp.where(line == lane, jnp.exp(lower), 0.0))


def head_kernel(
    n_dp, n_rep, side,
    counts, labels, indices, table, k2_in, y_in, slope_in, windows, stem_pool, stats, norms,
    inducing, lengthscale, var_mean, var_lower,
    cat_out, k8_out, head_out, grads_out, chol_out,
    k2, k8, y, d_pre, cat, pattern, z_pad, l_pad, v_pad, f_pad, x_pad, kx_pad, noise, d_rows,
    ex_a, ex_b, one_a, one_b, a_send, a_recv, b_send, b_recv, local,
):
    images = stem_pool.shape[0]
    width = stem_pool.shape[1]
    cells = side * side
    size = inducing.shape[0]
    classes = var_mean.shape[0]
    samples = indices.shape[1]
    dp, rep = lax.axis_index("dp"), lax.axis_index("replica")
    loads = [
        pltpu.make_async_copy(k2_in, k2, local.at[0]),
        pltpu.make_async_copy(y_in, y, local.at[1]),
        pltpu.make_async_copy(slope_in, d_pre, local.at[2]),
    ]
    for copy in loads:
        copy.start()
    greet(n_dp, n_rep)()

    sigma_one, sigma_two = stats[4:5, :], stats[5:6, :]
    pixels = stats[2:3, :]
    scale = cells / stats[2:3, 0:1]
    ell = lengthscale[...].reshape(1, width)

    z_pad[...] = jnp.zeros(z_pad.shape, F32)
    z_pad[0:size, :] = inducing[...] / ell
    zs = z_pad[...]
    ones = jnp.ones((8, width), F32)
    lane = lax.broadcasted_iota(jnp.int32, (size, IND), 1)
    line = lax.broadcasted_iota(jnp.int32, (size, IND), 0)
    kzz = jnp.zeros((size, IND), F32)
    for m in range(size):
        off = zs[0:size, :] - zs[m : m + 1, :]
        kzz = jnp.where(lane == m, jnp.exp(-0.5 * jnp.sum(off * off, axis=1, keepdims=True)), kzz)
    factor, inverse = cholesky_steps(jnp.where(lane == line, kzz + JITTER, kzz), size)
    chol_out[...] = jnp.zeros(chol_out.shape, F32)
    chol_out[0, 0:size, :] = kzz
    chol_out[1, 0:size, :] = factor
    chol_out[2, 0:size, :] = inverse
    l_pad[...] = jnp.zeros(l_pad.shape, F32)
    l_pad[0:size, :] = inverse
    v_pad[...] = jnp.zeros(v_pad.shape, F32)
    v_pad[0:classes, 0:size] = var_mean[...]
    f_pad[...] = jnp.zeros(f_pad.shape, F32)
    for c in range(classes):
        f_pad[0:size, c * IND : c * IND + size] = scale_rows(var_lower[c])
    group = lax.broadcasted_iota(jnp.int32, (classes * IND, 16), 0) // IND
    which = lax.broadcasted_iota(jnp.int32, (classes * IND, 16), 1)
    groups = jnp.where(group == which, 1.0, 0.0)
    noise[...] = jnp.zeros(noise.shape, F32)
    table_lane = lax.broadcasted_iota(jnp.int32, (1, table.shape[1]), 1)
    for n in range(images):
        chosen = [jnp.where(table_lane == indices[n, s], 1.0, 0.0) for s in range(samples)]
        chosen.append(jnp.zeros((16 - samples, table.shape[1]), F32))
        noise[n, :, 0:classes] = hdot(jnp.concatenate(chosen, axis=0), table[...], ((1,), (1,)))

    loads[0].wait()
    pooled_raw = jnp.zeros((16, width), F32)
    for t in range(9):
        parts = []
        rest = [windows[n, t : t + 1, :] for n in range(images)]
        for _ in range(3):
            parts += [r.astype(BF16).astype(F32) for r in rest]
            rest = [r - p for r, p in zip(rest, parts[-images:])]
        parts.append(jnp.zeros((16 - 3 * images, width), F32))
        lhs = jnp.concatenate(parts, axis=0).astype(BF16)
        pooled_raw = pooled_raw + bdot(lhs, k2[t * width : (t + 1) * width, :])
    x_pad[...] = jnp.zeros(x_pad.shape, F32)
    branch_pool = []
    for n in range(images):
        row = total([pooled_raw[k * images + n : k * images + n + 1] for k in range(3)])
        branch_pool.append(row / (cells * sigma_two))
        x_pad[n : n + 1, :] = (stem_pool[n : n + 1, :] + branch_pool[n]) / ell
    xs = x_pad[...]

    kx_pad[...] = jnp.zeros(kx_pad.shape, F32)
    for n in range(images):
        off = zs - xs[n : n + 1, :]
        kx_pad[n : n + 1, :] = jnp.exp(-0.5 * hdot(ones, off * off, ((1,), (1,))))[0:1]
    lanes = lax.broadcasted_iota(jnp.int32, (8, IND), 1)
    kx = jnp.where(lanes < size, kx_pad[...], 0.0)
    inv = l_pad[...]
    means = v_pad[...]
    factors = f_pad[...]
    proj = hdot(kx, inv, ((1,), (1,)))
    average = hdot(proj, means, ((1,), (1,)))
    spread = hdot(proj, factors)
    variance = (
        1.0 - jnp.sum(proj * proj, axis=1, keepdims=True) + hdot(spread * spread, groups)
    )
    std = jnp.sqrt(variance)
    class_lane = lax.broadcasted_iota(jnp.int32, (1, 16), 1)
    sample_row = lax.broadcasted_iota(jnp.int32, (16, 16), 0)
    inside = (lax.broadcasted_iota(jnp.int32, (16, 16), 1) < classes) & (sample_row < samples)
    count = counts[0]
    loss = jnp.zeros((1, 1), F32)
    g_avg_rows, g_var_rows = [], []
    for n in range(images):
        drawn = average[n : n + 1, :] + std[n : n + 1, :] * noise[n]
        drawn = jnp.where(inside, drawn, -1e30)
        shifted = drawn - jnp.max(drawn, axis=1, keepdims=True)
        exps = jnp.where(inside, jnp.exp(shifted), 0.0)
        sums = jnp.sum(exps, axis=1, keepdims=True)
        sums = jnp.where(sample_row[:, 0:1] < samples, sums, 1.0)
        hot = jnp.where(class_lane == labels[n], 1.0, 0.0)
        picked = jnp.where(inside, (shifted - jnp.log(sums)) * hot, 0.0)
        held = jnp.where(count > n, 1.0 / samples, 0.0)
        loss = loss - held * jnp.sum(jnp.sum(picked, axis=1, keepdims=True), axis=0, keepdims=True)
        g_samples = jnp.where(inside, exps / sums - hot, 0.0) * (held * scale)
        g_avg_rows.append(jnp.sum(g_samples, axis=0, keepdims=True))
        g_var_rows.append(
            0.5 * jnp.sum(g_samples * noise[n], axis=0, keepdims=True) / std[n : n + 1, :]
        )
    blank = [jnp.zeros((8 - images, 16), F32)]
    g_avg = jnp.concatenate(g_avg_rows + blank, axis=0)
    g_var = jnp.concatenate(g_var_rows + blank, axis=0)
    g_spread = 2.0 * spread * hdot(g_var, groups, ((1,), (1,)))
    g_proj = (
        hdot(g_avg, means)
        - 2.0 * proj * jnp.sum(g_var, axis=1, keepdims=True)
        + hdot(g_spread, factors, ((1,), (1,)))
    )
    g_kx = hdot(g_proj, inv)
    weights = -kx * g_kx
    g_x = xs * jnp.sum(weights, axis=1, keepdims=True) - hdot(weights, zs)
    d_pooled = g_x / ell
    d_rows[...] = jnp.zeros(d_rows.shape, BF16)
    d_rows[0:8, :] = (d_pooled / cells).astype(BF16)
    d_two = d_rows[...]

    taps = [
        bdot(d_two, k2[t * width : (t + 1) * width, :], ((1,), (1,))) / sigma_two for t in range(9)
    ]
    wide = lax.broadcasted_iota(jnp.int32, (side, 1), 0)
    for n in range(images):
        for kind, kept in enumerate(((0, 1), (0, 1, 2), (1, 2))):
            across = [total([taps[3 * r + c][n : n + 1] for r in kept]) for c in range(3)]
            middle = across[0] + across[1] + across[2]
            pattern[n, kind] = jnp.where(
                wide == 0, across[0] + across[1],
                jnp.where(wide == side - 1, across[1] + across[2], middle),
            )

    loads[1].wait()
    loads[2].wait()
    mean_two, inverse_two = stats[3:4, :], stats[11:12, :]
    gain = norms[2:3, :]
    none = jnp.zeros((8, width), F32)
    sums = (none, none)
    for n in range(images):
        def step(h, carry):
            kind = jnp.where(h == 0, 0, jnp.where(h == side - 1, 2, 1))
            at = pl.ds(pl.multiple_of(n * cells + h * side, side), side)
            normed = (y[at, :] - mean_two) * inverse_two
            grad = d_pre[at, :] * pattern[n, kind]
            d_pre[at, :] = grad
            return carry[0] + fold(grad), carry[1] + fold(grad * normed)
        sums = lax.fori_loop(0, side, step, sums)
    one_a[...] = jnp.zeros(one_a.shape, F32)
    one_a[0:1, :] = jnp.sum(sums[0], axis=0, keepdims=True)
    one_a[1:2, :] = jnp.sum(sums[1], axis=0, keepdims=True)
    one_a[2:3, :] = total([
        cells * branch_pool[n] * d_two[n : n + 1, :].astype(F32) for n in range(images)
    ])
    ex_a[dp] = one_a[...]
    first = Spread("dp", n_dp, one_a, ex_a, a_send, a_recv)
    first.start()

    grads_out[...] = jnp.zeros(grads_out.shape, F32)
    over = hdot(weights, jnp.ones((8, 128), F32), ((0,), (0,)))[:, 0:1]
    g_z = zs * over - hdot(weights, xs, ((0,), (0,)))
    grads_out[0:size, :] = g_z[0:size]
    grads_out[20:21, :] = jnp.sum(g_x * xs, axis=0, keepdims=True)
    grads_out[23:24, :] = jnp.zeros((1, width), F32) + loss
    grads_out[32:64, 0 : classes * IND] = hdot(proj, g_spread, ((0,), (0,)))
    grads_out[32:64, 384 : 384 + IND] = hdot(g_kx, proj, ((0,), (0,)))
    grads_out[32:48, 512 : 512 + IND] = hdot(g_avg, proj, ((0,), (0,)))
    head_out[...] = jnp.zeros(head_out.shape, F32)
    head_out[0:8, :] = d_pooled
    head_out[18:19, :] = cells / pixels
    head_out[8:16, :] = d_two[0:8, :].astype(F32)
    for n in range(images):
        edge = jnp.zeros((1, side, 3 * width), BF16)
        cat[n, 0:1] = edge
        cat[n, side + 1 : side + 2] = edge

    def eighth(t, carry):
        at = pl.ds(pl.multiple_of(t * (width // 2), width // 2), width // 2)
        k8[at, :] = (k2[at, :].astype(F32) * KERNEL_SCALE).astype(F8)
        return carry

    lax.fori_loop(0, 9, eighth, 0)
    first.wait()
    one_b[...] = total([ex_a[i] for i in range(n_dp)])
    ex_b[rep] = one_b[...]
    second = Spread("replica", n_rep, one_b, ex_b, b_send, b_recv)
    second.start()
    lax.fori_loop(9, 18, eighth, 0)
    k8_copy = pltpu.make_async_copy(k8, k8_out, local.at[3 + images])
    k8_copy.start()
    second.wait()
    joined = total([ex_b[i] for i in range(n_rep)])
    d_bias, d_gain = joined[0:1, :], joined[1:2, :]
    head_out[16:17, :] = d_gain
    head_out[17:18, :] = d_bias
    head_out[19:20, :] = joined[2:3, :]
    true_scale = inverse_two * sigma_one * gain
    cat_copies = []
    for n in range(images):
        held = jnp.where(count > n, 1.0, 0.0)
        def step(i, carry):
            rows = BLOCK * side
            at = pl.ds(pl.multiple_of(n * cells + i * rows, rows), rows)
            normed = (y[at, :] - mean_two) * inverse_two
            grad = (true_scale * held) * (
                d_pre[at, :] - d_bias / pixels - normed * (d_gain / pixels)
            )
            grad = grad.astype(BF16).astype(F32)
            store_shifted(cat, n, i * BLOCK, BLOCK, grad, side)
            return carry
        lax.fori_loop(0, side // BLOCK, step, 0)
        copy = pltpu.make_async_copy(cat.at[n], cat_out.at[n], local.at[3 + n])
        copy.start()
        cat_copies.append(copy)
    for level in (first, second):
        level.drain()
    for copy in cat_copies + [k8_copy]:
        copy.wait()


def head(n_dp, n_rep, side, counts, labels, indices, table, k2, y, slope, windows, stem_pool, stats,
         norms, inducing, lengthscale, var_mean, var_lower):
    images, width = stem_pool.shape
    cells = side * side
    classes = var_mean.shape[0]
    shape = jax.ShapeDtypeStruct
    sem = pltpu.SemaphoreType.DMA
    return pl.pallas_call(
        functools.partial(head_kernel, n_dp, n_rep, side),
        out_shape=(
            shape((images, side + 2, side, 3 * width), BF16),
            shape(k2.shape, F8),
            shape((24, width), F32),
            shape((64, width), F32),
            shape((3, IND, IND), F32),
        ),
        in_specs=[SMEM, SMEM, SMEM, VMEM, ANY, ANY, ANY] + [VMEM] * 8,
        out_specs=(ANY, ANY, VMEM, VMEM, VMEM),
        scratch_shapes=[
            pltpu.VMEM(k2.shape, BF16),
            pltpu.VMEM(k2.shape, F8),
            pltpu.VMEM(y.shape, F32),
            pltpu.VMEM(y.shape, F32),
            pltpu.VMEM((images, side + 2, side, 3 * width), BF16),
            pltpu.VMEM((images, 3, side, width), F32),
            pltpu.VMEM((IND, width), F32),
            pltpu.VMEM((IND, IND), F32),
            pltpu.VMEM((16, IND), F32),
            pltpu.VMEM((IND, classes * IND), F32),
            pltpu.VMEM((8, width), F32),
            pltpu.VMEM((8, IND), F32),
            pltpu.VMEM((images, 16, 16), F32),
            pltpu.VMEM((16, width), BF16),
            pltpu.VMEM((n_dp, 4, width), F32),
            pltpu.VMEM((n_rep, 4, width), F32),
            pltpu.VMEM((4, width), F32),
            pltpu.VMEM((4, width), F32),
            sem((n_dp,)), sem((n_dp,)), sem((n_rep,)), sem((n_rep,)),
            sem((4 + images,)),
        ],
        compiler_params=pltpu.CompilerParams(
            collective_id=1, has_side_effects=True, vmem_limit_bytes=56 << 20
        ),
    )(counts, labels, indices, table, k2, y, slope, windows, stem_pool, stats, norms,
      inducing, lengthscale, var_mean, var_lower)


def greet_all(n_dp, n_rep):
    here = lax.axis_index("dp") * n_rep + lax.axis_index("replica")
    count = n_dp * n_rep
    barrier = pltpu.get_barrier_semaphore()

    def signal(j, carry):
        other = lax.rem(here + j, count)
        pl.semaphore_signal(
            barrier, inc=1, device_id={"dp": other // n_rep, "replica": lax.rem(other, n_rep)},
            device_id_type=MESH,
        )
        return carry

    lax.fori_loop(1, count, signal, 0)
    pl.semaphore_wait(barrier, count - 1)


def chunk_plan(share, width, count):
    def segments(first, last, base):
        result = []
        while first < last:
            c = (first - base) // width
            end = min(last, base + (c + 1) * width)
            result.append((c, first - base - c * width, end - base - c * width))
            first = end
        return result

    plan, done, carried = [], 0, 0
    for r in range(3):
        first, last = r * 3 * width, (r + 1) * 3 * width
        items = []
        while done < count and (done + 1) * share <= last:
            begin = max(done * share, first)
            items.append((done, carried, segments(begin, (done + 1) * share, first)))
            carried = 0
            done += 1
        begin = max(done * share, first)
        plan.append((items, segments(begin, last, first)))
        carried = last - begin
    return plan


def backward_kernel(
    n_dp, n_rep, side, share, fused,
    counts, cat_in, x_in, k1_in, k8_in, cat8_in, patches, stem, stats, norms, windows, head_rows, grads,
    part_out, big_out, sums_out, late_out,
    cat, x, k1, k8, cat8, held_rows, carry, mine, sib, rin, zin, zout, part, comb, wall, flat, flat_d,
    *rest,
):
    early = rest[0:11]
    late = rest[11:15]
    (c_send, c_recv, r_send, r_recv, z_send, z_recv, w_send, w_recv, local) = rest[15:]
    images = patches.shape[0]
    width = stem.shape[1]
    cells = side * side
    dp, rep = lax.axis_index("dp"), lax.axis_index("replica")
    core, z = lax.rem(dp, 2), dp // 2
    n_z, half = n_dp // 2, n_dp // 2
    sources = max(n_dp // 4, 1)
    owners = half * n_rep
    here = dp * n_rep + rep
    loads = [
        pltpu.make_async_copy(cat_in, cat, local.at[0]),
        pltpu.make_async_copy(x_in, x, local.at[1]),
        pltpu.make_async_copy(k1_in, k1, local.at[2]),
        pltpu.make_async_copy(k8_in, k8, local.at[3]),
        pltpu.make_async_copy(cat8_in.at[0], cat8, local.at[5]),
    ]
    for copy in loads:
        copy.start()
    greet_all(n_dp, n_rep)
    count = counts[0]
    valid = [jnp.where(count > n, 1.0, 0.0) for n in range(images)]

    early_sum = Reduce(("dp", n_dp), ("replica", n_rep), *early[:5], early[5:])
    source = early[0]
    source[...] = jnp.zeros(source.shape, F32)
    put_rows(source, 0, grads[...])
    gram = total([
        bdot(patches[n], patches[n], ((1,), (1,))) * valid[n] for n in range(images)
    ])
    wide = jnp.concatenate([gram, jnp.zeros((32, 128 - 32), F32)], axis=1)
    per = source.shape[1]
    for k in range(32):
        row = 64 + k
        source[row // per, row % per : row % per + 1, 0:128] = wide[k : k + 1, :]
    early_sum.start()

    if fused:
        for t in range(9):
            comb[t, 0:images, :] = jnp.concatenate(
                [windows[n, t : t + 1, :] for n in range(images)], axis=0
            )
            comb[t, images : 2 * images, :] = head_rows[8 : 8 + images, :]

        def first_tap(owner):
            return jnp.minimum((owner * share) // width, 7)

        def window_copy(owner):
            return remote(
                comb.at[pl.ds(first_tap(owner), 2)], wall.at[here], w_send.at[owner], w_recv.at[here],
                {"dp": half + owner // n_rep, "replica": lax.rem(owner, n_rep)},
            )

        def send_windows(j, c):
            owner = lax.rem(here + j, owners)

            @pl.when(half * n_rep + owner != here)
            def _():
                window_copy(owner).start()
            return c

        lax.fori_loop(0, owners, send_windows, 0)

    def row_of_taps(r):
        return total([
            lax.dot_general(
                x[n].reshape(cells, width),
                cat[n, pl.ds(2 - r, side)].reshape(cells, 3 * width),
                (((0,), (0,)), ((), ())),
                preferred_element_type=F32,
            )
            for n in range(images)
        ])

    def joined(acc, parts):
        pieces = [acc[a:b, (2 - c) * width : (3 - c) * width] for c, a, b in parts]
        return pieces[0] if len(pieces) == 1 else jnp.concatenate(pieces, axis=0)

    def sib_copy(o):
        return remote(
            mine.at[o], sib.at[(o // (2 * n_rep)) * n_rep + o % n_rep],
            c_send.at[o], c_recv.at[(o // (2 * n_rep)) * n_rep + o % n_rep],
            {"dp": dp + 1 - 2 * core},
        )

    def ship(acc, items, leftover):
        for o, carried, parts in items:
            value = joined(acc, parts)
            if carried:
                value = jnp.concatenate([carry[0:carried, :], value], axis=0)
            mine[o, 0:share, :] = value.astype(BF16)
            pl.when(core != (o // n_rep) % 2)(sib_copy(o).start)
        if leftover:
            value = joined(acc, leftover)
            carry[0 : value.shape[0], :] = value

    reps = (rep, rep + 1 - 2 * lax.rem(rep, 2), rep + 2 - 4 * (rep // 2), 3 - rep)
    cut = (share + 8) // 32 * 16
    halves = (pl.ds(0, cut), pl.ds(cut, share + 8 - cut))

    def slot(zi, k):
        return (zi * 2 + core) * n_rep + reps[k]

    def plane_copies(zi, step):
        for h in range(2):
            near, far = 1 + h, 2 - h
            at = halves[h]
            if step == 0:
                for s, k in enumerate((near, 3)):
                    yield remote(
                        mine.at[slot(zi, k), at, :], rin.at[zi, s, at, :],
                        r_send.at[zi, 2 * s + h], r_recv.at[zi, 2 * s + h], {"replica": reps[near]},
                    )
            else:
                yield remote(
                    mine.at[slot(zi, far), at, :], rin.at[zi, 2, at, :],
                    r_send.at[zi, 4 + h], r_recv.at[zi, 4 + h], {"replica": reps[far]},
                )

    def join_cores(zi):
        for k in (3, 1, 2, 0):
            at = zi * n_rep + reps[k]
            remote(
                mine.at[0], sib.at[at], c_send.at[0], c_recv.at[at], {"dp": dp + 1 - 2 * core}
            ).wait_recv()
            mine[slot(zi, k)] = (
                mine[slot(zi, k)].astype(F32) + sib[at].astype(F32)
            ).astype(BF16)
        for copy in plane_copies(zi, 0):
            copy.start()

    def join_near(zi):
        for copy in plane_copies(zi, 0):
            copy.wait_recv()
        for h in range(2):
            at, o = halves[h], slot(zi, 2 - h)
            mine[o, at, :] = (
                mine[o, at, :].astype(F32) + rin[zi, 1, at, :].astype(F32)
            ).astype(BF16)
        for copy in plane_copies(zi, 1):
            copy.start()

    def join_far(zi):
        for copy in plane_copies(zi, 1):
            copy.wait_recv()
        part[zi] = (
            mine[slot(zi, 0)].astype(F32) + rin[zi, 0].astype(F32) + rin[zi, 2].astype(F32)
        )

    z_pieces = ((0, 192), (192, share + 8 - 192)) if share > 200 else ((0, share + 8),)

    def z_copy(zi, piece, down):
        start, rows = z_pieces[piece]
        at = pl.ds(start, rows)
        step = n_dp - 2 if down else 2
        return remote(
            zout.at[zi, at, :], zin.at[zi, int(down), at, :],
            z_send.at[zi, piece], z_recv.at[zi, piece, int(down)],
            {"dp": lax.rem(dp + step, n_dp)},
        )

    def chain(zi, distance, pieces=(0, 1)):
        for down in (True, False):
            reach = n_z - 1 - zi if down else zi
            if distance > reach:
                continue
            offset = distance if down else -distance
            @pl.when(z == zi + offset)
            def _():
                for piece in pieces:
                    start, rows = z_pieces[piece]
                    at = pl.ds(start, rows)
                    if distance < reach:
                        z_copy(zi, piece, down).wait_recv()
                        part[zi, at, :] += zin[zi, int(down), at, :].astype(F32)
                    if distance:
                        zout[zi, at, :] = part[zi, at, :].astype(BF16)
                        z_copy(zi, piece, down).start()

    def window_part():
        @pl.when(dp >= half)
        def _():
            owner = here - owners
            wall[here] = comb[pl.ds(first_tap(owner), 2)]

            def take(j, c):
                origin = lax.rem(here + j, n_dp * n_rep)
                remote(
                    comb.at[pl.ds(0, 2)], wall.at[origin], w_send.at[0], w_recv.at[origin],
                    {"dp": origin // n_rep, "replica": lax.rem(origin, n_rep)},
                ).wait_recv()
                return c

            lax.fori_loop(1, n_dp * n_rep, take, 0)
            for s in range(n_dp * n_rep):
                for tap in range(2):
                    flat[tap, s * images : (s + 1) * images, :] = wall[s, tap, 0:images, :]
                flat_d[s * images : (s + 1) * images, :] = wall[s, 0, images : 2 * images, :]
            for tap in range(2):
                held_rows[tap * width : (tap + 1) * width, :] = hdot(
                    flat[tap], flat_d[...], ((0,), (0,))
                )
            offset = owner * share - first_tap(owner) * width
            part_out[...] = held_rows[pl.ds(pl.multiple_of(offset, 8), share), :]

    loads[0].wait()
    loads[1].wait()
    if fused:
        plan = chunk_plan(share, width, owners)
        for r in range(3):
            acc = row_of_taps(r)
            if r > 0:
                pl.when(core == r - 1)(lambda: join_cores(0))
            ship(acc, *plan[r])
            if r == 1:
                early_sum.middle()
    else:
        for r in range(3):
            acc = row_of_taps(r)
            for c in range(3):
                held_rows[0:width, :] = acc[:, (2 - c) * width : (3 - c) * width]
                out_copy = pltpu.make_async_copy(
                    held_rows.at[pl.ds(0, width), :],
                    part_out.at[pl.ds((3 * r + c) * width, width), :],
                    local.at[4],
                )
                out_copy.start()
                out_copy.wait()
        early_sum.middle()

    loads[2].wait()
    sigma = stats[4:5, :]
    mean_one, inverse_one, pixels = stats[0:1, :], stats[1:2, :], stats[2:3, :]
    gain, bias = norms[0:1, :], norms[1:2, :]
    none = jnp.zeros((8, width), F32)
    block_rows = 2 * BLOCK * side
    per_image = side // (2 * BLOCK)
    blocks = images * per_image

    def input_gradient(b):
        n, i = b // per_image, b % per_image
        acc = None
        for r in range(3):
            for c in range(3):
                t = 8 - (3 * r + c)
                lhs = cat[
                    n, pl.ds(i * 2 * BLOCK + r, 2 * BLOCK), :, c * width : (c + 1) * width
                ].reshape(block_rows, width)
                one = bdot(lhs, k1[t * width : (t + 1) * width, :], ((1,), (1,)))
                acc = one if acc is None else acc + one
        first = (b % 2) * width
        held_rows[first : first + block_rows, :] = acc

    def through_gelu(b, carried):
        n, i = b // per_image, b % per_image
        first = (b % 2) * width
        pixel = patches[n, :, i * block_rows : (i + 1) * block_rows]
        normed = (bdot(pixel, stem[...], ((0,), (0,))) - mean_one) * inverse_one
        grad = gelu_slope(normed * gain + bias) * held_rows[first : first + block_rows, :] * (
            valid[n] / sigma
        )
        down = (grad * (inverse_one * gain) + head_rows[n : n + 1, :] / cells).astype(BF16)
        return (
            carried[0] + fold(grad),
            carried[1] + fold(grad * normed),
            carried[2] + bdot(pixel, down),
        )

    sums = (none, none, jnp.zeros((32, width), F32))
    between = {
        0: [lambda: join_near(0), lambda: join_cores(1)],
        1: [lambda: join_far(0), lambda: chain(0, 3)],
        2: [lambda: chain(0, 2, (0,)), lambda: join_near(1)],
        3: [lambda: chain(0, 2, (1,)), lambda: chain(0, 1, (0,))],
        4: [lambda: join_far(1), lambda: chain(1, 2)],
    }
    for b in range(blocks + 1):
        if b < blocks:
            input_gradient(b)
        if b > 0:
            sums = through_gelu(b - 1, sums)
        if fused:
            for event in between.get(b, ()):
                event()
    late_sum = Reduce(
        ("dp", n_dp), ("replica", n_rep), late[0], late[1], late_out, None, None, late[2:]
    )
    late[0][...] = jnp.zeros(late[0].shape, F32)
    put_rows(late[0], 0, sums[2][0:27])
    put_rows(late[0], 27, jnp.sum(sums[0], axis=0, keepdims=True))
    put_rows(late[0], 28, jnp.sum(sums[1], axis=0, keepdims=True))
    late_sum.start()
    early_sum.last()

    squares = none
    between = {
        0: [lambda: chain(0, 1, (1,)), lambda: chain(1, 1, (0,)), window_part],
        1: [lambda: chain(1, 1, (1,)), lambda: chain(0, 0, (0,))],
        2: [lambda: chain(1, 0, (0,)), lambda: chain(0, 0, (1,))],
        3: [lambda: chain(1, 0, (1,))],
    }
    for b in range(blocks):
        n, i = b // per_image, b % per_image
        if b == 0:
            loads[3].wait()
            loads[4].wait()
        elif i == 0:
            copy = pltpu.make_async_copy(cat8_in.at[n], cat8, local.at[5])
            copy.start()
            copy.wait()
        acc = None
        for r in range(3):
            lhs = cat8[pl.ds(i * 2 * BLOCK + r, 2 * BLOCK)].reshape(block_rows, 3 * width)
            one = bdot(lhs, k8[r * 3 * width : (r + 1) * 3 * width, :])
            acc = one if acc is None else acc + one
        squares = squares + valid[n] * fold(acc * acc)
        if fused:
            for event in between.get(b, ()):
                event()
    sigma_two = stats[5:6, :] * (ACT_SCALE * KERNEL_SCALE)
    sums_out[...] = jnp.zeros(sums_out.shape, F32)
    sums_out[0:1, :] = jnp.sum(squares, axis=0, keepdims=True) / (sigma_two * sigma_two)

    if fused:
        @pl.when(dp < half)
        def _():
            for zi in range(sources):
                @pl.when(z == zi)
                def _():
                    part_out[...] = part[zi, 0:share, :]

        def drain_windows(j, c):
            owner = lax.rem(here + j, owners)

            @pl.when(half * n_rep + owner != here)
            def _():
                window_copy(owner).wait_send()
            return c

        lax.fori_loop(0, owners, drain_windows, 0)
        for o in range(owners):
            pl.when(core != (o // n_rep) % 2)(sib_copy(o).wait_send)
        for zi in range(sources):
            for step in range(2):
                for copy in plane_copies(zi, step):
                    copy.wait_send()
            for piece in range(len(z_pieces)):
                pl.when(z > zi)(z_copy(zi, piece, True).wait_send)
                pl.when(z < zi)(z_copy(zi, piece, False).wait_send)
    early_sum.finish()
    late_sum.arrive()
    late_sum.drain()
    per = early[4].shape[1]
    for s in range(n_dp):
        for j in range(per):
            big_out[s * per + j : s * per + j + 1, :] = early[4][s, j : j + 1, :]


def backward(n_dp, n_rep, side, share, fused, counts, cat, x, k1, k8, cat8, patches, stem, stats, norms,
             windows, head_rows, grads):
    images, width = patches.shape[0], stem.shape[1]
    half = n_dp // 2
    sources = max(n_dp // 4, 1)
    owners = half * n_rep
    devices = n_dp * n_rep
    shape = jax.ShapeDtypeStruct
    sem = pltpu.SemaphoreType.DMA
    rows = share + 8
    small = (1, 8, 128)
    early = reduce_scratch(n_dp, n_rep, 96, width)
    early_rows = early[0].shape[0] * early[0].shape[1]
    part_rows = share if fused else 9 * width
    pieces = 2 if share > 200 else 1
    return pl.pallas_call(
        functools.partial(backward_kernel, n_dp, n_rep, side, share, fused),
        out_shape=(
            shape((part_rows, width), F32),
            shape((early_rows, width), F32),
            shape((8, width), F32),
            shape((-(-32 // n_dp), width), F32),
        ),
        in_specs=[SMEM] + [ANY] * 5 + [VMEM] * 7,
        out_specs=(VMEM if fused else ANY, VMEM, VMEM, VMEM),
        scratch_shapes=[
            pltpu.VMEM(cat.shape, BF16),
            pltpu.VMEM(x.shape, BF16),
            pltpu.VMEM(k1.shape, BF16),
            pltpu.VMEM(k8.shape, F8),
            pltpu.VMEM(cat8.shape[1:], F8),
            pltpu.VMEM((2 * width, width), F32),
            pltpu.VMEM((rows if fused else 8, width), F32),
            pltpu.VMEM((owners, rows, width) if fused else small, BF16),
            pltpu.VMEM((sources * n_rep, rows, width) if fused else small, BF16),
            pltpu.VMEM((sources, 3, rows, width) if fused else small, BF16),
            pltpu.VMEM((sources, 2, rows, width) if fused else small, BF16),
            pltpu.VMEM((sources, rows, width) if fused else small, BF16),
            pltpu.VMEM((sources, rows, width) if fused else small, F32),
            pltpu.VMEM((10, 2 * images, width) if fused else small, F32),
            pltpu.VMEM((devices, 2, 2 * images, width) if fused else small, F32),
            pltpu.VMEM((2, devices * images, width) if fused else small, F32),
            pltpu.VMEM((devices * images, width) if fused else small[1:], F32),
            *early,
            pltpu.VMEM((n_dp, -(-32 // n_dp), width), F32),
            pltpu.VMEM((n_dp, -(-32 // n_dp), width), F32),
            sem((n_dp,)), sem((n_dp,)),
            sem((owners,)), sem((sources * n_rep,)),
            sem((sources, 6)), sem((sources, 6)),
            sem((sources, pieces)), sem((sources, pieces, 2)),
            sem((owners,)), sem((devices,)),
            sem((6,)),
        ],
        compiler_params=pltpu.CompilerParams(
            collective_id=2, has_side_effects=True, vmem_limit_bytes=62 << 20
        ),
    )(counts, cat, x, k1, k8, cat8, patches, stem, stats, norms, windows, head_rows, grads)


def whole_sum(values):
    return jnp.sum(jnp.sum(values, axis=1, keepdims=True), axis=0, keepdims=True)


def lamb_step(weight, gradient, first, second, out, rows=False):
    new_one, new_two, direction = lamb_moments(weight, gradient, first, second)
    if rows:
        sizes = [jnp.sum(v * v, axis=1, keepdims=True) for v in (weight, direction)]
    else:
        sizes = [whole_sum(v * v) for v in (weight, direction)]
    new_weight = weight - RATE * (jnp.sqrt(sizes[0]) / jnp.sqrt(sizes[1])) * direction
    for ref, value in zip(out, (new_weight, new_one, new_two)):
        ref[...] = value.reshape(ref.shape)


def conv_kernel(kernel_of, part, conv_w, conv_m, conv_s, start, sums, head_rows, stats, norm_w,
                conv_one, conv_two, conv_step, tally, flat, own):
    width = stats.shape[1]
    share = part.shape[0]
    lanes = width // 128
    first = kernel_of[0] == 0
    def pick(row):
        return jnp.where(first, stats[row : row + 1, :], stats[row + 1 : row + 2, :])
    sigma, norm, unit = pick(4)[:, 0:1], pick(6)[:, 0:1], pick(8)
    inverse = stats[11:12, :] * stats[4:5, :]
    along = jnp.where(
        first,
        norm_w[2:3, :] * head_rows[16:17, :] * (EPS_NORM * inverse * inverse),
        head_rows[19:20, :],
    )
    d_sigma = -jnp.sum(along, axis=1, keepdims=True) / sigma
    vector = jnp.where(first, start[0:1, :], start[1:2, :])
    for k in range(lanes):
        own[:, k * 128 : (k + 1) * 128] = (
            conv_w[pl.ds(k, share, stride=lanes), :].astype(BF16).astype(F32)
        )
    rows = own[...]
    left = jnp.sum(rows * vector, axis=1, keepdims=True) / norm
    back = jnp.sum(rows * (unit / norm), axis=1, keepdims=True) - left * (sigma / norm)
    grad = part[...] / sigma + (left * d_sigma) * unit + (back * d_sigma) * vector
    for k in range(lanes):
        flat[pl.ds(k, share, stride=lanes), :] = grad[:, k * 128 : (k + 1) * 128]
    weight = conv_w[...]
    new_one, new_two, direction = lamb_moments(weight, flat[...], conv_m[...], conv_s[...])
    conv_one[...] = new_one
    conv_two[...] = new_two
    conv_step[...] = direction
    tally[...] = jnp.zeros(tally.shape, F32)
    tally[0:1, :] = jnp.sum(weight * weight, axis=0, keepdims=True)
    tally[1:2, :] = jnp.sum(direction * direction, axis=0, keepdims=True)
    tally[2:3, :] = total([sums[0:1, k * 128 : (k + 1) * 128] for k in range(lanes)])


def small_kernel(
    conv_ratio, conv_w, conv_step, big, late, joined, head_rows, stats, chol, stem_w, stem_m, stem_s,
    norm_w, norm_m, norm_s, ind_w, ind_m, ind_s, len_w, len_m, len_s,
    mean_w, mean_m, mean_s, low_w, low_m, low_s, *rest,
):
    outs = rest[2:20]
    parts_out, sigmas_out, rms_out, z_pad, stem_pad = rest[20:]
    new_conv = conv_w[...] - conv_ratio[0] * conv_step[...]
    rest[0][...] = new_conv
    rest[1][...] = new_conv.astype(BF16)
    width = stem_w.shape[1]
    size, classes = ind_w.shape[0], mean_w.shape[0]
    pixels = stats[2:3, :]
    mean_one, inverse_one = stats[0:1, :], stats[1:2, :]
    scale = head_rows[18:19, 0:1]
    parts_out[1] = jnp.sum(1.0 / scale)
    sigmas_out[0] = jnp.sum(stats[4:5, 0:1])
    sigmas_out[1] = jnp.sum(stats[5:6, 0:1])
    cells_all = pixels[:, 0:1] * width
    rms_out[0] = jnp.sum(
        jnp.sqrt(jnp.sum(stats[10:11, :], axis=1, keepdims=True) / cells_all)
    )
    rms_out[1] = jnp.sum(jnp.sqrt(joined[4:5, 0:1] / cells_all))

    gram = big[64:96, 0:32]
    patch_sums = gram[:, 31:32]
    stem_pad[...] = jnp.zeros(stem_pad.shape, F32)
    stem_pad[0 : stem_w.shape[0], :] = stem_w[...].astype(BF16).astype(F32)
    weights = stem_pad[...]
    centred = inverse_one * (hdot(gram, weights) - patch_sums * mean_one)
    d_bias, d_gain = late[27:28, :], late[28:29, :]
    stem_grad = late[0:32, :] - (inverse_one * norm_w[0:1, :] / pixels) * (
        patch_sums * d_bias + centred * d_gain
    )
    lamb_step(stem_w[...], stem_grad[0 : stem_w.shape[0]], stem_m[...], stem_s[...], outs[0:3])
    norm_grad = jnp.concatenate([d_gain, d_bias, head_rows[16:18, :]], axis=0)
    lamb_step(norm_w[...], norm_grad, norm_m[...], norm_s[...], outs[3:6], rows=True)

    ell = len_w[...].reshape(1, width)
    z_pad[...] = jnp.zeros(z_pad.shape, F32)
    z_pad[0:size, :] = ind_w[...] / ell
    zs = z_pad[...]
    kzz, factor, inverse = chol[0], chol[1], chol[2]
    line = lax.broadcasted_iota(jnp.int32, (IND, IND), 0)
    lane = lax.broadcasted_iota(jnp.int32, (IND, IND), 1)
    g_chol = jnp.where(line >= lane, -big[32:64, 384 : 384 + IND], 0.0)
    lower = hdot(factor, g_chol, ((0,), (0,)))
    phi = jnp.where(line > lane, lower, jnp.where(line == lane, 0.5 * lower, 0.0))
    back = hdot(inverse, hdot(phi, inverse), ((0,), (0,)))
    back_t = hdot(inverse, hdot(phi, inverse, ((0,), (0,))), ((0,), (0,)))
    weights_z = -0.5 * kzz * (back + back_t)
    g_z = big[0:32, :]
    g_z = jnp.where(lax.broadcasted_iota(jnp.int32, (IND, 1), 0) < size, g_z, 0.0) + 2.0 * (
        zs * jnp.sum(weights_z, axis=1, keepdims=True) - hdot(weights_z, zs)
    )
    lamb_step(ind_w[...], (g_z / ell)[0:size], ind_m[...], ind_s[...], outs[6:9])
    g_len = -(big[20:21, :] + jnp.sum(g_z * zs, axis=0, keepdims=True)) / ell
    lamb_step(ell, g_len, len_m[...].reshape(1, width), len_s[...].reshape(1, width), outs[9:12])

    means = mean_w[...]
    g_mean = big[32 : 32 + classes, 512 : 512 + size] + means * scale
    lamb_step(means, g_mean, mean_m[...], mean_s[...], outs[12:15])
    small_line = lax.broadcasted_iota(jnp.int32, (size, size), 0)
    small_lane = lax.broadcasted_iota(jnp.int32, (size, size), 1)
    kl = 0.5 * jnp.sum(means * means, axis=0, keepdims=True)
    weight_sq = jnp.zeros((1, size), F32)
    step_sq = weight_sq
    steps = []
    for c in range(classes):
        weight = low_w[c]
        factors = scale_rows(weight)
        inner = big[32 : 32 + size, c * IND : c * IND + size] + factors * scale
        grad = jnp.where(
            small_line > small_lane, inner,
            jnp.where(small_line == small_lane, factors * inner - scale, 0.0),
        )
        new_one, new_two, direction = lamb_moments(weight, grad, low_m[c], low_s[c])
        outs[16][c] = new_one
        outs[17][c] = new_two
        weight_sq = weight_sq + jnp.sum(weight * weight, axis=0, keepdims=True)
        step_sq = step_sq + jnp.sum(direction * direction, axis=0, keepdims=True)
        diagonal = jnp.where(small_line == small_lane, weight, 0.0)
        kl = kl + jnp.sum(0.5 * factors * factors - diagonal, axis=0, keepdims=True)
        steps.append(direction)
    ratio = RATE * jnp.sqrt(jnp.sum(weight_sq, axis=1, keepdims=True)) / jnp.sqrt(
        jnp.sum(step_sq, axis=1, keepdims=True)
    )
    for c in range(classes):
        outs[15][c] = low_w[c] - ratio * steps[c]
    kl = jnp.sum(kl, axis=1, keepdims=True) - 0.5 * classes * size
    parts_out[0] = jnp.sum(big[23:24, 0:1] + kl)


def staged(body, n_in, n_out, n_first, n_last, *refs):
    first, refs = refs[:n_first], refs[n_first:]
    ins, refs = refs[:n_in], refs[n_in:]
    outs, refs = refs[:n_out], refs[n_out:]
    last, refs = refs[:n_last], refs[n_last:]
    held, refs = refs[:n_in], refs[n_in:]
    made, refs = refs[:n_out], refs[n_out:]
    scratch, (sem_in, sem_out) = refs[:-2], refs[-2:]
    loads = [
        pltpu.make_async_copy(ref, held[i], sem_in.at[i]) for i, ref in enumerate(ins)
    ]
    for copy in loads:
        copy.start()
    for copy in loads:
        copy.wait()
    body(*first, *held, *made, *last, *scratch)
    stores = [
        pltpu.make_async_copy(made[i], ref, sem_out.at[i]) for i, ref in enumerate(outs)
    ]
    for copy in stores:
        copy.start()
    for copy in stores:
        copy.wait()


def local_call(body, first, ins, outs, last, scratch):
    sem = pltpu.SemaphoreType.DMA
    return pl.pallas_call(
        functools.partial(staged, body, len(ins), len(outs), len(first), len(last)),
        out_shape=tuple(outs) + tuple(last),
        in_specs=[SMEM] * len(first) + [ANY] * len(ins),
        out_specs=(ANY,) * len(outs) + (SMEM,) * len(last),
        scratch_shapes=[
            *[pltpu.VMEM(a.shape, a.dtype) for a in ins],
            *[pltpu.VMEM(o.shape, o.dtype) for o in outs],
            *scratch,
            sem((len(ins),)),
            sem((len(outs),)),
        ],
        compiler_params=pltpu.CompilerParams(vmem_limit_bytes=60 << 20),
    )(*first, *ins)


def update_conv(kernel_of, *ins):
    shape = jax.ShapeDtypeStruct
    part, conv = ins[0], ins[1]
    outs = [shape(conv.shape, F32)] * 3 + [shape((8, 128), F32)]
    return local_call(
        conv_kernel, [kernel_of], ins, outs, [],
        [pltpu.VMEM(conv.shape, F32), pltpu.VMEM(part.shape, F32)],
    )


def update_small(ratio, *ins):
    shape = jax.ShapeDtypeStruct
    conv, params = ins[0], ins[8:26:3]
    width = params[0].shape[1]
    outs = [shape(conv.shape, F32), shape(conv.shape, BF16)]
    outs += [shape(p.shape, F32) for p in params for _ in range(3)]
    return local_call(
        small_kernel, [ratio], ins, outs, [shape((2,), F32)] * 3,
        [pltpu.VMEM((IND, width), F32), pltpu.VMEM((32, width), F32)],
    )


def tally_kernel(n_dp, n_rep, tally, late, out, ratio, late_out, ex_a, ex_b, one_b,
                 a_send, a_recv, b_send, b_recv, *scratch):
    half = n_dp // 2
    dp, rep = lax.axis_index("dp"), lax.axis_index("replica")
    greeted = greet(n_dp, n_rep)
    planes, made = scratch[:2]
    late_sum = Reduce(
        ("dp", n_dp), ("replica", n_rep), None, None, late, planes, made, scratch[2:4] + scratch[2:]
    )
    ex_a[dp] = tally[...]
    first = Spread("dp", n_dp, tally, ex_a, a_send, a_recv)
    greeted()
    first.start()
    late_sum.across()
    first.wait()
    one_b[...] = jnp.zeros(one_b.shape, F32)
    for l in range(2):
        near = range(l * half, (l + 1) * half)
        one_b[l : l + 1, :] = total([ex_a[i, 0:1, :] for i in near])
        one_b[2 + l : 3 + l, :] = total([ex_a[i, 1:2, :] for i in near])
    one_b[4:5, :] = total(rows_of(ex_a, 2))
    ex_b[rep] = one_b[...]
    second = Spread("replica", n_rep, one_b, ex_b, b_send, b_recv)
    second.start()
    late_sum.last()
    second.wait()
    joined = jnp.sum(total([ex_b[i] for i in range(n_rep)]), axis=1, keepdims=True)
    out[...] = jnp.zeros(out.shape, F32) + joined
    trust = jnp.sqrt(joined[0:2]) / jnp.sqrt(joined[2:4])
    ratio[0] = RATE * jnp.sum(jnp.where(dp < half, trust[0:1], trust[1:2]))
    first.drain()
    second.drain()
    late_sum.finish_last()
    per = made.shape[1]
    for k in range(32):
        late_out[k : k + 1, :] = made[k // per, k % per : k % per + 1, :]


def join_tally(n_dp, n_rep, tally, late):
    sem = pltpu.SemaphoreType.DMA
    shape = jax.ShapeDtypeStruct
    return pl.pallas_call(
        functools.partial(tally_kernel, n_dp, n_rep),
        out_shape=(shape((8, 128), F32), shape((1,), F32), shape((32, late.shape[1]), F32)),
        in_specs=[VMEM, VMEM],
        out_specs=(VMEM, SMEM, VMEM),
        scratch_shapes=[
            pltpu.VMEM((n_dp, 8, 128), F32),
            pltpu.VMEM((n_rep, 8, 128), F32),
            pltpu.VMEM((8, 128), F32),
            sem((n_dp,)), sem((n_dp,)), sem((n_rep,)), sem((n_rep,)),
            pltpu.VMEM((n_rep, *late.shape), F32),
            pltpu.VMEM((n_dp, *late.shape), F32),
            sem((n_rep,)), sem((n_rep,)), sem((n_dp,)), sem((n_dp,)),
        ],
        compiler_params=pltpu.CompilerParams(collective_id=3, has_side_effects=True),
    )(tally, late)


def on_device(
    images, labels, counts, noise_table, noise_index, power_start,
    conv_weight, conv_first, conv_second,
    stem_weight, stem_first, stem_second,
    norm_params, norm_first, norm_second,
    inducing, inducing_first, inducing_second,
    lengthscale, length_first, length_second,
    var_mean, mean_first, mean_second,
    var_lower, lower_first, lower_second,
):
    width = stem_weight.shape[1]
    side = images.shape[2]
    cells = side * side
    n_dp, n_rep = lax.axis_size("dp"), lax.axis_size("replica")
    here = lax.axis_index(AXES)
    per_kernel = n_dp * n_rep // 2
    owner = here // per_kernel
    select = (jnp.arange(2) == owner).astype(F32)
    geometry = (n_dp, n_rep, side)

    share = conv_weight.shape[0] // width
    wide = (-1, 128)
    fused = share % 16 == 8 and n_rep == 4 and n_dp == 8
    if fused:
        weights, extra = conv_weight.reshape(wide), power_start
    else:
        rows = conv_weight.astype(BF16).reshape(-1, width)
        gathered = lax.all_gather(rows, AXES, axis=0, tiled=True)
        weights = gathered[: 9 * width]
        own = rows.astype(F32)
        start = jnp.sum(select[:, None] * power_start, axis=0)
        own_along = jnp.sum(own * start, axis=1)
        back_rows = jnp.sum(own * own_along[:, None], axis=0)
        extra = jnp.stack([back_rows, jnp.full((width,), jnp.sum(own_along * own_along))])
    pictures = images.astype(F32).reshape(images.shape[0], images.shape[1], cells)
    k_one, k_two, act_one, raw_one, slope, cat8, windows, stem_pool, stats, patches, stem_kernel = forward(
        *geometry, share, fused, counts, weights, pictures, stem_weight, extra, norm_params
    )
    if not fused:
        k_two = gathered[9 * width :]
    cat, k8, head_rows, grads, chol = head(
        *geometry, counts, labels, noise_index, noise_table.T, k_two, raw_one, slope, windows, stem_pool,
        stats, norm_params, inducing, lengthscale, var_mean, var_lower,
    )
    part, big, sums, late = backward(
        *geometry, share, fused, counts, cat, act_one, k_one, k8, cat8, patches, stem_kernel, stats, norm_params, windows,
        head_rows, grads,
    )
    if not fused:
        part_one = lax.psum_scatter(
            jnp.concatenate([part.reshape(-1), jnp.zeros((part.size,), F32)]),
            AXES, scatter_dimension=0, tiled=True,
        ).reshape(-1, width)
        all_windows, all_grads = lax.all_gather(
            (windows[:, :9], head_rows[8 : 8 + images.shape[0]]), AXES, tiled=True
        )
        all_windows = all_windows.reshape(all_windows.shape[0], -1)
        mine = lax.dynamic_slice_in_dim(
            all_windows, lax.rem(here, per_kernel) * share, share, axis=1
        )
        part = jnp.where(owner == 0, part_one, jnp.dot(mine.T, all_grads, precision=HIGH))

    new_one, new_two, direction, tally = update_conv(
        owner.astype(jnp.int32)[None], part, conv_weight.reshape(wide),
        conv_first.reshape(wide), conv_second.reshape(wide), power_start,
        sums, head_rows, stats, norm_params,
    )
    joined, ratio, late = join_tally(n_dp, n_rep, tally, late)
    small = update_small(
        ratio, conv_weight.reshape(wide), direction, big, late, joined, head_rows, stats, chol,
        stem_weight, stem_first, stem_second, norm_params, norm_first, norm_second,
        inducing, inducing_first, inducing_second, lengthscale, length_first, length_second,
        var_mean, mean_first, mean_second, var_lower, lower_first, lower_second,
    )
    loss_parts, sigmas, rms = small[20:]
    flat = [v.reshape(-1) for v in (small[0], new_one, new_two, small[1])]
    return (loss_parts, *flat, *small[2:20], sigmas, rms)


def solution(mesh):
    split = P(AXES)
    return jax.shard_map(
        on_device,
        mesh=mesh,
        in_specs=(split, split, split, P(), split, P(), split, split, split) + (P(),) * 18,
        out_specs=(P(),) + (split,) * 4 + (P(),) * 20,
        check_vma=False,
    )
```

```python
import functools

import jax
import jax.numpy as jnp
from jax import lax
from jax.experimental import pallas as pl
from jax.experimental.pallas import tpu as pltpu
from jax.sharding import PartitionSpec as P

STEP = 10
HIGH = lax.Precision.HIGHEST
EPS_NORM = 1e-05
JITTER = 0.001
BETA_ONE = 0.9
BETA_TWO = 0.999
RATE = 0.3
DECAY = 0.01
EPS_ADAM = 1e-08
AXES = ("dp", "replica")


def lamb_moments(weight, gradient, moment_one, moment_two):
    new_one = BETA_ONE * moment_one + (1.0 - BETA_ONE) * gradient
    new_two = BETA_TWO * moment_two + (1.0 - BETA_TWO) * gradient * gradient
    direction = (
        new_one / (1.0 - BETA_ONE**STEP) / (jnp.sqrt(new_two / (1.0 - BETA_TWO**STEP)) + EPS_ADAM)
        + DECAY * weight
    )
    return (new_one, new_two, direction)


MESH = pl.DeviceIdType.MESH
ANY = pl.BlockSpec(memory_space=pl.ANY)
VMEM = pl.BlockSpec(memory_space=pltpu.VMEM)
SMEM = pl.BlockSpec(memory_space=pltpu.SMEM)
F32 = jnp.float32
BF16 = jnp.bfloat16
F8 = jnp.float8_e4m3fn
ACT_SCALE = 0.25
KERNEL_SCALE = 2048.0


def remote(src, dst, send, recv, where):
    return pltpu.make_async_remote_copy(
        src_ref=src, dst_ref=dst, send_sem=send, recv_sem=recv,
        device_id=where, device_id_type=MESH,
    )


def greet(n_dp, n_rep):
    dp, rep = lax.axis_index("dp"), lax.axis_index("replica")
    barrier = pltpu.get_barrier_semaphore()
    for j in range(1, n_dp):
        pl.semaphore_signal(
            barrier, inc=1, device_id={"dp": lax.rem(dp + j, n_dp)}, device_id_type=MESH
        )
    for j in range(1, n_rep):
        pl.semaphore_signal(
            barrier, inc=1, device_id={"replica": lax.rem(rep + j, n_rep)}, device_id_type=MESH
        )
    return lambda: pl.semaphore_wait(barrier, n_dp + n_rep - 2)


class Spread:
    def __init__(self, axis, size, src, dst, send, recv):
        self.axis, self.size, self.src, self.dst, self.send, self.recv = axis, size, src, dst, send, recv
        self.me = lax.axis_index(axis)

    def copies(self):
        for j in range(1, self.size):
            yield remote(
                self.src, self.dst.at[self.me], self.send.at[j], self.recv.at[j],
                {self.axis: lax.rem(self.me + j, self.size)},
            )

    def start(self):
        for copy in self.copies():
            copy.start()

    def wait(self):
        for j in range(1, self.size):
            source = lax.rem(self.me + self.size - j, self.size)
            remote(
                self.src, self.dst.at[source], self.send.at[j], self.recv.at[j],
                {self.axis: source},
            ).wait_recv()

    def drain(self):
        for copy in self.copies():
            copy.wait_send()


def rows_of(refs, row):
    return [refs[i, row : row + 1, :] for i in range(refs.shape[0])]


def total(values):
    result = values[0]
    for value in values[1:]:
        result = result + value
    return result


def join_moments(refs):
    averages, squares, counts = rows_of(refs, 0), rows_of(refs, 1), rows_of(refs, 2)
    count = total(counts)
    average = total([a * n for a, n in zip(averages, counts)]) / count
    spread = total(
        [s + n * (a - average) * (a - average) for a, s, n in zip(averages, squares, counts)]
    )
    return average, spread, count


def hdot(a, b, dims=((1,), (0,))):
    return lax.dot_general(
        a, b, (dims, ((), ())), precision=HIGH, preferred_element_type=F32
    )


def bdot(a, b, dims=((1,), (0,))):
    return lax.dot_general(a, b, (dims, ((), ())), preferred_element_type=F32)


class Gather:
    def __init__(self, which, n_dp, share, buffer, sems):
        self.which, self.n_dp, self.share, self.buffer = which, n_dp, share, buffer
        tiles = (share - 8) // 16
        edges = [tiles * i // PIECES * 16 for i in range(PIECES + 1)]
        self.pieces = list(zip(edges, [hi - lo for lo, hi in zip(edges, edges[1:])]))
        self.z_send, self.z_recv, self.r_send, self.r_recv, self.c_send, self.c_recv = [
            s.at[which] for s in sems
        ]
        self.dp, rep = lax.axis_index("dp"), lax.axis_index("replica")
        self.reps = (rep, rep + 1 - 2 * lax.rem(rep, 2), rep + 2 - 4 * (rep // 2), 3 - rep)
        self.core, self.z = lax.rem(self.dp, 2), self.dp // 2
        self.n_z = n_dp // 2
        self.sources = n_dp // 4
        self.order = range(self.sources) if which else range(self.sources - 1, -1, -1)

    def first(self, zi, core, k):
        owner = (zi * 2 + core) * 4 + self.reps[k]
        return (owner // 2) * (2 * self.share) + lax.rem(owner, 2) * (self.share + 8)

    def each(self, zi, core, k, piece, act):
        start, rows = self.pieces[piece]
        begin = pl.multiple_of(self.first(zi, core, k) + start, 16)
        if piece < len(self.pieces) - 1:
            act(self.buffer.at[pl.ds(begin, rows), :])
            return
        even = lax.rem(self.reps[k], 2) == 0
        pl.when(even)(lambda: act(self.buffer.at[pl.ds(begin, rows + 16), :]))
        pl.when(~even)(lambda: act(self.buffer.at[pl.ds(begin, rows), :]))

    def source(self, zi):
        return zi + self.which * self.sources

    def along(self, zi, piece, what, ways=(0, 1)):
        def act(ref):
            for way in ways:
                condition = (
                    ((self.z <= self.source(zi)) & (self.z > 0)) if way
                    else ((self.z >= self.source(zi)) & (self.z < self.n_z - 1))
                )
                step = self.n_dp - 2 if way else 2
                copy = remote(
                    ref, ref, self.z_send.at[zi, piece, way], self.z_recv.at[zi, piece],
                    {"dp": lax.rem(self.dp + step, self.n_dp)},
                )
                if what == "wait_recv":
                    copy.wait_recv()
                    return
                pl.when(condition)(getattr(copy, what))
        self.each(zi, self.core, 0, piece, act)

    def goes_on(self, zi):
        gap = self.z - self.source(zi)
        return ((gap < 0) & (self.z > 0)) | ((gap > 0) & (self.z < self.n_z - 1))

    def near(self, zi, piece, k, what):
        def act(ref):
            getattr(remote(
                ref, ref, self.r_send.at[zi, piece, k], self.r_recv.at[zi, piece, k],
                {"replica": self.reps[k]},
            ), what)()
        self.each(zi, self.core, k if what == "wait_recv" else 0, piece, act)

    def passed(self, zi, piece, what):
        k = 1 + piece % 2
        def act(ref):
            getattr(remote(
                ref, ref, self.r_send.at[zi, piece, 3], self.r_recv.at[zi, piece, 3],
                {"replica": self.reps[3 - k]},
            ), what)()
        self.each(zi, self.core, 3 if what == "wait_recv" else k, piece, act)

    def over(self, zi, piece, k, what):
        def act(ref):
            getattr(remote(
                ref, ref, self.c_send.at[zi, piece, k], self.c_recv.at[zi, piece, k],
                {"dp": self.dp + 1 - 2 * self.core},
            ), what)()
        self.each(zi, 1 - self.core if what == "wait_recv" else self.core, k, piece, act)

    def send_plane(self, zi, piece):
        for k in (1, 2):
            self.near(zi, piece, k, "start")
        self.over(zi, piece, 0, "start")

    def own(self, pieces, ways, plane):
        for zi in range(self.sources):
            @pl.when(self.z == self.source(zi))
            def _():
                for piece in pieces:
                    self.along(zi, piece, "start", ways)
                    if plane:
                        self.send_plane(zi, piece)

    def column(self, zi, pieces):
        @pl.when(self.z != self.source(zi))
        def _():
            for piece in pieces:
                self.along(zi, piece, "wait_recv")
                self.along(zi, piece, "start")
                self.send_plane(zi, piece)

    def hop(self, distance):
        for zi in self.order:
            gap = self.z - self.source(zi)
            @pl.when(self.goes_on(zi) & ((gap == distance) | (gap == -distance)))
            def _():
                for piece in range(len(self.pieces)):
                    self.along(zi, piece, "wait_recv")
                    self.along(zi, piece, "start")

    def plane(self, zi, condition, sent=0):
        @pl.when(condition)
        def _():
            for piece in range(len(self.pieces)):
                pl.when((self.z != self.source(zi)) & ~self.goes_on(zi))(
                    functools.partial(self.along, zi, piece, "wait_recv")
                )
                if piece < sent:
                    pl.when(self.z != self.source(zi))(
                        functools.partial(self.send_plane, zi, piece)
                    )
                else:
                    self.send_plane(zi, piece)

    def neighbours(self, zi, pieces):
        for piece in pieces:
            for k in (1, 2):
                self.near(zi, piece, k, "wait_recv")
                if k == 1 + piece % 2:
                    self.passed(zi, piece, "start")
                self.over(zi, piece, k, "start")

    def opposite(self, zi):
        for piece in range(len(self.pieces)):
            self.passed(zi, piece, "wait_recv")
            self.over(zi, piece, 3, "start")

    def from_core(self, zi):
        for piece in range(len(self.pieces)):
            for k in range(4):
                self.over(zi, piece, k, "wait_recv")

    def drain(self):
        for piece in range(len(self.pieces)):
            for zi in range(self.sources):
                self.along(zi, piece, "wait_send")
                for k in (1, 2):
                    self.near(zi, piece, k, "wait_send")
                self.passed(zi, piece, "wait_send")
                for k in range(4):
                    self.over(zi, piece, k, "wait_send")


PIECES = 4


def pixel_column(rows, side):
    return lax.rem(lax.broadcasted_iota(jnp.int32, (rows, 1), 0), side)


def store_shifted(ref, image, first, block, values, side):
    width = values.shape[1]
    rows = block * side
    column = pixel_column(rows, side)
    left = jnp.where(column == 0, 0.0, pltpu.roll(values, 1, 0))
    right = jnp.where(column == side - 1, 0.0, pltpu.roll(values, rows - 1, 0))
    for c, moved in enumerate((left, values, right)):
        ref[image, pl.ds(first + 1, block), :, c * width : (c + 1) * width] = (
            moved.astype(ref.dtype).reshape(block, side, width)
        )


def gelu_both(x):
    c = 0.7978845608028654
    square = x * x
    th = jnp.tanh(c * x * (1.0 + 0.044715 * square))
    half = 0.5 * (1.0 + th)
    return x * half, half + 0.5 * x * (1.0 - th * th) * (c * (1.0 + 3 * 0.044715 * square))


def window_matrix(side):
    shape = (side * side, 16)
    pixel = lax.broadcasted_iota(jnp.int32, shape, 0)
    tap = lax.broadcasted_iota(jnp.int32, shape, 1)
    r, c = tap // 3, lax.rem(tap, 3)
    h, w = pixel // side, lax.rem(pixel, side)
    keep = (
        (tap < 9)
        & ~((r == 0) & (h == side - 1)) & ~((r == 2) & (h == 0))
        & ~((c == 0) & (w == side - 1)) & ~((c == 2) & (w == 0))
    )
    return jnp.where(keep, 1.0, 0.0).astype(BF16)


BLOCK = 8


def make_patches(images, side, patches, line):
    cells = side * side
    pixel = lax.broadcasted_iota(jnp.int32, (1, cells), 1)
    h, w = pixel // side, lax.rem(pixel, side)
    colours = images.shape[1]
    for n in range(images.shape[0]):
        line[...] = jnp.where(
            lax.broadcasted_iota(jnp.int32, line.shape, 0) == 31, 1.0, 0.0
        )
        values = images[n]
        for t in range(9):
            down, right = t // 3 - 1, t % 3 - 1
            shift = down * side + right
            moved = pltpu.roll(values, (-shift) % cells, 1) if shift else values
            inside = (h + down >= 0) & (h + down < side) & (w + right >= 0) & (w + right < side)
            line[colours * t : colours * (t + 1), :] = jnp.where(inside, moved, 0.0)
        patches[n] = line[...].astype(BF16)


IND = 32


def cholesky_steps(matrix, size):
    lane = lax.broadcasted_iota(jnp.int32, (size, IND), 1)
    line = lax.broadcasted_iota(jnp.int32, (size, IND), 0)
    left = matrix
    right = jnp.where(lane == line, 1.0, 0.0)
    factor = jnp.zeros((size, IND), F32)
    row_of = lax.broadcasted_iota(jnp.int32, (size, 1), 0)
    for k in range(size):
        inverse = lax.rsqrt(left[k : k + 1, k : k + 1])
        column = jnp.where(row_of >= k, left[:, k : k + 1] * inverse, 0.0)
        below = jnp.where(row_of > k, column, 0.0)
        row = left[k : k + 1, :] * inverse
        other = right[k : k + 1, :] * inverse
        factor = jnp.where(lane == k, column, factor)
        left = left - below * row
        right = jnp.where(line == k, other, right - below * other)
    return factor, right


def scale_rows(lower):
    size = lower.shape[0]
    line = lax.broadcasted_iota(jnp.int32, (size, size), 0)
    lane = lax.broadcasted_iota(jnp.int32, (size, size), 1)
    return jnp.where(line > lane, lower, jnp.where(line == lane, jnp.exp(lower), 0.0))


def prepare_head(indices, table, inducing, lengthscale, var_mean, var_lower, chol_out, z_pad, v_pad, f_pad, noise):
    size, width = inducing.shape
    classes = var_mean.shape[0]
    images, samples = indices.shape
    ell = lengthscale[...].reshape(1, width)
    z_pad[...] = jnp.zeros(z_pad.shape, F32)
    z_pad[0:size, :] = inducing[...] / ell
    zs = z_pad[...]
    lane = lax.broadcasted_iota(jnp.int32, (size, IND), 1)
    line = lax.broadcasted_iota(jnp.int32, (size, IND), 0)
    kzz = jnp.zeros((size, IND), F32)
    for m in range(size):
        off = zs[0:size, :] - zs[m : m + 1, :]
        kzz = jnp.where(lane == m, jnp.exp(-0.5 * jnp.sum(off * off, axis=1, keepdims=True)), kzz)
    factor, inverse = cholesky_steps(jnp.where(lane == line, kzz + JITTER, kzz), size)
    chol_out[...] = jnp.zeros(chol_out.shape, F32)
    chol_out[0, 0:size, :] = kzz
    chol_out[1, 0:size, :] = factor
    chol_out[2, 0:size, :] = inverse
    v_pad[...] = jnp.zeros(v_pad.shape, F32)
    v_pad[0:classes, 0:size] = var_mean[...]
    f_pad[...] = jnp.zeros(f_pad.shape, F32)
    for c in range(classes):
        f_pad[0:size, c * IND : c * IND + size] = scale_rows(var_lower[c])
    noise[...] = jnp.zeros(noise.shape, F32)
    table_lane = lax.broadcasted_iota(jnp.int32, (1, table.shape[1]), 1)
    for n in range(images):
        chosen = [jnp.where(table_lane == indices[n, s], 1.0, 0.0) for s in range(samples)]
        chosen.append(jnp.zeros((16 - samples, table.shape[1]), F32))
        noise[n, :, 0:classes] = hdot(jnp.concatenate(chosen, axis=0), table[...], ((1,), (1,)))


def forward_kernel(
    n_dp, n_rep, side, share, fused,
    counts, indices, weights, pictures, stem_in, start, norms, table, inducing, lengthscale, var_mean, var_lower,
    k1_out, k2_out, x_out, y_out, slope_out, act_out, windows, stem_pool, stats, patches, stem,
    chol_out, z_pad, v_pad, f_pad, noise,
    line, own_f32, main, bound, k1, xcat, y, act, slope, seam, ex_a, ex_b, one_a, one_b, tw_a, tw_b, tw_one,
    z_send, z_recv, r_send, r_recv, c_send, c_recv,
    a_send, a_recv, b_send, b_recv, s_send, s_recv, local, turn,
):
    images = pictures.shape[0]
    width = stem_in.shape[1]
    cells = side * side
    dp, rep = lax.axis_index("dp"), lax.axis_index("replica")
    half = n_dp // 2
    greeted = greet(n_dp, n_rep)

    if fused:
        rows = share - 8
        sems = (z_send, z_recv, r_send, r_recv, c_send, c_recv)
        one, two = [
            Gather(l, n_dp, share, buffer, sems) for l, buffer in enumerate((k1, k2_out))
        ]
        every = range(PIECES)
        early, final = every[:-1], every[-1:]
        even = lax.rem(rep, 2) == 0
        owner = lax.rem(dp, half) * n_rep + rep
        own_first = (owner // 2) * (2 * share) + lax.rem(owner, 2) * (share + 8)
        seam_copy = remote(
            bound, seam.at[1], s_send.at[0], s_recv.at[0],
            {"replica": rep + 1 - 2 * lax.rem(rep, 2)},
        )

        def own_copies(what):
            for l, buffer in enumerate((k1, k2_out)):
                @pl.when((dp < half) if l == 0 else (dp >= half))
                def _():
                    at = pl.ds(pl.multiple_of(own_first, 16), rows)
                    getattr(pltpu.make_async_copy(main, buffer.at[at, :], local.at[0]), what)()

        def put_seam():
            @pl.when(even)
            def _():
                seam_copy.wait_recv()
                seam[0] = (bound[...].astype(F32) + seam[1].astype(F32)).astype(BF16)
                for l, buffer in enumerate((k1, k2_out)):
                    @pl.when((dp < half) if l == 0 else (dp >= half))
                    def _():
                        at = pl.ds(pl.multiple_of(own_first + rows, 16), 16)
                        copy = pltpu.make_async_copy(seam.at[0], buffer.at[at, :], local.at[10])
                        copy.start()
                        copy.wait()

        lanes = width // 128
        for k in range(lanes):
            own_f32[:, k * 128 : (k + 1) * 128] = weights[pl.ds(k, share, stride=lanes), :]
        blank = jnp.zeros((8, width), F32)
        head_rows, tail_rows = own_f32[0:8, :], own_f32[share - 8 : share, :]
        main[...] = jnp.where(even, own_f32[0:rows, :], own_f32[8:share, :]).astype(BF16)
        bound[...] = jnp.where(
            even,
            jnp.concatenate([tail_rows, blank], axis=0),
            jnp.concatenate([blank, head_rows], axis=0),
        ).astype(BF16)
        own_copies("start")
    else:
        copy_in = pltpu.make_async_copy(weights, k1, local.at[0])
        copy_in.start()

    if fused:
        own_copies("wait")
    greeted()
    if fused:
        pl.when(~even)(seam_copy.start)
        one.own(every[:2], (0, 1), True)
        two.own(every[:2], (1,), True)
    line[:, 0:width] = jnp.zeros((32, width), F32)
    line[0 : stem_in.shape[0], 0:width] = stem_in[...]
    stem[...] = line[:, 0:width].astype(BF16)
    weight = stem[...].astype(F32)
    count = counts[0]
    valid = [jnp.where(count > n, 1.0, 0.0) for n in range(images)]
    held = count.astype(F32) * cells
    make_patches(pictures, side, patches, line)
    grams, sums = [], []
    for n in range(images):
        grams.append(bdot(patches[n], patches[n], ((1,), (1,))))
        sums.append(grams[n][24:32])
        stem_pool[n : n + 1, :] = hdot(sums[n], weight)[7:8] * (1.0 / cells)
    gram = total([g * v for g, v in zip(grams, valid)])
    summed = total([s * v for s, v in zip(sums, valid)])
    square = jnp.sum(weight * hdot(gram, weight), axis=0, keepdims=True)
    last = jnp.where(lax.broadcasted_iota(jnp.int32, summed.shape, 0) == 7, summed, 0.0)
    cover = gram - hdot(last, last, ((0,), (0,))) / held
    zero = jnp.zeros((1, width), F32)
    payload = one_a.at[0]
    payload[...] = jnp.zeros(payload.shape, F32)
    payload[0:1, :] = hdot(summed, weight)[7:8] / held
    payload[1:2, :] = jnp.sum(weight * hdot(cover, weight), axis=0, keepdims=True)
    payload[2:3, :] = zero + held
    payload[5:6, :] = square

    if fused:
        vector = jnp.where(dp < half, start[0:1, :], start[1:2, :])
        own_rows = main[...].astype(F32)
        edge_rows = bound[...].astype(F32)
        along = jnp.sum(own_rows * vector, axis=1, keepdims=True)
        edge_along = jnp.sum(edge_rows * vector, axis=1, keepdims=True)
        payload[3:4, :] = jnp.sum(own_rows * along, axis=0, keepdims=True) + jnp.sum(
            edge_rows * edge_along, axis=0, keepdims=True
        )
        payload[4:5, :] = zero + (
            jnp.sum(along * along, axis=0, keepdims=True)
            + jnp.sum(edge_along * edge_along, axis=0, keepdims=True)
        )
    else:
        payload[3:4, :] = start[0:1, :]
        payload[4:5, :] = start[1:2, :]

    first = ex_a.at[0]
    first[dp] = payload[...]
    one_level = Spread("dp", n_dp, payload, first, a_send.at[0], a_recv.at[0])
    one_level.start()
    if fused:
        one.own(early[2:], (0, 1), True)
        two.own(early[2:], (1,), False)
        put_seam()
        one.own(final, (0, 1), True)
        two.own(final, (1,), False)
    for n in range(images):
        blank = jnp.zeros((1, side, 3 * width), BF16)
        xcat[n, 0:1] = blank
        xcat[n, side + 1 : side + 2] = blank
    if fused:
        one.column(1, every)
    one_level.wait()
    second = ex_b.at[0]
    mean, spread, cell_count = join_moments(first)
    passed = one_b.at[0]
    passed[...] = jnp.zeros(passed.shape, F32)
    passed[0:1, :] = mean
    passed[1:2, :] = spread
    passed[2:3, :] = cell_count
    vectors, squares = rows_of(first, 3), rows_of(first, 4)
    passed[3:4, :] = total(vectors[:half])
    passed[4:5, :] = total(vectors[half:])
    passed[5:6, :] = total(squares[:half])
    passed[6:7, :] = total(squares[half:])
    passed[7:8, :] = total(rows_of(first, 5))
    second[rep] = passed[...]
    two_level = Spread("replica", n_rep, passed, second, b_send.at[0], b_recv.at[0])
    two_level.start()
    if fused:
        one.neighbours(1, every[:2])
        one.column(0, every[:2])
        one.neighbours(1, every[2:])
        one.column(0, every[2:])
        two.own(every, (0,), False)
        two.hop(1)
    prepare_head(
        indices, table, inducing, lengthscale, var_mean, var_lower, chol_out, z_pad, v_pad, f_pad, noise
    )
    two_level.wait()
    mean, spread, pixels = join_moments(second)
    inverse_one = lax.rsqrt(spread / pixels + EPS_NORM)
    joined = [total(rows_of(second, row)) for row in range(3, 8)]
    sigma_rows, start_rows = [], []
    for l in range(2):
        vec = jnp.sqrt(jnp.sum(joined[l] * joined[l], axis=1, keepdims=True))
        base = jnp.sqrt(joined[2 + l])
        sigma_rows.append(zero + vec / base)
        start_rows.append(base)
        stats[8 + l : 9 + l, :] = joined[l] / vec
    stats[0:1, :] = mean
    stats[1:2, :] = inverse_one
    stats[2:3, :] = pixels
    stats[4:5, :] = sigma_rows[0]
    stats[5:6, :] = sigma_rows[1]
    stats[6:7, :] = start_rows[0]
    stats[7:8, :] = start_rows[1]
    stats[10:11, :] = joined[4]
    scale_one = inverse_one * norms[0:1, :]
    shift_one = norms[1:2, :] - mean * scale_one

    def act_one(n, part):
        def step(i, carry):
            first_row = i * BLOCK
            pixel = pl.ds(pl.multiple_of(first_row * side, BLOCK * side), BLOCK * side)
            out = bdot(patches[n, :, pixel], stem[...], ((0,), (0,)))
            values = jax.nn.gelu(out * scale_one + shift_one)
            store_shifted(xcat, n, first_row, BLOCK, values, side)
            return carry
        half_steps = side // BLOCK // 2
        lax.fori_loop(part * half_steps, (part + 1) * half_steps, step, 0)

    for n in range(images):
        for part in range(2):
            act_one(n, part)
        if fused and n == 0:
            one.neighbours(0, every[:2])
    if fused:
        one.opposite(1)
        one.from_core(1)
    else:
        copy_in.wait()
    x_copies = [
        pltpu.make_async_copy(
            xcat.at[n, pl.ds(1, side), :, pl.ds(width, width)], x_out.at[n], local.at[2 + n]
        )
        for n in range(images)
    ]
    for copy in x_copies:
        copy.start()

    tap_row = 3 * width
    middle = -(-(9 * width // 2 - tap_row) // 128) * 128
    rows_step = 2 * BLOCK * side

    def window(n, i, r, lanes):
        return xcat[n, pl.ds(i * 2 * BLOCK + r, 2 * BLOCK), :, lanes].reshape(rows_step, -1)

    def at_rows(n, i):
        return pl.ds(pl.multiple_of(n * cells + i * rows_step, rows_step), rows_step)

    for n in range(images):
        def later_half(i, carry):
            y[at_rows(n, i), :] = bdot(
                window(n, i, 2, slice(0, tap_row)), k1[2 * tap_row : 3 * tap_row, :]
            ) + bdot(
                window(n, i, 1, slice(middle, tap_row)), k1[tap_row + middle : 2 * tap_row, :]
            )
            return carry
        lax.fori_loop(0, side // (2 * BLOCK), later_half, 0)
        if fused and n == 0:
            one.neighbours(0, every[2:])
            two.hop(2)
            two.plane(0, two.z >= 0, 2)
            two.plane(1, two.z > 0, 2)
    if fused:
        one.opposite(0)
        one.from_core(0)
    k1_copies = [
        pltpu.make_async_copy(
            k1.at[pl.ds((8 - t) * width, width), :],
            k1_out.at[t // 3, :, pl.ds((t % 3) * width, width)],
            turn.at[t],
        )
        for t in range(9)
    ]
    for copy in k1_copies:
        copy.start()
    moments = []
    y_copies = []
    for n in range(images):
        def first_half(i, carry):
            acc = (
                y[at_rows(n, i), :]
                + bdot(window(n, i, 0, slice(0, tap_row)), k1[0:tap_row, :])
                + bdot(window(n, i, 1, slice(0, middle)), k1[tap_row : tap_row + middle, :])
            )
            y[at_rows(n, i), :] = acc
            return carry + jnp.sum(acc, axis=0, keepdims=True)
        whole = lax.fori_loop(0, side // (2 * BLOCK), first_half, zero)
        if fused and n == 0:
            two.plane(1, two.z == 0, 2)
        average = whole / cells
        def spread_step(i, carry):
            pixel = pl.ds(pl.multiple_of(n * cells + i * BLOCK * side, 16), BLOCK * side)
            off = y[pixel, :] - average
            return carry + jnp.sum(off * off, axis=0, keepdims=True)
        moments.append((average, lax.fori_loop(0, side // BLOCK, spread_step, zero)))
        copy = pltpu.make_async_copy(
            y.at[pl.ds(n * cells, cells), :], y_out.at[pl.ds(n * cells, cells), :], local.at[4 + n]
        )
        copy.start()
        y_copies.append(copy)
    payload_two = tw_one.at[0]
    counts_in = [v * cells for v in valid]
    average = total([m[0] * c for m, c in zip(moments, counts_in)]) / held
    payload_two[...] = jnp.zeros(payload_two.shape, F32)
    payload_two[0:1, :] = average
    payload_two[1:2, :] = total([
        v * m[1] + c * (m[0] - average) * (m[0] - average)
        for m, c, v in zip(moments, counts_in, valid)
    ])
    payload_two[2:3, :] = zero + held
    first = tw_a
    first[dp] = payload_two[...]
    three_level = Spread("dp", n_dp, payload_two, first, a_send.at[1], a_recv.at[1])
    three_level.start()
    if fused:
        two.neighbours(0, every)
    three_level.wait()
    mean, spread, cell_count = join_moments(first)
    second = tw_b
    passed = tw_one.at[1]
    passed[...] = jnp.zeros(passed.shape, F32)
    passed[0:1, :] = mean
    passed[1:2, :] = spread
    passed[2:3, :] = cell_count
    second[rep] = passed[...]
    four_level = Spread("replica", n_rep, passed, second, b_send.at[1], b_recv.at[1])
    four_level.start()
    if fused:
        two.neighbours(1, every[:2])
    four_level.wait()
    mean, spread, _ = join_moments(second)
    sigma = sigma_rows[0]
    variance = spread / pixels / (sigma * sigma)
    inverse_two = lax.rsqrt(variance + EPS_NORM) / sigma
    stats[3:4, :] = mean
    stats[11:12, :] = inverse_two
    scale_two = inverse_two * norms[2:3, :]
    shift_two = norms[3:4, :] - mean * scale_two
    select = window_matrix(side)
    act_copies = []
    for n in range(images):
        def step(i, carry):
            pixel = pl.ds(pl.multiple_of(n * cells + i * BLOCK * side, 16), BLOCK * side)
            values, steep = gelu_both(y[pixel, :] * scale_two + shift_two)
            slope[pixel, :] = steep
            act[pixel, :] = values.astype(BF16)
            return carry
        lax.fori_loop(0, side // BLOCK, step, 0)
        pixels_of = pl.ds(n * cells, cells)
        for k, (made, out) in enumerate((
            (slope.at[pixels_of, :], slope_out.at[pixels_of, :]),
            (act.at[pixels_of, :], act_out.at[pixels_of, :]),
        )):
            copy = pltpu.make_async_copy(made, out, local.at[6 + 2 * k + n])
            copy.start()
            act_copies.append(copy)
        windows[n] = bdot(select, act[n * cells : (n + 1) * cells, :], ((0,), (0,)))
        if fused and n == 0:
            two.neighbours(1, every[2:])
            two.opposite(two.order[0])
    if fused:
        two.opposite(two.order[1])
        for zi in two.order:
            two.from_core(zi)
        one.drain()
        two.drain()
        pl.when(~even)(seam_copy.wait_send)
    for level in (one_level, two_level, three_level, four_level):
        level.drain()
    for copy in k1_copies + x_copies + y_copies + act_copies:
        copy.wait()


def forward(n_dp, n_rep, side, share, fused, counts, indices, weights, pictures, stem, start, norms,
            table, inducing, lengthscale, var_mean, var_lower):
    images, cells = pictures.shape[0], side * side
    width = stem.shape[1]
    half = n_dp // 2
    sources = max(n_dp // 4, 1)
    shape = jax.ShapeDtypeStruct
    sem = pltpu.SemaphoreType.DMA
    kernel_rows = 9 * width
    return pl.pallas_call(
        functools.partial(forward_kernel, n_dp, n_rep, side, share, fused),
        out_shape=(
            shape((3, width, 3 * width), BF16),
            shape((kernel_rows, width), BF16),
            shape((images, side, side, width), BF16),
            shape((images * cells, width), F32),
            shape((images * cells, width), F32),
            shape((images * cells, width), BF16),
            shape((images, 16, width), F32),
            shape((images, width), F32),
            shape((16, width), F32),
            shape((images, 32, cells), BF16),
            shape((32, width), BF16),
            shape((3, IND, IND), F32),
            shape((IND, width), F32),
            shape((16, IND), F32),
            shape((IND, var_mean.shape[0] * IND), F32),
            shape((images, 16, 16), F32),
        ),
        in_specs=[SMEM, SMEM, VMEM if fused else ANY] + [VMEM] * 9,
        out_specs=(ANY,) * 6 + (VMEM,) * 10,
        scratch_shapes=[
            pltpu.VMEM((32, cells), F32),
            pltpu.VMEM((share if fused else 8, width), F32),
            pltpu.VMEM((share - 8 if fused else 16, width), BF16),
            pltpu.VMEM((16, width), BF16),
            pltpu.VMEM((kernel_rows, width), BF16),
            pltpu.VMEM((images, side + 2, side, 3 * width), BF16),
            pltpu.VMEM((images * cells, width), F32),
            pltpu.VMEM((images * cells, width), BF16),
            pltpu.VMEM((images * cells, width), F32),
            pltpu.VMEM((2, 16, width), BF16),
            pltpu.VMEM((1, n_dp, 8, width), F32),
            pltpu.VMEM((1, n_rep, 8, width), F32),
            pltpu.VMEM((1, 8, width), F32),
            pltpu.VMEM((1, 8, width), F32),
            pltpu.VMEM((n_dp, 4, width), F32),
            pltpu.VMEM((n_rep, 4, width), F32),
            pltpu.VMEM((2, 4, width), F32),
            sem((2, sources, PIECES, 2)),
            sem((2, sources, PIECES)),
            sem((2, sources, PIECES, 4)),
            sem((2, sources, PIECES, 4)),
            sem((2, sources, PIECES, 4)),
            sem((2, sources, PIECES, 4)),
            sem((2, n_dp)),
            sem((2, n_dp)),
            sem((2, n_rep)),
            sem((2, n_rep)),
            sem((1,)),
            sem((1,)),
            sem((11,)),
            sem((9,)),
        ],
        compiler_params=pltpu.CompilerParams(
            collective_id=0, has_side_effects=True, vmem_limit_bytes=56 << 20
        ),
    )(counts, indices, weights, pictures, stem, start, norms,
      table, inducing, lengthscale, var_mean, var_lower)


class Reduce:
    def __init__(self, near, far, src, parts, whole, planes, out, sems):
        (self.axis, self.size), (self.other, self.others) = near, far
        self.src, self.parts, self.whole, self.planes, self.out = src, parts, whole, planes, out
        self.a_send, self.a_recv = sems[:2]
        self.b_send, self.b_recv, self.c_send, self.c_recv = sems[2:] or [None] * 4
        self.me = lax.axis_index(self.axis)

    def scatter(self):
        for j in range(1, self.size):
            peer = lax.rem(self.me + j, self.size)
            yield remote(
                self.src.at[peer], self.parts.at[self.me], self.a_send.at[j], self.a_recv.at[j],
                {self.axis: peer},
            )

    def start(self):
        for copy in self.scatter():
            copy.start()
        self.parts[self.me] = self.src[self.me]

    def arrive(self):
        for j in range(1, self.size):
            source = lax.rem(self.me + self.size - j, self.size)
            remote(
                self.src.at[source], self.parts.at[source], self.a_send.at[j], self.a_recv.at[j],
                {self.axis: source},
            ).wait_recv()
        self.whole[...] = total([self.parts[i] for i in range(self.size)])

    def middle(self):
        self.arrive()
        self.across()

    def across(self):
        self.planes[lax.axis_index(self.other)] = self.whole[...]
        self.second = Spread(
            self.other, self.others, self.whole, self.planes, self.b_send, self.b_recv
        )
        self.second.start()

    def last(self):
        self.second.wait()
        self.out[self.me] = total([self.planes[i] for i in range(self.others)])
        self.third = Spread(
            self.axis, self.size, self.out.at[self.me], self.out, self.c_send, self.c_recv
        )
        self.third.start()

    def finish(self):
        self.finish_last()
        self.drain()

    def drain(self):
        for copy in self.scatter():
            copy.wait_send()

    def finish_last(self):
        self.third.wait()
        self.second.drain()
        self.third.drain()


def reduce_scratch(size, others, rows, width):
    per = -(-rows // size)
    sem = pltpu.SemaphoreType.DMA
    return [
        pltpu.VMEM((size, per, width), F32),
        pltpu.VMEM((size, per, width), F32),
        pltpu.VMEM((per, width), F32),
        pltpu.VMEM((others, per, width), F32),
        pltpu.VMEM((size, per, width), F32),
        sem((size,)), sem((size,)), sem((others,)), sem((others,)), sem((size,)), sem((size,)),
    ]


def put_rows(ref, first, values):
    per = ref.shape[1]
    for k in range(values.shape[0]):
        row = first + k
        ref[row // per, row % per : row % per + 1, :] = values[k : k + 1, :]


def gelu_slope(x):
    return gelu_both(x)[1]


def fold(values):
    return jnp.sum(values.reshape(values.shape[0] // 8, 8, values.shape[1]), axis=0)


def head_kernel(
    n_dp, n_rep, side, size, classes, samples,
    counts, labels, k2_in, y_in, slope_in, windows, stem_pool, stats, norms,
    lengthscale, chol, z_pad, v_pad, f_pad, noise,
    cat_out, k8_out, head_out, grads_out,
    k2, k8, y, d_pre, cat, pattern, x_pad, kx_pad, d_rows,
    ex_a, ex_b, one_a, one_b, a_send, a_recv, b_send, b_recv, local,
):
    images = stem_pool.shape[0]
    width = stem_pool.shape[1]
    cells = side * side
    dp, rep = lax.axis_index("dp"), lax.axis_index("replica")
    loads = [
        pltpu.make_async_copy(k2_in, k2, local.at[0]),
        pltpu.make_async_copy(y_in, y, local.at[1]),
        pltpu.make_async_copy(slope_in, d_pre, local.at[2]),
    ]
    for copy in loads:
        copy.start()
    greet(n_dp, n_rep)()

    sigma_one, sigma_two = stats[4:5, :], stats[5:6, :]
    pixels = stats[2:3, :]
    scale = cells / stats[2:3, 0:1]
    ell = lengthscale[...].reshape(1, width)
    zs = z_pad[...]
    ones = jnp.ones((8, width), F32)
    group = lax.broadcasted_iota(jnp.int32, (classes * IND, 16), 0) // IND
    which = lax.broadcasted_iota(jnp.int32, (classes * IND, 16), 1)
    groups = jnp.where(group == which, 1.0, 0.0)

    loads[0].wait()
    pooled_raw = jnp.zeros((16, width), F32)
    for t in range(9):
        parts = []
        rest = [windows[n, t : t + 1, :] for n in range(images)]
        for _ in range(3):
            parts += [r.astype(BF16).astype(F32) for r in rest]
            rest = [r - p for r, p in zip(rest, parts[-images:])]
        parts.append(jnp.zeros((16 - 3 * images, width), F32))
        lhs = jnp.concatenate(parts, axis=0).astype(BF16)
        pooled_raw = pooled_raw + bdot(lhs, k2[t * width : (t + 1) * width, :])
    x_pad[...] = jnp.zeros(x_pad.shape, F32)
    branch_pool = []
    for n in range(images):
        row = total([pooled_raw[k * images + n : k * images + n + 1] for k in range(3)])
        branch_pool.append(row / (cells * sigma_two))
        x_pad[n : n + 1, :] = (stem_pool[n : n + 1, :] + branch_pool[n]) / ell
    xs = x_pad[...]

    kx_pad[...] = jnp.zeros(kx_pad.shape, F32)
    for n in range(images):
        off = zs - xs[n : n + 1, :]
        kx_pad[n : n + 1, :] = jnp.exp(-0.5 * hdot(ones, off * off, ((1,), (1,))))[0:1]
    lanes = lax.broadcasted_iota(jnp.int32, (8, IND), 1)
    kx = jnp.where(lanes < size, kx_pad[...], 0.0)
    inv = chol[2]
    means = v_pad[...]
    factors = f_pad[...]
    proj = hdot(kx, inv, ((1,), (1,)))
    average = hdot(proj, means, ((1,), (1,)))
    spread = hdot(proj, factors)
    variance = (
        1.0 - jnp.sum(proj * proj, axis=1, keepdims=True) + hdot(spread * spread, groups)
    )
    std = jnp.sqrt(variance)
    class_lane = lax.broadcasted_iota(jnp.int32, (1, 16), 1)
    sample_row = lax.broadcasted_iota(jnp.int32, (16, 16), 0)
    inside = (lax.broadcasted_iota(jnp.int32, (16, 16), 1) < classes) & (sample_row < samples)
    count = counts[0]
    loss = jnp.zeros((1, 1), F32)
    g_avg_rows, g_var_rows = [], []
    for n in range(images):
        drawn = average[n : n + 1, :] + std[n : n + 1, :] * noise[n]
        drawn = jnp.where(inside, drawn, -1e30)
        shifted = drawn - jnp.max(drawn, axis=1, keepdims=True)
        exps = jnp.where(inside, jnp.exp(shifted), 0.0)
        sums = jnp.sum(exps, axis=1, keepdims=True)
        sums = jnp.where(sample_row[:, 0:1] < samples, sums, 1.0)
        hot = jnp.where(class_lane == labels[n], 1.0, 0.0)
        picked = jnp.where(inside, (shifted - jnp.log(sums)) * hot, 0.0)
        held = jnp.where(count > n, 1.0 / samples, 0.0)
        loss = loss - held * jnp.sum(jnp.sum(picked, axis=1, keepdims=True), axis=0, keepdims=True)
        g_samples = jnp.where(inside, exps / sums - hot, 0.0) * (held * scale)
        g_avg_rows.append(jnp.sum(g_samples, axis=0, keepdims=True))
        g_var_rows.append(
            0.5 * jnp.sum(g_samples * noise[n], axis=0, keepdims=True) / std[n : n + 1, :]
        )
    blank = [jnp.zeros((8 - images, 16), F32)]
    g_avg = jnp.concatenate(g_avg_rows + blank, axis=0)
    g_var = jnp.concatenate(g_var_rows + blank, axis=0)
    g_spread = 2.0 * spread * hdot(g_var, groups, ((1,), (1,)))
    g_proj = (
        hdot(g_avg, means)
        - 2.0 * proj * jnp.sum(g_var, axis=1, keepdims=True)
        + hdot(g_spread, factors, ((1,), (1,)))
    )
    g_kx = hdot(g_proj, inv)
    weights = -kx * g_kx
    g_x = xs * jnp.sum(weights, axis=1, keepdims=True) - hdot(weights, zs)
    d_pooled = g_x / ell
    d_rows[...] = jnp.zeros(d_rows.shape, BF16)
    d_rows[0:8, :] = (d_pooled / cells).astype(BF16)
    d_two = d_rows[...]

    taps = [
        bdot(d_two, k2[t * width : (t + 1) * width, :], ((1,), (1,))) / sigma_two for t in range(9)
    ]
    wide = lax.broadcasted_iota(jnp.int32, (side, 1), 0)
    for n in range(images):
        for kind, kept in enumerate(((0, 1), (0, 1, 2), (1, 2))):
            across = [total([taps[3 * r + c][n : n + 1] for r in kept]) for c in range(3)]
            middle = across[0] + across[1] + across[2]
            pattern[n, kind] = jnp.where(
                wide == 0, across[0] + across[1],
                jnp.where(wide == side - 1, across[1] + across[2], middle),
            )

    loads[1].wait()
    loads[2].wait()
    mean_two, inverse_two = stats[3:4, :], stats[11:12, :]
    gain = norms[2:3, :]
    none = jnp.zeros((8, width), F32)
    sums = (none, none)
    for n in range(images):
        def step(h, carry):
            kind = jnp.where(h == 0, 0, jnp.where(h == side - 1, 2, 1))
            at = pl.ds(pl.multiple_of(n * cells + h * side, side), side)
            normed = (y[at, :] - mean_two) * inverse_two
            grad = d_pre[at, :] * pattern[n, kind]
            d_pre[at, :] = grad
            return carry[0] + fold(grad), carry[1] + fold(grad * normed)
        sums = lax.fori_loop(0, side, step, sums)
    one_a[...] = jnp.zeros(one_a.shape, F32)
    one_a[0:1, :] = jnp.sum(sums[0], axis=0, keepdims=True)
    one_a[1:2, :] = jnp.sum(sums[1], axis=0, keepdims=True)
    one_a[2:3, :] = total([
        cells * branch_pool[n] * d_two[n : n + 1, :].astype(F32) for n in range(images)
    ])
    ex_a[dp] = one_a[...]
    first = Spread("dp", n_dp, one_a, ex_a, a_send, a_recv)
    first.start()

    grads_out[...] = jnp.zeros(grads_out.shape, F32)
    over = hdot(weights, jnp.ones((8, 128), F32), ((0,), (0,)))[:, 0:1]
    g_z = zs * over - hdot(weights, xs, ((0,), (0,)))
    grads_out[0:size, :] = g_z[0:size]
    grads_out[20:21, :] = jnp.sum(g_x * xs, axis=0, keepdims=True)
    grads_out[23:24, :] = jnp.zeros((1, width), F32) + loss
    grads_out[32:64, 0 : classes * IND] = hdot(proj, g_spread, ((0,), (0,)))
    grads_out[32:64, 384 : 384 + IND] = hdot(g_kx, proj, ((0,), (0,)))
    grads_out[32:48, 512 : 512 + IND] = hdot(g_avg, proj, ((0,), (0,)))
    head_out[...] = jnp.zeros(head_out.shape, F32)
    head_out[0:8, :] = d_pooled
    head_out[18:19, :] = cells / pixels
    head_out[8:16, :] = d_two[0:8, :].astype(F32)

    def eighth(t, carry):
        at = pl.ds(pl.multiple_of(t * (width // 2), width // 2), width // 2)
        k8[at, :] = (k2[at, :].astype(F32) * KERNEL_SCALE).astype(F8)
        return carry

    lax.fori_loop(0, 9, eighth, 0)
    first.wait()
    one_b[...] = total([ex_a[i] for i in range(n_dp)])
    ex_b[rep] = one_b[...]
    second = Spread("replica", n_rep, one_b, ex_b, b_send, b_recv)
    second.start()
    lax.fori_loop(9, 18, eighth, 0)
    k8_copy = pltpu.make_async_copy(k8, k8_out, local.at[3 + images])
    k8_copy.start()
    second.wait()
    joined = total([ex_b[i] for i in range(n_rep)])
    d_bias, d_gain = joined[0:1, :], joined[1:2, :]
    head_out[16:17, :] = d_gain
    head_out[17:18, :] = d_bias
    head_out[19:20, :] = joined[2:3, :]
    true_scale = inverse_two * sigma_one * gain
    cat_copies = []
    for n in range(images):
        held = jnp.where(count > n, 1.0, 0.0)
        def step(i, carry):
            rows = BLOCK * side
            at = pl.ds(pl.multiple_of(n * cells + i * rows, rows), rows)
            normed = (y[at, :] - mean_two) * inverse_two
            grad = (true_scale * held) * (
                d_pre[at, :] - d_bias / pixels - normed * (d_gain / pixels)
            )
            cat[at, :] = grad.astype(BF16)
            return carry
        lax.fori_loop(0, side // BLOCK, step, 0)
        here = pl.ds(n * cells, cells)
        copy = pltpu.make_async_copy(cat.at[here, :], cat_out.at[here, :], local.at[3 + n])
        copy.start()
        cat_copies.append(copy)
    for level in (first, second):
        level.drain()
    for copy in cat_copies + [k8_copy]:
        copy.wait()


def head(n_dp, n_rep, side, size, classes, samples, counts, labels, k2, y, slope, windows, stem_pool,
         stats, norms, lengthscale, chol, z_pad, v_pad, f_pad, noise):
    images, width = stem_pool.shape
    shape = jax.ShapeDtypeStruct
    sem = pltpu.SemaphoreType.DMA
    return pl.pallas_call(
        functools.partial(head_kernel, n_dp, n_rep, side, size, classes, samples),
        out_shape=(
            shape(y.shape, BF16),
            shape(k2.shape, F8),
            shape((24, width), F32),
            shape((64, width), F32),
        ),
        in_specs=[SMEM, SMEM, ANY, ANY, ANY] + [VMEM] * 10,
        out_specs=(ANY, ANY, VMEM, VMEM),
        scratch_shapes=[
            pltpu.VMEM(k2.shape, BF16),
            pltpu.VMEM(k2.shape, F8),
            pltpu.VMEM(y.shape, F32),
            pltpu.VMEM(y.shape, F32),
            pltpu.VMEM(y.shape, BF16),
            pltpu.VMEM((images, 3, side, width), F32),
            pltpu.VMEM((8, width), F32),
            pltpu.VMEM((8, IND), F32),
            pltpu.VMEM((16, width), BF16),
            pltpu.VMEM((n_dp, 4, width), F32),
            pltpu.VMEM((n_rep, 4, width), F32),
            pltpu.VMEM((4, width), F32),
            pltpu.VMEM((4, width), F32),
            sem((n_dp,)), sem((n_dp,)), sem((n_rep,)), sem((n_rep,)),
            sem((4 + images,)),
        ],
        compiler_params=pltpu.CompilerParams(
            collective_id=1, has_side_effects=True, vmem_limit_bytes=56 << 20
        ),
    )(counts, labels, k2, y, slope, windows, stem_pool, stats, norms,
      lengthscale, chol, z_pad, v_pad, f_pad, noise)


def greet_all(n_dp, n_rep):
    here = lax.axis_index("dp") * n_rep + lax.axis_index("replica")
    count = n_dp * n_rep
    barrier = pltpu.get_barrier_semaphore()

    def signal(j, carry):
        other = lax.rem(here + j, count)
        pl.semaphore_signal(
            barrier, inc=1, device_id={"dp": other // n_rep, "replica": lax.rem(other, n_rep)},
            device_id_type=MESH,
        )
        return carry

    lax.fori_loop(1, count, signal, 0)
    pl.semaphore_wait(barrier, count - 1)


def chunk_plan(share, width, count):
    def segments(first, last, base):
        result = []
        while first < last:
            c = (first - base) // width
            end = min(last, base + (c + 1) * width)
            result.append((c, first - base - c * width, end - base - c * width))
            first = end
        return result

    plan, done, carried = [], 0, 0
    for r in range(3):
        first, last = r * 3 * width, (r + 1) * 3 * width
        items = []
        while done < count and (done + 1) * share <= last:
            begin = max(done * share, first)
            items.append((done, carried, segments(begin, (done + 1) * share, first)))
            carried = 0
            done += 1
        begin = max(done * share, first)
        plan.append((items, segments(begin, last, first)))
        carried = last - begin
    return plan


def chain_pieces(share):
    tiles = (share + 8) // 16
    count = min(4, max(tiles, 1))
    edges = [tiles * i // count * 16 for i in range(count + 1)]
    return [(lo, hi - lo) for lo, hi in zip(edges, edges[1:])]


def backward_kernel(
    n_dp, n_rep, side, share, fused,
    counts, d_in, x_in, k1_in, k8_in, act_in, patches, stem, stats, norms, windows, head_rows, grads,
    part_out, big_out, sums_out, late_out,
    cat, d_one, x, k1, k8, cat8, held_rows, carry, mine, sib, rin, zin, zout, part, comb, wall, flat, flat_d,
    *rest,
):
    early = rest[0:11]
    late = rest[11:15]
    (c_send, c_recv, r_send, r_recv, z_send, z_recv, w_send, w_recv, local) = rest[15:]
    images = patches.shape[0]
    width = stem.shape[1]
    cells = side * side
    dp, rep = lax.axis_index("dp"), lax.axis_index("replica")
    core, z = lax.rem(dp, 2), dp // 2
    n_z, half = n_dp // 2, n_dp // 2
    sources = max(n_dp // 4, 1)
    owners = half * n_rep
    here = dp * n_rep + rep
    loads = [
        pltpu.make_async_copy(d_in, d_one, local.at[0]),
        pltpu.make_async_copy(x_in, x, local.at[1]),
        pltpu.make_async_copy(k1_in, k1, local.at[2]),
        pltpu.make_async_copy(k8_in, k8, local.at[3]),
    ]
    for copy in loads:
        copy.start()
    greet_all(n_dp, n_rep)
    count = counts[0]
    valid = [jnp.where(count > n, 1.0, 0.0) for n in range(images)]

    early_sum = Reduce(("dp", n_dp), ("replica", n_rep), *early[:5], early[5:])
    source = early[0]
    source[...] = jnp.zeros(source.shape, F32)
    put_rows(source, 0, grads[...])
    gram = total([
        bdot(patches[n], patches[n], ((1,), (1,))) * valid[n] for n in range(images)
    ])
    wide = jnp.concatenate([gram, jnp.zeros((32, 128 - 32), F32)], axis=1)
    per = source.shape[1]
    for k in range(32):
        row = 64 + k
        source[row // per, row % per : row % per + 1, 0:128] = wide[k : k + 1, :]
    early_sum.start()

    if fused:
        for t in range(9):
            comb[t, 0:images, :] = jnp.concatenate(
                [windows[n, t : t + 1, :] for n in range(images)], axis=0
            )
            comb[t, images : 2 * images, :] = head_rows[8 : 8 + images, :]

        def first_tap(owner):
            return jnp.minimum((owner * share) // width, 7)

        def window_copy(owner):
            return remote(
                comb.at[pl.ds(first_tap(owner), 2)], wall.at[here], w_send.at[owner], w_recv.at[here],
                {"dp": half + owner // n_rep, "replica": lax.rem(owner, n_rep)},
            )

        def send_windows(j, c):
            owner = lax.rem(here + j, owners)

            @pl.when(half * n_rep + owner != here)
            def _():
                window_copy(owner).start()
            return c

        lax.fori_loop(0, owners, send_windows, 0)

    def row_of_taps(r):
        return total([
            lax.dot_general(
                x[n].reshape(cells, width),
                cat[n, pl.ds(2 - r, side)].reshape(cells, 3 * width),
                (((0,), (0,)), ((), ())),
                preferred_element_type=F32,
            )
            for n in range(images)
        ])

    def joined(acc, parts):
        pieces = [acc[a:b, (2 - c) * width : (3 - c) * width] for c, a, b in parts]
        return pieces[0] if len(pieces) == 1 else jnp.concatenate(pieces, axis=0)

    def sib_copy(o):
        return remote(
            mine.at[o], sib.at[(o // (2 * n_rep)) * n_rep + o % n_rep],
            c_send.at[o], c_recv.at[(o // (2 * n_rep)) * n_rep + o % n_rep],
            {"dp": dp + 1 - 2 * core},
        )

    def ship(acc, items, leftover):
        for o, carried, parts in items:
            value = joined(acc, parts)
            if carried:
                value = jnp.concatenate([carry[0:carried, :], value], axis=0)
            mine[o, 0:share, :] = value.astype(BF16)
            pl.when(core != (o // n_rep) % 2)(sib_copy(o).start)
        if leftover:
            value = joined(acc, leftover)
            carry[0 : value.shape[0], :] = value

    reps = (rep, rep + 1 - 2 * lax.rem(rep, 2), rep + 2 - 4 * (rep // 2), 3 - rep)
    cut = (share + 8) // 32 * 16
    halves = (pl.ds(0, cut), pl.ds(cut, share + 8 - cut))

    def slot(zi, k):
        return (zi * 2 + core) * n_rep + reps[k]

    def plane_copies(zi, step):
        for h in range(2):
            near, far = 1 + h, 2 - h
            at = halves[h]
            if step == 0:
                for s, k in enumerate((near, 3)):
                    yield remote(
                        mine.at[slot(zi, k), at, :], rin.at[zi, s, at, :],
                        r_send.at[zi, 2 * s + h], r_recv.at[zi, 2 * s + h], {"replica": reps[near]},
                    )
            else:
                yield remote(
                    mine.at[slot(zi, far), at, :], rin.at[zi, 2, at, :],
                    r_send.at[zi, 4 + h], r_recv.at[zi, 4 + h], {"replica": reps[far]},
                )

    def join_cores(zi):
        for k in (3, 1, 2, 0):
            at = zi * n_rep + reps[k]
            remote(
                mine.at[0], sib.at[at], c_send.at[0], c_recv.at[at], {"dp": dp + 1 - 2 * core}
            ).wait_recv()
            mine[slot(zi, k)] = (
                mine[slot(zi, k)].astype(F32) + sib[at].astype(F32)
            ).astype(BF16)
        for copy in plane_copies(zi, 0):
            copy.start()

    def join_near(zi):
        for copy in plane_copies(zi, 0):
            copy.wait_recv()
        for h in range(2):
            at, o = halves[h], slot(zi, 2 - h)
            mine[o, at, :] = (
                mine[o, at, :].astype(F32) + rin[zi, 1, at, :].astype(F32)
            ).astype(BF16)
        for copy in plane_copies(zi, 1):
            copy.start()

    def join_far(zi):
        for copy in plane_copies(zi, 1):
            copy.wait_recv()
        part[zi] = (
            mine[slot(zi, 0)].astype(F32) + rin[zi, 0].astype(F32) + rin[zi, 2].astype(F32)
        )

    z_pieces = chain_pieces(share)
    every = range(len(z_pieces))

    def z_copy(zi, piece, down):
        start, rows = z_pieces[piece]
        at = pl.ds(start, rows)
        step = n_dp - 2 if down else 2
        return remote(
            zout.at[zi, at, :], zin.at[zi, int(down), at, :],
            z_send.at[zi, piece], z_recv.at[zi, piece, int(down)],
            {"dp": lax.rem(dp + step, n_dp)},
        )

    def chain(zi, distance, *pieces):
        for down in (True, False):
            reach = n_z - 1 - zi if down else zi
            if distance > reach:
                continue
            offset = distance if down else -distance
            @pl.when(z == zi + offset)
            def _():
                for piece in pieces or every:
                    start, rows = z_pieces[piece]
                    at = pl.ds(start, rows)
                    if distance < reach:
                        z_copy(zi, piece, down).wait_recv()
                        part[zi, at, :] += zin[zi, int(down), at, :].astype(F32)
                    if distance:
                        zout[zi, at, :] = part[zi, at, :].astype(BF16)
                        z_copy(zi, piece, down).start()

    def window_part():
        @pl.when(dp >= half)
        def _():
            owner = here - owners
            wall[here] = comb[pl.ds(first_tap(owner), 2)]

            def take(j, c):
                origin = lax.rem(here + j, n_dp * n_rep)
                remote(
                    comb.at[pl.ds(0, 2)], wall.at[origin], w_send.at[0], w_recv.at[origin],
                    {"dp": origin // n_rep, "replica": lax.rem(origin, n_rep)},
                ).wait_recv()
                return c

            lax.fori_loop(1, n_dp * n_rep, take, 0)
            for s in range(n_dp * n_rep):
                for tap in range(2):
                    flat[tap, s * images : (s + 1) * images, :] = wall[s, tap, 0:images, :]
                flat_d[s * images : (s + 1) * images, :] = wall[s, 0, images : 2 * images, :]
            for tap in range(2):
                held_rows[tap * width : (tap + 1) * width, :] = hdot(
                    flat[tap], flat_d[...], ((0,), (0,))
                )
            offset = owner * share - first_tap(owner) * width
            part_out[...] = held_rows[pl.ds(pl.multiple_of(offset, 8), share), :]

    for n in range(images):
        edge = jnp.zeros((1, side, 3 * width), BF16)
        cat[n, 0:1] = edge
        cat[n, side + 1 : side + 2] = edge
    loads[0].wait()
    for n in range(images):
        def shift_gradient(i, carried):
            rows = BLOCK * side
            at = pl.ds(pl.multiple_of(n * cells + i * rows, rows), rows)
            store_shifted(cat, n, i * BLOCK, BLOCK, d_one[at, :].astype(F32), side)
            return carried
        lax.fori_loop(0, side // BLOCK, shift_gradient, 0)
    loads[1].wait()
    if fused:
        plan = chunk_plan(share, width, owners)
        for r in range(3):
            acc = row_of_taps(r)
            if r > 0:
                pl.when(core == r - 1)(lambda: join_cores(0))
            ship(acc, *plan[r])
            if r == 1:
                early_sum.middle()
    else:
        for r in range(3):
            acc = row_of_taps(r)
            for c in range(3):
                held_rows[0:width, :] = acc[:, (2 - c) * width : (3 - c) * width]
                out_copy = pltpu.make_async_copy(
                    held_rows.at[pl.ds(0, width), :],
                    part_out.at[pl.ds((3 * r + c) * width, width), :],
                    local.at[4],
                )
                out_copy.start()
                out_copy.wait()
        early_sum.middle()

    loads[2].wait()
    sigma = stats[4:5, :]
    mean_one, inverse_one, pixels = stats[0:1, :], stats[1:2, :], stats[2:3, :]
    gain, bias = norms[0:1, :], norms[1:2, :]
    none = jnp.zeros((8, width), F32)
    block_rows = 2 * BLOCK * side
    per_image = side // (2 * BLOCK)
    blocks = images * per_image

    def input_gradient(b):
        n, i = b // per_image, b % per_image
        acc = None
        for r in range(3):
            lhs = cat[n, pl.ds(i * 2 * BLOCK + r, 2 * BLOCK)].reshape(block_rows, 3 * width)
            one = bdot(lhs, k1[r], ((1,), (1,)))
            acc = one if acc is None else acc + one
        first = (b % 2) * width
        held_rows[first : first + block_rows, :] = acc

    def through_gelu(b, carried):
        n, i = b // per_image, b % per_image
        first = (b % 2) * width
        pixel = patches[n, :, i * block_rows : (i + 1) * block_rows]
        normed = (bdot(pixel, stem[...], ((0,), (0,))) - mean_one) * inverse_one
        grad = gelu_slope(normed * gain + bias) * held_rows[first : first + block_rows, :] * (
            valid[n] / sigma
        )
        down = (grad * (inverse_one * gain) + head_rows[n : n + 1, :] / cells).astype(BF16)
        return (
            carried[0] + fold(grad),
            carried[1] + fold(grad * normed),
            carried[2] + bdot(pixel, down),
        )

    sums = (none, none, jnp.zeros((32, width), F32))
    between = {
        0: [lambda: join_near(0), lambda: join_cores(1)],
        1: [lambda: join_far(0), lambda: chain(0, 3)],
        2: [lambda: chain(0, 2, 0, 1), lambda: join_near(1)],
        3: [lambda: chain(0, 2, 2, 3), lambda: chain(0, 1, 0, 1)],
        4: [lambda: join_far(1), lambda: chain(1, 2)],
    }
    for b in range(blocks + 1):
        if b < blocks:
            input_gradient(b)
        if b > 0:
            sums = through_gelu(b - 1, sums)
        if fused:
            for event in between.get(b, ()):
                event()
    late_sum = Reduce(
        ("dp", n_dp), ("replica", n_rep), late[0], late[1], late_out, None, None, late[2:]
    )
    late[0][...] = jnp.zeros(late[0].shape, F32)
    put_rows(late[0], 0, sums[2][0:27])
    put_rows(late[0], 27, jnp.sum(sums[0], axis=0, keepdims=True))
    put_rows(late[0], 28, jnp.sum(sums[1], axis=0, keepdims=True))
    late_sum.start()
    early_sum.last()

    act_copy = pltpu.make_async_copy(act_in, d_one, local.at[5])
    act_copy.start()
    edge = jnp.zeros((1, side, 3 * width), F8)
    cat8[0, 0:1] = edge
    cat8[0, side + 1 : side + 2] = edge

    def shift_act(n):
        def step(i, carried):
            rows = BLOCK * side
            at = pl.ds(pl.multiple_of(n * cells + i * rows, rows), rows)
            store_shifted(
                cat8, 0, i * BLOCK, BLOCK, d_one[at, :].astype(F32) * ACT_SCALE, side
            )
            return carried
        lax.fori_loop(0, side // BLOCK, step, 0)

    squares = none
    between = {
        0: [lambda: chain(0, 1, 2, 3), lambda: chain(1, 1, 0)],
        1: [lambda: chain(1, 1, 1), lambda: chain(0, 0, 0, 1), window_part],
        2: [lambda: chain(1, 1, 2), lambda: chain(1, 0, 0)],
        3: [lambda: chain(1, 1, 3), lambda: chain(0, 0, 2, 3), lambda: chain(1, 0, 1, 2, 3)],
    }
    for b in range(blocks):
        n, i = b // per_image, b % per_image
        if b == 0:
            act_copy.wait()
            loads[3].wait()
        if i == 0:
            shift_act(n)
        acc = None
        for r in range(3):
            lhs = cat8[0, pl.ds(i * 2 * BLOCK + r, 2 * BLOCK)].reshape(block_rows, 3 * width)
            one = bdot(lhs, k8[r * 3 * width : (r + 1) * 3 * width, :])
            acc = one if acc is None else acc + one
        squares = squares + valid[n] * fold(acc * acc)
        if fused:
            for event in between.get(b, ()):
                event()
    sigma_two = stats[5:6, :] * (ACT_SCALE * KERNEL_SCALE)
    sums_out[...] = jnp.zeros(sums_out.shape, F32)
    sums_out[0:1, :] = jnp.sum(squares, axis=0, keepdims=True) / (sigma_two * sigma_two)

    if fused:
        @pl.when(dp < half)
        def _():
            for zi in range(sources):
                @pl.when(z == zi)
                def _():
                    part_out[...] = part[zi, 0:share, :]

        def drain_windows(j, c):
            owner = lax.rem(here + j, owners)

            @pl.when(half * n_rep + owner != here)
            def _():
                window_copy(owner).wait_send()
            return c

        lax.fori_loop(0, owners, drain_windows, 0)
        for o in range(owners):
            pl.when(core != (o // n_rep) % 2)(sib_copy(o).wait_send)
        for zi in range(sources):
            for step in range(2):
                for copy in plane_copies(zi, step):
                    copy.wait_send()
            for piece in range(len(z_pieces)):
                pl.when(z > zi)(z_copy(zi, piece, True).wait_send)
                pl.when(z < zi)(z_copy(zi, piece, False).wait_send)
    early_sum.finish()
    late_sum.arrive()
    late_sum.drain()
    per = early[4].shape[1]
    for s in range(n_dp):
        for j in range(per):
            big_out[s * per + j : s * per + j + 1, :] = early[4][s, j : j + 1, :]


def backward(n_dp, n_rep, side, share, fused, counts, d_one, x, k1, k8, act, patches, stem, stats, norms,
             windows, head_rows, grads):
    images, width = patches.shape[0], stem.shape[1]
    half = n_dp // 2
    sources = max(n_dp // 4, 1)
    owners = half * n_rep
    devices = n_dp * n_rep
    shape = jax.ShapeDtypeStruct
    sem = pltpu.SemaphoreType.DMA
    rows = share + 8
    small = (1, 8, 128)
    early = reduce_scratch(n_dp, n_rep, 96, width)
    early_rows = early[0].shape[0] * early[0].shape[1]
    part_rows = share if fused else 9 * width
    pieces = len(chain_pieces(share))
    return pl.pallas_call(
        functools.partial(backward_kernel, n_dp, n_rep, side, share, fused),
        out_shape=(
            shape((part_rows, width), F32),
            shape((early_rows, width), F32),
            shape((8, width), F32),
            shape((-(-32 // n_dp), width), F32),
        ),
        in_specs=[SMEM] + [ANY] * 5 + [VMEM] * 7,
        out_specs=(VMEM if fused else ANY, VMEM, VMEM, VMEM),
        scratch_shapes=[
            pltpu.VMEM((images, side + 2, side, 3 * width), BF16),
            pltpu.VMEM(d_one.shape, BF16),
            pltpu.VMEM(x.shape, BF16),
            pltpu.VMEM(k1.shape, BF16),
            pltpu.VMEM(k8.shape, F8),
            pltpu.VMEM((1, side + 2, side, 3 * width), F8),
            pltpu.VMEM((2 * width, width), F32),
            pltpu.VMEM((rows if fused else 8, width), F32),
            pltpu.VMEM((owners, rows, width) if fused else small, BF16),
            pltpu.VMEM((sources * n_rep, rows, width) if fused else small, BF16),
            pltpu.VMEM((sources, 3, rows, width) if fused else small, BF16),
            pltpu.VMEM((sources, 2, rows, width) if fused else small, BF16),
            pltpu.VMEM((sources, rows, width) if fused else small, BF16),
            pltpu.VMEM((sources, rows, width) if fused else small, F32),
            pltpu.VMEM((10, 2 * images, width) if fused else small, F32),
            pltpu.VMEM((devices, 2, 2 * images, width) if fused else small, F32),
            pltpu.VMEM((2, devices * images, width) if fused else small, F32),
            pltpu.VMEM((devices * images, width) if fused else small[1:], F32),
            *early,
            pltpu.VMEM((n_dp, -(-32 // n_dp), width), F32),
            pltpu.VMEM((n_dp, -(-32 // n_dp), width), F32),
            sem((n_dp,)), sem((n_dp,)),
            sem((owners,)), sem((sources * n_rep,)),
            sem((sources, 6)), sem((sources, 6)),
            sem((sources, pieces)), sem((sources, pieces, 2)),
            sem((owners,)), sem((devices,)),
            sem((6,)),
        ],
        compiler_params=pltpu.CompilerParams(
            collective_id=2, has_side_effects=True, vmem_limit_bytes=62 << 20
        ),
    )(counts, d_one, x, k1, k8, act, patches, stem, stats, norms, windows, head_rows, grads)


def whole_sum(values):
    return jnp.sum(jnp.sum(values, axis=1, keepdims=True), axis=0, keepdims=True)


def lamb_step(weight, gradient, first, second, out, rows=False):
    new_one, new_two, direction = lamb_moments(weight, gradient, first, second)
    if rows:
        sizes = [jnp.sum(v * v, axis=1, keepdims=True) for v in (weight, direction)]
    else:
        sizes = [whole_sum(v * v) for v in (weight, direction)]
    new_weight = weight - RATE * (jnp.sqrt(sizes[0]) / jnp.sqrt(sizes[1])) * direction
    for ref, value in zip(out, (new_weight, new_one, new_two)):
        ref[...] = value.reshape(ref.shape)


def conv_gradient(first, part, conv_w, start, head_rows, stats, norm_w, flat, own):
    width = stats.shape[1]
    share = part.shape[0]
    lanes = width // 128
    def pick(row):
        return jnp.where(first, stats[row : row + 1, :], stats[row + 1 : row + 2, :])
    sigma, norm, unit = pick(4)[:, 0:1], pick(6)[:, 0:1], pick(8)
    inverse = stats[11:12, :] * stats[4:5, :]
    along = jnp.where(
        first,
        norm_w[2:3, :] * head_rows[16:17, :] * (EPS_NORM * inverse * inverse),
        head_rows[19:20, :],
    )
    d_sigma = -jnp.sum(along, axis=1, keepdims=True) / sigma
    vector = jnp.where(first, start[0:1, :], start[1:2, :])
    for k in range(lanes):
        own[:, k * 128 : (k + 1) * 128] = (
            conv_w[pl.ds(k, share, stride=lanes), :].astype(BF16).astype(F32)
        )
    rows = own[...]
    left = jnp.sum(rows * vector, axis=1, keepdims=True) / norm
    back = jnp.sum(rows * (unit / norm), axis=1, keepdims=True) - left * (sigma / norm)
    grad = part[...] / sigma + (left * d_sigma) * unit + (back * d_sigma) * vector
    for k in range(lanes):
        flat[pl.ds(k, share, stride=lanes), :] = grad[:, k * 128 : (k + 1) * 128]


def small_kernel(
    conv_ratio, conv_grad, conv_w, conv_m, conv_s, big, late, joined, head_rows, stats, chol, stem_w, stem_m, stem_s,
    norm_w, norm_m, norm_s, ind_w, ind_m, ind_s, len_w, len_m, len_s,
    mean_w, mean_m, mean_s, low_w, low_m, low_s, *rest,
):
    outs = rest[4:22]
    parts_out, sigmas_out, rms_out, z_pad, stem_pad = rest[22:]

    def conv_step():
        weight = conv_w[...]
        new_one, new_two, direction = lamb_moments(weight, conv_grad[...], conv_m[...], conv_s[...])
        new_conv = weight - conv_ratio[0] * direction
        for ref, value in zip(rest[:4], (new_conv, new_one, new_two, new_conv)):
            ref[...] = value.astype(ref.dtype)

    def small_step():
        small_updates(
            big, late, joined, head_rows, stats, chol, stem_w, stem_m, stem_s,
            norm_w, norm_m, norm_s, ind_w, ind_m, ind_s, len_w, len_m, len_s,
            mean_w, mean_m, mean_s, low_w, low_m, low_s, outs,
            parts_out, sigmas_out, rms_out, z_pad, stem_pad,
        )

    return ((4, slice(0, 4), conv_step), (28, slice(4, 22), small_step))


def small_updates(
    big, late, joined, head_rows, stats, chol, stem_w, stem_m, stem_s,
    norm_w, norm_m, norm_s, ind_w, ind_m, ind_s, len_w, len_m, len_s,
    mean_w, mean_m, mean_s, low_w, low_m, low_s, outs,
    parts_out, sigmas_out, rms_out, z_pad, stem_pad,
):
    width = stem_w.shape[1]
    size, classes = ind_w.shape[0], mean_w.shape[0]
    pixels = stats[2:3, :]
    mean_one, inverse_one = stats[0:1, :], stats[1:2, :]
    scale = head_rows[18:19, 0:1]
    parts_out[1] = jnp.sum(1.0 / scale)
    sigmas_out[0] = jnp.sum(stats[4:5, 0:1])
    sigmas_out[1] = jnp.sum(stats[5:6, 0:1])
    cells_all = pixels[:, 0:1] * width
    rms_out[0] = jnp.sum(
        jnp.sqrt(jnp.sum(stats[10:11, :], axis=1, keepdims=True) / cells_all)
    )
    rms_out[1] = jnp.sum(jnp.sqrt(joined[4:5, 0:1] / cells_all))

    gram = big[64:96, 0:32]
    patch_sums = gram[:, 31:32]
    stem_pad[...] = jnp.zeros(stem_pad.shape, F32)
    stem_pad[0 : stem_w.shape[0], :] = stem_w[...].astype(BF16).astype(F32)
    weights = stem_pad[...]
    centred = inverse_one * (hdot(gram, weights) - patch_sums * mean_one)
    d_bias, d_gain = late[27:28, :], late[28:29, :]
    stem_grad = late[0:32, :] - (inverse_one * norm_w[0:1, :] / pixels) * (
        patch_sums * d_bias + centred * d_gain
    )
    lamb_step(stem_w[...], stem_grad[0 : stem_w.shape[0]], stem_m[...], stem_s[...], outs[0:3])
    norm_grad = jnp.concatenate([d_gain, d_bias, head_rows[16:18, :]], axis=0)
    lamb_step(norm_w[...], norm_grad, norm_m[...], norm_s[...], outs[3:6], rows=True)

    ell = len_w[...].reshape(1, width)
    z_pad[...] = jnp.zeros(z_pad.shape, F32)
    z_pad[0:size, :] = ind_w[...] / ell
    zs = z_pad[...]
    kzz, factor, inverse = chol[0], chol[1], chol[2]
    line = lax.broadcasted_iota(jnp.int32, (IND, IND), 0)
    lane = lax.broadcasted_iota(jnp.int32, (IND, IND), 1)
    g_chol = jnp.where(line >= lane, -big[32:64, 384 : 384 + IND], 0.0)
    lower = hdot(factor, g_chol, ((0,), (0,)))
    phi = jnp.where(line > lane, lower, jnp.where(line == lane, 0.5 * lower, 0.0))
    back = hdot(inverse, hdot(phi, inverse), ((0,), (0,)))
    back_t = hdot(inverse, hdot(phi, inverse, ((0,), (0,))), ((0,), (0,)))
    weights_z = -0.5 * kzz * (back + back_t)
    g_z = big[0:32, :]
    g_z = jnp.where(lax.broadcasted_iota(jnp.int32, (IND, 1), 0) < size, g_z, 0.0) + 2.0 * (
        zs * jnp.sum(weights_z, axis=1, keepdims=True) - hdot(weights_z, zs)
    )
    lamb_step(ind_w[...], (g_z / ell)[0:size], ind_m[...], ind_s[...], outs[6:9])
    g_len = -(big[20:21, :] + jnp.sum(g_z * zs, axis=0, keepdims=True)) / ell
    lamb_step(ell, g_len, len_m[...].reshape(1, width), len_s[...].reshape(1, width), outs[9:12])

    means = mean_w[...]
    g_mean = big[32 : 32 + classes, 512 : 512 + size] + means * scale
    lamb_step(means, g_mean, mean_m[...], mean_s[...], outs[12:15])
    small_line = lax.broadcasted_iota(jnp.int32, (size, size), 0)
    small_lane = lax.broadcasted_iota(jnp.int32, (size, size), 1)
    kl = 0.5 * jnp.sum(means * means, axis=0, keepdims=True)
    weight_sq = jnp.zeros((1, size), F32)
    step_sq = weight_sq
    steps = []
    for c in range(classes):
        weight = low_w[c]
        factors = scale_rows(weight)
        inner = big[32 : 32 + size, c * IND : c * IND + size] + factors * scale
        grad = jnp.where(
            small_line > small_lane, inner,
            jnp.where(small_line == small_lane, factors * inner - scale, 0.0),
        )
        new_one, new_two, direction = lamb_moments(weight, grad, low_m[c], low_s[c])
        outs[16][c] = new_one
        outs[17][c] = new_two
        weight_sq = weight_sq + jnp.sum(weight * weight, axis=0, keepdims=True)
        step_sq = step_sq + jnp.sum(direction * direction, axis=0, keepdims=True)
        diagonal = jnp.where(small_line == small_lane, weight, 0.0)
        kl = kl + jnp.sum(0.5 * factors * factors - diagonal, axis=0, keepdims=True)
        steps.append(direction)
    ratio = RATE * jnp.sqrt(jnp.sum(weight_sq, axis=1, keepdims=True)) / jnp.sqrt(
        jnp.sum(step_sq, axis=1, keepdims=True)
    )
    for c in range(classes):
        outs[15][c] = low_w[c] - ratio * steps[c]
    kl = jnp.sum(kl, axis=1, keepdims=True) - 0.5 * classes * size
    parts_out[0] = jnp.sum(big[23:24, 0:1] + kl)


def staged(body, n_in, n_out, n_first, n_last, *refs):
    first, refs = refs[:n_first], refs[n_first:]
    ins, refs = refs[:n_in], refs[n_in:]
    outs, refs = refs[:n_out], refs[n_out:]
    last, refs = refs[:n_last], refs[n_last:]
    held, refs = refs[:n_in], refs[n_in:]
    made, refs = refs[:n_out], refs[n_out:]
    scratch, (sem_in, sem_out) = refs[:-2], refs[-2:]
    loads = [
        pltpu.make_async_copy(ref, held[i], sem_in.at[i]) for i, ref in enumerate(ins)
    ]
    for copy in loads:
        copy.start()
    stores = [
        pltpu.make_async_copy(made[i], ref, sem_out.at[i]) for i, ref in enumerate(outs)
    ]
    done = 0
    for ready, finished, step in body(*first, *held, *made, *last, *scratch):
        for copy in loads[done:ready]:
            copy.wait()
        done = ready
        step()
        for copy in stores[finished]:
            copy.start()
    for copy in stores:
        copy.wait()


def local_call(body, first, ins, outs, last, scratch):
    sem = pltpu.SemaphoreType.DMA
    return pl.pallas_call(
        functools.partial(staged, body, len(ins), len(outs), len(first), len(last)),
        out_shape=tuple(outs) + tuple(last),
        in_specs=[SMEM] * len(first) + [ANY] * len(ins),
        out_specs=(ANY,) * len(outs) + (SMEM,) * len(last),
        scratch_shapes=[
            *[pltpu.VMEM(a.shape, a.dtype) for a in ins],
            *[pltpu.VMEM(o.shape, o.dtype) for o in outs],
            *scratch,
            sem((len(ins),)),
            sem((len(outs),)),
        ],
        compiler_params=pltpu.CompilerParams(vmem_limit_bytes=60 << 20),
    )(*first, *ins)


def update_small(ratio, *ins):
    shape = jax.ShapeDtypeStruct
    conv, params = ins[0], ins[10:28:3]
    width = params[0].shape[1]
    outs = [shape(conv.shape, F32)] * 3 + [shape(conv.shape, BF16)]
    outs += [shape(p.shape, F32) for p in params for _ in range(3)]
    return local_call(
        small_kernel, [ratio], ins, outs, [shape((2,), F32)] * 3,
        [pltpu.VMEM((IND, width), F32), pltpu.VMEM((32, width), F32)],
    )


def tally_kernel(n_dp, n_rep, *refs):
    ins, refs = refs[:10], refs[10:]
    grad_out, out, ratio, late_out = refs[:4]
    held, refs = refs[4:14], refs[14:]
    flat, own, tally, ex_a, ex_b, one_b, planes, made = refs[:8]
    a_send, a_recv, b_send, b_recv, sem_in, sem_out = refs[8:14]
    half = n_dp // 2
    dp, rep = lax.axis_index("dp"), lax.axis_index("replica")
    greeted = greet(n_dp, n_rep)
    loads = [pltpu.make_async_copy(ref, held[i], sem_in.at[i]) for i, ref in enumerate(ins)]
    for copy in loads:
        copy.start()
    for copy in loads:
        copy.wait()
    part, conv_w, conv_m, conv_s, start, sums, head_rows, stats, norm_w, late = held
    greeted()
    late_sum = Reduce(
        ("dp", n_dp), ("replica", n_rep), None, None, late, planes, made, (None, None) + refs[14:]
    )
    late_sum.across()
    conv_gradient(dp < half, part, conv_w, start, head_rows, stats, norm_w, flat, own)
    store = pltpu.make_async_copy(flat, grad_out, sem_out.at[0])
    store.start()
    weight = conv_w[...]
    direction = lamb_moments(weight, flat[...], conv_m[...], conv_s[...])[2]
    lanes = stats.shape[1] // 128
    tally[...] = jnp.zeros(tally.shape, F32)
    tally[0:1, :] = jnp.sum(weight * weight, axis=0, keepdims=True)
    tally[1:2, :] = jnp.sum(direction * direction, axis=0, keepdims=True)
    tally[2:3, :] = total([sums[0:1, k * 128 : (k + 1) * 128] for k in range(lanes)])
    ex_a[dp] = tally[...]
    first = Spread("dp", n_dp, tally, ex_a, a_send, a_recv)
    first.start()
    late_sum.last()
    first.wait()
    one_b[...] = jnp.zeros(one_b.shape, F32)
    for l in range(2):
        near = range(l * half, (l + 1) * half)
        one_b[l : l + 1, :] = total([ex_a[i, 0:1, :] for i in near])
        one_b[2 + l : 3 + l, :] = total([ex_a[i, 1:2, :] for i in near])
    one_b[4:5, :] = total(rows_of(ex_a, 2))
    ex_b[rep] = one_b[...]
    second = Spread("replica", n_rep, one_b, ex_b, b_send, b_recv)
    second.start()
    late_sum.finish_last()
    per = made.shape[1]
    for k in range(32):
        late_out[k : k + 1, :] = made[k // per, k % per : k % per + 1, :]
    second.wait()
    joined = jnp.sum(total([ex_b[i] for i in range(n_rep)]), axis=1, keepdims=True)
    out[...] = jnp.zeros(out.shape, F32) + joined
    trust = jnp.sqrt(joined[0:2]) / jnp.sqrt(joined[2:4])
    ratio[0] = RATE * jnp.sum(jnp.where(dp < half, trust[0:1], trust[1:2]))
    first.drain()
    second.drain()
    store.wait()


def join_tally(n_dp, n_rep, *ins):
    sem = pltpu.SemaphoreType.DMA
    shape = jax.ShapeDtypeStruct
    part, conv, late = ins[0], ins[1], ins[9]
    return pl.pallas_call(
        functools.partial(tally_kernel, n_dp, n_rep),
        out_shape=(
            shape(conv.shape, F32), shape((8, 128), F32), shape((1,), F32),
            shape((32, late.shape[1]), F32),
        ),
        in_specs=[ANY] * 10,
        out_specs=(ANY, VMEM, SMEM, VMEM),
        scratch_shapes=[
            *[pltpu.VMEM(a.shape, a.dtype) for a in ins],
            pltpu.VMEM(conv.shape, F32),
            pltpu.VMEM(part.shape, F32),
            pltpu.VMEM((8, 128), F32),
            pltpu.VMEM((n_dp, 8, 128), F32),
            pltpu.VMEM((n_rep, 8, 128), F32),
            pltpu.VMEM((8, 128), F32),
            pltpu.VMEM((n_rep, *late.shape), F32),
            pltpu.VMEM((n_dp, *late.shape), F32),
            sem((n_dp,)), sem((n_dp,)), sem((n_rep,)), sem((n_rep,)),
            sem((10,)), sem((1,)),
            sem((n_rep,)), sem((n_rep,)), sem((n_dp,)), sem((n_dp,)),
        ],
        compiler_params=pltpu.CompilerParams(
            collective_id=3, has_side_effects=True, vmem_limit_bytes=60 << 20
        ),
    )(*ins)


def on_device(
    images, labels, counts, noise_table, noise_index, power_start,
    conv_weight, conv_first, conv_second,
    stem_weight, stem_first, stem_second,
    norm_params, norm_first, norm_second,
    inducing, inducing_first, inducing_second,
    lengthscale, length_first, length_second,
    var_mean, mean_first, mean_second,
    var_lower, lower_first, lower_second,
):
    width = stem_weight.shape[1]
    side = images.shape[2]
    cells = side * side
    n_dp, n_rep = lax.axis_size("dp"), lax.axis_size("replica")
    here = lax.axis_index(AXES)
    per_kernel = n_dp * n_rep // 2
    owner = here // per_kernel
    select = (jnp.arange(2) == owner).astype(F32)
    geometry = (n_dp, n_rep, side)

    share = conv_weight.shape[0] // width
    wide = (-1, 128)
    fused = share % 16 == 8 and n_rep == 4 and n_dp == 8
    if fused:
        weights, extra = conv_weight.reshape(wide), power_start
    else:
        rows = conv_weight.astype(BF16).reshape(-1, width)
        gathered = lax.all_gather(rows, AXES, axis=0, tiled=True)
        weights = gathered[: 9 * width]
        own = rows.astype(F32)
        start = jnp.sum(select[:, None] * power_start, axis=0)
        own_along = jnp.sum(own * start, axis=1)
        back_rows = jnp.sum(own * own_along[:, None], axis=0)
        extra = jnp.stack([back_rows, jnp.full((width,), jnp.sum(own_along * own_along))])
    pictures = images.astype(F32).reshape(images.shape[0], images.shape[1], cells)
    (
        k_one, k_two, act_one, raw_one, slope, act_two, windows, stem_pool, stats, patches, stem_kernel,
        chol, *prepared,
    ) = forward(
        *geometry, share, fused, counts, noise_index, weights, pictures, stem_weight, extra,
        norm_params, noise_table.T, inducing, lengthscale, var_mean, var_lower,
    )
    if not fused:
        k_two = gathered[9 * width :]
    d_one, k8, head_rows, grads = head(
        *geometry, inducing.shape[0], var_mean.shape[0], noise_index.shape[1], counts, labels,
        k_two, raw_one, slope, windows, stem_pool, stats, norm_params, lengthscale, chol, *prepared,
    )
    part, big, sums, late = backward(
        *geometry, share, fused, counts, d_one, act_one, k_one, k8, act_two, patches, stem_kernel, stats, norm_params, windows,
        head_rows, grads,
    )
    if not fused:
        part_one = lax.psum_scatter(
            jnp.concatenate([part.reshape(-1), jnp.zeros((part.size,), F32)]),
            AXES, scatter_dimension=0, tiled=True,
        ).reshape(-1, width)
        all_windows, all_grads = lax.all_gather(
            (windows[:, :9], head_rows[8 : 8 + images.shape[0]]), AXES, tiled=True
        )
        all_windows = all_windows.reshape(all_windows.shape[0], -1)
        mine = lax.dynamic_slice_in_dim(
            all_windows, lax.rem(here, per_kernel) * share, share, axis=1
        )
        part = jnp.where(owner == 0, part_one, jnp.dot(mine.T, all_grads, precision=HIGH))

    conv = [v.reshape(wide) for v in (conv_weight, conv_first, conv_second)]
    conv_grad, joined, ratio, late = join_tally(
        n_dp, n_rep, part, *conv, power_start, sums, head_rows, stats, norm_params, late
    )
    done = update_small(
        ratio, conv_grad, *conv, big, late, joined, head_rows, stats, chol,
        stem_weight, stem_first, stem_second, norm_params, norm_first, norm_second,
        inducing, inducing_first, inducing_second, lengthscale, length_first, length_second,
        var_mean, mean_first, mean_second, var_lower, lower_first, lower_second,
    )
    loss_parts, sigmas, rms = done[22:]
    return (loss_parts, *[v.reshape(-1) for v in done[:4]], *done[4:22], sigmas, rms)


def solution(mesh):
    split = P(AXES)
    return jax.shard_map(
        on_device,
        mesh=mesh,
        in_specs=(split, split, split, P(), split, P(), split, split, split) + (P(),) * 18,
        out_specs=(P(),) + (split,) * 4 + (P(),) * 20,
        check_vma=False,
    )
```

```python
import functools

import jax
import jax.numpy as jnp
from jax import lax
from jax.experimental import pallas as pl
from jax.experimental.pallas import tpu as pltpu
from jax.sharding import PartitionSpec as P

STEP = 10
HIGH = lax.Precision.HIGHEST
EPS_NORM = 1e-05
JITTER = 0.001
BETA_ONE = 0.9
BETA_TWO = 0.999
RATE = 0.3
DECAY = 0.01
EPS_ADAM = 1e-08
AXES = ("dp", "replica")


def lamb_moments(weight, gradient, moment_one, moment_two):
    new_one = BETA_ONE * moment_one + (1.0 - BETA_ONE) * gradient
    new_two = BETA_TWO * moment_two + (1.0 - BETA_TWO) * gradient * gradient
    direction = (
        new_one / (1.0 - BETA_ONE**STEP) / (jnp.sqrt(new_two / (1.0 - BETA_TWO**STEP)) + EPS_ADAM)
        + DECAY * weight
    )
    return (new_one, new_two, direction)


MESH = pl.DeviceIdType.MESH
ANY = pl.BlockSpec(memory_space=pl.ANY)
VMEM = pl.BlockSpec(memory_space=pltpu.VMEM)
SMEM = pl.BlockSpec(memory_space=pltpu.SMEM)
F32 = jnp.float32
BF16 = jnp.bfloat16
F8 = jnp.float8_e4m3fn
ACT_SCALE = 0.25
KERNEL_SCALE = 2048.0


def remote(src, dst, send, recv, where):
    return pltpu.make_async_remote_copy(
        src_ref=src, dst_ref=dst, send_sem=send, recv_sem=recv,
        device_id=where, device_id_type=MESH,
    )


def greet(n_dp, n_rep):
    dp, rep = lax.axis_index("dp"), lax.axis_index("replica")
    barrier = pltpu.get_barrier_semaphore()
    for j in range(1, n_dp):
        pl.semaphore_signal(
            barrier, inc=1, device_id={"dp": lax.rem(dp + j, n_dp)}, device_id_type=MESH
        )
    for j in range(1, n_rep):
        pl.semaphore_signal(
            barrier, inc=1, device_id={"replica": lax.rem(rep + j, n_rep)}, device_id_type=MESH
        )
    return lambda: pl.semaphore_wait(barrier, n_dp + n_rep - 2)


class Spread:
    def __init__(self, axis, size, src, dst, send, recv):
        self.axis, self.size, self.src, self.dst, self.send, self.recv = axis, size, src, dst, send, recv
        self.me = lax.axis_index(axis)

    def copies(self):
        for j in range(1, self.size):
            yield remote(
                self.src, self.dst.at[self.me], self.send.at[j], self.recv.at[j],
                {self.axis: lax.rem(self.me + j, self.size)},
            )

    def start(self):
        for copy in self.copies():
            copy.start()

    def wait(self):
        for j in range(1, self.size):
            source = lax.rem(self.me + self.size - j, self.size)
            remote(
                self.src, self.dst.at[source], self.send.at[j], self.recv.at[j],
                {self.axis: source},
            ).wait_recv()

    def drain(self):
        for copy in self.copies():
            copy.wait_send()


def rows_of(refs, row):
    return [refs[i, row : row + 1, :] for i in range(refs.shape[0])]


def total(values):
    result = values[0]
    for value in values[1:]:
        result = result + value
    return result


def join_moments(refs):
    averages, squares, counts = rows_of(refs, 0), rows_of(refs, 1), rows_of(refs, 2)
    count = total(counts)
    average = total([a * n for a, n in zip(averages, counts)]) / count
    spread = total(
        [s + n * (a - average) * (a - average) for a, s, n in zip(averages, squares, counts)]
    )
    return average, spread, count


def hdot(a, b, dims=((1,), (0,))):
    return lax.dot_general(
        a, b, (dims, ((), ())), precision=HIGH, preferred_element_type=F32
    )


def bdot(a, b, dims=((1,), (0,))):
    return lax.dot_general(a, b, (dims, ((), ())), preferred_element_type=F32)


class Gather:
    def __init__(self, which, n_dp, share, buffer, sems):
        self.which, self.n_dp, self.share, self.buffer = which, n_dp, share, buffer
        tiles = (share - 8) // 16
        edges = [tiles * i // PIECES * 16 for i in range(PIECES + 1)]
        self.pieces = list(zip(edges, [hi - lo for lo, hi in zip(edges, edges[1:])]))
        self.z_send, self.z_recv, self.r_send, self.r_recv, self.c_send, self.c_recv = [
            s.at[which] for s in sems
        ]
        self.dp, rep = lax.axis_index("dp"), lax.axis_index("replica")
        self.reps = (rep, rep + 1 - 2 * lax.rem(rep, 2), rep + 2 - 4 * (rep // 2), 3 - rep)
        self.core, self.z = lax.rem(self.dp, 2), self.dp // 2
        self.n_z = n_dp // 2
        self.sources = n_dp // 4
        self.order = range(self.sources) if which else range(self.sources - 1, -1, -1)

    def first(self, zi, core, k):
        owner = (zi * 2 + core) * 4 + self.reps[k]
        return (owner // 2) * (2 * self.share) + lax.rem(owner, 2) * (self.share + 8)

    def each(self, zi, core, k, piece, act):
        start, rows = self.pieces[piece]
        begin = pl.multiple_of(self.first(zi, core, k) + start, 16)
        if piece < len(self.pieces) - 1:
            act(self.buffer.at[pl.ds(begin, rows), :])
            return
        even = lax.rem(self.reps[k], 2) == 0
        pl.when(even)(lambda: act(self.buffer.at[pl.ds(begin, rows + 16), :]))
        pl.when(~even)(lambda: act(self.buffer.at[pl.ds(begin, rows), :]))

    def source(self, zi):
        return zi + self.which * self.sources

    def along(self, zi, piece, what, ways=(0, 1)):
        def act(ref):
            for way in ways:
                condition = (
                    ((self.z <= self.source(zi)) & (self.z > 0)) if way
                    else ((self.z >= self.source(zi)) & (self.z < self.n_z - 1))
                )
                step = self.n_dp - 2 if way else 2
                copy = remote(
                    ref, ref, self.z_send.at[zi, piece, way], self.z_recv.at[zi, piece],
                    {"dp": lax.rem(self.dp + step, self.n_dp)},
                )
                if what == "wait_recv":
                    copy.wait_recv()
                    return
                pl.when(condition)(getattr(copy, what))
        self.each(zi, self.core, 0, piece, act)

    def goes_on(self, zi):
        gap = self.z - self.source(zi)
        return ((gap < 0) & (self.z > 0)) | ((gap > 0) & (self.z < self.n_z - 1))

    def near(self, zi, piece, k, what):
        def act(ref):
            getattr(remote(
                ref, ref, self.r_send.at[zi, piece, k], self.r_recv.at[zi, piece, k],
                {"replica": self.reps[k]},
            ), what)()
        self.each(zi, self.core, k if what == "wait_recv" else 0, piece, act)

    def passed(self, zi, piece, what):
        k = 1 + piece % 2
        def act(ref):
            getattr(remote(
                ref, ref, self.r_send.at[zi, piece, 3], self.r_recv.at[zi, piece, 3],
                {"replica": self.reps[3 - k]},
            ), what)()
        self.each(zi, self.core, 3 if what == "wait_recv" else k, piece, act)

    def over(self, zi, piece, k, what):
        def act(ref):
            getattr(remote(
                ref, ref, self.c_send.at[zi, piece, k], self.c_recv.at[zi, piece, k],
                {"dp": self.dp + 1 - 2 * self.core},
            ), what)()
        self.each(zi, 1 - self.core if what == "wait_recv" else self.core, k, piece, act)

    def send_plane(self, zi, piece):
        for k in (1, 2):
            self.near(zi, piece, k, "start")
        self.over(zi, piece, 0, "start")

    def own(self, pieces, ways, plane):
        for zi in range(self.sources):
            @pl.when(self.z == self.source(zi))
            def _():
                for piece in pieces:
                    self.along(zi, piece, "start", ways)
                    if plane:
                        self.send_plane(zi, piece)

    def column(self, zi, pieces):
        @pl.when(self.z != self.source(zi))
        def _():
            for piece in pieces:
                self.along(zi, piece, "wait_recv")
                self.along(zi, piece, "start")
                self.send_plane(zi, piece)

    def hop(self, distance):
        for zi in self.order:
            gap = self.z - self.source(zi)
            @pl.when(self.goes_on(zi) & ((gap == distance) | (gap == -distance)))
            def _():
                for piece in range(len(self.pieces)):
                    self.along(zi, piece, "wait_recv")
                    self.along(zi, piece, "start")

    def plane(self, zi, condition, sent=0):
        @pl.when(condition)
        def _():
            for piece in range(len(self.pieces)):
                pl.when((self.z != self.source(zi)) & ~self.goes_on(zi))(
                    functools.partial(self.along, zi, piece, "wait_recv")
                )
                if piece < sent:
                    pl.when(self.z != self.source(zi))(
                        functools.partial(self.send_plane, zi, piece)
                    )
                else:
                    self.send_plane(zi, piece)

    def neighbours(self, zi, pieces):
        for piece in pieces:
            for k in (1, 2):
                self.near(zi, piece, k, "wait_recv")
                if k == 1 + piece % 2:
                    self.passed(zi, piece, "start")
                self.over(zi, piece, k, "start")

    def opposite(self, zi):
        for piece in range(len(self.pieces)):
            self.passed(zi, piece, "wait_recv")
            self.over(zi, piece, 3, "start")

    def from_core(self, zi):
        for piece in range(len(self.pieces)):
            for k in range(4):
                self.over(zi, piece, k, "wait_recv")

    def drain(self):
        for piece in range(len(self.pieces)):
            for zi in range(self.sources):
                self.along(zi, piece, "wait_send")
                for k in (1, 2):
                    self.near(zi, piece, k, "wait_send")
                self.passed(zi, piece, "wait_send")
                for k in range(4):
                    self.over(zi, piece, k, "wait_send")


PIECES = 4


def pixel_column(rows, side):
    return lax.rem(lax.broadcasted_iota(jnp.int32, (rows, 1), 0), side)


def store_shifted(ref, image, first, block, values, side):
    width = values.shape[1]
    rows = block * side
    column = pixel_column(rows, side)
    left = jnp.where(column == 0, 0.0, pltpu.roll(values, 1, 0))
    right = jnp.where(column == side - 1, 0.0, pltpu.roll(values, rows - 1, 0))
    for c, moved in enumerate((left, values, right)):
        ref[image, pl.ds(first + 1, block), :, c * width : (c + 1) * width] = (
            moved.astype(ref.dtype).reshape(block, side, width)
        )


def gelu_both(x):
    c = 0.7978845608028654
    square = x * x
    th = jnp.tanh(c * x * (1.0 + 0.044715 * square))
    half = 0.5 * (1.0 + th)
    return x * half, half + 0.5 * x * (1.0 - th * th) * (c * (1.0 + 3 * 0.044715 * square))


def window_matrix(side):
    shape = (side * side, 16)
    pixel = lax.broadcasted_iota(jnp.int32, shape, 0)
    tap = lax.broadcasted_iota(jnp.int32, shape, 1)
    r, c = tap // 3, lax.rem(tap, 3)
    h, w = pixel // side, lax.rem(pixel, side)
    keep = (
        (tap < 9)
        & ~((r == 0) & (h == side - 1)) & ~((r == 2) & (h == 0))
        & ~((c == 0) & (w == side - 1)) & ~((c == 2) & (w == 0))
    )
    return jnp.where(keep, 1.0, 0.0).astype(BF16)


BLOCK = 8


def make_patches(images, side, patches, line):
    cells = side * side
    pixel = lax.broadcasted_iota(jnp.int32, (1, cells), 1)
    h, w = pixel // side, lax.rem(pixel, side)
    colours = images.shape[1]
    for n in range(images.shape[0]):
        for c in range(colours):
            picture = images[n, c].astype(F32)
            for row in range(side):
                line[c : c + 1, row * side : (row + 1) * side] = picture[row : row + 1, :]
        values = line[0:colours, :]
        line[...] = jnp.where(
            lax.broadcasted_iota(jnp.int32, line.shape, 0) == 31, 1.0, 0.0
        )
        for t in range(9):
            down, right = t // 3 - 1, t % 3 - 1
            shift = down * side + right
            moved = pltpu.roll(values, (-shift) % cells, 1) if shift else values
            inside = (h + down >= 0) & (h + down < side) & (w + right >= 0) & (w + right < side)
            line[colours * t : colours * (t + 1), :] = jnp.where(inside, moved, 0.0)
        patches[n] = line[...].astype(BF16)


IND = 32


def cholesky_steps(matrix, size):
    lane = lax.broadcasted_iota(jnp.int32, (size, IND), 1)
    line = lax.broadcasted_iota(jnp.int32, (size, IND), 0)
    left = matrix
    right = jnp.where(lane == line, 1.0, 0.0)
    factor = jnp.zeros((size, IND), F32)
    row_of = lax.broadcasted_iota(jnp.int32, (size, 1), 0)
    for k in range(size):
        inverse = lax.rsqrt(left[k : k + 1, k : k + 1])
        column = jnp.where(row_of >= k, left[:, k : k + 1] * inverse, 0.0)
        below = jnp.where(row_of > k, column, 0.0)
        row = left[k : k + 1, :] * inverse
        other = right[k : k + 1, :] * inverse
        factor = jnp.where(lane == k, column, factor)
        left = left - below * row
        right = jnp.where(line == k, other, right - below * other)
    return factor, right


def scale_rows(lower):
    size = lower.shape[0]
    line = lax.broadcasted_iota(jnp.int32, (size, size), 0)
    lane = lax.broadcasted_iota(jnp.int32, (size, size), 1)
    return jnp.where(line > lane, lower, jnp.where(line == lane, jnp.exp(lower), 0.0))


def prepare_head(indices, table, inducing, lengthscale, var_mean, var_lower, chol_out, z_pad, v_pad, f_pad, noise):
    size, width = inducing.shape
    classes = var_mean.shape[0]
    images, samples = indices.shape
    ell = lengthscale[...].reshape(1, width)
    z_pad[...] = jnp.zeros(z_pad.shape, F32)
    z_pad[0:size, :] = inducing[...] / ell
    zs = z_pad[...]
    lane = lax.broadcasted_iota(jnp.int32, (size, IND), 1)
    line = lax.broadcasted_iota(jnp.int32, (size, IND), 0)
    kzz = jnp.zeros((size, IND), F32)
    for m in range(size):
        off = zs[0:size, :] - zs[m : m + 1, :]
        kzz = jnp.where(lane == m, jnp.exp(-0.5 * jnp.sum(off * off, axis=1, keepdims=True)), kzz)
    factor, inverse = cholesky_steps(jnp.where(lane == line, kzz + JITTER, kzz), size)
    chol_out[...] = jnp.zeros(chol_out.shape, F32)
    chol_out[0, 0:size, :] = kzz
    chol_out[1, 0:size, :] = factor
    chol_out[2, 0:size, :] = inverse
    v_pad[...] = jnp.zeros(v_pad.shape, F32)
    v_pad[0:classes, 0:size] = var_mean[...]
    f_pad[...] = jnp.zeros(f_pad.shape, F32)
    for c in range(classes):
        f_pad[0:size, c * IND : c * IND + size] = scale_rows(var_lower[c])
    noise[...] = jnp.zeros(noise.shape, F32)
    table_lane = lax.broadcasted_iota(jnp.int32, (1, table.shape[1]), 1)
    for n in range(images):
        chosen = [jnp.where(table_lane == indices[n, s], 1.0, 0.0) for s in range(samples)]
        chosen.append(jnp.zeros((16 - samples, table.shape[1]), F32))
        noise[n, :, 0:classes] = hdot(jnp.concatenate(chosen, axis=0), table[...], ((1,), (1,)))


def forward_kernel(
    n_dp, n_rep, side, share, fused,
    counts, indices, weights, pictures, stem_in, start, norms, table, inducing, lengthscale, var_mean, var_lower,
    k1_out, k2_out, x_out, y_out, slope_out, act_out, windows, stem_pool, stats, patches, stem,
    chol_out, z_pad, v_pad, f_pad, noise,
    line, own_f32, main, bound, k1, xcat, y, act, slope, seam, ex_a, ex_b, one_a, one_b, tw_a, tw_b, tw_one,
    z_send, z_recv, r_send, r_recv, c_send, c_recv,
    a_send, a_recv, b_send, b_recv, s_send, s_recv, local, turn,
):
    images = pictures.shape[0]
    width = stem_in.shape[1]
    cells = side * side
    dp, rep = lax.axis_index("dp"), lax.axis_index("replica")
    half = n_dp // 2
    greeted = greet(n_dp, n_rep)

    if fused:
        rows = share - 8
        sems = (z_send, z_recv, r_send, r_recv, c_send, c_recv)
        one, two = [
            Gather(l, n_dp, share, buffer, sems) for l, buffer in enumerate((k1, k2_out))
        ]
        every = range(PIECES)
        early, final = every[:-1], every[-1:]
        even = lax.rem(rep, 2) == 0
        owner = lax.rem(dp, half) * n_rep + rep
        own_first = (owner // 2) * (2 * share) + lax.rem(owner, 2) * (share + 8)
        seam_copy = remote(
            bound, seam.at[1], s_send.at[0], s_recv.at[0],
            {"replica": rep + 1 - 2 * lax.rem(rep, 2)},
        )

        def own_copies(what):
            for l, buffer in enumerate((k1, k2_out)):
                @pl.when((dp < half) if l == 0 else (dp >= half))
                def _():
                    at = pl.ds(pl.multiple_of(own_first, 16), rows)
                    getattr(pltpu.make_async_copy(main, buffer.at[at, :], local.at[0]), what)()

        def put_seam():
            @pl.when(even)
            def _():
                seam_copy.wait_recv()
                seam[0] = (bound[...].astype(F32) + seam[1].astype(F32)).astype(BF16)
                for l, buffer in enumerate((k1, k2_out)):
                    @pl.when((dp < half) if l == 0 else (dp >= half))
                    def _():
                        at = pl.ds(pl.multiple_of(own_first + rows, 16), 16)
                        copy = pltpu.make_async_copy(seam.at[0], buffer.at[at, :], local.at[10])
                        copy.start()
                        copy.wait()

        lanes = width // 128
        for k in range(lanes):
            own_f32[:, k * 128 : (k + 1) * 128] = weights[pl.ds(k, share, stride=lanes), :]
        blank = jnp.zeros((8, width), F32)
        head_rows, tail_rows = own_f32[0:8, :], own_f32[share - 8 : share, :]
        main[...] = jnp.where(even, own_f32[0:rows, :], own_f32[8:share, :]).astype(BF16)
        bound[...] = jnp.where(
            even,
            jnp.concatenate([tail_rows, blank], axis=0),
            jnp.concatenate([blank, head_rows], axis=0),
        ).astype(BF16)
        own_copies("start")
    else:
        copy_in = pltpu.make_async_copy(weights, k1, local.at[0])
        copy_in.start()

    if fused:
        own_copies("wait")
    greeted()
    if fused:
        pl.when(~even)(seam_copy.start)
        one.own(every[:2], (0, 1), True)
        two.own(every[:2], (1,), True)
    line[:, 0:width] = jnp.zeros((32, width), F32)
    line[0 : stem_in.shape[0], 0:width] = stem_in[...]
    stem[...] = line[:, 0:width].astype(BF16)
    weight = stem[...].astype(F32)
    count = counts[0]
    valid = [jnp.where(count > n, 1.0, 0.0) for n in range(images)]
    held = count.astype(F32) * cells
    make_patches(pictures, side, patches, line)
    grams, sums = [], []
    for n in range(images):
        grams.append(bdot(patches[n], patches[n], ((1,), (1,))))
        sums.append(grams[n][24:32])
        stem_pool[n : n + 1, :] = hdot(sums[n], weight)[7:8] * (1.0 / cells)
    gram = total([g * v for g, v in zip(grams, valid)])
    summed = total([s * v for s, v in zip(sums, valid)])
    square = jnp.sum(weight * hdot(gram, weight), axis=0, keepdims=True)
    last = jnp.where(lax.broadcasted_iota(jnp.int32, summed.shape, 0) == 7, summed, 0.0)
    cover = gram - hdot(last, last, ((0,), (0,))) / held
    zero = jnp.zeros((1, width), F32)
    payload = one_a.at[0]
    payload[...] = jnp.zeros(payload.shape, F32)
    payload[0:1, :] = hdot(summed, weight)[7:8] / held
    payload[1:2, :] = jnp.sum(weight * hdot(cover, weight), axis=0, keepdims=True)
    payload[2:3, :] = zero + held
    payload[5:6, :] = square

    if fused:
        vector = jnp.where(dp < half, start[0:1, :], start[1:2, :])
        own_rows = main[...].astype(F32)
        edge_rows = bound[...].astype(F32)
        along = jnp.sum(own_rows * vector, axis=1, keepdims=True)
        edge_along = jnp.sum(edge_rows * vector, axis=1, keepdims=True)
        payload[3:4, :] = jnp.sum(own_rows * along, axis=0, keepdims=True) + jnp.sum(
            edge_rows * edge_along, axis=0, keepdims=True
        )
        payload[4:5, :] = zero + (
            jnp.sum(along * along, axis=0, keepdims=True)
            + jnp.sum(edge_along * edge_along, axis=0, keepdims=True)
        )
    else:
        payload[3:4, :] = start[0:1, :]
        payload[4:5, :] = start[1:2, :]

    first = ex_a.at[0]
    first[dp] = payload[...]
    one_level = Spread("dp", n_dp, payload, first, a_send.at[0], a_recv.at[0])
    one_level.start()
    if fused:
        one.own(early[2:], (0, 1), True)
        two.own(early[2:], (1,), False)
        put_seam()
        one.own(final, (0, 1), True)
        two.own(final, (1,), False)
    for n in range(images):
        blank = jnp.zeros((1, side, 3 * width), BF16)
        xcat[n, 0:1] = blank
        xcat[n, side + 1 : side + 2] = blank
    if fused:
        one.column(1, every)
    one_level.wait()
    second = ex_b.at[0]
    mean, spread, cell_count = join_moments(first)
    passed = one_b.at[0]
    passed[...] = jnp.zeros(passed.shape, F32)
    passed[0:1, :] = mean
    passed[1:2, :] = spread
    passed[2:3, :] = cell_count
    vectors, squares = rows_of(first, 3), rows_of(first, 4)
    passed[3:4, :] = total(vectors[:half])
    passed[4:5, :] = total(vectors[half:])
    passed[5:6, :] = total(squares[:half])
    passed[6:7, :] = total(squares[half:])
    passed[7:8, :] = total(rows_of(first, 5))
    second[rep] = passed[...]
    two_level = Spread("replica", n_rep, passed, second, b_send.at[0], b_recv.at[0])
    two_level.start()
    if fused:
        one.neighbours(1, every[:2])
        one.column(0, every[:2])
        one.neighbours(1, every[2:])
        one.column(0, every[2:])
        two.own(every, (0,), False)
        two.hop(1)
    prepare_head(
        indices, table, inducing, lengthscale, var_mean, var_lower, chol_out, z_pad, v_pad, f_pad, noise
    )
    two_level.wait()
    mean, spread, pixels = join_moments(second)
    inverse_one = lax.rsqrt(spread / pixels + EPS_NORM)
    joined = [total(rows_of(second, row)) for row in range(3, 8)]
    sigma_rows, start_rows = [], []
    for l in range(2):
        vec = jnp.sqrt(jnp.sum(joined[l] * joined[l], axis=1, keepdims=True))
        base = jnp.sqrt(joined[2 + l])
        sigma_rows.append(zero + vec / base)
        start_rows.append(base)
        stats[8 + l : 9 + l, :] = joined[l] / vec
    stats[0:1, :] = mean
    stats[1:2, :] = inverse_one
    stats[2:3, :] = pixels
    stats[4:5, :] = sigma_rows[0]
    stats[5:6, :] = sigma_rows[1]
    stats[6:7, :] = start_rows[0]
    stats[7:8, :] = start_rows[1]
    stats[10:11, :] = joined[4]
    scale_one = inverse_one * norms[0:1, :]
    shift_one = norms[1:2, :] - mean * scale_one

    def act_one(n, part):
        def step(i, carry):
            first_row = i * BLOCK
            pixel = pl.ds(pl.multiple_of(first_row * side, BLOCK * side), BLOCK * side)
            out = bdot(patches[n, :, pixel], stem[...], ((0,), (0,)))
            values = jax.nn.gelu(out * scale_one + shift_one)
            store_shifted(xcat, n, first_row, BLOCK, values, side)
            return carry
        half_steps = side // BLOCK // 2
        lax.fori_loop(part * half_steps, (part + 1) * half_steps, step, 0)

    for n in range(images):
        for part in range(2):
            act_one(n, part)
        if fused and n == 0:
            one.neighbours(0, every[:2])
    if fused:
        one.opposite(1)
        one.from_core(1)
    else:
        copy_in.wait()
    x_copies = [
        pltpu.make_async_copy(
            xcat.at[n, pl.ds(1, side), :, pl.ds(width, width)], x_out.at[n], local.at[2 + n]
        )
        for n in range(images)
    ]
    for copy in x_copies:
        copy.start()

    tap_row = 3 * width
    middle = -(-(9 * width // 2 - tap_row) // 128) * 128
    rows_step = 2 * BLOCK * side

    def window(n, i, r, lanes):
        return xcat[n, pl.ds(i * 2 * BLOCK + r, 2 * BLOCK), :, lanes].reshape(rows_step, -1)

    def at_rows(n, i):
        return pl.ds(pl.multiple_of(n * cells + i * rows_step, rows_step), rows_step)

    for n in range(images):
        def later_half(i, carry):
            y[at_rows(n, i), :] = bdot(
                window(n, i, 2, slice(0, tap_row)), k1[2 * tap_row : 3 * tap_row, :]
            ) + bdot(
                window(n, i, 1, slice(middle, tap_row)), k1[tap_row + middle : 2 * tap_row, :]
            )
            return carry
        lax.fori_loop(0, side // (2 * BLOCK), later_half, 0)
        if fused and n == 0:
            one.neighbours(0, every[2:])
            two.hop(2)
            two.plane(0, two.z >= 0, 2)
            two.plane(1, two.z > 0, 2)
    if fused:
        one.opposite(0)
        one.from_core(0)
    k1_copies = [
        pltpu.make_async_copy(
            k1.at[pl.ds((8 - t) * width, width), :],
            k1_out.at[t // 3, :, pl.ds((t % 3) * width, width)],
            turn.at[t],
        )
        for t in range(9)
    ]
    for copy in k1_copies:
        copy.start()
    moments = []
    y_copies = []
    for n in range(images):
        def first_half(i, carry):
            acc = (
                y[at_rows(n, i), :]
                + bdot(window(n, i, 0, slice(0, tap_row)), k1[0:tap_row, :])
                + bdot(window(n, i, 1, slice(0, middle)), k1[tap_row : tap_row + middle, :])
            )
            y[at_rows(n, i), :] = acc
            return carry + jnp.sum(acc, axis=0, keepdims=True)
        whole = lax.fori_loop(0, side // (2 * BLOCK), first_half, zero)
        if fused and n == 0:
            two.plane(1, two.z == 0, 2)
        average = whole / cells
        def spread_step(i, carry):
            pixel = pl.ds(pl.multiple_of(n * cells + i * BLOCK * side, 16), BLOCK * side)
            off = y[pixel, :] - average
            return carry + jnp.sum(off * off, axis=0, keepdims=True)
        moments.append((average, lax.fori_loop(0, side // BLOCK, spread_step, zero)))
        copy = pltpu.make_async_copy(
            y.at[pl.ds(n * cells, cells), :], y_out.at[pl.ds(n * cells, cells), :], local.at[4 + n]
        )
        copy.start()
        y_copies.append(copy)
    payload_two = tw_one.at[0]
    counts_in = [v * cells for v in valid]
    average = total([m[0] * c for m, c in zip(moments, counts_in)]) / held
    payload_two[...] = jnp.zeros(payload_two.shape, F32)
    payload_two[0:1, :] = average
    payload_two[1:2, :] = total([
        v * m[1] + c * (m[0] - average) * (m[0] - average)
        for m, c, v in zip(moments, counts_in, valid)
    ])
    payload_two[2:3, :] = zero + held
    first = tw_a
    first[dp] = payload_two[...]
    three_level = Spread("dp", n_dp, payload_two, first, a_send.at[1], a_recv.at[1])
    three_level.start()
    if fused:
        two.neighbours(0, every)
    three_level.wait()
    mean, spread, cell_count = join_moments(first)
    second = tw_b
    passed = tw_one.at[1]
    passed[...] = jnp.zeros(passed.shape, F32)
    passed[0:1, :] = mean
    passed[1:2, :] = spread
    passed[2:3, :] = cell_count
    second[rep] = passed[...]
    four_level = Spread("replica", n_rep, passed, second, b_send.at[1], b_recv.at[1])
    four_level.start()
    if fused:
        two.neighbours(1, every[:2])
    four_level.wait()
    mean, spread, _ = join_moments(second)
    sigma = sigma_rows[0]
    variance = spread / pixels / (sigma * sigma)
    inverse_two = lax.rsqrt(variance + EPS_NORM) / sigma
    stats[3:4, :] = mean
    stats[11:12, :] = inverse_two
    scale_two = inverse_two * norms[2:3, :]
    shift_two = norms[3:4, :] - mean * scale_two
    select = window_matrix(side)
    act_copies = []
    for n in range(images):
        def step(i, carry):
            pixel = pl.ds(pl.multiple_of(n * cells + i * BLOCK * side, 16), BLOCK * side)
            values, steep = gelu_both(y[pixel, :] * scale_two + shift_two)
            slope[pixel, :] = steep
            act[pixel, :] = values.astype(BF16)
            return carry
        lax.fori_loop(0, side // BLOCK, step, 0)
        pixels_of = pl.ds(n * cells, cells)
        for k, (made, out) in enumerate((
            (slope.at[pixels_of, :], slope_out.at[pixels_of, :]),
            (act.at[pixels_of, :], act_out.at[pixels_of, :]),
        )):
            copy = pltpu.make_async_copy(made, out, local.at[6 + 2 * k + n])
            copy.start()
            act_copies.append(copy)
        windows[n] = bdot(select, act[n * cells : (n + 1) * cells, :], ((0,), (0,)))
        if fused and n == 0:
            two.neighbours(1, every[2:])
            two.opposite(two.order[0])
    if fused:
        two.opposite(two.order[1])
        for zi in two.order:
            two.from_core(zi)
        one.drain()
        two.drain()
        pl.when(~even)(seam_copy.wait_send)
    for level in (one_level, two_level, three_level, four_level):
        level.drain()
    for copy in k1_copies + x_copies + y_copies + act_copies:
        copy.wait()


def forward(n_dp, n_rep, side, share, fused, counts, indices, weights, pictures, stem, start, norms,
            table, inducing, lengthscale, var_mean, var_lower):
    images, cells = pictures.shape[0], side * side
    width = stem.shape[1]
    half = n_dp // 2
    sources = max(n_dp // 4, 1)
    shape = jax.ShapeDtypeStruct
    sem = pltpu.SemaphoreType.DMA
    kernel_rows = 9 * width
    return pl.pallas_call(
        functools.partial(forward_kernel, n_dp, n_rep, side, share, fused),
        out_shape=(
            shape((3, width, 3 * width), BF16),
            shape((kernel_rows, width), BF16),
            shape((images, side, side, width), BF16),
            shape((images * cells, width), F32),
            shape((images * cells, width), F32),
            shape((images * cells, width), BF16),
            shape((images, 16, width), F32),
            shape((images, width), F32),
            shape((16, width), F32),
            shape((images, 32, cells), BF16),
            shape((32, width), BF16),
            shape((3, IND, IND), F32),
            shape((IND, width), F32),
            shape((16, IND), F32),
            shape((IND, var_mean.shape[0] * IND), F32),
            shape((images, 16, 16), F32),
        ),
        in_specs=[SMEM, SMEM, VMEM if fused else ANY] + [VMEM] * 9,
        out_specs=(ANY,) * 6 + (VMEM,) * 10,
        scratch_shapes=[
            pltpu.VMEM((32, cells), F32),
            pltpu.VMEM((share if fused else 8, width), F32),
            pltpu.VMEM((share - 8 if fused else 16, width), BF16),
            pltpu.VMEM((16, width), BF16),
            pltpu.VMEM((kernel_rows, width), BF16),
            pltpu.VMEM((images, side + 2, side, 3 * width), BF16),
            pltpu.VMEM((images * cells, width), F32),
            pltpu.VMEM((images * cells, width), BF16),
            pltpu.VMEM((images * cells, width), F32),
            pltpu.VMEM((2, 16, width), BF16),
            pltpu.VMEM((1, n_dp, 8, width), F32),
            pltpu.VMEM((1, n_rep, 8, width), F32),
            pltpu.VMEM((1, 8, width), F32),
            pltpu.VMEM((1, 8, width), F32),
            pltpu.VMEM((n_dp, 4, width), F32),
            pltpu.VMEM((n_rep, 4, width), F32),
            pltpu.VMEM((2, 4, width), F32),
            sem((2, sources, PIECES, 2)),
            sem((2, sources, PIECES)),
            sem((2, sources, PIECES, 4)),
            sem((2, sources, PIECES, 4)),
            sem((2, sources, PIECES, 4)),
            sem((2, sources, PIECES, 4)),
            sem((2, n_dp)),
            sem((2, n_dp)),
            sem((2, n_rep)),
            sem((2, n_rep)),
            sem((1,)),
            sem((1,)),
            sem((11,)),
            sem((9,)),
        ],
        compiler_params=pltpu.CompilerParams(
            collective_id=0, has_side_effects=True, vmem_limit_bytes=56 << 20
        ),
    )(counts, indices, weights, pictures, stem, start, norms,
      table, inducing, lengthscale, var_mean, var_lower)


class Reduce:
    def __init__(self, near, far, src, parts, whole, planes, out, sems):
        (self.axis, self.size), (self.other, self.others) = near, far
        self.src, self.parts, self.whole, self.planes, self.out = src, parts, whole, planes, out
        self.a_send, self.a_recv = sems[:2]
        self.b_send, self.b_recv, self.c_send, self.c_recv = sems[2:] or [None] * 4
        self.me = lax.axis_index(self.axis)

    def scatter(self):
        for j in range(1, self.size):
            peer = lax.rem(self.me + j, self.size)
            yield remote(
                self.src.at[peer], self.parts.at[self.me], self.a_send.at[j], self.a_recv.at[j],
                {self.axis: peer},
            )

    def start(self):
        for copy in self.scatter():
            copy.start()
        self.parts[self.me] = self.src[self.me]

    def arrive(self):
        for j in range(1, self.size):
            source = lax.rem(self.me + self.size - j, self.size)
            remote(
                self.src.at[source], self.parts.at[source], self.a_send.at[j], self.a_recv.at[j],
                {self.axis: source},
            ).wait_recv()
        self.whole[...] = total([self.parts[i] for i in range(self.size)])

    def middle(self):
        self.arrive()
        self.across()

    def across(self):
        self.planes[lax.axis_index(self.other)] = self.whole[...]
        self.second = Spread(
            self.other, self.others, self.whole, self.planes, self.b_send, self.b_recv
        )
        self.second.start()

    def last(self):
        self.second.wait()
        self.out[self.me] = total([self.planes[i] for i in range(self.others)])
        self.third = Spread(
            self.axis, self.size, self.out.at[self.me], self.out, self.c_send, self.c_recv
        )
        self.third.start()

    def finish(self):
        self.finish_last()
        self.drain()

    def drain(self):
        for copy in self.scatter():
            copy.wait_send()

    def finish_last(self):
        self.third.wait()
        self.second.drain()
        self.third.drain()


def reduce_scratch(size, others, rows, width):
    per = -(-rows // size)
    sem = pltpu.SemaphoreType.DMA
    return [
        pltpu.VMEM((size, per, width), F32),
        pltpu.VMEM((size, per, width), F32),
        pltpu.VMEM((per, width), F32),
        pltpu.VMEM((others, per, width), F32),
        pltpu.VMEM((size, per, width), F32),
        sem((size,)), sem((size,)), sem((others,)), sem((others,)), sem((size,)), sem((size,)),
    ]


def put_rows(ref, first, values):
    per = ref.shape[1]
    for k in range(values.shape[0]):
        row = first + k
        ref[row // per, row % per : row % per + 1, :] = values[k : k + 1, :]


def gelu_slope(x):
    return gelu_both(x)[1]


def fold(values):
    return jnp.sum(values.reshape(values.shape[0] // 8, 8, values.shape[1]), axis=0)


def head_kernel(
    n_dp, n_rep, side, size, classes, samples,
    counts, labels, k2_in, y_in, slope_in, windows, stem_pool, stats, norms,
    lengthscale, chol, z_pad, v_pad, f_pad, noise,
    cat_out, k8_out, head_out, grads_out,
    k2, k8, y, d_pre, cat, pattern, x_pad, kx_pad, d_rows,
    ex_a, ex_b, one_a, one_b, a_send, a_recv, b_send, b_recv, local,
):
    images = stem_pool.shape[0]
    width = stem_pool.shape[1]
    cells = side * side
    dp, rep = lax.axis_index("dp"), lax.axis_index("replica")
    loads = [
        pltpu.make_async_copy(k2_in, k2, local.at[0]),
        pltpu.make_async_copy(y_in, y, local.at[1]),
        pltpu.make_async_copy(slope_in, d_pre, local.at[2]),
    ]
    for copy in loads:
        copy.start()
    greeted = greet(n_dp, n_rep)

    sigma_one, sigma_two = stats[4:5, :], stats[5:6, :]
    pixels = stats[2:3, :]
    scale = cells / stats[2:3, 0:1]
    ell = lengthscale[...].reshape(1, width)
    zs = z_pad[...]
    ones = jnp.ones((8, width), F32)
    group = lax.broadcasted_iota(jnp.int32, (classes * IND, 16), 0) // IND
    which = lax.broadcasted_iota(jnp.int32, (classes * IND, 16), 1)
    groups = jnp.where(group == which, 1.0, 0.0)

    loads[0].wait()
    pooled_raw = jnp.zeros((16, width), F32)
    for t in range(9):
        parts = []
        rest = [windows[n, t : t + 1, :] for n in range(images)]
        for _ in range(3):
            parts += [r.astype(BF16).astype(F32) for r in rest]
            rest = [r - p for r, p in zip(rest, parts[-images:])]
        parts.append(jnp.zeros((16 - 3 * images, width), F32))
        lhs = jnp.concatenate(parts, axis=0).astype(BF16)
        pooled_raw = pooled_raw + bdot(lhs, k2[t * width : (t + 1) * width, :])
    x_pad[...] = jnp.zeros(x_pad.shape, F32)
    branch_pool = []
    for n in range(images):
        row = total([pooled_raw[k * images + n : k * images + n + 1] for k in range(3)])
        branch_pool.append(row / (cells * sigma_two))
        x_pad[n : n + 1, :] = (stem_pool[n : n + 1, :] + branch_pool[n]) / ell
    xs = x_pad[...]

    kx_pad[...] = jnp.zeros(kx_pad.shape, F32)
    for n in range(images):
        off = zs - xs[n : n + 1, :]
        kx_pad[n : n + 1, :] = jnp.exp(-0.5 * hdot(ones, off * off, ((1,), (1,))))[0:1]
    lanes = lax.broadcasted_iota(jnp.int32, (8, IND), 1)
    kx = jnp.where(lanes < size, kx_pad[...], 0.0)
    inv = chol[2]
    means = v_pad[...]
    factors = f_pad[...]
    proj = hdot(kx, inv, ((1,), (1,)))
    average = hdot(proj, means, ((1,), (1,)))
    spread = hdot(proj, factors)
    variance = (
        1.0 - jnp.sum(proj * proj, axis=1, keepdims=True) + hdot(spread * spread, groups)
    )
    std = jnp.sqrt(variance)
    class_lane = lax.broadcasted_iota(jnp.int32, (1, 16), 1)
    sample_row = lax.broadcasted_iota(jnp.int32, (16, 16), 0)
    inside = (lax.broadcasted_iota(jnp.int32, (16, 16), 1) < classes) & (sample_row < samples)
    count = counts[0]
    loss = jnp.zeros((1, 1), F32)
    g_avg_rows, g_var_rows = [], []
    for n in range(images):
        drawn = average[n : n + 1, :] + std[n : n + 1, :] * noise[n]
        drawn = jnp.where(inside, drawn, -1e30)
        shifted = drawn - jnp.max(drawn, axis=1, keepdims=True)
        exps = jnp.where(inside, jnp.exp(shifted), 0.0)
        sums = jnp.sum(exps, axis=1, keepdims=True)
        sums = jnp.where(sample_row[:, 0:1] < samples, sums, 1.0)
        hot = jnp.where(class_lane == labels[n], 1.0, 0.0)
        picked = jnp.where(inside, (shifted - jnp.log(sums)) * hot, 0.0)
        held = jnp.where(count > n, 1.0 / samples, 0.0)
        loss = loss - held * jnp.sum(jnp.sum(picked, axis=1, keepdims=True), axis=0, keepdims=True)
        g_samples = jnp.where(inside, exps / sums - hot, 0.0) * (held * scale)
        g_avg_rows.append(jnp.sum(g_samples, axis=0, keepdims=True))
        g_var_rows.append(
            0.5 * jnp.sum(g_samples * noise[n], axis=0, keepdims=True) / std[n : n + 1, :]
        )
    blank = [jnp.zeros((8 - images, 16), F32)]
    g_avg = jnp.concatenate(g_avg_rows + blank, axis=0)
    g_var = jnp.concatenate(g_var_rows + blank, axis=0)
    g_spread = 2.0 * spread * hdot(g_var, groups, ((1,), (1,)))
    g_proj = (
        hdot(g_avg, means)
        - 2.0 * proj * jnp.sum(g_var, axis=1, keepdims=True)
        + hdot(g_spread, factors, ((1,), (1,)))
    )
    g_kx = hdot(g_proj, inv)
    weights = -kx * g_kx
    g_x = xs * jnp.sum(weights, axis=1, keepdims=True) - hdot(weights, zs)
    d_pooled = g_x / ell
    d_rows[...] = jnp.zeros(d_rows.shape, BF16)
    d_rows[0:8, :] = (d_pooled / cells).astype(BF16)
    d_two = d_rows[...]

    taps = [
        bdot(d_two, k2[t * width : (t + 1) * width, :], ((1,), (1,))) / sigma_two for t in range(9)
    ]
    wide = lax.broadcasted_iota(jnp.int32, (side, 1), 0)
    for n in range(images):
        for kind, kept in enumerate(((0, 1), (0, 1, 2), (1, 2))):
            across = [total([taps[3 * r + c][n : n + 1] for r in kept]) for c in range(3)]
            middle = across[0] + across[1] + across[2]
            pattern[n, kind] = jnp.where(
                wide == 0, across[0] + across[1],
                jnp.where(wide == side - 1, across[1] + across[2], middle),
            )

    loads[1].wait()
    loads[2].wait()
    mean_two, inverse_two = stats[3:4, :], stats[11:12, :]
    gain = norms[2:3, :]
    none = jnp.zeros((8, width), F32)
    sums = (none, none)
    for n in range(images):
        def step(h, carry):
            kind = jnp.where(h == 0, 0, jnp.where(h == side - 1, 2, 1))
            at = pl.ds(pl.multiple_of(n * cells + h * side, side), side)
            normed = (y[at, :] - mean_two) * inverse_two
            grad = d_pre[at, :] * pattern[n, kind]
            d_pre[at, :] = grad
            return carry[0] + fold(grad), carry[1] + fold(grad * normed)
        sums = lax.fori_loop(0, side, step, sums)
    one_a[...] = jnp.zeros(one_a.shape, F32)
    one_a[0:1, :] = jnp.sum(sums[0], axis=0, keepdims=True)
    one_a[1:2, :] = jnp.sum(sums[1], axis=0, keepdims=True)
    one_a[2:3, :] = total([
        cells * branch_pool[n] * d_two[n : n + 1, :].astype(F32) for n in range(images)
    ])
    ex_a[dp] = one_a[...]
    first = Spread("dp", n_dp, one_a, ex_a, a_send, a_recv)
    greeted()
    first.start()

    grads_out[...] = jnp.zeros(grads_out.shape, F32)
    over = hdot(weights, jnp.ones((8, 128), F32), ((0,), (0,)))[:, 0:1]
    g_z = zs * over - hdot(weights, xs, ((0,), (0,)))
    grads_out[0:size, :] = g_z[0:size]
    grads_out[20:21, :] = jnp.sum(g_x * xs, axis=0, keepdims=True)
    grads_out[23:24, :] = jnp.zeros((1, width), F32) + loss
    grads_out[32:64, 0 : classes * IND] = hdot(proj, g_spread, ((0,), (0,)))
    grads_out[32:64, 384 : 384 + IND] = hdot(g_kx, proj, ((0,), (0,)))
    grads_out[32:48, 512 : 512 + IND] = hdot(g_avg, proj, ((0,), (0,)))
    head_out[...] = jnp.zeros(head_out.shape, F32)
    head_out[0:8, :] = d_pooled
    head_out[18:19, :] = cells / pixels
    head_out[8:16, :] = d_two[0:8, :].astype(F32)

    def eighth(t, carry):
        at = pl.ds(pl.multiple_of(t * (width // 2), width // 2), width // 2)
        k8[at, :] = (k2[at, :].astype(F32) * KERNEL_SCALE).astype(F8)
        return carry

    lax.fori_loop(0, 9, eighth, 0)
    first.wait()
    one_b[...] = total([ex_a[i] for i in range(n_dp)])
    ex_b[rep] = one_b[...]
    second = Spread("replica", n_rep, one_b, ex_b, b_send, b_recv)
    second.start()
    lax.fori_loop(9, 18, eighth, 0)
    k8_copy = pltpu.make_async_copy(k8, k8_out, local.at[3 + images])
    k8_copy.start()
    second.wait()
    joined = total([ex_b[i] for i in range(n_rep)])
    d_bias, d_gain = joined[0:1, :], joined[1:2, :]
    head_out[16:17, :] = d_gain
    head_out[17:18, :] = d_bias
    head_out[19:20, :] = joined[2:3, :]
    true_scale = inverse_two * sigma_one * gain
    cat_copies = []
    for n in range(images):
        held = jnp.where(count > n, 1.0, 0.0)
        def step(i, carry):
            rows = BLOCK * side
            at = pl.ds(pl.multiple_of(n * cells + i * rows, rows), rows)
            normed = (y[at, :] - mean_two) * inverse_two
            grad = (true_scale * held) * (
                d_pre[at, :] - d_bias / pixels - normed * (d_gain / pixels)
            )
            cat[at, :] = grad.astype(BF16)
            return carry
        lax.fori_loop(0, side // BLOCK, step, 0)
        here = pl.ds(n * cells, cells)
        copy = pltpu.make_async_copy(cat.at[here, :], cat_out.at[here, :], local.at[3 + n])
        copy.start()
        cat_copies.append(copy)
    for level in (first, second):
        level.drain()
    for copy in cat_copies + [k8_copy]:
        copy.wait()


def head(n_dp, n_rep, side, size, classes, samples, counts, labels, k2, y, slope, windows, stem_pool,
         stats, norms, lengthscale, chol, z_pad, v_pad, f_pad, noise):
    images, width = stem_pool.shape
    shape = jax.ShapeDtypeStruct
    sem = pltpu.SemaphoreType.DMA
    return pl.pallas_call(
        functools.partial(head_kernel, n_dp, n_rep, side, size, classes, samples),
        out_shape=(
            shape(y.shape, BF16),
            shape(k2.shape, F8),
            shape((24, width), F32),
            shape((64, width), F32),
        ),
        in_specs=[SMEM, SMEM, ANY, ANY, ANY] + [VMEM] * 10,
        out_specs=(ANY, ANY, VMEM, VMEM),
        scratch_shapes=[
            pltpu.VMEM(k2.shape, BF16),
            pltpu.VMEM(k2.shape, F8),
            pltpu.VMEM(y.shape, F32),
            pltpu.VMEM(y.shape, F32),
            pltpu.VMEM(y.shape, BF16),
            pltpu.VMEM((images, 3, side, width), F32),
            pltpu.VMEM((8, width), F32),
            pltpu.VMEM((8, IND), F32),
            pltpu.VMEM((16, width), BF16),
            pltpu.VMEM((n_dp, 4, width), F32),
            pltpu.VMEM((n_rep, 4, width), F32),
            pltpu.VMEM((4, width), F32),
            pltpu.VMEM((4, width), F32),
            sem((n_dp,)), sem((n_dp,)), sem((n_rep,)), sem((n_rep,)),
            sem((4 + images,)),
        ],
        compiler_params=pltpu.CompilerParams(
            collective_id=1, has_side_effects=True, vmem_limit_bytes=56 << 20
        ),
    )(counts, labels, k2, y, slope, windows, stem_pool, stats, norms,
      lengthscale, chol, z_pad, v_pad, f_pad, noise)


def greet_all(n_dp, n_rep):
    here = lax.axis_index("dp") * n_rep + lax.axis_index("replica")
    count = n_dp * n_rep
    barrier = pltpu.get_barrier_semaphore()

    def signal(j, carry):
        other = lax.rem(here + j, count)
        pl.semaphore_signal(
            barrier, inc=1, device_id={"dp": other // n_rep, "replica": lax.rem(other, n_rep)},
            device_id_type=MESH,
        )
        return carry

    lax.fori_loop(1, count, signal, 0)
    return lambda: pl.semaphore_wait(barrier, count - 1)


def chunk_plan(share, width, count):
    def segments(first, last, base):
        result = []
        while first < last:
            c = (first - base) // width
            end = min(last, base + (c + 1) * width)
            result.append((c, first - base - c * width, end - base - c * width))
            first = end
        return result

    plan, done, carried = [], 0, 0
    for r in range(3):
        first, last = r * 3 * width, (r + 1) * 3 * width
        items = []
        while done < count and (done + 1) * share <= last:
            begin = max(done * share, first)
            items.append((done, carried, segments(begin, (done + 1) * share, first)))
            carried = 0
            done += 1
        begin = max(done * share, first)
        plan.append((items, segments(begin, last, first)))
        carried = last - begin
    return plan


def chain_pieces(share):
    tiles = (share + 8) // 16
    count = min(4, max(tiles, 1))
    edges = [tiles * i // count * 16 for i in range(count + 1)]
    return [(lo, hi - lo) for lo, hi in zip(edges, edges[1:])]


def backward_kernel(
    n_dp, n_rep, side, share, fused,
    counts, d_in, x_in, k1_in, k8_in, act_in, patches, stem, stats, norms, windows, head_rows, grads,
    part_out, big_out, sums_out, late_out,
    cat, d_one, x, k1, k8, cat8, held_rows, carry, mine, sib, rin, zin, zout, part, comb, wall, flat, flat_d,
    *rest,
):
    early = rest[0:11]
    late = rest[11:15]
    (c_send, c_recv, r_send, r_recv, z_send, z_recv, w_send, w_recv, local) = rest[15:]
    images = patches.shape[0]
    width = stem.shape[1]
    cells = side * side
    dp, rep = lax.axis_index("dp"), lax.axis_index("replica")
    core, z = lax.rem(dp, 2), dp // 2
    n_z, half = n_dp // 2, n_dp // 2
    sources = max(n_dp // 4, 1)
    owners = half * n_rep
    here = dp * n_rep + rep
    loads = [
        pltpu.make_async_copy(d_in, d_one, local.at[0]),
        pltpu.make_async_copy(x_in, x, local.at[1]),
        pltpu.make_async_copy(k1_in, k1, local.at[2]),
        pltpu.make_async_copy(k8_in, k8, local.at[3]),
    ]
    for copy in loads:
        copy.start()
    greeted = greet_all(n_dp, n_rep)
    count = counts[0]
    valid = [jnp.where(count > n, 1.0, 0.0) for n in range(images)]

    early_sum = Reduce(("dp", n_dp), ("replica", n_rep), *early[:5], early[5:])

    def first_tap(owner):
        return jnp.minimum((owner * share) // width, 7)

    def window_copy(owner):
        return remote(
            comb.at[pl.ds(first_tap(owner), 2)], wall.at[here], w_send.at[owner], w_recv.at[here],
            {"dp": half + owner // n_rep, "replica": lax.rem(owner, n_rep)},
        )

    def send_windows(j, c):
        owner = lax.rem(here + j, owners)

        @pl.when(half * n_rep + owner != here)
        def _():
            window_copy(owner).start()
        return c

    def first_rows():
        source = early[0]
        source[...] = jnp.zeros(source.shape, F32)
        put_rows(source, 0, grads[...])
        gram = total([
            bdot(patches[n], patches[n], ((1,), (1,))) * valid[n] for n in range(images)
        ])
        wide = jnp.concatenate([gram, jnp.zeros((32, 128 - 32), F32)], axis=1)
        per = source.shape[1]
        for k in range(32):
            row = 64 + k
            source[row // per, row % per : row % per + 1, 0:128] = wide[k : k + 1, :]
        if fused:
            for t in range(9):
                comb[t, 0:images, :] = jnp.concatenate(
                    [windows[n, t : t + 1, :] for n in range(images)], axis=0
                )
                comb[t, images : 2 * images, :] = head_rows[8 : 8 + images, :]

    def first_sends():
        early_sum.start()
        if fused:
            lax.fori_loop(0, owners, send_windows, 0)

    def row_of_taps(r):
        return total([
            lax.dot_general(
                x[n].reshape(cells, width),
                cat[n, pl.ds(2 - r, side)].reshape(cells, 3 * width),
                (((0,), (0,)), ((), ())),
                preferred_element_type=F32,
            )
            for n in range(images)
        ])

    def joined(acc, parts):
        pieces = [acc[a:b, (2 - c) * width : (3 - c) * width] for c, a, b in parts]
        return pieces[0] if len(pieces) == 1 else jnp.concatenate(pieces, axis=0)

    def sib_copy(o):
        return remote(
            mine.at[o], sib.at[(o // (2 * n_rep)) * n_rep + o % n_rep],
            c_send.at[o], c_recv.at[(o // (2 * n_rep)) * n_rep + o % n_rep],
            {"dp": dp + 1 - 2 * core},
        )

    def ship(acc, items, leftover):
        for o, carried, parts in items:
            value = joined(acc, parts)
            if carried:
                value = jnp.concatenate([carry[0:carried, :], value], axis=0)
            mine[o, 0:share, :] = value.astype(BF16)
            pl.when(core != (o // n_rep) % 2)(sib_copy(o).start)
        if leftover:
            value = joined(acc, leftover)
            carry[0 : value.shape[0], :] = value

    reps = (rep, rep + 1 - 2 * lax.rem(rep, 2), rep + 2 - 4 * (rep // 2), 3 - rep)
    cut = (share + 8) // 32 * 16
    halves = (pl.ds(0, cut), pl.ds(cut, share + 8 - cut))

    def slot(zi, k):
        return (zi * 2 + core) * n_rep + reps[k]

    def plane_copies(zi, step):
        for h in range(2):
            near, far = 1 + h, 2 - h
            at = halves[h]
            if step == 0:
                for s, k in enumerate((near, 3)):
                    yield remote(
                        mine.at[slot(zi, k), at, :], rin.at[zi, s, at, :],
                        r_send.at[zi, 2 * s + h], r_recv.at[zi, 2 * s + h], {"replica": reps[near]},
                    )
            else:
                yield remote(
                    mine.at[slot(zi, far), at, :], rin.at[zi, 2, at, :],
                    r_send.at[zi, 4 + h], r_recv.at[zi, 4 + h], {"replica": reps[far]},
                )

    def join_cores(zi):
        for k in (3, 1, 2, 0):
            at = zi * n_rep + reps[k]
            remote(
                mine.at[0], sib.at[at], c_send.at[0], c_recv.at[at], {"dp": dp + 1 - 2 * core}
            ).wait_recv()
            mine[slot(zi, k)] = (
                mine[slot(zi, k)].astype(F32) + sib[at].astype(F32)
            ).astype(BF16)
        for copy in plane_copies(zi, 0):
            copy.start()

    def join_near(zi):
        for copy in plane_copies(zi, 0):
            copy.wait_recv()
        for h in range(2):
            at, o = halves[h], slot(zi, 2 - h)
            mine[o, at, :] = (
                mine[o, at, :].astype(F32) + rin[zi, 1, at, :].astype(F32)
            ).astype(BF16)
        for copy in plane_copies(zi, 1):
            copy.start()

    def join_far(zi):
        for copy in plane_copies(zi, 1):
            copy.wait_recv()
        part[zi] = (
            mine[slot(zi, 0)].astype(F32) + rin[zi, 0].astype(F32) + rin[zi, 2].astype(F32)
        )

    z_pieces = chain_pieces(share)
    every = range(len(z_pieces))

    def z_copy(zi, piece, down):
        start, rows = z_pieces[piece]
        at = pl.ds(start, rows)
        step = n_dp - 2 if down else 2
        return remote(
            zout.at[zi, at, :], zin.at[zi, int(down), at, :],
            z_send.at[zi, piece], z_recv.at[zi, piece, int(down)],
            {"dp": lax.rem(dp + step, n_dp)},
        )

    def chain(zi, distance, *pieces):
        for down in (True, False):
            reach = n_z - 1 - zi if down else zi
            if distance > reach:
                continue
            offset = distance if down else -distance
            @pl.when(z == zi + offset)
            def _():
                for piece in pieces or every:
                    start, rows = z_pieces[piece]
                    at = pl.ds(start, rows)
                    if distance < reach:
                        z_copy(zi, piece, down).wait_recv()
                        part[zi, at, :] += zin[zi, int(down), at, :].astype(F32)
                    if distance:
                        zout[zi, at, :] = part[zi, at, :].astype(BF16)
                        z_copy(zi, piece, down).start()

    def window_part():
        @pl.when(dp >= half)
        def _():
            owner = here - owners
            wall[here] = comb[pl.ds(first_tap(owner), 2)]

            def take(j, c):
                origin = lax.rem(here + j, n_dp * n_rep)
                remote(
                    comb.at[pl.ds(0, 2)], wall.at[origin], w_send.at[0], w_recv.at[origin],
                    {"dp": origin // n_rep, "replica": lax.rem(origin, n_rep)},
                ).wait_recv()
                return c

            lax.fori_loop(1, n_dp * n_rep, take, 0)
            for s in range(n_dp * n_rep):
                for tap in range(2):
                    flat[tap, s * images : (s + 1) * images, :] = wall[s, tap, 0:images, :]
                flat_d[s * images : (s + 1) * images, :] = wall[s, 0, images : 2 * images, :]
            for tap in range(2):
                held_rows[tap * width : (tap + 1) * width, :] = hdot(
                    flat[tap], flat_d[...], ((0,), (0,))
                )
            offset = owner * share - first_tap(owner) * width
            part_out[...] = held_rows[pl.ds(pl.multiple_of(offset, 8), share), :]

    for n in range(images):
        edge = jnp.zeros((1, side, 3 * width), BF16)
        cat[n, 0:1] = edge
        cat[n, side + 1 : side + 2] = edge
    first_rows()
    loads[0].wait()
    for n in range(images):
        def shift_gradient(i, carried):
            rows = BLOCK * side
            at = pl.ds(pl.multiple_of(n * cells + i * rows, rows), rows)
            store_shifted(cat, n, i * BLOCK, BLOCK, d_one[at, :].astype(F32), side)
            return carried
        lax.fori_loop(0, side // BLOCK, shift_gradient, 0)
    greeted()
    first_sends()
    loads[1].wait()
    if fused:
        plan = chunk_plan(share, width, owners)
        for r in range(3):
            acc = row_of_taps(r)
            if r > 0:
                pl.when(core == r - 1)(lambda: join_cores(0))
            ship(acc, *plan[r])
            if r == 1:
                early_sum.middle()
    else:
        for r in range(3):
            acc = row_of_taps(r)
            for c in range(3):
                held_rows[0:width, :] = acc[:, (2 - c) * width : (3 - c) * width]
                out_copy = pltpu.make_async_copy(
                    held_rows.at[pl.ds(0, width), :],
                    part_out.at[pl.ds((3 * r + c) * width, width), :],
                    local.at[4],
                )
                out_copy.start()
                out_copy.wait()
        early_sum.middle()

    loads[2].wait()
    sigma = stats[4:5, :]
    mean_one, inverse_one, pixels = stats[0:1, :], stats[1:2, :], stats[2:3, :]
    gain, bias = norms[0:1, :], norms[1:2, :]
    none = jnp.zeros((8, width), F32)
    block_rows = 2 * BLOCK * side
    per_image = side // (2 * BLOCK)
    blocks = images * per_image

    def input_gradient(b):
        n, i = b // per_image, b % per_image
        acc = None
        for r in range(3):
            lhs = cat[n, pl.ds(i * 2 * BLOCK + r, 2 * BLOCK)].reshape(block_rows, 3 * width)
            one = bdot(lhs, k1[r], ((1,), (1,)))
            acc = one if acc is None else acc + one
        first = (b % 2) * width
        held_rows[first : first + block_rows, :] = acc

    def through_gelu(b, carried):
        n, i = b // per_image, b % per_image
        first = (b % 2) * width
        pixel = patches[n, :, i * block_rows : (i + 1) * block_rows]
        normed = (bdot(pixel, stem[...], ((0,), (0,))) - mean_one) * inverse_one
        grad = gelu_slope(normed * gain + bias) * held_rows[first : first + block_rows, :] * (
            valid[n] / sigma
        )
        down = (grad * (inverse_one * gain) + head_rows[n : n + 1, :] / cells).astype(BF16)
        return (
            carried[0] + fold(grad),
            carried[1] + fold(grad * normed),
            carried[2] + bdot(pixel, down),
        )

    sums = (none, none, jnp.zeros((32, width), F32))
    between = {
        0: [lambda: join_near(0), lambda: join_cores(1)],
        1: [lambda: join_far(0), lambda: chain(0, 3)],
        2: [lambda: chain(0, 2, 0, 1), lambda: join_near(1)],
        3: [lambda: chain(0, 2, 2, 3), lambda: chain(0, 1, 0, 1)],
        4: [lambda: join_far(1), lambda: chain(1, 2)],
    }
    for b in range(blocks + 1):
        if b < blocks:
            input_gradient(b)
        if b > 0:
            sums = through_gelu(b - 1, sums)
        if fused:
            for event in between.get(b, ()):
                event()
    late_sum = Reduce(
        ("dp", n_dp), ("replica", n_rep), late[0], late[1], late_out, None, None, late[2:]
    )
    late[0][...] = jnp.zeros(late[0].shape, F32)
    put_rows(late[0], 0, sums[2][0:27])
    put_rows(late[0], 27, jnp.sum(sums[0], axis=0, keepdims=True))
    put_rows(late[0], 28, jnp.sum(sums[1], axis=0, keepdims=True))
    late_sum.start()
    early_sum.last()

    act_copy = pltpu.make_async_copy(act_in, d_one, local.at[5])
    act_copy.start()
    edge = jnp.zeros((1, side, 3 * width), F8)
    cat8[0, 0:1] = edge
    cat8[0, side + 1 : side + 2] = edge

    def shift_act(n):
        def step(i, carried):
            rows = BLOCK * side
            at = pl.ds(pl.multiple_of(n * cells + i * rows, rows), rows)
            store_shifted(
                cat8, 0, i * BLOCK, BLOCK, d_one[at, :].astype(F32) * ACT_SCALE, side
            )
            return carried
        lax.fori_loop(0, side // BLOCK, step, 0)

    squares = none
    between = {
        0: [lambda: chain(0, 1, 2, 3), lambda: chain(1, 1, 0)],
        1: [lambda: chain(1, 1, 1), lambda: chain(0, 0, 0, 1), window_part],
        2: [lambda: chain(1, 1, 2), lambda: chain(1, 0, 0)],
        3: [lambda: chain(1, 1, 3), lambda: chain(0, 0, 2, 3), lambda: chain(1, 0, 1, 2, 3)],
    }
    for b in range(blocks):
        n, i = b // per_image, b % per_image
        if b == 0:
            act_copy.wait()
            loads[3].wait()
        if i == 0:
            shift_act(n)
        acc = None
        for r in range(3):
            lhs = cat8[0, pl.ds(i * 2 * BLOCK + r, 2 * BLOCK)].reshape(block_rows, 3 * width)
            one = bdot(lhs, k8[r * 3 * width : (r + 1) * 3 * width, :])
            acc = one if acc is None else acc + one
        squares = squares + valid[n] * fold(acc * acc)
        if fused:
            for event in between.get(b, ()):
                event()
    sigma_two = stats[5:6, :] * (ACT_SCALE * KERNEL_SCALE)
    sums_out[...] = jnp.zeros(sums_out.shape, F32)
    sums_out[0:1, :] = jnp.sum(squares, axis=0, keepdims=True) / (sigma_two * sigma_two)

    if fused:
        @pl.when(dp < half)
        def _():
            for zi in range(sources):
                @pl.when(z == zi)
                def _():
                    part_out[...] = part[zi, 0:share, :]

        def drain_windows(j, c):
            owner = lax.rem(here + j, owners)

            @pl.when(half * n_rep + owner != here)
            def _():
                window_copy(owner).wait_send()
            return c

        lax.fori_loop(0, owners, drain_windows, 0)
        for o in range(owners):
            pl.when(core != (o // n_rep) % 2)(sib_copy(o).wait_send)
        for zi in range(sources):
            for step in range(2):
                for copy in plane_copies(zi, step):
                    copy.wait_send()
            for piece in range(len(z_pieces)):
                pl.when(z > zi)(z_copy(zi, piece, True).wait_send)
                pl.when(z < zi)(z_copy(zi, piece, False).wait_send)
    early_sum.finish()
    late_sum.arrive()
    late_sum.drain()
    per = early[4].shape[1]
    for s in range(n_dp):
        for j in range(per):
            big_out[s * per + j : s * per + j + 1, :] = early[4][s, j : j + 1, :]


def backward(n_dp, n_rep, side, share, fused, counts, d_one, x, k1, k8, act, patches, stem, stats, norms,
             windows, head_rows, grads):
    images, width = patches.shape[0], stem.shape[1]
    half = n_dp // 2
    sources = max(n_dp // 4, 1)
    owners = half * n_rep
    devices = n_dp * n_rep
    shape = jax.ShapeDtypeStruct
    sem = pltpu.SemaphoreType.DMA
    rows = share + 8
    small = (1, 8, 128)
    early = reduce_scratch(n_dp, n_rep, 96, width)
    early_rows = early[0].shape[0] * early[0].shape[1]
    part_rows = share if fused else 9 * width
    pieces = len(chain_pieces(share))
    return pl.pallas_call(
        functools.partial(backward_kernel, n_dp, n_rep, side, share, fused),
        out_shape=(
            shape((part_rows, width), F32),
            shape((early_rows, width), F32),
            shape((8, width), F32),
            shape((-(-32 // n_dp), width), F32),
        ),
        in_specs=[SMEM] + [ANY] * 5 + [VMEM] * 7,
        out_specs=(VMEM if fused else ANY, VMEM, VMEM, VMEM),
        scratch_shapes=[
            pltpu.VMEM((images, side + 2, side, 3 * width), BF16),
            pltpu.VMEM(d_one.shape, BF16),
            pltpu.VMEM(x.shape, BF16),
            pltpu.VMEM(k1.shape, BF16),
            pltpu.VMEM(k8.shape, F8),
            pltpu.VMEM((1, side + 2, side, 3 * width), F8),
            pltpu.VMEM((2 * width, width), F32),
            pltpu.VMEM((rows if fused else 8, width), F32),
            pltpu.VMEM((owners, rows, width) if fused else small, BF16),
            pltpu.VMEM((sources * n_rep, rows, width) if fused else small, BF16),
            pltpu.VMEM((sources, 3, rows, width) if fused else small, BF16),
            pltpu.VMEM((sources, 2, rows, width) if fused else small, BF16),
            pltpu.VMEM((sources, rows, width) if fused else small, BF16),
            pltpu.VMEM((sources, rows, width) if fused else small, F32),
            pltpu.VMEM((10, 2 * images, width) if fused else small, F32),
            pltpu.VMEM((devices, 2, 2 * images, width) if fused else small, F32),
            pltpu.VMEM((2, devices * images, width) if fused else small, F32),
            pltpu.VMEM((devices * images, width) if fused else small[1:], F32),
            *early,
            pltpu.VMEM((n_dp, -(-32 // n_dp), width), F32),
            pltpu.VMEM((n_dp, -(-32 // n_dp), width), F32),
            sem((n_dp,)), sem((n_dp,)),
            sem((owners,)), sem((sources * n_rep,)),
            sem((sources, 6)), sem((sources, 6)),
            sem((sources, pieces)), sem((sources, pieces, 2)),
            sem((owners,)), sem((devices,)),
            sem((6,)),
        ],
        compiler_params=pltpu.CompilerParams(
            collective_id=2, has_side_effects=True, vmem_limit_bytes=62 << 20
        ),
    )(counts, d_one, x, k1, k8, act, patches, stem, stats, norms, windows, head_rows, grads)


def whole_sum(values):
    return jnp.sum(jnp.sum(values, axis=1, keepdims=True), axis=0, keepdims=True)


def lamb_step(weight, gradient, first, second, out, rows=False):
    new_one, new_two, direction = lamb_moments(weight, gradient, first, second)
    if rows:
        sizes = [jnp.sum(v * v, axis=1, keepdims=True) for v in (weight, direction)]
    else:
        sizes = [whole_sum(v * v) for v in (weight, direction)]
    new_weight = weight - RATE * (jnp.sqrt(sizes[0]) / jnp.sqrt(sizes[1])) * direction
    for ref, value in zip(out, (new_weight, new_one, new_two)):
        ref[...] = value.reshape(ref.shape)


def conv_gradient(first, part, conv_w, start, head_rows, stats, norm_w, flat, own):
    width = stats.shape[1]
    share = part.shape[0]
    lanes = width // 128
    def pick(row):
        return jnp.where(first, stats[row : row + 1, :], stats[row + 1 : row + 2, :])
    sigma, norm, unit = pick(4)[:, 0:1], pick(6)[:, 0:1], pick(8)
    inverse = stats[11:12, :] * stats[4:5, :]
    along = jnp.where(
        first,
        norm_w[2:3, :] * head_rows[16:17, :] * (EPS_NORM * inverse * inverse),
        head_rows[19:20, :],
    )
    d_sigma = -jnp.sum(along, axis=1, keepdims=True) / sigma
    vector = jnp.where(first, start[0:1, :], start[1:2, :])
    for k in range(lanes):
        own[:, k * 128 : (k + 1) * 128] = (
            conv_w[pl.ds(k, share, stride=lanes), :].astype(BF16).astype(F32)
        )
    rows = own[...]
    left = jnp.sum(rows * vector, axis=1, keepdims=True) / norm
    back = jnp.sum(rows * (unit / norm), axis=1, keepdims=True) - left * (sigma / norm)
    grad = part[...] / sigma + (left * d_sigma) * unit + (back * d_sigma) * vector
    for k in range(lanes):
        flat[pl.ds(k, share, stride=lanes), :] = grad[:, k * 128 : (k + 1) * 128]


def small_kernel(
    conv_ratio, conv_grad, conv_w, conv_m, conv_s, big, late, joined, head_rows, stats, chol, stem_w, stem_m, stem_s,
    norm_w, norm_m, norm_s, ind_w, ind_m, ind_s, len_w, len_m, len_s,
    mean_w, mean_m, mean_s, low_w, low_m, low_s, *rest,
):
    outs = rest[4:22]
    parts_out, sigmas_out, rms_out, z_pad, stem_pad = rest[22:]

    def conv_step():
        weight = conv_w[...]
        new_one, new_two, direction = lamb_moments(weight, conv_grad[...], conv_m[...], conv_s[...])
        new_conv = weight - conv_ratio[0] * direction
        for ref, value in zip(rest[:4], (new_conv, new_one, new_two, new_conv)):
            ref[...] = value.astype(ref.dtype)

    def small_step():
        small_updates(
            big, late, joined, head_rows, stats, chol, stem_w, stem_m, stem_s,
            norm_w, norm_m, norm_s, ind_w, ind_m, ind_s, len_w, len_m, len_s,
            mean_w, mean_m, mean_s, low_w, low_m, low_s, outs,
            parts_out, sigmas_out, rms_out, z_pad, stem_pad,
        )

    return ((4, slice(0, 4), conv_step), (28, slice(4, 22), small_step))


def small_updates(
    big, late, joined, head_rows, stats, chol, stem_w, stem_m, stem_s,
    norm_w, norm_m, norm_s, ind_w, ind_m, ind_s, len_w, len_m, len_s,
    mean_w, mean_m, mean_s, low_w, low_m, low_s, outs,
    parts_out, sigmas_out, rms_out, z_pad, stem_pad,
):
    width = stem_w.shape[1]
    size, classes = ind_w.shape[0], mean_w.shape[0]
    pixels = stats[2:3, :]
    mean_one, inverse_one = stats[0:1, :], stats[1:2, :]
    scale = head_rows[18:19, 0:1]
    parts_out[1] = jnp.sum(1.0 / scale)
    sigmas_out[0] = jnp.sum(stats[4:5, 0:1])
    sigmas_out[1] = jnp.sum(stats[5:6, 0:1])
    cells_all = pixels[:, 0:1] * width
    rms_out[0] = jnp.sum(
        jnp.sqrt(jnp.sum(stats[10:11, :], axis=1, keepdims=True) / cells_all)
    )
    rms_out[1] = jnp.sum(jnp.sqrt(joined[4:5, 0:1] / cells_all))

    gram = big[64:96, 0:32]
    patch_sums = gram[:, 31:32]
    stem_pad[...] = jnp.zeros(stem_pad.shape, F32)
    stem_pad[0 : stem_w.shape[0], :] = stem_w[...].astype(BF16).astype(F32)
    weights = stem_pad[...]
    centred = inverse_one * (hdot(gram, weights) - patch_sums * mean_one)
    d_bias, d_gain = late[27:28, :], late[28:29, :]
    stem_grad = late[0:32, :] - (inverse_one * norm_w[0:1, :] / pixels) * (
        patch_sums * d_bias + centred * d_gain
    )
    lamb_step(stem_w[...], stem_grad[0 : stem_w.shape[0]], stem_m[...], stem_s[...], outs[0:3])
    norm_grad = jnp.concatenate([d_gain, d_bias, head_rows[16:18, :]], axis=0)
    lamb_step(norm_w[...], norm_grad, norm_m[...], norm_s[...], outs[3:6], rows=True)

    ell = len_w[...].reshape(1, width)
    z_pad[...] = jnp.zeros(z_pad.shape, F32)
    z_pad[0:size, :] = ind_w[...] / ell
    zs = z_pad[...]
    kzz, factor, inverse = chol[0], chol[1], chol[2]
    line = lax.broadcasted_iota(jnp.int32, (IND, IND), 0)
    lane = lax.broadcasted_iota(jnp.int32, (IND, IND), 1)
    g_chol = jnp.where(line >= lane, -big[32:64, 384 : 384 + IND], 0.0)
    lower = hdot(factor, g_chol, ((0,), (0,)))
    phi = jnp.where(line > lane, lower, jnp.where(line == lane, 0.5 * lower, 0.0))
    back = hdot(inverse, hdot(phi, inverse), ((0,), (0,)))
    back_t = hdot(inverse, hdot(phi, inverse, ((0,), (0,))), ((0,), (0,)))
    weights_z = -0.5 * kzz * (back + back_t)
    g_z = big[0:32, :]
    g_z = jnp.where(lax.broadcasted_iota(jnp.int32, (IND, 1), 0) < size, g_z, 0.0) + 2.0 * (
        zs * jnp.sum(weights_z, axis=1, keepdims=True) - hdot(weights_z, zs)
    )
    lamb_step(ind_w[...], (g_z / ell)[0:size], ind_m[...], ind_s[...], outs[6:9])
    g_len = -(big[20:21, :] + jnp.sum(g_z * zs, axis=0, keepdims=True)) / ell
    lamb_step(ell, g_len, len_m[...].reshape(1, width), len_s[...].reshape(1, width), outs[9:12])

    means = mean_w[...]
    g_mean = big[32 : 32 + classes, 512 : 512 + size] + means * scale
    lamb_step(means, g_mean, mean_m[...], mean_s[...], outs[12:15])
    small_line = lax.broadcasted_iota(jnp.int32, (size, size), 0)
    small_lane = lax.broadcasted_iota(jnp.int32, (size, size), 1)
    kl = 0.5 * jnp.sum(means * means, axis=0, keepdims=True)
    weight_sq = jnp.zeros((1, size), F32)
    step_sq = weight_sq
    steps = []
    for c in range(classes):
        weight = low_w[c]
        factors = scale_rows(weight)
        inner = big[32 : 32 + size, c * IND : c * IND + size] + factors * scale
        grad = jnp.where(
            small_line > small_lane, inner,
            jnp.where(small_line == small_lane, factors * inner - scale, 0.0),
        )
        new_one, new_two, direction = lamb_moments(weight, grad, low_m[c], low_s[c])
        outs[16][c] = new_one
        outs[17][c] = new_two
        weight_sq = weight_sq + jnp.sum(weight * weight, axis=0, keepdims=True)
        step_sq = step_sq + jnp.sum(direction * direction, axis=0, keepdims=True)
        diagonal = jnp.where(small_line == small_lane, weight, 0.0)
        kl = kl + jnp.sum(0.5 * factors * factors - diagonal, axis=0, keepdims=True)
        steps.append(direction)
    ratio = RATE * jnp.sqrt(jnp.sum(weight_sq, axis=1, keepdims=True)) / jnp.sqrt(
        jnp.sum(step_sq, axis=1, keepdims=True)
    )
    for c in range(classes):
        outs[15][c] = low_w[c] - ratio * steps[c]
    kl = jnp.sum(kl, axis=1, keepdims=True) - 0.5 * classes * size
    parts_out[0] = jnp.sum(big[23:24, 0:1] + kl)


def staged(body, n_in, n_out, n_first, n_last, *refs):
    first, refs = refs[:n_first], refs[n_first:]
    ins, refs = refs[:n_in], refs[n_in:]
    outs, refs = refs[:n_out], refs[n_out:]
    last, refs = refs[:n_last], refs[n_last:]
    held, refs = refs[:n_in], refs[n_in:]
    made, refs = refs[:n_out], refs[n_out:]
    scratch, (sem_in, sem_out) = refs[:-2], refs[-2:]
    loads = [
        pltpu.make_async_copy(ref, held[i], sem_in.at[i]) for i, ref in enumerate(ins)
    ]
    for copy in loads:
        copy.start()
    stores = [
        pltpu.make_async_copy(made[i], ref, sem_out.at[i]) for i, ref in enumerate(outs)
    ]
    done = 0
    for ready, finished, step in body(*first, *held, *made, *last, *scratch):
        for copy in loads[done:ready]:
            copy.wait()
        done = ready
        step()
        for copy in stores[finished]:
            copy.start()
    for copy in stores:
        copy.wait()


def local_call(body, first, ins, outs, last, scratch):
    sem = pltpu.SemaphoreType.DMA
    return pl.pallas_call(
        functools.partial(staged, body, len(ins), len(outs), len(first), len(last)),
        out_shape=tuple(outs) + tuple(last),
        in_specs=[SMEM] * len(first) + [ANY] * len(ins),
        out_specs=(ANY,) * len(outs) + (SMEM,) * len(last),
        scratch_shapes=[
            *[pltpu.VMEM(a.shape, a.dtype) for a in ins],
            *[pltpu.VMEM(o.shape, o.dtype) for o in outs],
            *scratch,
            sem((len(ins),)),
            sem((len(outs),)),
        ],
        compiler_params=pltpu.CompilerParams(vmem_limit_bytes=60 << 20),
    )(*first, *ins)


def update_small(ratio, *ins):
    shape = jax.ShapeDtypeStruct
    conv, params = ins[0], ins[10:28:3]
    width = params[0].shape[1]
    outs = [shape(conv.shape, F32)] * 3 + [shape(conv.shape, BF16)]
    outs += [shape(p.shape, F32) for p in params for _ in range(3)]
    return local_call(
        small_kernel, [ratio], ins, outs, [shape((2,), F32)] * 3,
        [pltpu.VMEM((IND, width), F32), pltpu.VMEM((32, width), F32)],
    )


def tally_kernel(n_dp, n_rep, *refs):
    ins, refs = refs[:10], refs[10:]
    grad_out, out, ratio, late_out = refs[:4]
    held, refs = refs[4:14], refs[14:]
    flat, own, tally, ex_a, ex_b, one_b, planes, made = refs[:8]
    a_send, a_recv, b_send, b_recv, sem_in, sem_out = refs[8:14]
    half = n_dp // 2
    dp, rep = lax.axis_index("dp"), lax.axis_index("replica")
    greeted = greet(n_dp, n_rep)
    loads = [pltpu.make_async_copy(ref, held[i], sem_in.at[i]) for i, ref in enumerate(ins)]
    for copy in loads:
        copy.start()
    for copy in loads:
        copy.wait()
    part, conv_w, conv_m, conv_s, start, sums, head_rows, stats, norm_w, late = held
    greeted()
    late_sum = Reduce(
        ("dp", n_dp), ("replica", n_rep), None, None, late, planes, made, (None, None) + refs[14:]
    )
    late_sum.across()
    conv_gradient(dp < half, part, conv_w, start, head_rows, stats, norm_w, flat, own)
    store = pltpu.make_async_copy(flat, grad_out, sem_out.at[0])
    store.start()
    weight = conv_w[...]
    direction = lamb_moments(weight, flat[...], conv_m[...], conv_s[...])[2]
    lanes = stats.shape[1] // 128
    tally[...] = jnp.zeros(tally.shape, F32)
    tally[0:1, :] = jnp.sum(weight * weight, axis=0, keepdims=True)
    tally[1:2, :] = jnp.sum(direction * direction, axis=0, keepdims=True)
    tally[2:3, :] = total([sums[0:1, k * 128 : (k + 1) * 128] for k in range(lanes)])
    ex_a[dp] = tally[...]
    first = Spread("dp", n_dp, tally, ex_a, a_send, a_recv)
    first.start()
    late_sum.last()
    first.wait()
    one_b[...] = jnp.zeros(one_b.shape, F32)
    for l in range(2):
        near = range(l * half, (l + 1) * half)
        one_b[l : l + 1, :] = total([ex_a[i, 0:1, :] for i in near])
        one_b[2 + l : 3 + l, :] = total([ex_a[i, 1:2, :] for i in near])
    one_b[4:5, :] = total(rows_of(ex_a, 2))
    ex_b[rep] = one_b[...]
    second = Spread("replica", n_rep, one_b, ex_b, b_send, b_recv)
    second.start()
    late_sum.finish_last()
    per = made.shape[1]
    for k in range(32):
        late_out[k : k + 1, :] = made[k // per, k % per : k % per + 1, :]
    second.wait()
    joined = jnp.sum(total([ex_b[i] for i in range(n_rep)]), axis=1, keepdims=True)
    out[...] = jnp.zeros(out.shape, F32) + joined
    trust = jnp.sqrt(joined[0:2]) / jnp.sqrt(joined[2:4])
    ratio[0] = RATE * jnp.sum(jnp.where(dp < half, trust[0:1], trust[1:2]))
    first.drain()
    second.drain()
    store.wait()


def join_tally(n_dp, n_rep, *ins):
    sem = pltpu.SemaphoreType.DMA
    shape = jax.ShapeDtypeStruct
    part, conv, late = ins[0], ins[1], ins[9]
    return pl.pallas_call(
        functools.partial(tally_kernel, n_dp, n_rep),
        out_shape=(
            shape(conv.shape, F32), shape((8, 128), F32), shape((1,), F32),
            shape((32, late.shape[1]), F32),
        ),
        in_specs=[ANY] * 10,
        out_specs=(ANY, VMEM, SMEM, VMEM),
        scratch_shapes=[
            *[pltpu.VMEM(a.shape, a.dtype) for a in ins],
            pltpu.VMEM(conv.shape, F32),
            pltpu.VMEM(part.shape, F32),
            pltpu.VMEM((8, 128), F32),
            pltpu.VMEM((n_dp, 8, 128), F32),
            pltpu.VMEM((n_rep, 8, 128), F32),
            pltpu.VMEM((8, 128), F32),
            pltpu.VMEM((n_rep, *late.shape), F32),
            pltpu.VMEM((n_dp, *late.shape), F32),
            sem((n_dp,)), sem((n_dp,)), sem((n_rep,)), sem((n_rep,)),
            sem((10,)), sem((1,)),
            sem((n_rep,)), sem((n_rep,)), sem((n_dp,)), sem((n_dp,)),
        ],
        compiler_params=pltpu.CompilerParams(
            collective_id=3, has_side_effects=True, vmem_limit_bytes=60 << 20
        ),
    )(*ins)


def on_device(
    images, labels, counts, noise_table, noise_index, power_start,
    conv_weight, conv_first, conv_second,
    stem_weight, stem_first, stem_second,
    norm_params, norm_first, norm_second,
    inducing, inducing_first, inducing_second,
    lengthscale, length_first, length_second,
    var_mean, mean_first, mean_second,
    var_lower, lower_first, lower_second,
):
    width = stem_weight.shape[1]
    side = images.shape[2]
    cells = side * side
    n_dp, n_rep = lax.axis_size("dp"), lax.axis_size("replica")
    here = lax.axis_index(AXES)
    per_kernel = n_dp * n_rep // 2
    owner = here // per_kernel
    select = (jnp.arange(2) == owner).astype(F32)
    geometry = (n_dp, n_rep, side)

    share = conv_weight.shape[0] // width
    wide = (-1, 128)
    fused = share % 16 == 8 and n_rep == 4 and n_dp == 8
    if fused:
        weights, extra = conv_weight.reshape(wide), power_start
    else:
        rows = conv_weight.astype(BF16).reshape(-1, width)
        gathered = lax.all_gather(rows, AXES, axis=0, tiled=True)
        weights = gathered[: 9 * width]
        own = rows.astype(F32)
        start = jnp.sum(select[:, None] * power_start, axis=0)
        own_along = jnp.sum(own * start, axis=1)
        back_rows = jnp.sum(own * own_along[:, None], axis=0)
        extra = jnp.stack([back_rows, jnp.full((width,), jnp.sum(own_along * own_along))])
    (
        k_one, k_two, act_one, raw_one, slope, act_two, windows, stem_pool, stats, patches, stem_kernel,
        chol, *prepared,
    ) = forward(
        *geometry, share, fused, counts, noise_index, weights, images, stem_weight, extra,
        norm_params, noise_table.T, inducing, lengthscale, var_mean, var_lower,
    )
    if not fused:
        k_two = gathered[9 * width :]
    d_one, k8, head_rows, grads = head(
        *geometry, inducing.shape[0], var_mean.shape[0], noise_index.shape[1], counts, labels,
        k_two, raw_one, slope, windows, stem_pool, stats, norm_params, lengthscale, chol, *prepared,
    )
    part, big, sums, late = backward(
        *geometry, share, fused, counts, d_one, act_one, k_one, k8, act_two, patches, stem_kernel, stats, norm_params, windows,
        head_rows, grads,
    )
    if not fused:
        part_one = lax.psum_scatter(
            jnp.concatenate([part.reshape(-1), jnp.zeros((part.size,), F32)]),
            AXES, scatter_dimension=0, tiled=True,
        ).reshape(-1, width)
        all_windows, all_grads = lax.all_gather(
            (windows[:, :9], head_rows[8 : 8 + images.shape[0]]), AXES, tiled=True
        )
        all_windows = all_windows.reshape(all_windows.shape[0], -1)
        mine = lax.dynamic_slice_in_dim(
            all_windows, lax.rem(here, per_kernel) * share, share, axis=1
        )
        part = jnp.where(owner == 0, part_one, jnp.dot(mine.T, all_grads, precision=HIGH))

    conv = [v.reshape(wide) for v in (conv_weight, conv_first, conv_second)]
    conv_grad, joined, ratio, late = join_tally(
        n_dp, n_rep, part, *conv, power_start, sums, head_rows, stats, norm_params, late
    )
    done = update_small(
        ratio, conv_grad, *conv, big, late, joined, head_rows, stats, chol,
        stem_weight, stem_first, stem_second, norm_params, norm_first, norm_second,
        inducing, inducing_first, inducing_second, lengthscale, length_first, length_second,
        var_mean, mean_first, mean_second, var_lower, lower_first, lower_second,
    )
    loss_parts, sigmas, rms = done[22:]
    return (loss_parts, *[v.reshape(-1) for v in done[:4]], *done[4:22], sigmas, rms)


def solution(mesh):
    split = P(AXES)
    return jax.shard_map(
        on_device,
        mesh=mesh,
        in_specs=(split, split, split, P(), split, P(), split, split, split) + (P(),) * 18,
        out_specs=(P(),) + (split,) * 4 + (P(),) * 20,
        check_vma=False,
    )
```

```python
import functools

import jax
import jax.numpy as jnp
from jax import lax
from jax.experimental import pallas as pl
from jax.experimental.pallas import tpu as pltpu
from jax.sharding import PartitionSpec as P

STEP = 10
HIGH = lax.Precision.HIGHEST
EPS_NORM = 1e-05
JITTER = 0.001
BETA_ONE = 0.9
BETA_TWO = 0.999
RATE = 0.3
DECAY = 0.01
EPS_ADAM = 1e-08
AXES = ("dp", "replica")


def lamb_moments(weight, gradient, moment_one, moment_two):
    new_one = BETA_ONE * moment_one + (1.0 - BETA_ONE) * gradient
    new_two = BETA_TWO * moment_two + (1.0 - BETA_TWO) * gradient * gradient
    direction = (
        new_one / (1.0 - BETA_ONE**STEP) / (jnp.sqrt(new_two / (1.0 - BETA_TWO**STEP)) + EPS_ADAM)
        + DECAY * weight
    )
    return (new_one, new_two, direction)


MESH = pl.DeviceIdType.MESH
ANY = pl.BlockSpec(memory_space=pl.ANY)
VMEM = pl.BlockSpec(memory_space=pltpu.VMEM)
SMEM = pl.BlockSpec(memory_space=pltpu.SMEM)
F32 = jnp.float32
BF16 = jnp.bfloat16
F8 = jnp.float8_e4m3fn
ACT_SCALE = 0.25
KERNEL_SCALE = 2048.0


def remote(src, dst, send, recv, where):
    return pltpu.make_async_remote_copy(
        src_ref=src, dst_ref=dst, send_sem=send, recv_sem=recv,
        device_id=where, device_id_type=MESH,
    )


def greet(n_dp, n_rep):
    dp, rep = lax.axis_index("dp"), lax.axis_index("replica")
    barrier = pltpu.get_barrier_semaphore()
    for j in range(1, n_dp):
        pl.semaphore_signal(
            barrier, inc=1, device_id={"dp": lax.rem(dp + j, n_dp)}, device_id_type=MESH
        )
    for j in range(1, n_rep):
        pl.semaphore_signal(
            barrier, inc=1, device_id={"replica": lax.rem(rep + j, n_rep)}, device_id_type=MESH
        )
    return lambda: pl.semaphore_wait(barrier, n_dp + n_rep - 2)


class Spread:
    def __init__(self, axis, size, src, dst, send, recv):
        self.axis, self.size, self.src, self.dst, self.send, self.recv = axis, size, src, dst, send, recv
        self.me = lax.axis_index(axis)

    def copies(self):
        for j in range(1, self.size):
            yield remote(
                self.src, self.dst.at[self.me], self.send.at[j], self.recv.at[j],
                {self.axis: lax.rem(self.me + j, self.size)},
            )

    def start(self):
        for copy in self.copies():
            copy.start()

    def wait(self):
        for j in range(1, self.size):
            source = lax.rem(self.me + self.size - j, self.size)
            remote(
                self.src, self.dst.at[source], self.send.at[j], self.recv.at[j],
                {self.axis: source},
            ).wait_recv()

    def drain(self):
        for copy in self.copies():
            copy.wait_send()


def rows_of(refs, row):
    return [refs[i, row : row + 1, :] for i in range(refs.shape[0])]


def total(values):
    result = values[0]
    for value in values[1:]:
        result = result + value
    return result


def join_moments(refs):
    averages, squares, counts = rows_of(refs, 0), rows_of(refs, 1), rows_of(refs, 2)
    count = total(counts)
    average = total([a * n for a, n in zip(averages, counts)]) / count
    spread = total(
        [s + n * (a - average) * (a - average) for a, s, n in zip(averages, squares, counts)]
    )
    return average, spread, count


def hdot(a, b, dims=((1,), (0,))):
    return lax.dot_general(
        a, b, (dims, ((), ())), precision=HIGH, preferred_element_type=F32
    )


def bdot(a, b, dims=((1,), (0,))):
    return lax.dot_general(a, b, (dims, ((), ())), preferred_element_type=F32)


class Gather:
    def __init__(self, which, n_dp, share, buffer, sems):
        self.which, self.n_dp, self.share, self.buffer = which, n_dp, share, buffer
        tiles = (share - 8) // 16
        edges = [tiles * i // PIECES * 16 for i in range(PIECES + 1)]
        self.pieces = list(zip(edges, [hi - lo for lo, hi in zip(edges, edges[1:])]))
        self.z_send, self.z_recv, self.r_send, self.r_recv, self.c_send, self.c_recv = [
            s.at[which] for s in sems
        ]
        self.dp, rep = lax.axis_index("dp"), lax.axis_index("replica")
        self.reps = (rep, rep + 1 - 2 * lax.rem(rep, 2), rep + 2 - 4 * (rep // 2), 3 - rep)
        self.core, self.z = lax.rem(self.dp, 2), self.dp // 2
        self.n_z = n_dp // 2
        self.sources = n_dp // 4
        self.order = range(self.sources) if which else range(self.sources - 1, -1, -1)

    def first(self, zi, core, k):
        owner = (zi * 2 + core) * 4 + self.reps[k]
        return (owner // 2) * (2 * self.share) + lax.rem(owner, 2) * (self.share + 8)

    def each(self, zi, core, k, piece, act):
        start, rows = self.pieces[piece]
        begin = pl.multiple_of(self.first(zi, core, k) + start, 16)
        if piece < len(self.pieces) - 1:
            act(self.buffer.at[pl.ds(begin, rows), :])
            return
        even = lax.rem(self.reps[k], 2) == 0
        pl.when(even)(lambda: act(self.buffer.at[pl.ds(begin, rows + 16), :]))
        pl.when(~even)(lambda: act(self.buffer.at[pl.ds(begin, rows), :]))

    def source(self, zi):
        return zi + self.which * self.sources

    def along(self, zi, piece, what, ways=(0, 1)):
        def act(ref):
            for way in ways:
                condition = (
                    ((self.z <= self.source(zi)) & (self.z > 0)) if way
                    else ((self.z >= self.source(zi)) & (self.z < self.n_z - 1))
                )
                step = self.n_dp - 2 if way else 2
                copy = remote(
                    ref, ref, self.z_send.at[zi, piece, way], self.z_recv.at[zi, piece],
                    {"dp": lax.rem(self.dp + step, self.n_dp)},
                )
                if what == "wait_recv":
                    copy.wait_recv()
                    return
                pl.when(condition)(getattr(copy, what))
        self.each(zi, self.core, 0, piece, act)

    def goes_on(self, zi):
        gap = self.z - self.source(zi)
        return ((gap < 0) & (self.z > 0)) | ((gap > 0) & (self.z < self.n_z - 1))

    def near(self, zi, piece, k, what):
        def act(ref):
            getattr(remote(
                ref, ref, self.r_send.at[zi, piece, k], self.r_recv.at[zi, piece, k],
                {"replica": self.reps[k]},
            ), what)()
        self.each(zi, self.core, k if what == "wait_recv" else 0, piece, act)

    def passed(self, zi, piece, what):
        k = 1 + piece % 2
        def act(ref):
            getattr(remote(
                ref, ref, self.r_send.at[zi, piece, 3], self.r_recv.at[zi, piece, 3],
                {"replica": self.reps[3 - k]},
            ), what)()
        self.each(zi, self.core, 3 if what == "wait_recv" else k, piece, act)

    def over(self, zi, piece, k, what):
        def act(ref):
            getattr(remote(
                ref, ref, self.c_send.at[zi, piece, k], self.c_recv.at[zi, piece, k],
                {"dp": self.dp + 1 - 2 * self.core},
            ), what)()
        self.each(zi, 1 - self.core if what == "wait_recv" else self.core, k, piece, act)

    def send_plane(self, zi, piece):
        for k in (1, 2):
            self.near(zi, piece, k, "start")
        self.over(zi, piece, 0, "start")

    def own(self, pieces, ways, plane):
        for zi in range(self.sources):
            @pl.when(self.z == self.source(zi))
            def _():
                for piece in pieces:
                    self.along(zi, piece, "start", ways)
                    if plane:
                        self.send_plane(zi, piece)

    def column(self, zi, pieces):
        @pl.when(self.z != self.source(zi))
        def _():
            for piece in pieces:
                self.along(zi, piece, "wait_recv")
                self.along(zi, piece, "start")
                self.send_plane(zi, piece)

    def hop(self, distance):
        for zi in self.order:
            gap = self.z - self.source(zi)
            @pl.when(self.goes_on(zi) & ((gap == distance) | (gap == -distance)))
            def _():
                for piece in range(len(self.pieces)):
                    self.along(zi, piece, "wait_recv")
                    self.along(zi, piece, "start")

    def plane(self, zi, condition, sent=0):
        @pl.when(condition)
        def _():
            for piece in range(len(self.pieces)):
                pl.when((self.z != self.source(zi)) & ~self.goes_on(zi))(
                    functools.partial(self.along, zi, piece, "wait_recv")
                )
                if piece < sent:
                    pl.when(self.z != self.source(zi))(
                        functools.partial(self.send_plane, zi, piece)
                    )
                else:
                    self.send_plane(zi, piece)

    def neighbours(self, zi, pieces):
        for piece in pieces:
            for k in (1, 2):
                self.near(zi, piece, k, "wait_recv")
                if k == 1 + piece % 2:
                    self.passed(zi, piece, "start")
                self.over(zi, piece, k, "start")

    def opposite(self, zi):
        for piece in range(len(self.pieces)):
            self.passed(zi, piece, "wait_recv")
            self.over(zi, piece, 3, "start")

    def from_core(self, zi):
        for piece in range(len(self.pieces)):
            for k in range(4):
                self.over(zi, piece, k, "wait_recv")

    def drain(self):
        for piece in range(len(self.pieces)):
            for zi in range(self.sources):
                self.along(zi, piece, "wait_send")
                for k in (1, 2):
                    self.near(zi, piece, k, "wait_send")
                self.passed(zi, piece, "wait_send")
                for k in range(4):
                    self.over(zi, piece, k, "wait_send")


PIECES = 4


def pixel_column(rows, side):
    return lax.rem(lax.broadcasted_iota(jnp.int32, (rows, 1), 0), side)


def store_shifted(ref, image, first, block, values, side):
    width = values.shape[1]
    rows = block * side
    column = pixel_column(rows, side)
    left = jnp.where(column == 0, 0.0, pltpu.roll(values, 1, 0))
    right = jnp.where(column == side - 1, 0.0, pltpu.roll(values, rows - 1, 0))
    for c, moved in enumerate((left, values, right)):
        ref[image, pl.ds(first + 1, block), :, c * width : (c + 1) * width] = (
            moved.astype(ref.dtype).reshape(block, side, width)
        )


def gelu_both(x):
    c = 0.7978845608028654
    square = x * x
    th = jnp.tanh(c * x * (1.0 + 0.044715 * square))
    half = 0.5 * (1.0 + th)
    return x * half, half + 0.5 * x * (1.0 - th * th) * (c * (1.0 + 3 * 0.044715 * square))


def window_matrix(side):
    shape = (16, side * side)
    pixel = lax.broadcasted_iota(jnp.int32, shape, 1)
    tap = lax.broadcasted_iota(jnp.int32, shape, 0)
    r, c = tap // 3, lax.rem(tap, 3)
    h, w = pixel // side, lax.rem(pixel, side)
    keep = (
        (tap < 9)
        & ~((r == 0) & (h == side - 1)) & ~((r == 2) & (h == 0))
        & ~((c == 0) & (w == side - 1)) & ~((c == 2) & (w == 0))
    )
    return jnp.where(keep, 1.0, 0.0).astype(BF16)


BLOCK = 8


def make_patches(images, side, patches, line):
    cells = side * side
    pixel = lax.broadcasted_iota(jnp.int32, (1, cells), 1)
    h, w = pixel // side, lax.rem(pixel, side)
    colours = images.shape[1]
    for n in range(images.shape[0]):
        for c in range(colours):
            picture = images[n, c].astype(F32)
            for row in range(side):
                line[c : c + 1, row * side : (row + 1) * side] = picture[row : row + 1, :]
        values = line[0:colours, :]
        line[...] = jnp.where(
            lax.broadcasted_iota(jnp.int32, line.shape, 0) == 31, 1.0, 0.0
        )
        for t in range(9):
            down, right = t // 3 - 1, t % 3 - 1
            shift = down * side + right
            moved = pltpu.roll(values, (-shift) % cells, 1) if shift else values
            inside = (h + down >= 0) & (h + down < side) & (w + right >= 0) & (w + right < side)
            line[colours * t : colours * (t + 1), :] = jnp.where(inside, moved, 0.0)
        patches[n] = line[...].astype(BF16)


IND = 32


def cholesky_steps(matrix, size):
    lane = lax.broadcasted_iota(jnp.int32, (size, IND), 1)
    line = lax.broadcasted_iota(jnp.int32, (size, IND), 0)
    left = matrix
    right = jnp.where(lane == line, 1.0, 0.0)
    factor = jnp.zeros((size, IND), F32)
    row_of = lax.broadcasted_iota(jnp.int32, (size, 1), 0)
    for k in range(size):
        inverse = lax.rsqrt(left[k : k + 1, k : k + 1])
        column = jnp.where(row_of >= k, left[:, k : k + 1] * inverse, 0.0)
        below = jnp.where(row_of > k, column, 0.0)
        row = left[k : k + 1, :] * inverse
        other = right[k : k + 1, :] * inverse
        factor = jnp.where(lane == k, column, factor)
        left = left - below * row
        right = jnp.where(line == k, other, right - below * other)
    return factor, right


def scale_rows(lower):
    size = lower.shape[0]
    line = lax.broadcasted_iota(jnp.int32, (size, size), 0)
    lane = lax.broadcasted_iota(jnp.int32, (size, size), 1)
    return jnp.where(line > lane, lower, jnp.where(line == lane, jnp.exp(lower), 0.0))


def prepare_head(indices, table, inducing, lengthscale, var_mean, var_lower, chol_out, z_pad, v_pad, f_pad, noise):
    size, width = inducing.shape
    classes = var_mean.shape[0]
    images, samples = indices.shape
    ell = lengthscale[...].reshape(1, width)
    z_pad[...] = jnp.zeros(z_pad.shape, F32)
    z_pad[0:size, :] = inducing[...] / ell
    zs = z_pad[...]
    lane = lax.broadcasted_iota(jnp.int32, (size, IND), 1)
    line = lax.broadcasted_iota(jnp.int32, (size, IND), 0)
    kzz = jnp.zeros((size, IND), F32)
    for m in range(size):
        off = zs[0:size, :] - zs[m : m + 1, :]
        kzz = jnp.where(lane == m, jnp.exp(-0.5 * jnp.sum(off * off, axis=1, keepdims=True)), kzz)
    factor, inverse = cholesky_steps(jnp.where(lane == line, kzz + JITTER, kzz), size)
    chol_out[...] = jnp.zeros(chol_out.shape, F32)
    chol_out[0, 0:size, :] = kzz
    chol_out[1, 0:size, :] = factor
    chol_out[2, 0:size, :] = inverse
    v_pad[...] = jnp.zeros(v_pad.shape, F32)
    v_pad[0:classes, 0:size] = var_mean[...]
    f_pad[...] = jnp.zeros(f_pad.shape, F32)
    for c in range(classes):
        f_pad[0:size, c * IND : c * IND + size] = scale_rows(var_lower[c])
    noise[...] = jnp.zeros(noise.shape, F32)
    table_lane = lax.broadcasted_iota(jnp.int32, (1, table.shape[1]), 1)
    for n in range(images):
        chosen = [jnp.where(table_lane == indices[n, s], 1.0, 0.0) for s in range(samples)]
        chosen.append(jnp.zeros((16 - samples, table.shape[1]), F32))
        noise[n, :, 0:classes] = hdot(jnp.concatenate(chosen, axis=0), table[...], ((1,), (1,)))


def forward_kernel(
    n_dp, n_rep, side, share, fused,
    counts, indices, weights, pictures, stem_in, start, norms, table, inducing, lengthscale, var_mean, var_lower,
    k1_out, k2_out, x_out, y_out, slope_out, act_out, windows, stem_pool, stats, patches, stem,
    chol_out, z_pad, v_pad, f_pad, noise,
    line, own_f32, main, bound, k1, xcat, y, act, slope, seam, ex_a, ex_b, one_a, one_b, tw_a, tw_b, tw_one,
    z_send, z_recv, r_send, r_recv, c_send, c_recv,
    a_send, a_recv, b_send, b_recv, s_send, s_recv, local, turn,
):
    images = pictures.shape[0]
    width = stem_in.shape[1]
    cells = side * side
    dp, rep = lax.axis_index("dp"), lax.axis_index("replica")
    half = n_dp // 2
    greeted = greet(n_dp, n_rep)

    if fused:
        rows = share - 8
        sems = (z_send, z_recv, r_send, r_recv, c_send, c_recv)
        one, two = [
            Gather(l, n_dp, share, buffer, sems) for l, buffer in enumerate((k1, k2_out))
        ]
        every = range(PIECES)
        early, final = every[:-1], every[-1:]
        even = lax.rem(rep, 2) == 0
        owner = lax.rem(dp, half) * n_rep + rep
        own_first = (owner // 2) * (2 * share) + lax.rem(owner, 2) * (share + 8)
        seam_copy = remote(
            bound, seam.at[1], s_send.at[0], s_recv.at[0],
            {"replica": rep + 1 - 2 * lax.rem(rep, 2)},
        )

        def own_copies(what):
            for l, buffer in enumerate((k1, k2_out)):
                @pl.when((dp < half) if l == 0 else (dp >= half))
                def _():
                    at = pl.ds(pl.multiple_of(own_first, 16), rows)
                    getattr(pltpu.make_async_copy(main, buffer.at[at, :], local.at[0]), what)()

        def put_seam():
            @pl.when(even)
            def _():
                seam_copy.wait_recv()
                seam[0] = (bound[...].astype(F32) + seam[1].astype(F32)).astype(BF16)
                for l, buffer in enumerate((k1, k2_out)):
                    @pl.when((dp < half) if l == 0 else (dp >= half))
                    def _():
                        at = pl.ds(pl.multiple_of(own_first + rows, 16), 16)
                        copy = pltpu.make_async_copy(seam.at[0], buffer.at[at, :], local.at[10])
                        copy.start()
                        copy.wait()

        lanes = width // 128
        for k in range(lanes):
            own_f32[:, k * 128 : (k + 1) * 128] = weights[pl.ds(k, share, stride=lanes), :]
        blank = jnp.zeros((8, width), F32)
        head_rows, tail_rows = own_f32[0:8, :], own_f32[share - 8 : share, :]
        main[...] = jnp.where(even, own_f32[0:rows, :], own_f32[8:share, :]).astype(BF16)
        bound[...] = jnp.where(
            even,
            jnp.concatenate([tail_rows, blank], axis=0),
            jnp.concatenate([blank, head_rows], axis=0),
        ).astype(BF16)
        own_copies("start")
    else:
        copy_in = pltpu.make_async_copy(weights, k1, local.at[0])
        copy_in.start()

    if fused:
        own_copies("wait")
    greeted()
    if fused:
        pl.when(~even)(seam_copy.start)
        one.own(every[:2], (0, 1), True)
        two.own(every[:2], (1,), True)
    line[:, 0:width] = jnp.zeros((32, width), F32)
    line[0 : stem_in.shape[0], 0:width] = stem_in[...]
    stem[...] = line[:, 0:width].astype(BF16)
    weight = stem[...].astype(F32)
    count = counts[0]
    valid = [jnp.where(count > n, 1.0, 0.0) for n in range(images)]
    held = count.astype(F32) * cells
    make_patches(pictures, side, patches, line)
    grams, sums = [], []
    for n in range(images):
        grams.append(bdot(patches[n], patches[n], ((1,), (1,))))
        sums.append(grams[n][24:32])
        stem_pool[n : n + 1, :] = hdot(sums[n], weight)[7:8] * (1.0 / cells)
    gram = total([g * v for g, v in zip(grams, valid)])
    summed = total([s * v for s, v in zip(sums, valid)])
    square = jnp.sum(weight * hdot(gram, weight), axis=0, keepdims=True)
    last = jnp.where(lax.broadcasted_iota(jnp.int32, summed.shape, 0) == 7, summed, 0.0)
    cover = gram - hdot(last, last, ((0,), (0,))) / held
    zero = jnp.zeros((1, width), F32)
    payload = one_a.at[0]
    payload[...] = jnp.zeros(payload.shape, F32)
    payload[0:1, :] = hdot(summed, weight)[7:8] / held
    payload[1:2, :] = jnp.sum(weight * hdot(cover, weight), axis=0, keepdims=True)
    payload[2:3, :] = zero + held
    payload[5:6, :] = square

    if fused:
        vector = jnp.where(dp < half, start[0:1, :], start[1:2, :])
        own_rows = main[...].astype(F32)
        edge_rows = bound[...].astype(F32)
        along = jnp.sum(own_rows * vector, axis=1, keepdims=True)
        edge_along = jnp.sum(edge_rows * vector, axis=1, keepdims=True)
        payload[3:4, :] = jnp.sum(own_rows * along, axis=0, keepdims=True) + jnp.sum(
            edge_rows * edge_along, axis=0, keepdims=True
        )
        payload[4:5, :] = zero + (
            jnp.sum(along * along, axis=0, keepdims=True)
            + jnp.sum(edge_along * edge_along, axis=0, keepdims=True)
        )
    else:
        payload[3:4, :] = start[0:1, :]
        payload[4:5, :] = start[1:2, :]

    first = ex_a.at[0]
    first[dp] = payload[...]
    one_level = Spread("dp", n_dp, payload, first, a_send.at[0], a_recv.at[0])
    one_level.start()
    if fused:
        one.own(early[2:], (0, 1), True)
        two.own(early[2:], (1,), False)
        put_seam()
        one.own(final, (0, 1), True)
        two.own(final, (1,), False)
    for n in range(images):
        blank = jnp.zeros((1, side, 3 * width), BF16)
        xcat[n, 0:1] = blank
        xcat[n, side + 1 : side + 2] = blank
    if fused:
        one.column(1, every)
    one_level.wait()
    second = ex_b.at[0]
    mean, spread, cell_count = join_moments(first)
    passed = one_b.at[0]
    passed[...] = jnp.zeros(passed.shape, F32)
    passed[0:1, :] = mean
    passed[1:2, :] = spread
    passed[2:3, :] = cell_count
    vectors, squares = rows_of(first, 3), rows_of(first, 4)
    passed[3:4, :] = total(vectors[:half])
    passed[4:5, :] = total(vectors[half:])
    passed[5:6, :] = total(squares[:half])
    passed[6:7, :] = total(squares[half:])
    passed[7:8, :] = total(rows_of(first, 5))
    second[rep] = passed[...]
    two_level = Spread("replica", n_rep, passed, second, b_send.at[0], b_recv.at[0])
    two_level.start()
    if fused:
        one.neighbours(1, every[:2])
        one.column(0, every[:2])
        one.neighbours(1, every[2:])
        one.column(0, every[2:])
        two.own(every, (0,), False)
        two.hop(1)
    prepare_head(
        indices, table, inducing, lengthscale, var_mean, var_lower, chol_out, z_pad, v_pad, f_pad, noise
    )
    two_level.wait()
    mean, spread, pixels = join_moments(second)
    inverse_one = lax.rsqrt(spread / pixels + EPS_NORM)
    joined = [total(rows_of(second, row)) for row in range(3, 8)]
    sigma_rows, start_rows = [], []
    for l in range(2):
        vec = jnp.sqrt(jnp.sum(joined[l] * joined[l], axis=1, keepdims=True))
        base = jnp.sqrt(joined[2 + l])
        sigma_rows.append(zero + vec / base)
        start_rows.append(base)
        stats[8 + l : 9 + l, :] = joined[l] / vec
    stats[0:1, :] = mean
    stats[1:2, :] = inverse_one
    stats[2:3, :] = pixels
    stats[4:5, :] = sigma_rows[0]
    stats[5:6, :] = sigma_rows[1]
    stats[6:7, :] = start_rows[0]
    stats[7:8, :] = start_rows[1]
    stats[10:11, :] = joined[4]
    scale_one = inverse_one * norms[0:1, :]
    shift_one = norms[1:2, :] - mean * scale_one

    def act_one(n, part):
        def step(i, carry):
            first_row = i * BLOCK
            pixel = pl.ds(pl.multiple_of(first_row * side, BLOCK * side), BLOCK * side)
            out = bdot(patches[n, :, pixel], stem[...], ((0,), (0,)))
            values = jax.nn.gelu(out * scale_one + shift_one)
            store_shifted(xcat, n, first_row, BLOCK, values, side)
            return carry
        half_steps = side // BLOCK // 2
        lax.fori_loop(part * half_steps, (part + 1) * half_steps, step, 0)

    for n in range(images):
        for part in range(2):
            act_one(n, part)
        if fused and n == 0:
            one.neighbours(0, every[:2])
    if fused:
        one.opposite(1)
        one.from_core(1)
    else:
        copy_in.wait()
    x_copies = [
        pltpu.make_async_copy(
            xcat.at[n, pl.ds(1, side), :, pl.ds(width, width)], x_out.at[n], local.at[2 + n]
        )
        for n in range(images)
    ]
    for copy in x_copies:
        copy.start()

    tap_row = 3 * width
    middle = -(-(9 * width // 2 - tap_row) // 128) * 128
    rows_step = 2 * BLOCK * side

    def window(n, i, r, lanes):
        return xcat[n, pl.ds(i * 2 * BLOCK + r, 2 * BLOCK), :, lanes].reshape(rows_step, -1)

    def at_rows(n, i):
        return pl.ds(pl.multiple_of(n * cells + i * rows_step, rows_step), rows_step)

    for n in range(images):
        def later_half(i, carry):
            y[at_rows(n, i), :] = bdot(
                window(n, i, 2, slice(0, tap_row)), k1[2 * tap_row : 3 * tap_row, :]
            ) + bdot(
                window(n, i, 1, slice(middle, tap_row)), k1[tap_row + middle : 2 * tap_row, :]
            )
            return carry
        lax.fori_loop(0, side // (2 * BLOCK), later_half, 0)
        if fused and n == 0:
            one.neighbours(0, every[2:])
            two.hop(2)
            two.plane(0, two.z >= 0, 2)
            two.plane(1, two.z > 0, 2)
    if fused:
        one.opposite(0)
        one.from_core(0)
    k1_copies = [
        pltpu.make_async_copy(
            k1.at[pl.ds((8 - t) * width, width), :],
            k1_out.at[t // 3, :, pl.ds((t % 3) * width, width)],
            turn.at[t],
        )
        for t in range(9)
    ]
    for copy in k1_copies:
        copy.start()
    moments = []
    y_copies = []
    for n in range(images):
        def first_half(i, carry):
            acc = (
                y[at_rows(n, i), :]
                + bdot(window(n, i, 0, slice(0, tap_row)), k1[0:tap_row, :])
                + bdot(window(n, i, 1, slice(0, middle)), k1[tap_row : tap_row + middle, :])
            )
            y[at_rows(n, i), :] = acc
            return carry + jnp.sum(acc, axis=0, keepdims=True)
        whole = lax.fori_loop(0, side // (2 * BLOCK), first_half, zero)
        if fused and n == 0:
            two.plane(1, two.z == 0, 2)
        average = whole / cells
        def spread_step(i, carry):
            pixel = pl.ds(pl.multiple_of(n * cells + i * BLOCK * side, 16), BLOCK * side)
            off = y[pixel, :] - average
            return carry + jnp.sum(off * off, axis=0, keepdims=True)
        moments.append((average, lax.fori_loop(0, side // BLOCK, spread_step, zero)))
        copy = pltpu.make_async_copy(
            y.at[pl.ds(n * cells, cells), :], y_out.at[pl.ds(n * cells, cells), :], local.at[4 + n]
        )
        copy.start()
        y_copies.append(copy)
    payload_two = tw_one.at[0]
    counts_in = [v * cells for v in valid]
    average = total([m[0] * c for m, c in zip(moments, counts_in)]) / held
    payload_two[...] = jnp.zeros(payload_two.shape, F32)
    payload_two[0:1, :] = average
    payload_two[1:2, :] = total([
        v * m[1] + c * (m[0] - average) * (m[0] - average)
        for m, c, v in zip(moments, counts_in, valid)
    ])
    payload_two[2:3, :] = zero + held
    first = tw_a
    first[dp] = payload_two[...]
    three_level = Spread("dp", n_dp, payload_two, first, a_send.at[1], a_recv.at[1])
    three_level.start()
    if fused:
        two.neighbours(0, every)
    three_level.wait()
    mean, spread, cell_count = join_moments(first)
    second = tw_b
    passed = tw_one.at[1]
    passed[...] = jnp.zeros(passed.shape, F32)
    passed[0:1, :] = mean
    passed[1:2, :] = spread
    passed[2:3, :] = cell_count
    second[rep] = passed[...]
    four_level = Spread("replica", n_rep, passed, second, b_send.at[1], b_recv.at[1])
    four_level.start()
    select = window_matrix(side)
    if fused:
        two.neighbours(1, every[:2])
    four_level.wait()
    mean, spread, _ = join_moments(second)
    sigma = sigma_rows[0]
    variance = spread / pixels / (sigma * sigma)
    inverse_two = lax.rsqrt(variance + EPS_NORM) / sigma
    stats[3:4, :] = mean
    stats[11:12, :] = inverse_two
    scale_two = inverse_two * norms[2:3, :]
    shift_two = norms[3:4, :] - mean * scale_two
    act_copies = []
    for n in range(images):
        def step(i, carry):
            pixel = pl.ds(pl.multiple_of(n * cells + i * BLOCK * side, 16), BLOCK * side)
            values, steep = gelu_both(y[pixel, :] * scale_two + shift_two)
            slope[pixel, :] = steep
            act[pixel, :] = values.astype(BF16)
            return carry
        lax.fori_loop(0, side // BLOCK, step, 0)
        pixels_of = pl.ds(n * cells, cells)
        for k, (made, out) in enumerate((
            (slope.at[pixels_of, :], slope_out.at[pixels_of, :]),
            (act.at[pixels_of, :], act_out.at[pixels_of, :]),
        )):
            copy = pltpu.make_async_copy(made, out, local.at[6 + 2 * k + n])
            copy.start()
            act_copies.append(copy)
        windows[n] = bdot(select, act[n * cells : (n + 1) * cells, :])
        if fused and n == 0:
            two.neighbours(1, every[2:])
            two.opposite(two.order[0])
    if fused:
        two.opposite(two.order[1])
        for zi in two.order:
            two.from_core(zi)
        one.drain()
        two.drain()
        pl.when(~even)(seam_copy.wait_send)
    for level in (one_level, two_level, three_level, four_level):
        level.drain()
    for copy in k1_copies + x_copies + y_copies + act_copies:
        copy.wait()


def forward(n_dp, n_rep, side, share, fused, counts, indices, weights, pictures, stem, start, norms,
            table, inducing, lengthscale, var_mean, var_lower):
    images, cells = pictures.shape[0], side * side
    width = stem.shape[1]
    half = n_dp // 2
    sources = max(n_dp // 4, 1)
    shape = jax.ShapeDtypeStruct
    sem = pltpu.SemaphoreType.DMA
    kernel_rows = 9 * width
    return pl.pallas_call(
        functools.partial(forward_kernel, n_dp, n_rep, side, share, fused),
        out_shape=(
            shape((3, width, 3 * width), BF16),
            shape((kernel_rows, width), BF16),
            shape((images, side, side, width), BF16),
            shape((images * cells, width), F32),
            shape((images * cells, width), F32),
            shape((images * cells, width), BF16),
            shape((images, 16, width), F32),
            shape((images, width), F32),
            shape((16, width), F32),
            shape((images, 32, cells), BF16),
            shape((32, width), BF16),
            shape((3, IND, IND), F32),
            shape((IND, width), F32),
            shape((16, IND), F32),
            shape((IND, var_mean.shape[0] * IND), F32),
            shape((images, 16, 16), F32),
        ),
        in_specs=[SMEM, SMEM, VMEM if fused else ANY] + [VMEM] * 9,
        out_specs=(ANY,) * 6 + (VMEM,) * 10,
        scratch_shapes=[
            pltpu.VMEM((32, cells), F32),
            pltpu.VMEM((share if fused else 8, width), F32),
            pltpu.VMEM((share - 8 if fused else 16, width), BF16),
            pltpu.VMEM((16, width), BF16),
            pltpu.VMEM((kernel_rows, width), BF16),
            pltpu.VMEM((images, side + 2, side, 3 * width), BF16),
            pltpu.VMEM((images * cells, width), F32),
            pltpu.VMEM((images * cells, width), BF16),
            pltpu.VMEM((images * cells, width), F32),
            pltpu.VMEM((2, 16, width), BF16),
            pltpu.VMEM((1, n_dp, 8, width), F32),
            pltpu.VMEM((1, n_rep, 8, width), F32),
            pltpu.VMEM((1, 8, width), F32),
            pltpu.VMEM((1, 8, width), F32),
            pltpu.VMEM((n_dp, 4, width), F32),
            pltpu.VMEM((n_rep, 4, width), F32),
            pltpu.VMEM((2, 4, width), F32),
            sem((2, sources, PIECES, 2)),
            sem((2, sources, PIECES)),
            sem((2, sources, PIECES, 4)),
            sem((2, sources, PIECES, 4)),
            sem((2, sources, PIECES, 4)),
            sem((2, sources, PIECES, 4)),
            sem((2, n_dp)),
            sem((2, n_dp)),
            sem((2, n_rep)),
            sem((2, n_rep)),
            sem((1,)),
            sem((1,)),
            sem((11,)),
            sem((9,)),
        ],
        compiler_params=pltpu.CompilerParams(
            collective_id=0, has_side_effects=True, vmem_limit_bytes=56 << 20
        ),
    )(counts, indices, weights, pictures, stem, start, norms,
      table, inducing, lengthscale, var_mean, var_lower)


class Reduce:
    def __init__(self, near, far, src, parts, whole, planes, out, sems):
        (self.axis, self.size), (self.other, self.others) = near, far
        self.src, self.parts, self.whole, self.planes, self.out = src, parts, whole, planes, out
        self.a_send, self.a_recv = sems[:2]
        self.b_send, self.b_recv, self.c_send, self.c_recv = sems[2:] or [None] * 4
        self.me = lax.axis_index(self.axis)

    def scatter(self):
        for j in range(1, self.size):
            peer = lax.rem(self.me + j, self.size)
            yield remote(
                self.src.at[peer], self.parts.at[self.me], self.a_send.at[j], self.a_recv.at[j],
                {self.axis: peer},
            )

    def start(self):
        for copy in self.scatter():
            copy.start()
        self.parts[self.me] = self.src[self.me]

    def arrive(self):
        for j in range(1, self.size):
            source = lax.rem(self.me + self.size - j, self.size)
            remote(
                self.src.at[source], self.parts.at[source], self.a_send.at[j], self.a_recv.at[j],
                {self.axis: source},
            ).wait_recv()
        self.whole[...] = total([self.parts[i] for i in range(self.size)])

    def middle(self):
        self.arrive()
        self.across()

    def across(self):
        self.planes[lax.axis_index(self.other)] = self.whole[...]
        self.second = Spread(
            self.other, self.others, self.whole, self.planes, self.b_send, self.b_recv
        )
        self.second.start()

    def last(self):
        self.second.wait()
        self.out[self.me] = total([self.planes[i] for i in range(self.others)])
        self.third = Spread(
            self.axis, self.size, self.out.at[self.me], self.out, self.c_send, self.c_recv
        )
        self.third.start()

    def finish(self):
        self.finish_last()
        self.drain()

    def drain(self):
        for copy in self.scatter():
            copy.wait_send()

    def finish_last(self):
        self.third.wait()
        self.second.drain()
        self.third.drain()


def reduce_scratch(size, others, rows, width):
    per = -(-rows // size)
    sem = pltpu.SemaphoreType.DMA
    return [
        pltpu.VMEM((size, per, width), F32),
        pltpu.VMEM((size, per, width), F32),
        pltpu.VMEM((per, width), F32),
        pltpu.VMEM((others, per, width), F32),
        pltpu.VMEM((size, per, width), F32),
        sem((size,)), sem((size,)), sem((others,)), sem((others,)), sem((size,)), sem((size,)),
    ]


def put_rows(ref, first, values):
    per = ref.shape[1]
    for k in range(values.shape[0]):
        row = first + k
        ref[row // per, row % per : row % per + 1, :] = values[k : k + 1, :]


def gelu_slope(x):
    return gelu_both(x)[1]


def fold(values):
    return jnp.sum(values.reshape(values.shape[0] // 8, 8, values.shape[1]), axis=0)


def head_kernel(
    n_dp, n_rep, side, size, classes, samples,
    counts, labels, k2_in, y_in, slope_in, windows, stem_pool, stats, norms,
    lengthscale, chol, z_pad, v_pad, f_pad, noise,
    cat_out, k8_out, head_out, grads_out,
    k2, k8, y, d_pre, cat, pattern, x_pad, kx_pad, d_rows,
    ex_a, ex_b, one_a, one_b, a_send, a_recv, b_send, b_recv, local,
):
    images = stem_pool.shape[0]
    width = stem_pool.shape[1]
    cells = side * side
    dp, rep = lax.axis_index("dp"), lax.axis_index("replica")
    loads = [
        pltpu.make_async_copy(k2_in, k2, local.at[0]),
        pltpu.make_async_copy(y_in, y, local.at[1]),
        pltpu.make_async_copy(slope_in, d_pre, local.at[2]),
    ]
    for copy in loads:
        copy.start()
    greeted = greet(n_dp, n_rep)

    sigma_one, sigma_two = stats[4:5, :], stats[5:6, :]
    pixels = stats[2:3, :]
    scale = cells / stats[2:3, 0:1]
    ell = lengthscale[...].reshape(1, width)
    zs = z_pad[...]
    ones = jnp.ones((8, width), F32)
    group = lax.broadcasted_iota(jnp.int32, (classes * IND, 16), 0) // IND
    which = lax.broadcasted_iota(jnp.int32, (classes * IND, 16), 1)
    groups = jnp.where(group == which, 1.0, 0.0)

    loads[0].wait()
    pooled_raw = jnp.zeros((16, width), F32)
    for t in range(9):
        parts = []
        rest = [windows[n, t : t + 1, :] for n in range(images)]
        for _ in range(3):
            parts += [r.astype(BF16).astype(F32) for r in rest]
            rest = [r - p for r, p in zip(rest, parts[-images:])]
        parts.append(jnp.zeros((16 - 3 * images, width), F32))
        lhs = jnp.concatenate(parts, axis=0).astype(BF16)
        pooled_raw = pooled_raw + bdot(lhs, k2[t * width : (t + 1) * width, :])
    x_pad[...] = jnp.zeros(x_pad.shape, F32)
    branch_pool = []
    for n in range(images):
        row = total([pooled_raw[k * images + n : k * images + n + 1] for k in range(3)])
        branch_pool.append(row / (cells * sigma_two))
        x_pad[n : n + 1, :] = (stem_pool[n : n + 1, :] + branch_pool[n]) / ell
    xs = x_pad[...]

    kx_pad[...] = jnp.zeros(kx_pad.shape, F32)
    for n in range(images):
        off = zs - xs[n : n + 1, :]
        kx_pad[n : n + 1, :] = jnp.exp(-0.5 * hdot(ones, off * off, ((1,), (1,))))[0:1]
    lanes = lax.broadcasted_iota(jnp.int32, (8, IND), 1)
    kx = jnp.where(lanes < size, kx_pad[...], 0.0)
    inv = chol[2]
    means = v_pad[...]
    factors = f_pad[...]
    proj = hdot(kx, inv, ((1,), (1,)))
    average = hdot(proj, means, ((1,), (1,)))
    spread = hdot(proj, factors)
    variance = (
        1.0 - jnp.sum(proj * proj, axis=1, keepdims=True) + hdot(spread * spread, groups)
    )
    std = jnp.sqrt(variance)
    class_lane = lax.broadcasted_iota(jnp.int32, (1, 16), 1)
    sample_row = lax.broadcasted_iota(jnp.int32, (16, 16), 0)
    inside = (lax.broadcasted_iota(jnp.int32, (16, 16), 1) < classes) & (sample_row < samples)
    count = counts[0]
    loss = jnp.zeros((1, 1), F32)
    g_avg_rows, g_var_rows = [], []
    for n in range(images):
        drawn = average[n : n + 1, :] + std[n : n + 1, :] * noise[n]
        drawn = jnp.where(inside, drawn, -1e30)
        shifted = drawn - jnp.max(drawn, axis=1, keepdims=True)
        exps = jnp.where(inside, jnp.exp(shifted), 0.0)
        sums = jnp.sum(exps, axis=1, keepdims=True)
        sums = jnp.where(sample_row[:, 0:1] < samples, sums, 1.0)
        hot = jnp.where(class_lane == labels[n], 1.0, 0.0)
        picked = jnp.where(inside, (shifted - jnp.log(sums)) * hot, 0.0)
        held = jnp.where(count > n, 1.0 / samples, 0.0)
        loss = loss - held * jnp.sum(jnp.sum(picked, axis=1, keepdims=True), axis=0, keepdims=True)
        g_samples = jnp.where(inside, exps / sums - hot, 0.0) * (held * scale)
        g_avg_rows.append(jnp.sum(g_samples, axis=0, keepdims=True))
        g_var_rows.append(
            0.5 * jnp.sum(g_samples * noise[n], axis=0, keepdims=True) / std[n : n + 1, :]
        )
    blank = [jnp.zeros((8 - images, 16), F32)]
    g_avg = jnp.concatenate(g_avg_rows + blank, axis=0)
    g_var = jnp.concatenate(g_var_rows + blank, axis=0)
    g_spread = 2.0 * spread * hdot(g_var, groups, ((1,), (1,)))
    g_proj = (
        hdot(g_avg, means)
        - 2.0 * proj * jnp.sum(g_var, axis=1, keepdims=True)
        + hdot(g_spread, factors, ((1,), (1,)))
    )
    g_kx = hdot(g_proj, inv)
    weights = -kx * g_kx
    g_x = xs * jnp.sum(weights, axis=1, keepdims=True) - hdot(weights, zs)
    d_pooled = g_x / ell
    d_rows[...] = jnp.zeros(d_rows.shape, BF16)
    d_rows[0:8, :] = (d_pooled / cells).astype(BF16)
    d_two = d_rows[...]

    taps = [
        bdot(d_two, k2[t * width : (t + 1) * width, :], ((1,), (1,))) / sigma_two for t in range(9)
    ]
    wide = lax.broadcasted_iota(jnp.int32, (side, 1), 0)
    for n in range(images):
        for kind, kept in enumerate(((0, 1), (0, 1, 2), (1, 2))):
            across = [total([taps[3 * r + c][n : n + 1] for r in kept]) for c in range(3)]
            middle = across[0] + across[1] + across[2]
            pattern[n, kind] = jnp.where(
                wide == 0, across[0] + across[1],
                jnp.where(wide == side - 1, across[1] + across[2], middle),
            )

    loads[1].wait()
    loads[2].wait()
    mean_two, inverse_two = stats[3:4, :], stats[11:12, :]
    gain = norms[2:3, :]
    none = jnp.zeros((8, width), F32)
    sums = (none, none)
    for n in range(images):
        def step(h, carry):
            kind = jnp.where(h == 0, 0, jnp.where(h == side - 1, 2, 1))
            at = pl.ds(pl.multiple_of(n * cells + h * side, side), side)
            normed = (y[at, :] - mean_two) * inverse_two
            grad = d_pre[at, :] * pattern[n, kind]
            d_pre[at, :] = grad
            return carry[0] + fold(grad), carry[1] + fold(grad * normed)
        sums = lax.fori_loop(0, side, step, sums)
    one_a[...] = jnp.zeros(one_a.shape, F32)
    one_a[0:1, :] = jnp.sum(sums[0], axis=0, keepdims=True)
    one_a[1:2, :] = jnp.sum(sums[1], axis=0, keepdims=True)
    one_a[2:3, :] = total([
        cells * branch_pool[n] * d_two[n : n + 1, :].astype(F32) for n in range(images)
    ])
    ex_a[dp] = one_a[...]
    first = Spread("dp", n_dp, one_a, ex_a, a_send, a_recv)
    greeted()
    first.start()

    grads_out[...] = jnp.zeros(grads_out.shape, F32)
    over = hdot(weights, jnp.ones((8, 128), F32), ((0,), (0,)))[:, 0:1]
    g_z = zs * over - hdot(weights, xs, ((0,), (0,)))
    grads_out[0:size, :] = g_z[0:size]
    grads_out[20:21, :] = jnp.sum(g_x * xs, axis=0, keepdims=True)
    grads_out[23:24, :] = jnp.zeros((1, width), F32) + loss
    grads_out[32:64, 0 : classes * IND] = hdot(proj, g_spread, ((0,), (0,)))
    grads_out[32:64, 384 : 384 + IND] = hdot(g_kx, proj, ((0,), (0,)))
    grads_out[32:48, 512 : 512 + IND] = hdot(g_avg, proj, ((0,), (0,)))
    head_out[...] = jnp.zeros(head_out.shape, F32)
    head_out[0:8, :] = d_pooled
    head_out[18:19, :] = cells / pixels
    head_out[8:16, :] = d_two[0:8, :].astype(F32)

    def eighth(t, carry):
        at = pl.ds(pl.multiple_of(t * (width // 2), width // 2), width // 2)
        k8[at, :] = (k2[at, :].astype(F32) * KERNEL_SCALE).astype(F8)
        return carry

    lax.fori_loop(0, 9, eighth, 0)
    first.wait()
    one_b[...] = total([ex_a[i] for i in range(n_dp)])
    ex_b[rep] = one_b[...]
    second = Spread("replica", n_rep, one_b, ex_b, b_send, b_recv)
    second.start()
    lax.fori_loop(9, 18, eighth, 0)
    k8_copy = pltpu.make_async_copy(k8, k8_out, local.at[3 + images])
    k8_copy.start()
    second.wait()
    joined = total([ex_b[i] for i in range(n_rep)])
    d_bias, d_gain = joined[0:1, :], joined[1:2, :]
    head_out[16:17, :] = d_gain
    head_out[17:18, :] = d_bias
    head_out[19:20, :] = joined[2:3, :]
    true_scale = inverse_two * sigma_one * gain
    cat_copies = []
    for n in range(images):
        held = jnp.where(count > n, 1.0, 0.0)
        def step(i, carry):
            rows = BLOCK * side
            at = pl.ds(pl.multiple_of(n * cells + i * rows, rows), rows)
            normed = (y[at, :] - mean_two) * inverse_two
            grad = (true_scale * held) * (
                d_pre[at, :] - d_bias / pixels - normed * (d_gain / pixels)
            )
            cat[at, :] = grad.astype(BF16)
            return carry
        lax.fori_loop(0, side // BLOCK, step, 0)
        here = pl.ds(n * cells, cells)
        copy = pltpu.make_async_copy(cat.at[here, :], cat_out.at[here, :], local.at[3 + n])
        copy.start()
        cat_copies.append(copy)
    for level in (first, second):
        level.drain()
    for copy in cat_copies + [k8_copy]:
        copy.wait()


def head(n_dp, n_rep, side, size, classes, samples, counts, labels, k2, y, slope, windows, stem_pool,
         stats, norms, lengthscale, chol, z_pad, v_pad, f_pad, noise):
    images, width = stem_pool.shape
    shape = jax.ShapeDtypeStruct
    sem = pltpu.SemaphoreType.DMA
    return pl.pallas_call(
        functools.partial(head_kernel, n_dp, n_rep, side, size, classes, samples),
        out_shape=(
            shape(y.shape, BF16),
            shape(k2.shape, F8),
            shape((24, width), F32),
            shape((64, width), F32),
        ),
        in_specs=[SMEM, SMEM, ANY, ANY, ANY] + [VMEM] * 10,
        out_specs=(ANY, ANY, VMEM, VMEM),
        scratch_shapes=[
            pltpu.VMEM(k2.shape, BF16),
            pltpu.VMEM(k2.shape, F8),
            pltpu.VMEM(y.shape, F32),
            pltpu.VMEM(y.shape, F32),
            pltpu.VMEM(y.shape, BF16),
            pltpu.VMEM((images, 3, side, width), F32),
            pltpu.VMEM((8, width), F32),
            pltpu.VMEM((8, IND), F32),
            pltpu.VMEM((16, width), BF16),
            pltpu.VMEM((n_dp, 4, width), F32),
            pltpu.VMEM((n_rep, 4, width), F32),
            pltpu.VMEM((4, width), F32),
            pltpu.VMEM((4, width), F32),
            sem((n_dp,)), sem((n_dp,)), sem((n_rep,)), sem((n_rep,)),
            sem((4 + images,)),
        ],
        compiler_params=pltpu.CompilerParams(
            collective_id=1, has_side_effects=True, vmem_limit_bytes=56 << 20
        ),
    )(counts, labels, k2, y, slope, windows, stem_pool, stats, norms,
      lengthscale, chol, z_pad, v_pad, f_pad, noise)


def greet_all(n_dp, n_rep):
    here = lax.axis_index("dp") * n_rep + lax.axis_index("replica")
    count = n_dp * n_rep
    barrier = pltpu.get_barrier_semaphore()

    def signal(j, carry):
        other = lax.rem(here + j, count)
        pl.semaphore_signal(
            barrier, inc=1, device_id={"dp": other // n_rep, "replica": lax.rem(other, n_rep)},
            device_id_type=MESH,
        )
        return carry

    lax.fori_loop(1, count, signal, 0)
    return lambda: pl.semaphore_wait(barrier, count - 1)


def chunk_plan(share, width, count):
    def segments(first, last, base):
        result = []
        while first < last:
            c = (first - base) // width
            end = min(last, base + (c + 1) * width)
            result.append((c, first - base - c * width, end - base - c * width))
            first = end
        return result

    plan, done, carried = [], 0, 0
    for r in range(3):
        first, last = r * 3 * width, (r + 1) * 3 * width
        items = []
        while done < count and (done + 1) * share <= last:
            begin = max(done * share, first)
            items.append((done, carried, segments(begin, (done + 1) * share, first)))
            carried = 0
            done += 1
        begin = max(done * share, first)
        plan.append((items, segments(begin, last, first)))
        carried = last - begin
    return plan


def chain_pieces(share):
    tiles = (share + 8) // 16
    count = min(4, max(tiles, 1))
    edges = [tiles * i // count * 16 for i in range(count + 1)]
    return [(lo, hi - lo) for lo, hi in zip(edges, edges[1:])]


def backward_kernel(
    n_dp, n_rep, side, share, fused,
    counts, d_in, x_in, k1_in, k8_in, act_in, patches, stem, stats, norms, windows, head_rows, grads,
    part_out, big_out, sums_out, late_out,
    cat, d_one, x, k1, k8, cat8, held_rows, carry, mine, sib, rin, zin, zout, part, comb, wall, flat, flat_d,
    *rest,
):
    early = rest[0:11]
    late = rest[11:15]
    (c_send, c_recv, r_send, r_recv, z_send, z_recv, w_send, w_recv, local) = rest[15:]
    images = patches.shape[0]
    width = stem.shape[1]
    cells = side * side
    dp, rep = lax.axis_index("dp"), lax.axis_index("replica")
    core, z = lax.rem(dp, 2), dp // 2
    n_z, half = n_dp // 2, n_dp // 2
    sources = max(n_dp // 4, 1)
    owners = half * n_rep
    here = dp * n_rep + rep
    loads = [
        pltpu.make_async_copy(d_in, d_one, local.at[0]),
        pltpu.make_async_copy(x_in, x, local.at[1]),
        pltpu.make_async_copy(k1_in, k1, local.at[2]),
        pltpu.make_async_copy(k8_in, k8, local.at[3]),
    ]
    for copy in loads:
        copy.start()
    greeted = greet_all(n_dp, n_rep)
    count = counts[0]
    valid = [jnp.where(count > n, 1.0, 0.0) for n in range(images)]

    early_sum = Reduce(("dp", n_dp), ("replica", n_rep), *early[:5], early[5:])

    def first_tap(owner):
        return jnp.minimum((owner * share) // width, 7)

    def window_copy(owner):
        return remote(
            comb.at[pl.ds(first_tap(owner), 2)], wall.at[here], w_send.at[owner], w_recv.at[here],
            {"dp": half + owner // n_rep, "replica": lax.rem(owner, n_rep)},
        )

    def send_windows(j, c):
        owner = lax.rem(here + j, owners)

        @pl.when(half * n_rep + owner != here)
        def _():
            window_copy(owner).start()
        return c

    def first_rows():
        source = early[0]
        source[...] = jnp.zeros(source.shape, F32)
        put_rows(source, 0, grads[...])
        gram = total([
            bdot(patches[n], patches[n], ((1,), (1,))) * valid[n] for n in range(images)
        ])
        wide = jnp.concatenate([gram, jnp.zeros((32, 128 - 32), F32)], axis=1)
        per = source.shape[1]
        for k in range(32):
            row = 64 + k
            source[row // per, row % per : row % per + 1, 0:128] = wide[k : k + 1, :]
        if fused:
            for t in range(9):
                comb[t, 0:images, :] = jnp.concatenate(
                    [windows[n, t : t + 1, :] for n in range(images)], axis=0
                )
                comb[t, images : 2 * images, :] = head_rows[8 : 8 + images, :]

    def first_sends():
        early_sum.start()
        if fused:
            lax.fori_loop(0, owners, send_windows, 0)

    def row_of_taps(r):
        return total([
            lax.dot_general(
                x[n].reshape(cells, width),
                cat[n, pl.ds(2 - r, side)].reshape(cells, 3 * width),
                (((0,), (0,)), ((), ())),
                preferred_element_type=F32,
            )
            for n in range(images)
        ])

    def joined(acc, parts):
        pieces = [acc[a:b, (2 - c) * width : (3 - c) * width] for c, a, b in parts]
        return pieces[0] if len(pieces) == 1 else jnp.concatenate(pieces, axis=0)

    def sib_copy(o):
        return remote(
            mine.at[o], sib.at[(o // (2 * n_rep)) * n_rep + o % n_rep],
            c_send.at[o], c_recv.at[(o // (2 * n_rep)) * n_rep + o % n_rep],
            {"dp": dp + 1 - 2 * core},
        )

    def ship(acc, items, leftover):
        for o, carried, parts in items:
            value = joined(acc, parts)
            if carried:
                value = jnp.concatenate([carry[0:carried, :], value], axis=0)
            mine[o, 0:share, :] = value.astype(BF16)
            pl.when(core != (o // n_rep) % 2)(sib_copy(o).start)
        if leftover:
            value = joined(acc, leftover)
            carry[0 : value.shape[0], :] = value

    reps = (rep, rep + 1 - 2 * lax.rem(rep, 2), rep + 2 - 4 * (rep // 2), 3 - rep)
    cut = (share + 8) // 32 * 16
    halves = (pl.ds(0, cut), pl.ds(cut, share + 8 - cut))

    def slot(zi, k):
        return (zi * 2 + core) * n_rep + reps[k]

    def plane_copies(zi, step):
        for h in range(2):
            near, far = 1 + h, 2 - h
            at = halves[h]
            if step == 0:
                for s, k in enumerate((near, 3)):
                    yield remote(
                        mine.at[slot(zi, k), at, :], rin.at[zi, s, at, :],
                        r_send.at[zi, 2 * s + h], r_recv.at[zi, 2 * s + h], {"replica": reps[near]},
                    )
            else:
                yield remote(
                    mine.at[slot(zi, far), at, :], rin.at[zi, 2, at, :],
                    r_send.at[zi, 4 + h], r_recv.at[zi, 4 + h], {"replica": reps[far]},
                )

    def join_cores(zi):
        for k in (3, 1, 2, 0):
            at = zi * n_rep + reps[k]
            remote(
                mine.at[0], sib.at[at], c_send.at[0], c_recv.at[at], {"dp": dp + 1 - 2 * core}
            ).wait_recv()
            mine[slot(zi, k)] = (
                mine[slot(zi, k)].astype(F32) + sib[at].astype(F32)
            ).astype(BF16)
        for copy in plane_copies(zi, 0):
            copy.start()

    def join_near(zi):
        for copy in plane_copies(zi, 0):
            copy.wait_recv()
        for h in range(2):
            at, o = halves[h], slot(zi, 2 - h)
            mine[o, at, :] = (
                mine[o, at, :].astype(F32) + rin[zi, 1, at, :].astype(F32)
            ).astype(BF16)
        for copy in plane_copies(zi, 1):
            copy.start()

    def join_far(zi):
        for copy in plane_copies(zi, 1):
            copy.wait_recv()
        part[zi] = (
            mine[slot(zi, 0)].astype(F32) + rin[zi, 0].astype(F32) + rin[zi, 2].astype(F32)
        )

    z_pieces = chain_pieces(share)
    every = range(len(z_pieces))

    def z_copy(zi, piece, down):
        start, rows = z_pieces[piece]
        at = pl.ds(start, rows)
        step = n_dp - 2 if down else 2
        return remote(
            zout.at[zi, at, :], zin.at[zi, int(down), at, :],
            z_send.at[zi, piece], z_recv.at[zi, piece, int(down)],
            {"dp": lax.rem(dp + step, n_dp)},
        )

    def chain(zi, distance, *pieces):
        for down in (True, False):
            reach = n_z - 1 - zi if down else zi
            if distance > reach:
                continue
            offset = distance if down else -distance
            @pl.when(z == zi + offset)
            def _():
                for piece in pieces or every:
                    start, rows = z_pieces[piece]
                    at = pl.ds(start, rows)
                    if distance < reach:
                        z_copy(zi, piece, down).wait_recv()
                        part[zi, at, :] += zin[zi, int(down), at, :].astype(F32)
                    if distance:
                        zout[zi, at, :] = part[zi, at, :].astype(BF16)
                        z_copy(zi, piece, down).start()

    def window_part():
        @pl.when(dp >= half)
        def _():
            owner = here - owners
            wall[here] = comb[pl.ds(first_tap(owner), 2)]

            def take(j, c):
                origin = lax.rem(here + j, n_dp * n_rep)
                remote(
                    comb.at[pl.ds(0, 2)], wall.at[origin], w_send.at[0], w_recv.at[origin],
                    {"dp": origin // n_rep, "replica": lax.rem(origin, n_rep)},
                ).wait_recv()
                return c

            lax.fori_loop(1, n_dp * n_rep, take, 0)
            for s in range(n_dp * n_rep):
                for tap in range(2):
                    flat[tap, s * images : (s + 1) * images, :] = wall[s, tap, 0:images, :]
                flat_d[s * images : (s + 1) * images, :] = wall[s, 0, images : 2 * images, :]
            for tap in range(2):
                held_rows[tap * width : (tap + 1) * width, :] = hdot(
                    flat[tap], flat_d[...], ((0,), (0,))
                )
            offset = owner * share - first_tap(owner) * width
            part_out[...] = held_rows[pl.ds(pl.multiple_of(offset, 8), share), :]

    for n in range(images):
        edge = jnp.zeros((1, side, 3 * width), BF16)
        cat[n, 0:1] = edge
        cat[n, side + 1 : side + 2] = edge
    first_rows()
    loads[0].wait()
    for n in range(images):
        def shift_gradient(i, carried):
            rows = BLOCK * side
            at = pl.ds(pl.multiple_of(n * cells + i * rows, rows), rows)
            store_shifted(cat, n, i * BLOCK, BLOCK, d_one[at, :].astype(F32), side)
            return carried
        lax.fori_loop(0, side // BLOCK, shift_gradient, 0)
    greeted()
    first_sends()
    loads[1].wait()
    if fused:
        plan = chunk_plan(share, width, owners)
        for r in range(3):
            acc = row_of_taps(r)
            if r > 0:
                pl.when(core == r - 1)(lambda: join_cores(0))
            ship(acc, *plan[r])
            if r == 1:
                early_sum.middle()
    else:
        for r in range(3):
            acc = row_of_taps(r)
            for c in range(3):
                held_rows[0:width, :] = acc[:, (2 - c) * width : (3 - c) * width]
                out_copy = pltpu.make_async_copy(
                    held_rows.at[pl.ds(0, width), :],
                    part_out.at[pl.ds((3 * r + c) * width, width), :],
                    local.at[4],
                )
                out_copy.start()
                out_copy.wait()
        early_sum.middle()

    loads[2].wait()
    sigma = stats[4:5, :]
    mean_one, inverse_one, pixels = stats[0:1, :], stats[1:2, :], stats[2:3, :]
    gain, bias = norms[0:1, :], norms[1:2, :]
    none = jnp.zeros((8, width), F32)
    block_rows = 2 * BLOCK * side
    per_image = side // (2 * BLOCK)
    blocks = images * per_image

    def input_gradient(b):
        n, i = b // per_image, b % per_image
        acc = None
        for r in range(3):
            lhs = cat[n, pl.ds(i * 2 * BLOCK + r, 2 * BLOCK)].reshape(block_rows, 3 * width)
            one = bdot(lhs, k1[r], ((1,), (1,)))
            acc = one if acc is None else acc + one
        first = (b % 2) * width
        held_rows[first : first + block_rows, :] = acc

    def through_gelu(b, carried):
        n, i = b // per_image, b % per_image
        first = (b % 2) * width
        pixel = patches[n, :, i * block_rows : (i + 1) * block_rows]
        normed = (bdot(pixel, stem[...], ((0,), (0,))) - mean_one) * inverse_one
        grad = gelu_slope(normed * gain + bias) * held_rows[first : first + block_rows, :] * (
            valid[n] / sigma
        )
        down = (grad * (inverse_one * gain) + head_rows[n : n + 1, :] / cells).astype(BF16)
        return (
            carried[0] + fold(grad),
            carried[1] + fold(grad * normed),
            carried[2] + bdot(pixel, down),
        )

    sums = (none, none, jnp.zeros((32, width), F32))
    between = {
        0: [lambda: join_near(0), lambda: join_cores(1)],
        1: [lambda: join_far(0), lambda: chain(0, 3)],
        2: [lambda: chain(0, 2, 0, 1), lambda: join_near(1)],
        3: [lambda: chain(0, 2, 2, 3), lambda: chain(0, 1, 0, 1)],
        4: [lambda: join_far(1), lambda: chain(1, 2)],
    }
    for b in range(blocks + 1):
        if b < blocks:
            input_gradient(b)
        if b > 0:
            sums = through_gelu(b - 1, sums)
        if fused:
            for event in between.get(b, ()):
                event()
    late_sum = Reduce(
        ("dp", n_dp), ("replica", n_rep), late[0], late[1], late_out, None, None, late[2:]
    )
    late[0][...] = jnp.zeros(late[0].shape, F32)
    put_rows(late[0], 0, sums[2][0:27])
    put_rows(late[0], 27, jnp.sum(sums[0], axis=0, keepdims=True))
    put_rows(late[0], 28, jnp.sum(sums[1], axis=0, keepdims=True))
    late_sum.start()
    early_sum.last()

    act_copy = pltpu.make_async_copy(act_in, d_one, local.at[5])
    act_copy.start()
    edge = jnp.zeros((1, side, 3 * width), F8)
    cat8[0, 0:1] = edge
    cat8[0, side + 1 : side + 2] = edge

    def shift_act(n):
        def step(i, carried):
            rows = BLOCK * side
            at = pl.ds(pl.multiple_of(n * cells + i * rows, rows), rows)
            store_shifted(
                cat8, 0, i * BLOCK, BLOCK, d_one[at, :].astype(F32) * ACT_SCALE, side
            )
            return carried
        lax.fori_loop(0, side // BLOCK, step, 0)

    squares = none
    between = {
        0: [lambda: chain(0, 1, 2, 3), lambda: chain(1, 1, 0)],
        1: [lambda: chain(1, 1, 1), lambda: chain(0, 0, 0, 1), window_part],
        2: [lambda: chain(1, 1, 2), lambda: chain(1, 0, 0)],
        3: [lambda: chain(1, 1, 3), lambda: chain(0, 0, 2, 3), lambda: chain(1, 0, 1, 2, 3)],
    }
    for b in range(blocks):
        n, i = b // per_image, b % per_image
        if b == 0:
            act_copy.wait()
            loads[3].wait()
        if i == 0:
            shift_act(n)
        acc = None
        for r in range(3):
            lhs = cat8[0, pl.ds(i * 2 * BLOCK + r, 2 * BLOCK)].reshape(block_rows, 3 * width)
            one = bdot(lhs, k8[r * 3 * width : (r + 1) * 3 * width, :])
            acc = one if acc is None else acc + one
        squares = squares + valid[n] * fold(acc * acc)
        if fused:
            for event in between.get(b, ()):
                event()
    sigma_two = stats[5:6, :] * (ACT_SCALE * KERNEL_SCALE)
    sums_out[...] = jnp.zeros(sums_out.shape, F32)
    sums_out[0:1, :] = jnp.sum(squares, axis=0, keepdims=True) / (sigma_two * sigma_two)

    if fused:
        @pl.when(dp < half)
        def _():
            for zi in range(sources):
                @pl.when(z == zi)
                def _():
                    part_out[...] = part[zi, 0:share, :]

        def drain_windows(j, c):
            owner = lax.rem(here + j, owners)

            @pl.when(half * n_rep + owner != here)
            def _():
                window_copy(owner).wait_send()
            return c

        lax.fori_loop(0, owners, drain_windows, 0)
        for o in range(owners):
            pl.when(core != (o // n_rep) % 2)(sib_copy(o).wait_send)
        for zi in range(sources):
            for step in range(2):
                for copy in plane_copies(zi, step):
                    copy.wait_send()
            for piece in range(len(z_pieces)):
                pl.when(z > zi)(z_copy(zi, piece, True).wait_send)
                pl.when(z < zi)(z_copy(zi, piece, False).wait_send)
    early_sum.finish()
    late_sum.arrive()
    late_sum.drain()
    per = early[4].shape[1]
    for s in range(n_dp):
        for j in range(per):
            big_out[s * per + j : s * per + j + 1, :] = early[4][s, j : j + 1, :]


def backward(n_dp, n_rep, side, share, fused, counts, d_one, x, k1, k8, act, patches, stem, stats, norms,
             windows, head_rows, grads):
    images, width = patches.shape[0], stem.shape[1]
    half = n_dp // 2
    sources = max(n_dp // 4, 1)
    owners = half * n_rep
    devices = n_dp * n_rep
    shape = jax.ShapeDtypeStruct
    sem = pltpu.SemaphoreType.DMA
    rows = share + 8
    small = (1, 8, 128)
    early = reduce_scratch(n_dp, n_rep, 96, width)
    early_rows = early[0].shape[0] * early[0].shape[1]
    part_rows = share if fused else 9 * width
    pieces = len(chain_pieces(share))
    return pl.pallas_call(
        functools.partial(backward_kernel, n_dp, n_rep, side, share, fused),
        out_shape=(
            shape((part_rows, width), F32),
            shape((early_rows, width), F32),
            shape((8, width), F32),
            shape((-(-32 // n_dp), width), F32),
        ),
        in_specs=[SMEM] + [ANY] * 5 + [VMEM] * 7,
        out_specs=(VMEM if fused else ANY, VMEM, VMEM, VMEM),
        scratch_shapes=[
            pltpu.VMEM((images, side + 2, side, 3 * width), BF16),
            pltpu.VMEM(d_one.shape, BF16),
            pltpu.VMEM(x.shape, BF16),
            pltpu.VMEM(k1.shape, BF16),
            pltpu.VMEM(k8.shape, F8),
            pltpu.VMEM((1, side + 2, side, 3 * width), F8),
            pltpu.VMEM((2 * width, width), F32),
            pltpu.VMEM((rows if fused else 8, width), F32),
            pltpu.VMEM((owners, rows, width) if fused else small, BF16),
            pltpu.VMEM((sources * n_rep, rows, width) if fused else small, BF16),
            pltpu.VMEM((sources, 3, rows, width) if fused else small, BF16),
            pltpu.VMEM((sources, 2, rows, width) if fused else small, BF16),
            pltpu.VMEM((sources, rows, width) if fused else small, BF16),
            pltpu.VMEM((sources, rows, width) if fused else small, F32),
            pltpu.VMEM((10, 2 * images, width) if fused else small, F32),
            pltpu.VMEM((devices, 2, 2 * images, width) if fused else small, F32),
            pltpu.VMEM((2, devices * images, width) if fused else small, F32),
            pltpu.VMEM((devices * images, width) if fused else small[1:], F32),
            *early,
            pltpu.VMEM((n_dp, -(-32 // n_dp), width), F32),
            pltpu.VMEM((n_dp, -(-32 // n_dp), width), F32),
            sem((n_dp,)), sem((n_dp,)),
            sem((owners,)), sem((sources * n_rep,)),
            sem((sources, 6)), sem((sources, 6)),
            sem((sources, pieces)), sem((sources, pieces, 2)),
            sem((owners,)), sem((devices,)),
            sem((6,)),
        ],
        compiler_params=pltpu.CompilerParams(
            collective_id=2, has_side_effects=True, vmem_limit_bytes=62 << 20
        ),
    )(counts, d_one, x, k1, k8, act, patches, stem, stats, norms, windows, head_rows, grads)


def whole_sum(values):
    return jnp.sum(jnp.sum(values, axis=1, keepdims=True), axis=0, keepdims=True)


def lamb_step(weight, gradient, first, second, out, rows=False):
    new_one, new_two, direction = lamb_moments(weight, gradient, first, second)
    if rows:
        sizes = [jnp.sum(v * v, axis=1, keepdims=True) for v in (weight, direction)]
    else:
        sizes = [whole_sum(v * v) for v in (weight, direction)]
    new_weight = weight - RATE * (jnp.sqrt(sizes[0]) / jnp.sqrt(sizes[1])) * direction
    for ref, value in zip(out, (new_weight, new_one, new_two)):
        ref[...] = value.reshape(ref.shape)


def conv_gradient(first, part, arrived, conv_w, start, head_rows, stats, norm_w, flat, own):
    width = stats.shape[1]
    share = own.shape[0]
    lanes = width // 128
    def pick(row):
        return jnp.where(first, stats[row : row + 1, :], stats[row + 1 : row + 2, :])
    sigma, norm, unit = pick(4)[:, 0:1], pick(6)[:, 0:1], pick(8)
    inverse = stats[11:12, :] * stats[4:5, :]
    along = jnp.where(
        first,
        norm_w[2:3, :] * head_rows[16:17, :] * (EPS_NORM * inverse * inverse),
        head_rows[19:20, :],
    )
    d_sigma = -jnp.sum(along, axis=1, keepdims=True) / sigma
    vector = jnp.where(first, start[0:1, :], start[1:2, :])
    for k in range(lanes):
        own[:, k * 128 : (k + 1) * 128] = (
            conv_w[pl.ds(k, share, stride=lanes), :].astype(BF16).astype(F32)
        )
    rows = own[...]
    left = jnp.sum(rows * vector, axis=1, keepdims=True) / norm
    back = jnp.sum(rows * (unit / norm), axis=1, keepdims=True) - left * (sigma / norm)
    arrived()
    grad = part[...] / sigma + (left * d_sigma) * unit + (back * d_sigma) * vector
    for k in range(lanes):
        flat[pl.ds(k, share, stride=lanes), :] = grad[:, k * 128 : (k + 1) * 128]


def small_kernel(
    conv_ratio, conv_grad, conv_w, conv_m, conv_s, big, late, joined, head_rows, stats, chol, stem_w, stem_m, stem_s,
    norm_w, norm_m, norm_s, ind_w, ind_m, ind_s, len_w, len_m, len_s,
    mean_w, mean_m, mean_s, low_w, low_m, low_s, *rest,
):
    outs = rest[4:22]
    parts_out, sigmas_out, rms_out, z_pad, stem_pad = rest[22:]

    def conv_step():
        weight = conv_w[...]
        new_one, new_two, direction = lamb_moments(weight, conv_grad[...], conv_m[...], conv_s[...])
        new_conv = weight - conv_ratio[0] * direction
        for ref, value in zip(rest[:4], (new_conv, new_one, new_two, new_conv)):
            ref[...] = value.astype(ref.dtype)

    def small_step():
        small_updates(
            big, late, joined, head_rows, stats, chol, stem_w, stem_m, stem_s,
            norm_w, norm_m, norm_s, ind_w, ind_m, ind_s, len_w, len_m, len_s,
            mean_w, mean_m, mean_s, low_w, low_m, low_s, outs,
            parts_out, sigmas_out, rms_out, z_pad, stem_pad,
        )

    return ((4, slice(0, 4), conv_step), (28, slice(4, 22), small_step))


def small_updates(
    big, late, joined, head_rows, stats, chol, stem_w, stem_m, stem_s,
    norm_w, norm_m, norm_s, ind_w, ind_m, ind_s, len_w, len_m, len_s,
    mean_w, mean_m, mean_s, low_w, low_m, low_s, outs,
    parts_out, sigmas_out, rms_out, z_pad, stem_pad,
):
    width = stem_w.shape[1]
    size, classes = ind_w.shape[0], mean_w.shape[0]
    pixels = stats[2:3, :]
    mean_one, inverse_one = stats[0:1, :], stats[1:2, :]
    scale = head_rows[18:19, 0:1]
    parts_out[1] = jnp.sum(1.0 / scale)
    sigmas_out[0] = jnp.sum(stats[4:5, 0:1])
    sigmas_out[1] = jnp.sum(stats[5:6, 0:1])
    cells_all = pixels[:, 0:1] * width
    rms_out[0] = jnp.sum(
        jnp.sqrt(jnp.sum(stats[10:11, :], axis=1, keepdims=True) / cells_all)
    )
    rms_out[1] = jnp.sum(jnp.sqrt(joined[4:5, 0:1] / cells_all))

    gram = big[64:96, 0:32]
    patch_sums = gram[:, 31:32]
    stem_pad[...] = jnp.zeros(stem_pad.shape, F32)
    stem_pad[0 : stem_w.shape[0], :] = stem_w[...].astype(BF16).astype(F32)
    weights = stem_pad[...]
    centred = inverse_one * (hdot(gram, weights) - patch_sums * mean_one)
    d_bias, d_gain = late[27:28, :], late[28:29, :]
    stem_grad = late[0:32, :] - (inverse_one * norm_w[0:1, :] / pixels) * (
        patch_sums * d_bias + centred * d_gain
    )
    lamb_step(stem_w[...], stem_grad[0 : stem_w.shape[0]], stem_m[...], stem_s[...], outs[0:3])
    norm_grad = jnp.concatenate([d_gain, d_bias, head_rows[16:18, :]], axis=0)
    lamb_step(norm_w[...], norm_grad, norm_m[...], norm_s[...], outs[3:6], rows=True)

    ell = len_w[...].reshape(1, width)
    z_pad[...] = jnp.zeros(z_pad.shape, F32)
    z_pad[0:size, :] = ind_w[...] / ell
    zs = z_pad[...]
    kzz, factor, inverse = chol[0], chol[1], chol[2]
    line = lax.broadcasted_iota(jnp.int32, (IND, IND), 0)
    lane = lax.broadcasted_iota(jnp.int32, (IND, IND), 1)
    g_chol = jnp.where(line >= lane, -big[32:64, 384 : 384 + IND], 0.0)
    lower = hdot(factor, g_chol, ((0,), (0,)))
    phi = jnp.where(line > lane, lower, jnp.where(line == lane, 0.5 * lower, 0.0))
    back = hdot(inverse, hdot(phi, inverse), ((0,), (0,)))
    back_t = hdot(inverse, hdot(phi, inverse, ((0,), (0,))), ((0,), (0,)))
    weights_z = -0.5 * kzz * (back + back_t)
    g_z = big[0:32, :]
    g_z = jnp.where(lax.broadcasted_iota(jnp.int32, (IND, 1), 0) < size, g_z, 0.0) + 2.0 * (
        zs * jnp.sum(weights_z, axis=1, keepdims=True) - hdot(weights_z, zs)
    )
    lamb_step(ind_w[...], (g_z / ell)[0:size], ind_m[...], ind_s[...], outs[6:9])
    g_len = -(big[20:21, :] + jnp.sum(g_z * zs, axis=0, keepdims=True)) / ell
    lamb_step(ell, g_len, len_m[...].reshape(1, width), len_s[...].reshape(1, width), outs[9:12])

    means = mean_w[...]
    g_mean = big[32 : 32 + classes, 512 : 512 + size] + means * scale
    lamb_step(means, g_mean, mean_m[...], mean_s[...], outs[12:15])
    small_line = lax.broadcasted_iota(jnp.int32, (size, size), 0)
    small_lane = lax.broadcasted_iota(jnp.int32, (size, size), 1)
    kl = 0.5 * jnp.sum(means * means, axis=0, keepdims=True)
    weight_sq = jnp.zeros((1, size), F32)
    step_sq = weight_sq
    steps = []
    for c in range(classes):
        weight = low_w[c]
        factors = scale_rows(weight)
        inner = big[32 : 32 + size, c * IND : c * IND + size] + factors * scale
        grad = jnp.where(
            small_line > small_lane, inner,
            jnp.where(small_line == small_lane, factors * inner - scale, 0.0),
        )
        new_one, new_two, direction = lamb_moments(weight, grad, low_m[c], low_s[c])
        outs[16][c] = new_one
        outs[17][c] = new_two
        weight_sq = weight_sq + jnp.sum(weight * weight, axis=0, keepdims=True)
        step_sq = step_sq + jnp.sum(direction * direction, axis=0, keepdims=True)
        diagonal = jnp.where(small_line == small_lane, weight, 0.0)
        kl = kl + jnp.sum(0.5 * factors * factors - diagonal, axis=0, keepdims=True)
        steps.append(direction)
    ratio = RATE * jnp.sqrt(jnp.sum(weight_sq, axis=1, keepdims=True)) / jnp.sqrt(
        jnp.sum(step_sq, axis=1, keepdims=True)
    )
    for c in range(classes):
        outs[15][c] = low_w[c] - ratio * steps[c]
    kl = jnp.sum(kl, axis=1, keepdims=True) - 0.5 * classes * size
    parts_out[0] = jnp.sum(big[23:24, 0:1] + kl)


def staged(body, n_in, n_out, n_first, n_last, *refs):
    first, refs = refs[:n_first], refs[n_first:]
    ins, refs = refs[:n_in], refs[n_in:]
    outs, refs = refs[:n_out], refs[n_out:]
    last, refs = refs[:n_last], refs[n_last:]
    held, refs = refs[:n_in], refs[n_in:]
    made, refs = refs[:n_out], refs[n_out:]
    scratch, (sem_in, sem_out) = refs[:-2], refs[-2:]
    loads = [
        pltpu.make_async_copy(ref, held[i], sem_in.at[i]) for i, ref in enumerate(ins)
    ]
    for copy in loads:
        copy.start()
    stores = [
        pltpu.make_async_copy(made[i], ref, sem_out.at[i]) for i, ref in enumerate(outs)
    ]
    done = 0
    for ready, finished, step in body(*first, *held, *made, *last, *scratch):
        for copy in loads[done:ready]:
            copy.wait()
        done = ready
        step()
        for copy in stores[finished]:
            copy.start()
    for copy in stores:
        copy.wait()


def local_call(body, first, ins, outs, last, scratch):
    sem = pltpu.SemaphoreType.DMA
    return pl.pallas_call(
        functools.partial(staged, body, len(ins), len(outs), len(first), len(last)),
        out_shape=tuple(outs) + tuple(last),
        in_specs=[SMEM] * len(first) + [ANY] * len(ins),
        out_specs=(ANY,) * len(outs) + (SMEM,) * len(last),
        scratch_shapes=[
            *[pltpu.VMEM(a.shape, a.dtype) for a in ins],
            *[pltpu.VMEM(o.shape, o.dtype) for o in outs],
            *scratch,
            sem((len(ins),)),
            sem((len(outs),)),
        ],
        compiler_params=pltpu.CompilerParams(vmem_limit_bytes=60 << 20),
    )(*first, *ins)


def update_small(ratio, *ins):
    shape = jax.ShapeDtypeStruct
    conv, params = ins[0], ins[10:28:3]
    width = params[0].shape[1]
    outs = [shape(conv.shape, F32)] * 3 + [shape(conv.shape, BF16)]
    outs += [shape(p.shape, F32) for p in params for _ in range(3)]
    return local_call(
        small_kernel, [ratio], ins, outs, [shape((2,), F32)] * 3,
        [pltpu.VMEM((IND, width), F32), pltpu.VMEM((32, width), F32)],
    )


def tally_kernel(n_dp, n_rep, *refs):
    ins, refs = refs[:10], refs[10:]
    grad_out, out, ratio, late_out = refs[:4]
    held, refs = refs[4:14], refs[14:]
    flat, own, tally, ex_a, ex_b, one_b, planes, made = refs[:8]
    a_send, a_recv, b_send, b_recv, sem_in, sem_out = refs[8:14]
    half = n_dp // 2
    dp, rep = lax.axis_index("dp"), lax.axis_index("replica")
    greeted = greet(n_dp, n_rep)
    loads = [pltpu.make_async_copy(ref, held[i], sem_in.at[i]) for i, ref in enumerate(ins)]
    later = (0, 2, 3)
    for i in (1, 4, 6, 7, 8, 9, 5) + later:
        loads[i].start()
    for i in (1, 4, 6, 7, 8, 9, 5):
        loads[i].wait()

    def arrived():
        for i in later:
            loads[i].wait()

    part, conv_w, conv_m, conv_s, start, sums, head_rows, stats, norm_w, late = held
    greeted()
    late_sum = Reduce(
        ("dp", n_dp), ("replica", n_rep), None, None, late, planes, made, (None, None) + refs[14:]
    )
    late_sum.across()
    conv_gradient(dp < half, part, arrived, conv_w, start, head_rows, stats, norm_w, flat, own)
    store = pltpu.make_async_copy(flat, grad_out, sem_out.at[0])
    store.start()
    weight = conv_w[...]
    direction = lamb_moments(weight, flat[...], conv_m[...], conv_s[...])[2]
    lanes = stats.shape[1] // 128
    tally[...] = jnp.zeros(tally.shape, F32)
    tally[0:1, :] = jnp.sum(weight * weight, axis=0, keepdims=True)
    tally[1:2, :] = jnp.sum(direction * direction, axis=0, keepdims=True)
    tally[2:3, :] = total([sums[0:1, k * 128 : (k + 1) * 128] for k in range(lanes)])
    ex_a[dp] = tally[...]
    first = Spread("dp", n_dp, tally, ex_a, a_send, a_recv)
    first.start()
    late_sum.last()
    first.wait()
    one_b[...] = jnp.zeros(one_b.shape, F32)
    for l in range(2):
        near = range(l * half, (l + 1) * half)
        one_b[l : l + 1, :] = total([ex_a[i, 0:1, :] for i in near])
        one_b[2 + l : 3 + l, :] = total([ex_a[i, 1:2, :] for i in near])
    one_b[4:5, :] = total(rows_of(ex_a, 2))
    ex_b[rep] = one_b[...]
    second = Spread("replica", n_rep, one_b, ex_b, b_send, b_recv)
    second.start()
    late_sum.finish_last()
    per = made.shape[1]
    for k in range(32):
        late_out[k : k + 1, :] = made[k // per, k % per : k % per + 1, :]
    second.wait()
    joined = jnp.sum(total([ex_b[i] for i in range(n_rep)]), axis=1, keepdims=True)
    out[...] = jnp.zeros(out.shape, F32) + joined
    trust = jnp.sqrt(joined[0:2]) / jnp.sqrt(joined[2:4])
    ratio[0] = RATE * jnp.sum(jnp.where(dp < half, trust[0:1], trust[1:2]))
    first.drain()
    second.drain()
    store.wait()


def join_tally(n_dp, n_rep, *ins):
    sem = pltpu.SemaphoreType.DMA
    shape = jax.ShapeDtypeStruct
    part, conv, late = ins[0], ins[1], ins[9]
    return pl.pallas_call(
        functools.partial(tally_kernel, n_dp, n_rep),
        out_shape=(
            shape(conv.shape, F32), shape((8, 128), F32), shape((1,), F32),
            shape((32, late.shape[1]), F32),
        ),
        in_specs=[ANY] * 10,
        out_specs=(ANY, VMEM, SMEM, VMEM),
        scratch_shapes=[
            *[pltpu.VMEM(a.shape, a.dtype) for a in ins],
            pltpu.VMEM(conv.shape, F32),
            pltpu.VMEM(part.shape, F32),
            pltpu.VMEM((8, 128), F32),
            pltpu.VMEM((n_dp, 8, 128), F32),
            pltpu.VMEM((n_rep, 8, 128), F32),
            pltpu.VMEM((8, 128), F32),
            pltpu.VMEM((n_rep, *late.shape), F32),
            pltpu.VMEM((n_dp, *late.shape), F32),
            sem((n_dp,)), sem((n_dp,)), sem((n_rep,)), sem((n_rep,)),
            sem((10,)), sem((1,)),
            sem((n_rep,)), sem((n_rep,)), sem((n_dp,)), sem((n_dp,)),
        ],
        compiler_params=pltpu.CompilerParams(
            collective_id=3, has_side_effects=True, vmem_limit_bytes=60 << 20
        ),
    )(*ins)


def on_device(
    images, labels, counts, noise_table, noise_index, power_start,
    conv_weight, conv_first, conv_second,
    stem_weight, stem_first, stem_second,
    norm_params, norm_first, norm_second,
    inducing, inducing_first, inducing_second,
    lengthscale, length_first, length_second,
    var_mean, mean_first, mean_second,
    var_lower, lower_first, lower_second,
):
    width = stem_weight.shape[1]
    side = images.shape[2]
    cells = side * side
    n_dp, n_rep = lax.axis_size("dp"), lax.axis_size("replica")
    here = lax.axis_index(AXES)
    per_kernel = n_dp * n_rep // 2
    owner = here // per_kernel
    select = (jnp.arange(2) == owner).astype(F32)
    geometry = (n_dp, n_rep, side)

    share = conv_weight.shape[0] // width
    wide = (-1, 128)
    fused = share % 16 == 8 and n_rep == 4 and n_dp == 8
    if fused:
        weights, extra = conv_weight.reshape(wide), power_start
    else:
        rows = conv_weight.astype(BF16).reshape(-1, width)
        gathered = lax.all_gather(rows, AXES, axis=0, tiled=True)
        weights = gathered[: 9 * width]
        own = rows.astype(F32)
        start = jnp.sum(select[:, None] * power_start, axis=0)
        own_along = jnp.sum(own * start, axis=1)
        back_rows = jnp.sum(own * own_along[:, None], axis=0)
        extra = jnp.stack([back_rows, jnp.full((width,), jnp.sum(own_along * own_along))])
    (
        k_one, k_two, act_one, raw_one, slope, act_two, windows, stem_pool, stats, patches, stem_kernel,
        chol, *prepared,
    ) = forward(
        *geometry, share, fused, counts, noise_index, weights, images, stem_weight, extra,
        norm_params, noise_table.T, inducing, lengthscale, var_mean, var_lower,
    )
    if not fused:
        k_two = gathered[9 * width :]
    d_one, k8, head_rows, grads = head(
        *geometry, inducing.shape[0], var_mean.shape[0], noise_index.shape[1], counts, labels,
        k_two, raw_one, slope, windows, stem_pool, stats, norm_params, lengthscale, chol, *prepared,
    )
    part, big, sums, late = backward(
        *geometry, share, fused, counts, d_one, act_one, k_one, k8, act_two, patches, stem_kernel, stats, norm_params, windows,
        head_rows, grads,
    )
    if not fused:
        part_one = lax.psum_scatter(
            jnp.concatenate([part.reshape(-1), jnp.zeros((part.size,), F32)]),
            AXES, scatter_dimension=0, tiled=True,
        ).reshape(-1, width)
        all_windows, all_grads = lax.all_gather(
            (windows[:, :9], head_rows[8 : 8 + images.shape[0]]), AXES, tiled=True
        )
        all_windows = all_windows.reshape(all_windows.shape[0], -1)
        mine = lax.dynamic_slice_in_dim(
            all_windows, lax.rem(here, per_kernel) * share, share, axis=1
        )
        part = jnp.where(owner == 0, part_one, jnp.dot(mine.T, all_grads, precision=HIGH))

    conv = [v.reshape(wide) for v in (conv_weight, conv_first, conv_second)]
    conv_grad, joined, ratio, late = join_tally(
        n_dp, n_rep, part, *conv, power_start, sums, head_rows, stats, norm_params, late
    )
    done = update_small(
        ratio, conv_grad, *conv, big, late, joined, head_rows, stats, chol,
        stem_weight, stem_first, stem_second, norm_params, norm_first, norm_second,
        inducing, inducing_first, inducing_second, lengthscale, length_first, length_second,
        var_mean, mean_first, mean_second, var_lower, lower_first, lower_second,
    )
    loss_parts, sigmas, rms = done[22:]
    return (loss_parts, *[v.reshape(-1) for v in done[:4]], *done[4:22], sigmas, rms)


def solution(mesh):
    split = P(AXES)
    return jax.shard_map(
        on_device,
        mesh=mesh,
        in_specs=(split, split, split, P(), split, P(), split, split, split) + (P(),) * 18,
        out_specs=(P(),) + (split,) * 4 + (P(),) * 20,
        check_vma=False,
    )
```
